32 devices in a mesh: seq: 8 (over z, x), exp: 4 (over y, core).
Axes of the slice: x: 2, y: 2, z: 4, core: 2. Of those that a mesh axis runs over, the one named last changes fastest.
Arguments:
- x_in: bfloat16 [512, 8192], P('seq', 'exp'), may hold values from -6 to 6
- z_in: bfloat16 [512, 8192], P('seq', 'exp'), may hold values from -6 to 6
- conv_weight: float32 [4, 8192], P(None, 'exp'), may hold values from -3 to 3
- conv_bias: float32 [8192], P('exp'), may hold values from -3 to 3
- x_proj: bfloat16 [8192, 544], P('exp'), may hold values from -0.0625 to 0.0625
- dt_proj: bfloat16 [512, 8192], P(None, 'exp'), may hold values from -0.25 to 0.25
- dt_bias: float32 [8192], P('exp'), may hold values from -7 to -2.3
- a_log: float32 [8192, 16], P('exp'), may hold values from -6 to 0
- d_skip: float32 [8192], P('exp'), may hold values from 0.5 to 1.5
- out_proj: bfloat16 [8192, 4096], P('exp', 'seq'), may hold values from -0.0625 to 0.0625
- resid: bfloat16 [512, 4096], P('seq', 'exp'), may hold values from -8 to 8
- norm_gain: float32 [4096], replicated, may hold values from 0.5 to 1.5
- routes: int32 [512, 2], P('seq'), may hold values from 0 to 3, all different within a row; in each aligned block of 64 rows (0 to 63, 64 to 127, ...) at most 34 rows name the same one
- route_gate: float32 [512, 2], P('seq'), may hold values from 0.1 to 0.9
- w_gate: bfloat16 [4, 4096, 12288], P('exp', None, 'seq'), may hold values from -0.09375 to 0.09375
- w_up: bfloat16 [4, 4096, 12288], P('exp', None, 'seq'), may hold values from -0.09375 to 0.09375
- w_down: bfloat16 [4, 12288, 4096], P('exp', 'seq'), may hold values from -0.078125 to 0.078125
Outputs:
- layer_out: bfloat16 [512, 4096], P('seq', 'exp')
The draws below stay inside these ranges and needn't reach their ends.
Inputs may be any that keep to these rules, and one draw needn't show every extreme that they name: `routes`: the 2 experts of a position differ; among the 64 positions of one index of seq no expert is named more than 34 times, and in some such block one expert is named exactly 34 times.
All inputs are finite; a program needn't handle non-finite values.
Results may differ from the reference program's by a relative error of at most 0.008.
Values may be sent and summed in bfloat16 or wider, within the bound.
No kernel may reach another device: no remote copies, remote signals or barrier semaphores. Data moves between devices by JAX's collectives and lax.ppermute only.
A program may use at most 128 MiB of HBM per device.

```python
import math
import jax
import jax.numpy as jnp
import numpy as np
from jax import lax

D = 4096
INNER = 8192
NS = 16
KC = 4
R = 512
FF = 12288
TOP = 2
TOK_DEV = 64
EXPERTS = 4
SEQLEN = 512
CAP = 34
N_SEQ = 8


def draw_resid(key, part):
    columns = jnp.arange(D, dtype=jnp.float32) / D
    values = jnp.clip(jax.random.normal(key, (SEQLEN, D), jnp.float32), -2.5, 2.5)
    scales = 0.5 + 2.5 * columns
    return (values * scales[None, :]).astype(jnp.bfloat16)


def spiked(values, rng, source, target, parts, factor):
    owner, partner = [(jnp.arange(values.shape[dim]) // (values.shape[dim] // parts)).reshape([-1 if axis == dim else 1 for axis in range(values.ndim)]) for dim in (source, target)]
    chosen = jax.random.permutation(rng, parts)[partner]
    strong = (owner == chosen) | (owner == (partner + parts // 2) % parts)
    return jnp.where(strong, factor * values, values)


def shard_levels(stream_key, dims, split, least, high):
    def one(axis_at, shards_of):
        draws = jax.random.uniform(jax.random.fold_in(jax.random.fold_in(stream_key, 6), axis_at), (shards_of,), jnp.float32, least / len(split), high / len(split))
        return jnp.repeat(jnp.exp(draws), dims[axis_at] // shards_of).reshape((-1,) + (1,) * (len(dims) - axis_at - 1))

    loudness = one(*split[0])
    for cut in split[1:]:
        loudness = loudness * one(*cut)
    return loudness


def shared_out(key, own, number, rows, count, top, bound, skew):
    sequence = jax.random.permutation(key, count)
    packed, common = portions_of(count, rows * top, bound, skew, True), portions_of(count, rows * top, bound, skew, False)
    places = jnp.arange(count)

    def named(tallies, rotation):
        used = int((tallies > 0).sum())
        fixed = max(1, used // 4)
        passed = fixed + (places - fixed + rotation * (used - fixed)) % max(1, count - fixed)
        return jnp.zeros((count,), jnp.int32).at[sequence[jnp.where(places < fixed, places, passed)]].set(jnp.asarray(tallies, jnp.int32))

    tallies = jnp.where(number % 4 == 0, named(packed, number // 4), named(common, number - number // 4 - 1))
    mixed = jax.random.permutation(jax.random.fold_in(own, 3), count)
    source_of, receiver = mixed[0:count // 2 * 2:2], mixed[1:count // 2 * 2:2]
    room = jnp.minimum(tallies[source_of] - 1, bound - tallies[receiver]) // 2
    room = jnp.where((source_of == sequence[0]) | (receiver == sequence[0]) | (tallies[receiver] == 0), 0, jnp.maximum(room, 0))
    passed = jax.random.randint(jax.random.fold_in(own, 4), (count // 2,), 0, 1 << 20) % (room + 1)
    tallies = tallies.at[source_of].add(-passed).at[receiver].add(passed)
    items = jnp.searchsorted(jnp.cumsum(tallies), jnp.arange(rows * top), side="right").astype(jnp.int32)
    table = items.reshape(top, rows).T
    table = table[jax.random.permutation(jax.random.fold_in(own, 1), rows)]
    rotation = jax.random.randint(jax.random.fold_in(own, 2), (rows, 1), 0, top)
    return jnp.take_along_axis(table, (jnp.arange(top)[None, :] + rotation) % top, axis=1)


def portions_of(count, total, most, lean, full):
    weights = [(1 << 20) // math.isqrt(rank ** lean) + 1 for rank in range(1, count + 1)]
    largest = most if full else min(most, max(-(-total // count), total * weights[0] // sum(weights)))
    least = 1 if total - largest >= count - 1 else 0
    counts, spare = [largest] + [least] * (count - 1), total - largest - least * (count - 1)
    while spare > 0:
        candidates = [i for i in range(1, count) if counts[i] < largest] or [i for i in range(1, count) if counts[i] < most]
        mass, remaining = sum([weights[i] for i in candidates]), spare
        for i in candidates:
            extra = min(most - counts[i], max(1, remaining * weights[i] // mass), spare)
            counts[i] = counts[i] + extra
            spare = spare - extra
    return np.array(counts)


def bell_draw(key, extent, width, reach, shards=(), kind=jnp.bfloat16):
    array = width * jax.random.normal(key, extent, jnp.float32)
    if shards:
        array = array * shard_levels(key, extent, shards, -0.22, 0.18)
    return jnp.clip(array, -reach, reach).astype(kind)


def noise_with(stream_key, dims, deviation, bound, split, heavy, held_as=jnp.bfloat16):
    entries = deviation * jax.random.normal(stream_key, dims, jnp.float32)
    if split:
        entries = entries * shard_levels(stream_key, dims, split, -0.22, 0.18)
    return jnp.clip(spiked(entries, jax.random.fold_in(stream_key, 3), *heavy), -bound, bound).astype(held_as)


def setup_inputs(seed: int = 0) -> dict:
    streams_of = jax.random.split(jax.random.key(seed), 18)
    x_in = bell_draw(streams_of[0], (SEQLEN, INNER), 1.0, 6.0, ((0, 8), (1, 4)))
    z_in = bell_draw(streams_of[1], (SEQLEN, INNER), 1.0, 6.0, ((0, 8), (1, 4)))
    conv_weight = bell_draw(streams_of[2], (KC, INNER), KC ** -0.5, 3.0, ((1, 4),), jnp.float32)
    conv_bias = bell_draw(streams_of[3], (INNER,), 0.5, 3.0, ((0, 4),), jnp.float32)
    x_proj = bell_draw(streams_of[4], (INNER, R + 2 * NS), INNER ** -0.5, 0.0625, ((0, 4),))
    dt_proj = bell_draw(streams_of[5], (R, INNER), R ** -0.5, 0.25, ((1, 4),))
    dt_bias = jnp.clip(-7.0 + 4.7 * jax.random.uniform(streams_of[6], (INNER,), jnp.float32) ** shard_levels(streams_of[6], (INNER,), ((0, 4),), -0.2, 0.2), -7.0, -2.3)
    a_log = jnp.clip(-6.0 + 6.0 * jax.random.uniform(streams_of[7], (INNER, NS), jnp.float32) ** shard_levels(streams_of[7], (INNER, NS), ((0, 4),), -0.2, 0.2), -6.0, 0.0)
    d_skip = jnp.clip(0.5 + 1.0 * jax.random.uniform(streams_of[8], (INNER,), jnp.float32) ** shard_levels(streams_of[8], (INNER,), ((0, 4),), -0.2, 0.2), 0.5, 1.5)
    out_proj = bell_draw(streams_of[9], (INNER, D), INNER ** -0.5, 0.0625, ((0, 4), (1, 8)))
    resid = draw_resid(jax.random.fold_in(streams_of[17], 71), 0)
    norm_gain = jnp.clip(1.0 + 0.1 * jax.random.normal(streams_of[11], (D,), jnp.float32), 0.5, 1.5)
    routes_keys = jax.random.split(jax.random.fold_in(streams_of[12], 1), SEQLEN // TOK_DEV)
    routes_turns = jax.random.permutation(jax.random.fold_in(streams_of[12], 3), SEQLEN // TOK_DEV)
    routes = jax.vmap(lambda own, number: shared_out(jax.random.fold_in(streams_of[12], 2), own, number, TOK_DEV, EXPERTS, TOP, CAP, 1))(routes_keys, routes_turns).reshape((SEQLEN, TOP))
    route_gate = jnp.clip(0.1 + 0.79999997 * jax.random.uniform(streams_of[13], (SEQLEN, TOP), jnp.float32) ** shard_levels(streams_of[13], (SEQLEN, TOP), ((0, 8),), -0.2, 0.2), 0.1, 0.9)
    w_gate = bell_draw(streams_of[14], (EXPERTS, D, FF), D ** -0.5, 0.09375, ((0, 4), (2, 8)))
    w_up = bell_draw(streams_of[15], (EXPERTS, D, FF), D ** -0.5, 0.09375, ((0, 4), (2, 8)))
    w_down = noise_with(streams_of[16], (EXPERTS, FF, D), FF ** -0.5, 0.078125, ((0, 4), (1, 8)), (1, 2, 8, 2.0))
    return {"x_in": x_in, "z_in": z_in, "conv_weight": conv_weight, "conv_bias": conv_bias, "x_proj": x_proj, "dt_proj": dt_proj, "dt_bias": dt_bias, "a_log": a_log, "d_skip": d_skip, "out_proj": out_proj, "resid": resid, "norm_gain": norm_gain, "routes": routes, "route_gate": route_gate, "w_gate": w_gate, "w_up": w_up, "w_down": w_down}


eps = 1e-05

def reference(x_in, z_in, conv_weight, conv_bias, x_proj, dt_proj, dt_bias, a_log, d_skip, out_proj, resid, norm_gain, routes, route_gate, w_gate, w_up, w_down):
    length = x_in.shape[0]
    padded = jnp.concatenate([jnp.zeros((KC - 1, INNER), x_in.dtype), x_in], axis=0).astype(jnp.float32)
    conv = jnp.zeros((length, INNER), jnp.float32) + conv_bias[None, :]
    for tap in range(KC):
        conv = conv + conv_weight[tap][None, :] * padded[tap:tap + length]
    xconv = jax.nn.silu(conv).astype(jnp.bfloat16)
    projected = jnp.dot(xconv, x_proj, preferred_element_type=jnp.float32)
    dt_low = projected[:, :R].astype(jnp.bfloat16)
    b_mat = projected[:, R:R + NS]
    c_mat = projected[:, R + NS:]
    step_size = jax.nn.softplus(jnp.dot(dt_low, dt_proj, preferred_element_type=jnp.float32) + dt_bias[None, :])
    rates = -jnp.exp(a_log)
    xconv_f = xconv.astype(jnp.float32)

    def advance(state, inputs):
        size_now, input_now, b_now, c_now = inputs
        state = jnp.exp(size_now[:, None] * rates) * state + (size_now * input_now)[:, None] * b_now[None, :]
        return (state, lax.optimization_barrier(jnp.sum(state * c_now[None, :], axis=1)))
    final_state, scanned = lax.scan(advance, jnp.zeros((INNER, NS), jnp.float32), (step_size, xconv_f, b_mat, c_mat))
    scanned = scanned + d_skip[None, :] * xconv_f
    mixed = (scanned * jax.nn.silu(z_in.astype(jnp.float32))).astype(jnp.bfloat16)
    mamba_out = jnp.dot(mixed, out_proj, preferred_element_type=jnp.float32)
    hidden_state = (resid.astype(jnp.float32) + mamba_out).astype(jnp.bfloat16)
    hidden_f = hidden_state.astype(jnp.float32)
    scale = lax.rsqrt(lax.optimization_barrier(jnp.mean(hidden_f * hidden_f, axis=1)) + eps)
    normed = (hidden_f * scale[:, None] * norm_gain[None, :]).astype(jnp.bfloat16)
    blocks = length // TOK_DEV
    flat = routes.reshape(blocks, TOK_DEV * TOP)
    onehot = (flat[:, :, None] == jnp.arange(EXPERTS, dtype=jnp.int32)[None, None, :]).astype(jnp.int32)
    slots = lax.optimization_barrier(jnp.sum((jnp.cumsum(onehot, axis=1) - 1) * onehot, axis=2))
    block_ids = jnp.arange(blocks, dtype=jnp.int32)[:, None]
    target = (flat * (blocks * CAP) + block_ids * CAP + slots).reshape(-1).astype(jnp.int32)
    token_ids = jnp.repeat(jnp.arange(length, dtype=jnp.int32), TOP)
    buffer = jnp.zeros((EXPERTS * blocks * CAP, D), jnp.bfloat16).at[target].set(normed[token_ids])
    buffer = buffer.reshape(EXPERTS, blocks * CAP, D)
    width_block = FF // N_SEQ

    def one_expert(items):
        rows_e, gate_e, up_e, down_e = items
        gate = jnp.dot(rows_e, gate_e, preferred_element_type=jnp.float32)
        upper = jnp.dot(rows_e, up_e, preferred_element_type=jnp.float32)
        act = (jax.nn.silu(gate) * upper).astype(jnp.bfloat16)
        act_blocks = act.reshape(rows_e.shape[0], N_SEQ, width_block).transpose(1, 0, 2)
        down_blocks = down_e.reshape(N_SEQ, width_block, D)

        def add_block(total, pair):
            act_piece, down_piece = pair
            part = jnp.dot(act_piece, down_piece, preferred_element_type=jnp.float32).astype(jnp.bfloat16)
            part = lax.optimization_barrier(part)
            return (total + part.astype(jnp.float32), None)
        total, unused_out = lax.scan(add_block, jnp.zeros((rows_e.shape[0], D), jnp.float32), (act_blocks, down_blocks))
        return total.astype(jnp.bfloat16)
    expert_out = lax.map(one_expert, (buffer, w_gate, w_up, w_down))
    picked = expert_out.reshape(-1, D)[target].reshape(length, TOP, D).astype(jnp.float32)
    moe = lax.optimization_barrier(jnp.sum(route_gate[:, :, None] * picked, axis=1))
    return (hidden_f + moe).astype(jnp.bfloat16)
```

```python
import functools
import math

import jax
import jax.numpy as jnp
from jax import lax
from jax.experimental import pallas as pl
from jax.experimental.pallas import tpu as pltpu
from jax.sharding import PartitionSpec as P

eps = 1e-05
LOG2E = 1.4426950408889634
MIB = 1 << 20


def tile_of(size, most=512):
    return max(t for t in range(128, most + 1, 128) if size % t == 0)


def whole_vmem():
    return pl.BlockSpec(memory_space=pltpu.VMEM)


def whole_smem():
    return pl.BlockSpec(memory_space=pltpu.SMEM)


def conv_kernel(x_ref, halo_ref, weight_ref, bias_ref, proj_ref, xconv_ref, partial_ref):
    rows = x_ref.shape[0]
    taps = weight_ref.shape[0]
    extended = jnp.concatenate(
        [halo_ref[...].astype(jnp.float32), x_ref[...].astype(jnp.float32)], axis=0
    )
    pad = halo_ref.shape[0]
    conv = jnp.zeros(x_ref.shape, jnp.float32) + bias_ref[...]
    for tap in range(taps):
        start = pad - (taps - 1) + tap
        conv = conv + weight_ref[tap : tap + 1, :] * extended[start : start + rows]
    xconv = (conv / (1.0 + jnp.exp(-conv))).astype(jnp.bfloat16)
    xconv_ref[...] = xconv

    @pl.when(pl.program_id(0) == 0)
    def _():
        partial_ref[...] = jnp.zeros_like(partial_ref)

    partial_ref[...] += jnp.dot(xconv, proj_ref[...], preferred_element_type=jnp.float32)


def conv_and_project(x_in, halo, conv_weight, conv_bias, x_proj):
    rows, channels = x_in.shape
    width = tile_of(channels)
    columns = x_proj.shape[1]
    return pl.pallas_call(
        conv_kernel,
        grid=(channels // width,),
        in_specs=[
            pl.BlockSpec((rows, width), lambda i: (0, i)),
            pl.BlockSpec((halo.shape[0], width), lambda i: (0, i)),
            pl.BlockSpec((conv_weight.shape[0], width), lambda i: (0, i)),
            pl.BlockSpec((1, width), lambda i: (0, i)),
            pl.BlockSpec((width, columns), lambda i: (i, 0)),
        ],
        out_specs=[
            pl.BlockSpec((rows, width), lambda i: (0, i)),
            pl.BlockSpec((rows, columns), lambda i: (0, 0)),
        ],
        out_shape=[
            jax.ShapeDtypeStruct((rows, channels), jnp.bfloat16),
            jax.ShapeDtypeStruct((rows, columns), jnp.float32),
        ],
        name="conv_project",
    )(x_in, halo, conv_weight, conv_bias, x_proj)


def softplus(v):
    return jnp.maximum(v, 0.0) + jnp.log1p(jnp.exp(-jnp.abs(v)))


def ends_kernel(low_ref, proj_ref, bias_ref, rate_ref, x_ref, b_ref, size_ref, load_ref, drive_ref):
    rows, width = x_ref.shape
    states = rate_ref.shape[0]
    groups = width // 128
    size = softplus(
        jnp.dot(low_ref[...], proj_ref[...], preferred_element_type=jnp.float32) + bias_ref[...]
    )
    size_ref[...] = size
    drive_ref[...] = size * x_ref[...].astype(jnp.float32)
    rates = rate_ref[...]

    def step(block, state):
        start = pl.multiple_of(block * 8, 8)
        sizes = size_ref[pl.ds(start, 8), :]
        drives = drive_ref[pl.ds(start, 8), :]
        state = list(state)
        for i in range(8):
            b_now = b_ref[start + i]
            for g in range(groups):
                lanes = slice(g * 128, g * 128 + 128)
                decay = jnp.exp2(sizes[i : i + 1, lanes] * rates[:, lanes])
                state[g] = decay * state[g] + drives[i : i + 1, lanes] * b_now
        return tuple(state)

    zero = jnp.zeros((states, 128), jnp.float32)
    state = lax.fori_loop(0, rows // 8, step, (zero,) * groups)
    total = jnp.sum(size, axis=0, keepdims=True)
    high = total.astype(jnp.bfloat16).astype(jnp.float32)
    low = total - high
    rest = jnp.zeros((load_ref.shape[0] - states - 2, width), jnp.float32)
    load_ref[...] = jnp.concatenate(
        [jnp.concatenate(state, axis=1), high, low, rest], axis=0
    ).astype(jnp.bfloat16)


def scan_ends(dt_low, dt_proj, dt_bias, rates, xconv, b_wide):
    rows, channels = xconv.shape
    states = rates.shape[0]
    width = tile_of(channels)
    load_rows = -(-(states + 2) // 16) * 16
    return pl.pallas_call(
        ends_kernel,
        grid=(channels // width,),
        in_specs=[
            pl.BlockSpec(dt_low.shape, lambda i: (0, 0)),
            pl.BlockSpec((dt_proj.shape[0], width), lambda i: (0, i)),
            pl.BlockSpec((1, width), lambda i: (0, i)),
            pl.BlockSpec((states, width), lambda i: (0, i)),
            pl.BlockSpec((rows, width), lambda i: (0, i)),
            pl.BlockSpec(b_wide.shape, lambda i: (0, 0, 0)),
        ],
        out_specs=[
            pl.BlockSpec((rows, width), lambda i: (0, i)),
            pl.BlockSpec((load_rows, width), lambda i: (0, i)),
        ],
        out_shape=[
            jax.ShapeDtypeStruct((rows, channels), jnp.float32),
            jax.ShapeDtypeStruct((load_rows, channels), jnp.bfloat16),
        ],
        scratch_shapes=[pltpu.VMEM((rows, width), jnp.float32)],
        name="scan_ends",
    )(dt_low, dt_proj, dt_bias, rates, xconv, b_wide)


def mix_kernel(
    place_ref, load_ref, size_ref, x_ref, z_ref, b_ref, c_ref, rate_ref, skip_ref, out_ref, drive_ref, y_ref
):
    rows, width = x_ref.shape
    states = rate_ref.shape[0]
    groups = width // 128
    rates = rate_ref[...]
    x_f = x_ref[...].astype(jnp.float32)
    drive_ref[...] = size_ref[...] * x_f

    def earlier(j, state):
        block = load_ref[j].astype(jnp.float32)
        total = block[states : states + 1] + block[states + 1 : states + 2]
        return jnp.exp2(total * rates) * state + block[:states]

    incoming = lax.fori_loop(0, place_ref[0], earlier, jnp.zeros((states, width), jnp.float32))

    def step(block, state):
        start = pl.multiple_of(block * 8, 8)
        sizes = size_ref[pl.ds(start, 8), :]
        drives = drive_ref[pl.ds(start, 8), :]
        state = list(state)
        outs = [[None] * 8 for _ in range(groups)]
        for i in range(8):
            b_now = b_ref[start + i]
            c_now = c_ref[start + i]
            for g in range(groups):
                lanes = slice(g * 128, g * 128 + 128)
                decay = jnp.exp2(sizes[i : i + 1, lanes] * rates[:, lanes])
                state[g] = decay * state[g] + drives[i : i + 1, lanes] * b_now
                outs[g][i] = jnp.sum(state[g] * c_now, axis=0, keepdims=True)
        for g in range(groups):
            y_ref[pl.ds(start, 8), g * 128 : g * 128 + 128] = jnp.concatenate(outs[g], axis=0)
        return tuple(state)

    start_state = tuple(incoming[:, g * 128 : g * 128 + 128] for g in range(groups))
    lax.fori_loop(0, rows // 8, step, start_state)
    z_f = z_ref[...].astype(jnp.float32)
    scanned = y_ref[...] + skip_ref[...] * x_f
    out_ref[...] = (scanned * (z_f / (1.0 + jnp.exp(-z_f)))).astype(jnp.bfloat16)


def scan_mix(place, loads, step_size, xconv, z_in, b_wide, c_wide, rates, d_skip):
    rows, channels = xconv.shape
    states = rates.shape[0]
    width = tile_of(channels)

    def by_lane(depth):
        return pl.BlockSpec((depth, width), lambda i: (0, i))

    return pl.pallas_call(
        mix_kernel,
        grid=(channels // width,),
        in_specs=[
            whole_smem(),
            pl.BlockSpec((loads.shape[0], loads.shape[1], width), lambda i: (0, 0, i)),
            by_lane(rows),
            by_lane(rows),
            by_lane(rows),
            pl.BlockSpec(b_wide.shape, lambda i: (0, 0, 0)),
            pl.BlockSpec(c_wide.shape, lambda i: (0, 0, 0)),
            by_lane(states),
            by_lane(1),
        ],
        out_specs=by_lane(rows),
        out_shape=jax.ShapeDtypeStruct((rows, channels), jnp.bfloat16),
        scratch_shapes=[pltpu.VMEM((rows, width), jnp.float32)] * 2,
        name="scan_mix",
    )(place, loads, step_size, xconv, z_in, b_wide, c_wide, rates, d_skip)


def out_kernel(count, order_ref, *refs):
    blocks, weight_ref, out_ref, held_ref = refs[:count], refs[count], refs[count + 1], refs[count + 2]
    rows = blocks[0].shape[0]
    for i in range(count):
        held_ref[pl.ds(pl.multiple_of(order_ref[i] * rows, rows), rows), :] = blocks[i][...]
    out_ref[...] = jnp.dot(
        held_ref[...], weight_ref[...], preferred_element_type=jnp.float32
    ).astype(jnp.bfloat16)


def out_product(order, blocks, weight):
    rows, depth = blocks[0].shape
    count = len(blocks)
    return pl.pallas_call(
        functools.partial(out_kernel, count),
        in_specs=[whole_smem()] + [whole_vmem()] * (count + 1),
        out_specs=whole_vmem(),
        out_shape=jax.ShapeDtypeStruct((count * rows, weight.shape[1]), jnp.bfloat16),
        scratch_shapes=[pltpu.VMEM((count * rows, depth), jnp.bfloat16)],
        compiler_params=pltpu.CompilerParams(vmem_limit_bytes=32 * MIB),
        name="out_product",
    )(order, *blocks, weight)


def hidden_kernel(count, order_ref, place_ref, *refs):
    chunks = refs[:count]
    gain_ref, gate_ref, up_ref, act_ref, own_ref, h_ref, gate_sum, up_sum, squares = refs[count:]
    step = pl.program_id(0)
    rows, depth = h_ref.shape
    columns = gate_sum.shape[1]
    width = tile_of(columns)
    own_rows = own_ref.shape[0]
    for i in range(count):

        @pl.when(step == i)
        def _(i=i):
            h_ref[...] = chunks[i][...].astype(jnp.float32)

    @pl.when(step == 0)
    def _():
        gate_sum[...] = jnp.zeros_like(gate_sum)
        up_sum[...] = jnp.zeros_like(up_sum)
        squares[...] = jnp.zeros_like(squares)

    own_ref[...] = h_ref[pl.ds(pl.multiple_of(place_ref[0] * own_rows, own_rows), own_rows), :]
    h = h_ref[...]
    squares[...] += jnp.sum(h * h, axis=1, keepdims=True)
    scaled = (h * gain_ref[0]).astype(jnp.bfloat16)
    for start in range(0, columns, width):
        at = slice(start, start + width)
        gate_sum[:, at] += jnp.dot(scaled, gate_ref[0, :, at], preferred_element_type=jnp.float32)
        up_sum[:, at] += jnp.dot(scaled, up_ref[0, :, at], preferred_element_type=jnp.float32)

    @pl.when(step == count - 1)
    def _():
        scale = lax.rsqrt(squares[...] / (depth * count) + eps)
        for start in range(0, columns, width):
            at = slice(start, start + width)
            gate = gate_sum[:, at] * scale
            upper = up_sum[:, at] * scale
            act_ref[:, at] = (gate / (1.0 + jnp.exp(-gate)) * upper).astype(jnp.bfloat16)


def expert_hidden(order, place, chunks, gain, w_gate, w_up, own_rows):
    rows, depth = chunks[0].shape
    count = len(chunks)
    columns = w_gate.shape[2]
    gain = gain.reshape(count, 1, depth)
    weight_spec = pl.BlockSpec((1, depth, columns), lambda k, order, place: (0, order[k], 0))
    return pl.pallas_call(
        functools.partial(hidden_kernel, count),
        grid_spec=pltpu.PrefetchScalarGridSpec(
            num_scalar_prefetch=2,
            grid=(count,),
            in_specs=[whole_vmem()] * count
            + [
                pl.BlockSpec((1, 1, depth), lambda k, order, place: (order[k], 0, 0)),
                weight_spec,
                weight_spec,
            ],
            out_specs=[
                pl.BlockSpec((rows, columns), lambda k, order, place: (0, 0)),
                pl.BlockSpec((own_rows, depth), lambda k, order, place: (0, order[k])),
            ],
            scratch_shapes=[
                pltpu.VMEM((rows, depth), jnp.float32),
                pltpu.VMEM((rows, columns), jnp.float32),
                pltpu.VMEM((rows, columns), jnp.float32),
                pltpu.VMEM((rows, 1), jnp.float32),
            ],
        ),
        out_shape=[
            jax.ShapeDtypeStruct((rows, columns), jnp.bfloat16),
            jax.ShapeDtypeStruct((own_rows, depth * count), jnp.float32),
        ],
        compiler_params=pltpu.CompilerParams(vmem_limit_bytes=40 * MIB),
        name="expert_hidden",
    )(order, place, *chunks, gain, w_gate, w_up)


def down_kernel(z_count, x_count, z_ref, x_ref, act_ref, weight_ref, *refs):
    outs, held_ref = refs[:-1], refs[-1]
    held_ref[...] = jnp.dot(act_ref[...], weight_ref[0], preferred_element_type=jnp.float32)
    pitch = outs[0].shape[0]
    for r in range(z_count):
        for i in range(x_count):
            block = lax.rem(z_ref[0] + r, z_count) * x_count + lax.rem(x_ref[0] + i, x_count)
            start = pl.multiple_of(block * pitch, pitch)
            outs[r * x_count + i][...] = held_ref[pl.ds(start, pitch), :].astype(jnp.bfloat16)


def expert_down(z_at, x_at, z_count, x_count, act, w_down):
    rows, depth = act.shape
    columns = w_down.shape[2]
    width = tile_of(columns)
    blocks = z_count * x_count
    pitch = rows // blocks
    outs = pl.pallas_call(
        functools.partial(down_kernel, z_count, x_count),
        grid_spec=pltpu.PrefetchScalarGridSpec(
            num_scalar_prefetch=2,
            grid=(columns // width,),
            in_specs=[
                pl.BlockSpec((rows, depth), lambda n, z, x: (0, 0)),
                pl.BlockSpec((1, depth, width), lambda n, z, x: (0, 0, n)),
            ],
            out_specs=[pl.BlockSpec((pitch, width), lambda n, z, x: (0, n))] * blocks,
            scratch_shapes=[pltpu.VMEM((rows, width), jnp.float32)],
        ),
        out_shape=[jax.ShapeDtypeStruct((pitch, columns), jnp.bfloat16)] * blocks,
        compiler_params=pltpu.CompilerParams(vmem_limit_bytes=32 * MIB),
        name="expert_down",
    )(z_at, x_at, act, w_down)
    return [outs[r * x_count : (r + 1) * x_count] for r in range(z_count)]


def per_device(
    x_in,
    z_in,
    conv_weight,
    conv_bias,
    x_proj,
    dt_proj,
    dt_bias,
    a_log,
    d_skip,
    out_proj,
    resid,
    norm_gain,
    routes,
    route_gate,
    w_gate,
    w_up,
    w_down,
):
    row_count, channels = x_in.shape
    seq_count = lax.axis_size("seq")
    exp_count = lax.axis_size("exp")
    x_count = seq_count // exp_count
    z_count = exp_count
    seq_at = lax.axis_index("seq")
    exp_at = lax.axis_index("exp")
    z_at, x_at = seq_at // x_count, seq_at % x_count
    z_one, x_one = z_at.reshape(1).astype(jnp.int32), x_at.reshape(1).astype(jnp.int32)
    seq_one = seq_at.reshape(1).astype(jnp.int32)
    top_count = routes.shape[1]
    capacity = row_count * top_count * 17 // (16 * exp_count)
    pitch = -(-capacity // 8) * 8
    group_tokens = x_count * row_count
    feature_slice = resid.shape[1]
    column_slice = out_proj.shape[1]

    def from_z(block, r):
        pairs = [
            (((z + r) % z_count) * x_count + x, z * x_count + x)
            for z in range(z_count)
            for x in range(x_count)
        ]
        return lax.ppermute(block, "seq", pairs)

    def from_x(block, i):
        pairs = [
            (z * x_count + (x + i) % x_count, z * x_count + x)
            for z in range(z_count)
            for x in range(x_count)
        ]
        return lax.ppermute(block, "seq", pairs)

    def gathered(block):
        along_z = [block] + [from_z(block, r) for r in range(1, z_count)]
        return [
            held if i == 0 else from_x(held, i) for held in along_z for i in range(x_count)
        ]

    order = jnp.stack(
        [
            ((z_at + r) % z_count) * x_count + (x_at + i) % x_count
            for r in range(z_count)
            for i in range(x_count)
        ]
    ).astype(jnp.int32)

    halo = lax.ppermute(
        x_in[row_count - 8 :], "seq", [(i, i + 1) for i in range(seq_count - 1)]
    )
    routes_all = lax.all_gather(routes, "seq", axis=0, tiled=True)

    resid_parts = []
    resid_cut = resid.reshape(row_count, x_count, column_slice)
    for k in range(x_count):
        piece = lax.dynamic_index_in_dim(resid_cut, (x_at - k) % x_count, 1, keepdims=False)
        pairs = []
        for s in range(seq_count):
            for e in range(exp_count):
                source_s = x_count * e + (s % x_count + k) % x_count
                pairs.append((source_s * exp_count + s // x_count, s * exp_count + e))
        resid_parts.append(lax.ppermute(piece, ("seq", "exp"), pairs))
    resid_stack = jnp.stack(resid_parts + resid_parts)
    resid_here = lax.dynamic_slice_in_dim(
        resid_stack, (x_count - x_at) % x_count, x_count, 0
    ).reshape(group_tokens, column_slice)

    def slots_of(named):
        flat = named.reshape(-1, row_count * top_count)
        onehot = (flat[:, :, None] == jnp.arange(exp_count, dtype=jnp.int32)).astype(jnp.float32)
        below = jnp.tril(jnp.ones((row_count * top_count,) * 2, jnp.float32), -1)
        counts = jnp.einsum("ij,bje->bie", below, onehot)
        slots = jnp.sum(counts * onehot, axis=2).astype(jnp.int32)
        return slots.reshape(-1, row_count, top_count)

    group_routes = lax.dynamic_slice_in_dim(routes_all, exp_at * group_tokens, group_tokens, 0)
    group_routes = group_routes.reshape(x_count, row_count, top_count)
    target = (
        group_routes * (x_count * pitch)
        + jnp.arange(x_count, dtype=jnp.int32)[:, None, None] * pitch
        + slots_of(group_routes)
    ).reshape(group_tokens, top_count)
    slot_ids = jnp.arange(exp_count * x_count * pitch, dtype=jnp.int32)
    dispatch = jnp.sum(
        (target[None, :, :] == slot_ids[:, None, None]).astype(jnp.float32), axis=2
    ).astype(jnp.bfloat16)

    own_slots = slots_of(routes)[0]
    at_slot = (routes == exp_at)[None] & (
        own_slots[None] == jnp.arange(pitch, dtype=jnp.int32)[:, None, None]
    )
    gate_here = jnp.sum(jnp.where(at_slot, route_gate[None], 0.0), axis=(1, 2))[:, None]
    first_here = jnp.sum(at_slot[:, :, 0].astype(jnp.float32), axis=1)[:, None]
    own_target = routes * pitch + own_slots
    back_ids = jnp.arange(exp_count * pitch, dtype=jnp.int32)
    choose = jnp.sum(
        (own_target[:, :, None] == back_ids[None, None, :]).astype(jnp.float32), axis=1
    ).astype(jnp.bfloat16)

    rates = -jnp.exp(a_log.T) * LOG2E
    xconv, partial = conv_and_project(x_in, halo, conv_weight, conv_bias[None], x_proj)
    partials = lax.all_to_all(
        jnp.broadcast_to(partial[None], (exp_count,) + partial.shape), "exp", 0, 0, tiled=True
    )
    projected = jnp.sum(partials, axis=0)
    low_rank = dt_proj.shape[0]
    state_count = a_log.shape[1]
    dt_low = projected[:, :low_rank].astype(jnp.bfloat16)
    b_mat = projected[:, low_rank : low_rank + state_count]
    c_mat = projected[:, low_rank + state_count :]
    b_wide = jnp.broadcast_to(b_mat[:, :, None], b_mat.shape + (128,))
    c_wide = jnp.broadcast_to(c_mat[:, :, None], c_mat.shape + (128,))
    step_size, load = scan_ends(dt_low, dt_proj, dt_bias[None], rates, xconv, b_wide)
    loads = lax.all_to_all(
        jnp.broadcast_to(load[None], (seq_count,) + load.shape), "seq", 0, 0, tiled=True
    )
    mixed = scan_mix(
        seq_one, loads, step_size, xconv, z_in, b_wide, c_wide, rates, d_skip[None]
    )
    partial_out = out_product(order, gathered(mixed), out_proj)
    arrived = lax.all_to_all(
        partial_out.reshape(exp_count, group_tokens, column_slice), "exp", 0, 0, tiled=True
    )
    mamba_out = jnp.sum(arrived.astype(jnp.float32), axis=0)
    hidden_state = (resid_here.astype(jnp.float32) + mamba_out).astype(jnp.bfloat16)

    outgoing = jnp.dot(dispatch, hidden_state, preferred_element_type=jnp.float32)
    outgoing = outgoing.astype(jnp.bfloat16).reshape(exp_count, x_count * pitch, column_slice)
    rows_here = lax.all_to_all(outgoing, "exp", 0, 0, tiled=True)
    rows_here = rows_here.reshape(exp_count * x_count * pitch, column_slice)
    act, own_hidden = expert_hidden(
        order, seq_one, gathered(rows_here), norm_gain, w_gate, w_up, pitch
    )
    down = expert_down(z_one, x_one, z_count, x_count, act, w_down)

    def over_x(r):
        pieces = [down[r][0]] + [
            from_x(down[r][i], x_count - i) for i in range(1, x_count)
        ]
        return functools.reduce(jnp.add, [p.astype(jnp.float32) for p in pieces])

    total = over_x(0)
    for r in range(1, z_count):
        sent = from_z(over_x(r).astype(jnp.bfloat16), z_count - r)
        total = total + sent.astype(jnp.float32)
    expert_out = total.astype(jnp.bfloat16).astype(jnp.float32)
    weighted = (gate_here * expert_out + first_here * own_hidden).astype(jnp.bfloat16)
    weighted = weighted.reshape(pitch, exp_count, feature_slice).transpose(1, 0, 2)
    back = lax.all_to_all(weighted, "exp", 0, 0, tiled=True)
    back = back.reshape(exp_count * pitch, feature_slice)
    return jnp.dot(choose, back, preferred_element_type=jnp.float32).astype(jnp.bfloat16)


def solution(mesh):
    return jax.shard_map(
        per_device,
        mesh=mesh,
        in_specs=(
            P("seq", "exp"),
            P("seq", "exp"),
            P(None, "exp"),
            P("exp"),
            P("exp", None),
            P(None, "exp"),
            P("exp"),
            P("exp", None),
            P("exp"),
            P("exp", "seq"),
            P("seq", "exp"),
            P(),
            P("seq", None),
            P("seq", None),
            P("exp", None, "seq"),
            P("exp", None, "seq"),
            P("exp", "seq", None),
        ),
        out_specs=P("seq", "exp"),
        check_vma=False,
    )
```

```python
import functools
import math

import jax
import jax.numpy as jnp
from jax import lax
from jax.experimental import pallas as pl
from jax.experimental.pallas import tpu as pltpu
from jax.sharding import PartitionSpec as P

eps = 1e-05
LOG2E = 1.4426950408889634
MIB = 1 << 20


def tile_of(size, most=512):
    return max(t for t in range(128, most + 1, 128) if size % t == 0)


def whole_vmem():
    return pl.BlockSpec(memory_space=pltpu.VMEM)


def whole_smem():
    return pl.BlockSpec(memory_space=pltpu.SMEM)


def conv_kernel(x_ref, halo_ref, weight_ref, bias_ref, proj_ref, xconv_ref, partial_ref):
    rows = x_ref.shape[0]
    taps = weight_ref.shape[0]
    extended = jnp.concatenate(
        [halo_ref[...].astype(jnp.float32), x_ref[...].astype(jnp.float32)], axis=0
    )
    pad = halo_ref.shape[0]
    conv = jnp.zeros(x_ref.shape, jnp.float32) + bias_ref[...]
    for tap in range(taps):
        start = pad - (taps - 1) + tap
        conv = conv + weight_ref[tap : tap + 1, :] * extended[start : start + rows]
    xconv = (conv / (1.0 + jnp.exp(-conv))).astype(jnp.bfloat16)
    xconv_ref[...] = xconv

    @pl.when(pl.program_id(0) == 0)
    def _():
        partial_ref[0] = jnp.zeros(partial_ref.shape[1:], jnp.float32)

    partial_ref[0] += lax.dot_general(
        xconv, proj_ref[...], (((1,), (1,)), ((), ())), preferred_element_type=jnp.float32
    )

    @pl.when(pl.program_id(0) == pl.num_programs(0) - 1)
    def _():
        for copy in range(1, partial_ref.shape[0]):
            partial_ref[copy] = partial_ref[0]


def conv_and_project(x_in, halo, conv_weight, conv_bias, x_proj_t, copies):
    rows, channels = x_in.shape
    width = tile_of(channels)
    columns = x_proj_t.shape[0]
    return pl.pallas_call(
        conv_kernel,
        grid=(channels // width,),
        in_specs=[
            pl.BlockSpec((rows, width), lambda i: (0, i)),
            pl.BlockSpec((halo.shape[0], width), lambda i: (0, i)),
            pl.BlockSpec((conv_weight.shape[0], width), lambda i: (0, i)),
            pl.BlockSpec((1, width), lambda i: (0, i)),
            pl.BlockSpec((columns, width), lambda i: (0, i)),
        ],
        out_specs=[
            pl.BlockSpec((rows, width), lambda i: (0, i)),
            pl.BlockSpec((copies, rows, columns), lambda i: (0, 0, 0)),
        ],
        out_shape=[
            jax.ShapeDtypeStruct((rows, channels), jnp.bfloat16),
            jax.ShapeDtypeStruct((copies, rows, columns), jnp.float32),
        ],
        name="conv_project",
    )(x_in, halo, conv_weight, conv_bias, x_proj_t)


def softplus(v):
    return jnp.maximum(v, 0.0) + jnp.log1p(jnp.exp(-jnp.abs(v)))


def ends_kernel(
    part_ref, proj_ref, bias_ref, rate_ref, x_ref, size_ref, load_ref, b_ref, c_ref, low_ref, drive_ref
):
    rows, width = x_ref.shape
    states = rate_ref.shape[0]
    low_rank = low_ref.shape[1]
    groups = width // 128

    @pl.when(pl.program_id(0) == 0)
    def _():
        total = part_ref[0]
        for e in range(1, part_ref.shape[0]):
            total = total + part_ref[e]
        low_ref[...] = total[:, :low_rank].astype(jnp.bfloat16)
        b_mat = total[:, low_rank : low_rank + states]
        c_mat = total[:, low_rank + states : low_rank + 2 * states]
        b_ref[...] = jnp.broadcast_to(b_mat[:, :, None], b_ref.shape)
        c_ref[...] = jnp.broadcast_to(c_mat[:, :, None], c_ref.shape)

    size = softplus(
        jnp.dot(low_ref[...], proj_ref[...], preferred_element_type=jnp.float32) + bias_ref[...]
    )
    size_ref[...] = size
    drive_ref[...] = size * x_ref[...].astype(jnp.float32)
    rates = rate_ref[...]

    def step(block, state):
        start = pl.multiple_of(block * 8, 8)
        sizes = size_ref[pl.ds(start, 8), :]
        drives = drive_ref[pl.ds(start, 8), :]
        state = list(state)
        for i in range(8):
            b_now = b_ref[start + i]
            for g in range(groups):
                lanes = slice(g * 128, g * 128 + 128)
                decay = jnp.exp2(sizes[i : i + 1, lanes] * rates[:, lanes])
                state[g] = decay * state[g] + drives[i : i + 1, lanes] * b_now
        return tuple(state)

    zero = jnp.zeros((states, 128), jnp.float32)
    state = lax.fori_loop(0, rows // 8, step, (zero,) * groups)
    total = jnp.sum(size, axis=0, keepdims=True)
    high = total.astype(jnp.bfloat16).astype(jnp.float32)
    low = total - high
    rest = jnp.zeros((load_ref.shape[0] - states - 2, width), jnp.float32)
    load_ref[...] = jnp.concatenate(
        [jnp.concatenate(state, axis=1), high, low, rest], axis=0
    ).astype(jnp.bfloat16)


def scan_ends(partials, dt_proj, dt_bias, rates, xconv):
    rows, channels = xconv.shape
    states = rates.shape[0]
    width = tile_of(channels)
    load_rows = -(-(states + 2) // 8) * 8
    wide = jax.ShapeDtypeStruct((rows, states, 128), jnp.float32)
    return pl.pallas_call(
        ends_kernel,
        grid=(channels // width,),
        in_specs=[
            pl.BlockSpec(partials.shape, lambda i: (0, 0, 0)),
            pl.BlockSpec((dt_proj.shape[0], width), lambda i: (0, i)),
            pl.BlockSpec((1, width), lambda i: (0, i)),
            pl.BlockSpec((states, width), lambda i: (0, i)),
            pl.BlockSpec((rows, width), lambda i: (0, i)),
        ],
        out_specs=[
            pl.BlockSpec((rows, width), lambda i: (0, i)),
            pl.BlockSpec((load_rows, width), lambda i: (0, i)),
            pl.BlockSpec(wide.shape, lambda i: (0, 0, 0)),
            pl.BlockSpec(wide.shape, lambda i: (0, 0, 0)),
        ],
        out_shape=[
            jax.ShapeDtypeStruct((rows, channels), jnp.float32),
            jax.ShapeDtypeStruct((load_rows, channels), jnp.bfloat16),
            wide,
            wide,
        ],
        scratch_shapes=[
            pltpu.VMEM((rows, dt_proj.shape[0]), jnp.bfloat16),
            pltpu.VMEM((rows, width), jnp.float32),
        ],
        name="scan_ends",
    )(partials, dt_proj, dt_bias, rates, xconv)


def mix_kernel(count, order_ref, *refs):
    loads = refs[:count]
    size_ref, x_ref, z_ref, b_ref, c_ref, rate_ref, skip_ref, out_ref = refs[count : count + 8]
    drive_ref, y_ref, load_ref = refs[count + 8 :]
    for k in range(count):
        load_ref[order_ref[k]] = loads[k][...].astype(jnp.float32)
    rows, width = x_ref.shape
    states = rate_ref.shape[0]
    groups = width // 128
    rates = rate_ref[...]
    x_f = x_ref[...].astype(jnp.float32)
    drive_ref[...] = size_ref[...] * x_f

    def earlier(j, state):
        block = load_ref[j]
        total = block[states : states + 1] + block[states + 1 : states + 2]
        return jnp.exp2(total * rates) * state + block[:states]

    incoming = lax.fori_loop(0, order_ref[0], earlier, jnp.zeros((states, width), jnp.float32))

    def step(block, state):
        start = pl.multiple_of(block * 8, 8)
        sizes = size_ref[pl.ds(start, 8), :]
        drives = drive_ref[pl.ds(start, 8), :]
        state = list(state)
        outs = [[None] * 8 for _ in range(groups)]
        for i in range(8):
            b_now = b_ref[start + i]
            c_now = c_ref[start + i]
            for g in range(groups):
                lanes = slice(g * 128, g * 128 + 128)
                decay = jnp.exp2(sizes[i : i + 1, lanes] * rates[:, lanes])
                state[g] = decay * state[g] + drives[i : i + 1, lanes] * b_now
                outs[g][i] = jnp.sum(state[g] * c_now, axis=0, keepdims=True)
        for g in range(groups):
            y_ref[pl.ds(start, 8), g * 128 : g * 128 + 128] = jnp.concatenate(outs[g], axis=0)
        return tuple(state)

    start_state = tuple(incoming[:, g * 128 : g * 128 + 128] for g in range(groups))
    lax.fori_loop(0, rows // 8, step, start_state)
    z_f = z_ref[...].astype(jnp.float32)
    scanned = y_ref[...] + skip_ref[...] * x_f
    out_ref[...] = (scanned * (z_f / (1.0 + jnp.exp(-z_f)))).astype(jnp.bfloat16)


def scan_mix(order, loads, step_size, xconv, z_in, b_wide, c_wide, rates, d_skip):
    rows, channels = xconv.shape
    states = rates.shape[0]
    width = tile_of(channels)

    def by_lane(depth):
        return pl.BlockSpec((depth, width), lambda i: (0, i))

    return pl.pallas_call(
        functools.partial(mix_kernel, len(loads)),
        grid=(channels // width,),
        in_specs=[
            whole_smem(),
            *[by_lane(load.shape[0]) for load in loads],
            by_lane(rows),
            by_lane(rows),
            by_lane(rows),
            pl.BlockSpec(b_wide.shape, lambda i: (0, 0, 0)),
            pl.BlockSpec(c_wide.shape, lambda i: (0, 0, 0)),
            by_lane(states),
            by_lane(1),
        ],
        out_specs=by_lane(rows),
        out_shape=jax.ShapeDtypeStruct((rows, channels), jnp.bfloat16),
        scratch_shapes=[pltpu.VMEM((rows, width), jnp.float32)] * 2
        + [pltpu.VMEM((len(loads), loads[0].shape[0], width), jnp.float32)],
        name="scan_mix",
    )(order, *loads, step_size, xconv, z_in, b_wide, c_wide, rates, d_skip)


def out_kernel(count, order_ref, *refs):
    blocks, weight_ref, out_ref, held_ref = refs[:count], refs[count], refs[count + 1], refs[count + 2]
    rows = blocks[0].shape[0]
    for i in range(count):
        held_ref[pl.ds(pl.multiple_of(order_ref[i] * rows, rows), rows), :] = blocks[i][...]
    out_ref[...] = jnp.dot(
        held_ref[...], weight_ref[...], preferred_element_type=jnp.float32
    ).astype(jnp.bfloat16)


def out_product(order, blocks, weight):
    rows, depth = blocks[0].shape
    count = len(blocks)
    return pl.pallas_call(
        functools.partial(out_kernel, count),
        in_specs=[whole_smem()] + [whole_vmem()] * (count + 1),
        out_specs=whole_vmem(),
        out_shape=jax.ShapeDtypeStruct((count * rows, weight.shape[1]), jnp.bfloat16),
        scratch_shapes=[pltpu.VMEM((count * rows, depth), jnp.bfloat16)],
        compiler_params=pltpu.CompilerParams(vmem_limit_bytes=32 * MIB),
        name="out_product",
    )(order, *blocks, weight)


def hidden_kernel(count, order_ref, *refs):
    chunks = refs[:count]
    gain_ref, gate_ref, up_ref, act_ref, scaled_ref = refs[count:]
    rows, depth = chunks[0].shape

    @pl.when(pl.program_id(0) == 0)
    def _():
        squares = jnp.zeros((rows, 1), jnp.float32)
        for i in range(count):
            h = chunks[i][...].astype(jnp.float32)
            squares = squares + jnp.sum(h * h, axis=1, keepdims=True)
        scale = lax.rsqrt(squares / (depth * count) + eps)
        for i in range(count):
            h = chunks[i][...].astype(jnp.float32)
            at = pl.ds(pl.multiple_of(order_ref[i] * depth, depth), depth)
            scaled_ref[:, at] = (h * scale * gain_ref[order_ref[i]]).astype(jnp.bfloat16)

    scaled = scaled_ref[...]
    gate = jnp.dot(scaled, gate_ref[0], preferred_element_type=jnp.float32)
    upper = jnp.dot(scaled, up_ref[0], preferred_element_type=jnp.float32)
    act_ref[...] = (gate / (1.0 + jnp.exp(-gate)) * upper).astype(jnp.bfloat16)


def expert_hidden(order, chunks, gain, w_gate, w_up):
    rows, depth = chunks[0].shape
    count = len(chunks)
    columns = w_gate.shape[2]
    width = tile_of(columns, 256)
    gain = gain.reshape(count, 1, depth)
    weight_spec = pl.BlockSpec((1, depth * count, width), lambda n: (0, 0, n))
    return pl.pallas_call(
        functools.partial(hidden_kernel, count),
        grid=(columns // width,),
        in_specs=[whole_smem()]
        + [whole_vmem()] * (count + 1)
        + [weight_spec, weight_spec],
        out_specs=pl.BlockSpec((rows, width), lambda n: (0, n)),
        out_shape=jax.ShapeDtypeStruct((rows, columns), jnp.bfloat16),
        scratch_shapes=[pltpu.VMEM((rows, depth * count), jnp.bfloat16)],
        compiler_params=pltpu.CompilerParams(vmem_limit_bytes=40 * MIB),
        name="expert_hidden",
    )(order, *chunks, gain, w_gate, w_up)


def down_kernel(z_count, z_ref, half_ref, act_ref, weight_ref, *refs):
    outs, held_ref = refs[:-1], refs[-1]
    held_ref[...] = jnp.dot(act_ref[...], weight_ref[0], preferred_element_type=jnp.float32)
    pitch = outs[0].shape[0]
    for r in range(z_count):
        start = pl.multiple_of(lax.rem(z_ref[0] + r, z_count) * pitch, pitch)
        outs[r][...] = held_ref[pl.ds(start, pitch), :].astype(jnp.bfloat16)


def expert_down(z_at, half, z_count, x_count, act, w_down):
    rows, depth = act.shape
    columns = w_down.shape[2] // x_count
    width = tile_of(columns)
    tiles = columns // width
    pitch = rows // z_count
    return pl.pallas_call(
        functools.partial(down_kernel, z_count),
        grid_spec=pltpu.PrefetchScalarGridSpec(
            num_scalar_prefetch=2,
            grid=(tiles,),
            in_specs=[
                pl.BlockSpec((rows, depth), lambda n, z, half: (0, 0)),
                pl.BlockSpec((1, depth, width), lambda n, z, half: (0, 0, half[0] * tiles + n)),
            ],
            out_specs=[pl.BlockSpec((pitch, width), lambda n, z, half: (0, n))] * z_count,
            scratch_shapes=[pltpu.VMEM((rows, width), jnp.float32)],
        ),
        out_shape=[jax.ShapeDtypeStruct((pitch, columns), jnp.bfloat16)] * z_count,
        compiler_params=pltpu.CompilerParams(vmem_limit_bytes=32 * MIB),
        name="expert_down",
    )(z_at, half, act, w_down)


def per_device(
    x_in,
    z_in,
    conv_weight,
    conv_bias,
    x_proj,
    dt_proj,
    dt_bias,
    a_log,
    d_skip,
    out_proj,
    resid,
    norm_gain,
    routes,
    route_gate,
    w_gate,
    w_up,
    w_down,
):
    row_count, channels = x_in.shape
    seq_count = lax.axis_size("seq")
    exp_count = lax.axis_size("exp")
    x_count = seq_count // exp_count
    z_count = exp_count
    seq_at = lax.axis_index("seq")
    exp_at = lax.axis_index("exp")
    z_at, x_at = seq_at // x_count, seq_at % x_count
    z_one = z_at.reshape(1).astype(jnp.int32)
    top_count = routes.shape[1]
    capacity = row_count * top_count * 17 // (16 * exp_count)
    pitch = -(-(x_count * capacity) // 8) * 8 // x_count
    group_tokens = x_count * row_count
    feature_slice = resid.shape[1]
    column_slice = out_proj.shape[1]

    def from_z(block, r):
        pairs = [
            (((z + r) % z_count) * x_count + x, z * x_count + x)
            for z in range(z_count)
            for x in range(x_count)
        ]
        return lax.ppermute(block, "seq", pairs)

    def from_x(block, i):
        pairs = [
            (z * x_count + (x + i) % x_count, z * x_count + x)
            for z in range(z_count)
            for x in range(x_count)
        ]
        return lax.ppermute(block, "seq", pairs)

    def gathered(block, chained=True):
        along_z = {0: block}
        for r in range(1, z_count // 2 + 1):
            both = sorted({r, z_count - r})
            for q in both:
                along_z[q] = from_z(block, q)
            if chained and r < z_count // 2:
                held = lax.optimization_barrier((block,) + tuple(along_z[q] for q in both))
                block = held[0]
                along_z.update(zip(both, held[1:]))
        return [
            along_z[r] if i == 0 else from_x(along_z[r], i)
            for r in range(z_count)
            for i in range(x_count)
        ]

    order = jnp.stack(
        [
            ((z_at + r) % z_count) * x_count + (x_at + i) % x_count
            for r in range(z_count)
            for i in range(x_count)
        ]
    ).astype(jnp.int32)

    halo = lax.ppermute(
        x_in[row_count - 8 :], "seq", [(i, i + 1) for i in range(seq_count - 1)]
    )

    resid_parts = []
    resid_cut = resid.reshape(row_count, x_count, column_slice)
    routes_wide = jnp.pad(routes.astype(jnp.bfloat16), ((0, 0), (0, 128 - top_count)))
    swaps = []
    for k in range(x_count):
        piece = lax.dynamic_index_in_dim(resid_cut, (x_at - k) % x_count, 1, keepdims=False)
        pairs = []
        for s in range(seq_count):
            for e in range(exp_count):
                source_s = x_count * e + (s % x_count + k) % x_count
                pairs.append((source_s * exp_count + s // x_count, s * exp_count + e))
        swaps.append(pairs)
        resid_parts.append(
            lax.ppermute(jnp.concatenate([piece, routes_wide], axis=1), ("seq", "exp"), pairs)
        )
    resid_stack = jnp.stack(resid_parts + resid_parts)
    group_stack = lax.dynamic_slice_in_dim(
        resid_stack, (x_count - x_at) % x_count, x_count, 0
    ).reshape(group_tokens, column_slice + 128)
    resid_here = group_stack[:, :column_slice]
    group_routes = group_stack[:, column_slice : column_slice + top_count].astype(jnp.int32)

    def slots_of(named):
        flat = named.reshape(-1, row_count * top_count)
        onehot = (flat[:, :, None] == jnp.arange(exp_count, dtype=jnp.int32)).astype(jnp.float32)
        below = jnp.tril(jnp.ones((row_count * top_count,) * 2, jnp.float32), -1)
        counts = jnp.einsum("ij,bje->bie", below, onehot)
        slots = jnp.sum(counts * onehot, axis=2).astype(jnp.int32)
        return slots.reshape(-1, row_count, top_count)

    group_routes = group_routes.reshape(x_count, row_count, top_count)
    target = (
        group_routes * (x_count * pitch)
        + jnp.arange(x_count, dtype=jnp.int32)[:, None, None] * pitch
        + slots_of(group_routes)
    ).reshape(group_tokens, top_count)
    slot_ids = jnp.arange(exp_count * x_count * pitch, dtype=jnp.int32)
    dispatch = jnp.sum(
        (target[None, :, :] == slot_ids[:, None, None]).astype(jnp.float32), axis=2
    ).astype(jnp.bfloat16)

    own_slots = slots_of(routes)[0]
    half_experts = exp_count // x_count
    turn = (exp_at % half_experts) * x_count + x_at
    own_target = (routes - turn) % exp_count * pitch + own_slots
    back_ids = jnp.arange(exp_count * pitch, dtype=jnp.int32)
    choose = (own_target.T[:, :, None] == back_ids[None, None, :]).astype(jnp.bfloat16)
    choose = choose.reshape(top_count * row_count, exp_count * pitch)

    rates = -jnp.exp(a_log.T) * LOG2E
    xconv, copies = conv_and_project(
        x_in, halo, conv_weight, conv_bias[None], x_proj.T, exp_count
    )
    partials = lax.all_to_all(copies, "exp", 0, 0, tiled=True)
    step_size, load, b_wide, c_wide = scan_ends(partials, dt_proj, dt_bias[None], rates, xconv)
    loads = gathered(load, chained=False)
    mixed = scan_mix(
        order, loads, step_size, xconv, z_in, b_wide, c_wide, rates, d_skip[None]
    )
    partial_out = out_product(order, gathered(mixed), out_proj)
    arrived = lax.all_to_all(
        partial_out.reshape(exp_count, group_tokens, column_slice), "exp", 0, 0, tiled=True
    )
    mamba_out = jnp.sum(arrived.astype(jnp.float32), axis=0)
    hidden_state = (resid_here.astype(jnp.float32) + mamba_out).astype(jnp.bfloat16)

    outgoing = jnp.dot(dispatch, hidden_state, preferred_element_type=jnp.float32)
    outgoing = outgoing.astype(jnp.bfloat16).reshape(exp_count, x_count * pitch, column_slice)
    rows_here = lax.all_to_all(outgoing, "exp", 0, 0, tiled=True)
    rows_here = rows_here.reshape(exp_count * x_count * pitch, column_slice)
    act = expert_hidden(order, gathered(rows_here), norm_gain, w_gate, w_up)

    hidden_cut = hidden_state.reshape(x_count, row_count, column_slice)
    returned = []
    for k in range(x_count):
        piece = lax.dynamic_index_in_dim(hidden_cut, (x_at + k) % x_count, 0, keepdims=False)
        back_pairs = [(target_at, source_at) for source_at, target_at in swaps[k]]
        returned.append(lax.ppermute(piece, ("seq", "exp"), back_pairs))
    returned = jnp.stack(returned)
    hidden_own = jnp.concatenate(
        [
            lax.dynamic_index_in_dim(returned, (x_at - j) % x_count, 0, keepdims=False)
            for j in range(x_count)
        ],
        axis=1,
    )

    down = {}
    for i in list(range(1, x_count)) + [0]:
        half = ((x_at + i) % x_count).reshape(1).astype(jnp.int32)
        down[i] = expert_down(z_one, half, z_count, x_count, act, w_down)
    crossed = {}
    by_distance = sorted(range(1, z_count), key=lambda r: abs(r - z_count // 2)) + [0]
    for r in by_distance:
        crossed[r] = [from_x(down[i][r], x_count - i) for i in range(1, x_count)]

    def over_x(r):
        return functools.reduce(
            jnp.add, [p.astype(jnp.float32) for p in [down[0][r]] + crossed[r]]
        )

    arrivals = [
        from_z(over_x(r).astype(jnp.bfloat16), z_count - r) for r in by_distance if r
    ]
    total = over_x(0)
    for sent in arrivals:
        total = total + sent.astype(jnp.float32)
    expert_out = total.astype(jnp.bfloat16)
    pieces = jnp.stack(
        [
            expert_out[
                m % x_count * pitch : (m % x_count + 1) * pitch,
                m // x_count * feature_slice : (m // x_count + 1) * feature_slice,
            ]
            for m in range(exp_count)
        ]
    )
    back = []
    for k in range(exp_count):
        piece = lax.dynamic_index_in_dim(pieces, (exp_at - k) % exp_count, 0, keepdims=False)
        pairs = []
        for z in range(z_count):
            for x in range(x_count):
                for e in range(exp_count):
                    source_e = (e % half_experts * x_count + x + k) % exp_count
                    source_s = z * x_count + e // half_experts
                    pairs.append(
                        (source_s * exp_count + source_e, (z * x_count + x) * exp_count + e)
                    )
        back.append(lax.ppermute(piece, ("seq", "exp"), pairs))
    back = jnp.concatenate(back, axis=0)
    picked = jnp.dot(choose, back, preferred_element_type=jnp.float32)
    picked = picked.reshape(top_count, row_count, feature_slice)
    moe = jnp.sum(route_gate.T[:, :, None] * picked, axis=0)
    return (hidden_own.astype(jnp.float32) + moe).astype(jnp.bfloat16)


def solution(mesh):
    return jax.shard_map(
        per_device,
        mesh=mesh,
        in_specs=(
            P("seq", "exp"),
            P("seq", "exp"),
            P(None, "exp"),
            P("exp"),
            P("exp", None),
            P(None, "exp"),
            P("exp"),
            P("exp", None),
            P("exp"),
            P("exp", "seq"),
            P("seq", "exp"),
            P(),
            P("seq", None),
            P("seq", None),
            P("exp", None, "seq"),
            P("exp", None, "seq"),
            P("exp", "seq", None),
        ),
        out_specs=P("seq", "exp"),
        check_vma=False,
    )
```

```python
import functools
import math

import jax
import jax.numpy as jnp
from jax import lax
from jax.experimental import pallas as pl
from jax.experimental.pallas import tpu as pltpu
from jax.sharding import PartitionSpec as P

eps = 1e-05
LOG2E = 1.4426950408889634
MIB = 1 << 20


def tile_of(size, most=512):
    return max(t for t in range(128, most + 1, 128) if size % t == 0)


def whole_vmem():
    return pl.BlockSpec(memory_space=pltpu.VMEM)


def whole_smem():
    return pl.BlockSpec(memory_space=pltpu.SMEM)


def conv_kernel(x_ref, halo_ref, weight_ref, bias_ref, proj_ref, xconv_ref, partial_ref):
    rows = x_ref.shape[0]
    taps = weight_ref.shape[0]
    extended = jnp.concatenate(
        [halo_ref[...].astype(jnp.float32), x_ref[...].astype(jnp.float32)], axis=0
    )
    pad = halo_ref.shape[0]
    conv = jnp.zeros(x_ref.shape, jnp.float32) + bias_ref[...]
    for tap in range(taps):
        start = pad - (taps - 1) + tap
        conv = conv + weight_ref[tap : tap + 1, :] * extended[start : start + rows]
    xconv = (conv / (1.0 + jnp.exp(-conv))).astype(jnp.bfloat16)
    xconv_ref[...] = xconv

    @pl.when(pl.program_id(0) == 0)
    def _():
        partial_ref[0] = jnp.zeros(partial_ref.shape[1:], jnp.float32)

    partial_ref[0] += lax.dot_general(
        xconv, proj_ref[...], (((1,), (1,)), ((), ())), preferred_element_type=jnp.float32
    )

    @pl.when(pl.program_id(0) == pl.num_programs(0) - 1)
    def _():
        for copy in range(1, partial_ref.shape[0]):
            partial_ref[copy] = partial_ref[0]


def conv_and_project(x_in, halo, conv_weight, conv_bias, x_proj_t, copies):
    rows, channels = x_in.shape
    width = tile_of(channels)
    columns = x_proj_t.shape[0]
    return pl.pallas_call(
        conv_kernel,
        grid=(channels // width,),
        in_specs=[
            pl.BlockSpec((rows, width), lambda i: (0, i)),
            pl.BlockSpec((halo.shape[0], width), lambda i: (0, i)),
            pl.BlockSpec((conv_weight.shape[0], width), lambda i: (0, i)),
            pl.BlockSpec((1, width), lambda i: (0, i)),
            pl.BlockSpec((columns, width), lambda i: (0, i)),
        ],
        out_specs=[
            pl.BlockSpec((rows, width), lambda i: (0, i)),
            pl.BlockSpec((copies, rows, columns), lambda i: (0, 0, 0)),
        ],
        out_shape=[
            jax.ShapeDtypeStruct((rows, channels), jnp.bfloat16),
            jax.ShapeDtypeStruct((copies, rows, columns), jnp.float32),
        ],
        name="conv_project",
    )(x_in, halo, conv_weight, conv_bias, x_proj_t)


def softplus(v):
    return jnp.maximum(v, 0.0) + jnp.log1p(jnp.exp(-jnp.abs(v)))


def ends_kernel(
    part_ref, proj_ref, bias_ref, rate_ref, x_ref, size_ref, load_ref, b_ref, c_ref, low_ref, drive_ref
):
    rows, width = x_ref.shape
    states = rate_ref.shape[0]
    low_rank = low_ref.shape[1]
    groups = width // 128

    @pl.when(pl.program_id(0) == 0)
    def _():
        total = part_ref[0]
        for e in range(1, part_ref.shape[0]):
            total = total + part_ref[e]
        low_ref[...] = total[:, :low_rank].astype(jnp.bfloat16)
        b_mat = total[:, low_rank : low_rank + states]
        c_mat = total[:, low_rank + states : low_rank + 2 * states]
        b_ref[...] = jnp.broadcast_to(b_mat[:, :, None], b_ref.shape)
        c_ref[...] = jnp.broadcast_to(c_mat[:, :, None], c_ref.shape)

    size = softplus(
        jnp.dot(low_ref[...], proj_ref[...], preferred_element_type=jnp.float32) + bias_ref[...]
    )
    size_ref[...] = size
    drive_ref[...] = size * x_ref[...].astype(jnp.float32)
    rates = rate_ref[...]

    def step(block, state):
        start = pl.multiple_of(block * 8, 8)
        sizes = size_ref[pl.ds(start, 8), :]
        drives = drive_ref[pl.ds(start, 8), :]
        state = list(state)
        for i in range(8):
            b_now = b_ref[start + i]
            for g in range(groups):
                lanes = slice(g * 128, g * 128 + 128)
                decay = jnp.exp2(sizes[i : i + 1, lanes] * rates[:, lanes])
                state[g] = decay * state[g] + drives[i : i + 1, lanes] * b_now
        return tuple(state)

    zero = jnp.zeros((states, 128), jnp.float32)
    state = lax.fori_loop(0, rows // 8, step, (zero,) * groups)
    total = jnp.sum(size, axis=0, keepdims=True)
    high = total.astype(jnp.bfloat16).astype(jnp.float32)
    low = total - high
    rest = jnp.zeros((load_ref.shape[0] - states - 2, width), jnp.float32)
    load_ref[...] = jnp.concatenate(
        [jnp.concatenate(state, axis=1), high, low, rest], axis=0
    ).astype(jnp.bfloat16)


def scan_ends(partials, dt_proj, dt_bias, rates, xconv):
    rows, channels = xconv.shape
    states = rates.shape[0]
    width = tile_of(channels, 1024)
    load_rows = -(-(states + 2) // 8) * 8
    wide = jax.ShapeDtypeStruct((rows, states, 128), jnp.float32)
    return pl.pallas_call(
        ends_kernel,
        grid=(channels // width,),
        in_specs=[
            pl.BlockSpec(partials.shape, lambda i: (0, 0, 0)),
            pl.BlockSpec((dt_proj.shape[0], width), lambda i: (0, i)),
            pl.BlockSpec((1, width), lambda i: (0, i)),
            pl.BlockSpec((states, width), lambda i: (0, i)),
            pl.BlockSpec((rows, width), lambda i: (0, i)),
        ],
        out_specs=[
            pl.BlockSpec((rows, width), lambda i: (0, i)),
            pl.BlockSpec((load_rows, width), lambda i: (0, i)),
            pl.BlockSpec(wide.shape, lambda i: (0, 0, 0)),
            pl.BlockSpec(wide.shape, lambda i: (0, 0, 0)),
        ],
        out_shape=[
            jax.ShapeDtypeStruct((rows, channels), jnp.float32),
            jax.ShapeDtypeStruct((load_rows, channels), jnp.bfloat16),
            wide,
            wide,
        ],
        scratch_shapes=[
            pltpu.VMEM((rows, dt_proj.shape[0]), jnp.bfloat16),
            pltpu.VMEM((rows, width), jnp.float32),
        ],
        name="scan_ends",
    )(partials, dt_proj, dt_bias, rates, xconv)


def mix_kernel(count, order_ref, *refs):
    loads = refs[:count]
    size_ref, x_ref, z_ref, b_ref, c_ref, rate_ref, skip_ref, out_ref = refs[count : count + 8]
    drive_ref, y_ref, load_ref = refs[count + 8 :]
    for k in range(count):
        load_ref[order_ref[k]] = loads[k][...].astype(jnp.float32)
    rows, width = x_ref.shape
    states = rate_ref.shape[0]
    groups = width // 128
    rates = rate_ref[...]
    x_f = x_ref[...].astype(jnp.float32)
    drive_ref[...] = size_ref[...] * x_f

    def earlier(j, state):
        block = load_ref[j]
        total = block[states : states + 1] + block[states + 1 : states + 2]
        return jnp.exp2(total * rates) * state + block[:states]

    incoming = lax.fori_loop(0, order_ref[0], earlier, jnp.zeros((states, width), jnp.float32))

    def step(block, state):
        start = pl.multiple_of(block * 8, 8)
        sizes = size_ref[pl.ds(start, 8), :]
        drives = drive_ref[pl.ds(start, 8), :]
        state = list(state)
        outs = [[None] * 8 for _ in range(groups)]
        for i in range(8):
            b_now = b_ref[start + i]
            c_now = c_ref[start + i]
            for g in range(groups):
                lanes = slice(g * 128, g * 128 + 128)
                decay = jnp.exp2(sizes[i : i + 1, lanes] * rates[:, lanes])
                state[g] = decay * state[g] + drives[i : i + 1, lanes] * b_now
                outs[g][i] = jnp.sum(state[g] * c_now, axis=0, keepdims=True)
        for g in range(groups):
            y_ref[pl.ds(start, 8), g * 128 : g * 128 + 128] = jnp.concatenate(outs[g], axis=0)
        return tuple(state)

    start_state = tuple(incoming[:, g * 128 : g * 128 + 128] for g in range(groups))
    lax.fori_loop(0, rows // 8, step, start_state)
    z_f = z_ref[...].astype(jnp.float32)
    scanned = y_ref[...] + skip_ref[...] * x_f
    out_ref[...] = (scanned * (z_f / (1.0 + jnp.exp(-z_f)))).astype(jnp.bfloat16)


def scan_mix(order, loads, step_size, xconv, z_in, b_wide, c_wide, rates, d_skip):
    rows, channels = xconv.shape
    states = rates.shape[0]
    width = tile_of(channels, 1024)

    def by_lane(depth):
        return pl.BlockSpec((depth, width), lambda i: (0, i))

    return pl.pallas_call(
        functools.partial(mix_kernel, len(loads)),
        grid=(channels // width,),
        in_specs=[
            whole_smem(),
            *[by_lane(load.shape[0]) for load in loads],
            by_lane(rows),
            by_lane(rows),
            by_lane(rows),
            pl.BlockSpec(b_wide.shape, lambda i: (0, 0, 0)),
            pl.BlockSpec(c_wide.shape, lambda i: (0, 0, 0)),
            by_lane(states),
            by_lane(1),
        ],
        out_specs=by_lane(rows),
        out_shape=jax.ShapeDtypeStruct((rows, channels), jnp.bfloat16),
        scratch_shapes=[pltpu.VMEM((rows, width), jnp.float32)] * 2
        + [pltpu.VMEM((len(loads), loads[0].shape[0], width), jnp.float32)],
        name="scan_mix",
    )(order, *loads, step_size, xconv, z_in, b_wide, c_wide, rates, d_skip)


def out_kernel(z_count, x_count, z_ref, x_ref, *refs):
    blocks, weights = refs[:z_count], refs[z_count : z_count + x_count]
    out_ref, held_ref = refs[z_count + x_count :]
    rows = blocks[0].shape[0]
    columns = weights[0].shape[1]
    for r in range(z_count):
        at = pl.multiple_of(lax.rem(z_ref[0] + r, z_count) * rows, rows)
        held_ref[pl.ds(at, rows), :] = blocks[r][...]
    for i in range(x_count):
        at = pl.multiple_of(lax.rem(x_ref[0] + i, x_count) * columns, columns)
        out_ref[:, pl.ds(at, columns)] = jnp.dot(
            held_ref[...], weights[i][...], preferred_element_type=jnp.float32
        ).astype(jnp.bfloat16)


def out_product(z_at, x_at, blocks, weights):
    rows, depth = blocks[0].shape
    z_count, x_count = len(blocks), len(weights)
    return pl.pallas_call(
        functools.partial(out_kernel, z_count, x_count),
        in_specs=[whole_smem()] * 2 + [whole_vmem()] * (z_count + x_count),
        out_specs=whole_vmem(),
        out_shape=jax.ShapeDtypeStruct(
            (z_count * rows, x_count * weights[0].shape[1]), jnp.bfloat16
        ),
        scratch_shapes=[pltpu.VMEM((z_count * rows, depth), jnp.bfloat16)],
        compiler_params=pltpu.CompilerParams(vmem_limit_bytes=32 * MIB),
        name="out_product",
    )(z_at, x_at, *blocks, *weights)


def hidden_kernel(z_count, x_count, z_ref, x_ref, *refs):
    count = z_count * x_count
    chunks = refs[:count]
    gain_ref, gate_ref, up_ref, act_ref, scaled_ref = refs[count:]
    rows, depth = chunks[0].shape

    @pl.when(pl.program_id(0) == 0)
    def _():
        for i in range(x_count):
            own = [chunks[r * x_count + i] for r in range(z_count)]
            squares = jnp.zeros((rows, 1), jnp.float32)
            for chunk in own:
                h = chunk[...].astype(jnp.float32)
                squares = squares + jnp.sum(h * h, axis=1, keepdims=True)
            scale = lax.rsqrt(squares / (depth * z_count) + eps)
            down = pl.multiple_of(lax.rem(x_ref[0] + i, x_count) * rows, rows)
            for r, chunk in enumerate(own):
                z_at = lax.rem(z_ref[0] + r, z_count)
                across = pl.multiple_of(z_at * depth, depth)
                h = chunk[...].astype(jnp.float32)
                scaled_ref[pl.ds(down, rows), pl.ds(across, depth)] = (
                    h * scale * gain_ref[z_at]
                ).astype(jnp.bfloat16)

    scaled = scaled_ref[...]
    gate = jnp.dot(scaled, gate_ref[0], preferred_element_type=jnp.float32)
    upper = jnp.dot(scaled, up_ref[0], preferred_element_type=jnp.float32)
    act_ref[...] = (gate / (1.0 + jnp.exp(-gate)) * upper).astype(jnp.bfloat16)


def expert_hidden(z_at, x_at, chunks, gain, w_gate, w_up):
    z_count, x_count = len(chunks), len(chunks[0])
    rows, depth = chunks[0][0].shape
    columns = w_gate.shape[2]
    width = tile_of(columns, 256)
    gain = gain.reshape(z_count, 1, depth)
    weight_spec = pl.BlockSpec((1, depth * z_count, width), lambda n: (0, 0, n))
    return pl.pallas_call(
        functools.partial(hidden_kernel, z_count, x_count),
        grid=(columns // width,),
        in_specs=[whole_smem()] * 2
        + [whole_vmem()] * (z_count * x_count + 1)
        + [weight_spec, weight_spec],
        out_specs=pl.BlockSpec((rows * x_count, width), lambda n: (0, n)),
        out_shape=jax.ShapeDtypeStruct((rows * x_count, columns), jnp.bfloat16),
        scratch_shapes=[pltpu.VMEM((rows * x_count, depth * z_count), jnp.bfloat16)],
        compiler_params=pltpu.CompilerParams(vmem_limit_bytes=40 * MIB),
        name="expert_hidden",
    )(z_at, x_at, *[chunk for pair in chunks for chunk in pair], gain, w_gate, w_up)


def down_kernel(x_count, x_ref, block_ref, act_ref, weight_ref, *refs):
    outs, held_ref = refs[:-1], refs[-1]
    held_ref[...] = jnp.dot(act_ref[...], weight_ref[0], preferred_element_type=jnp.float32)
    rows = outs[0].shape[0]
    for i in range(x_count):
        start = pl.multiple_of(lax.rem(x_ref[0] + i, x_count) * rows, rows)
        outs[i][...] = held_ref[pl.ds(start, rows), :].astype(jnp.bfloat16)


def expert_down(x_at, block, x_count, z_count, act, w_down):
    rows, depth = act.shape
    columns = w_down.shape[2] // z_count
    width = tile_of(columns)
    tiles = columns // width
    return pl.pallas_call(
        functools.partial(down_kernel, x_count),
        grid_spec=pltpu.PrefetchScalarGridSpec(
            num_scalar_prefetch=2,
            grid=(tiles,),
            in_specs=[
                pl.BlockSpec((rows, depth), lambda n, x, block: (0, 0)),
                pl.BlockSpec((1, depth, width), lambda n, x, block: (0, 0, block[0] * tiles + n)),
            ],
            out_specs=[pl.BlockSpec((rows // x_count, width), lambda n, x, block: (0, n))] * x_count,
            scratch_shapes=[pltpu.VMEM((rows, width), jnp.float32)],
        ),
        out_shape=[jax.ShapeDtypeStruct((rows // x_count, columns), jnp.bfloat16)] * x_count,
        compiler_params=pltpu.CompilerParams(vmem_limit_bytes=32 * MIB),
        name="expert_down",
    )(x_at, block, act, w_down)


def per_device(
    x_in,
    z_in,
    conv_weight,
    conv_bias,
    x_proj,
    dt_proj,
    dt_bias,
    a_log,
    d_skip,
    out_proj,
    resid,
    norm_gain,
    routes,
    route_gate,
    w_gate,
    w_up,
    w_down,
):
    row_count, channels = x_in.shape
    seq_count = lax.axis_size("seq")
    exp_count = lax.axis_size("exp")
    x_count = seq_count // exp_count
    z_count = exp_count
    seq_at = lax.axis_index("seq")
    exp_at = lax.axis_index("exp")
    z_at, x_at = seq_at // x_count, seq_at % x_count
    z_one = z_at.reshape(1).astype(jnp.int32)
    x_one = x_at.reshape(1).astype(jnp.int32)
    top_count = routes.shape[1]
    capacity = row_count * top_count * 17 // (16 * exp_count)
    pitch = -(-(z_count * capacity) // 16) * 16 // z_count
    feature_slice = resid.shape[1]

    def from_z(block, r):
        pairs = [
            (((z + r) % z_count) * x_count + x, z * x_count + x)
            for z in range(z_count)
            for x in range(x_count)
        ]
        return lax.ppermute(block, "seq", pairs)

    def from_x(block, i):
        pairs = [
            (z * x_count + (x + i) % x_count, z * x_count + x)
            for z in range(z_count)
            for x in range(x_count)
        ]
        return lax.ppermute(block, "seq", pairs)

    def gathered(block, chained=True):
        rows = {(0, 0): block}
        for i in range(1, x_count):
            rows[0, i] = from_x(block, i)
        for r in range(1, z_count // 2 + 1):
            both = sorted({r, z_count - r})
            for q in both:
                rows[q, 0] = from_z(block, q)
            if chained and r < z_count // 2:
                keys = [key for key in rows if key != (0, 0)]
                held = lax.optimization_barrier((block,) + tuple(rows[key] for key in keys))
                block = held[0]
                rows.update(zip(keys, held[1:]))
            for q in both:
                for i in range(1, x_count):
                    rows[q, i] = from_x(rows[q, 0], i)
        return [[rows[r, i] for i in range(x_count)] for r in range(z_count)]

    swap = [
        ((e * x_count + x) * exp_count + z, (z * x_count + x) * exp_count + e)
        for z in range(z_count)
        for x in range(x_count)
        for e in range(exp_count)
    ]

    order = jnp.stack(
        [
            ((z_at + r) % z_count) * x_count + (x_at + i) % x_count
            for r in range(z_count)
            for i in range(x_count)
        ]
    ).astype(jnp.int32)

    halo = lax.ppermute(
        x_in[row_count - 8 :], "seq", [(i, i + 1) for i in range(seq_count - 1)]
    )

    routes_wide = jnp.pad(routes.astype(jnp.bfloat16), ((0, 0), (0, 128 - top_count)))
    group = lax.ppermute(jnp.concatenate([resid, routes_wide], axis=1), ("seq", "exp"), swap)

    cut = channels // 2
    early = [from_x(out_proj[:cut], i) for i in range(1, x_count)]

    def slots_of(named):
        flat = named.reshape(-1, row_count * top_count)
        onehot = (flat[:, :, None] == jnp.arange(exp_count, dtype=jnp.int32)).astype(jnp.float32)
        below = jnp.tril(jnp.ones((row_count * top_count,) * 2, jnp.float32), -1)
        counts = jnp.einsum("ij,bje->bie", below, onehot)
        slots = jnp.sum(counts * onehot, axis=2).astype(jnp.int32)
        return slots.reshape(-1, row_count, top_count)

    own_slots = slots_of(routes)[0]
    own_target = (routes - z_at) % exp_count * pitch + own_slots
    slot_ids = jnp.arange(exp_count * pitch, dtype=jnp.int32)
    choose = (own_target.T[:, :, None] == slot_ids[None, None, :]).astype(jnp.bfloat16)
    choose = choose.reshape(top_count * row_count, exp_count * pitch)

    rates = -jnp.exp(a_log.T) * LOG2E
    xconv, copies = conv_and_project(
        x_in, halo, conv_weight, conv_bias[None], x_proj.T, exp_count
    )
    partials = lax.all_to_all(copies, "exp", 0, 0, tiled=True)
    partials, group, later, *early = lax.optimization_barrier(
        (partials, group, out_proj[cut:], *early)
    )
    later = [from_x(later, i) for i in range(1, x_count)]
    columns = [out_proj] + [jnp.concatenate(pair, axis=0) for pair in zip(early, later)]
    resid_here = group[:, :feature_slice]
    group_routes = group[:, feature_slice : feature_slice + top_count].astype(jnp.int32)
    target = group_routes * pitch + slots_of(group_routes)[0]
    dispatch = jnp.sum(
        (target[None, :, :] == slot_ids[:, None, None]).astype(jnp.float32), axis=2
    ).astype(jnp.bfloat16)
    step_size, load, b_wide, c_wide = scan_ends(partials, dt_proj, dt_bias[None], rates, xconv)
    loads = sum(gathered(load, chained=False), [])
    mixed = scan_mix(
        order, loads, step_size, xconv, z_in, b_wide, c_wide, rates, d_skip[None]
    )
    along_z = [mixed] + [from_z(mixed, r) for r in range(1, z_count)]
    partial_out = out_product(z_one, x_one, along_z, columns)
    arrived = lax.all_to_all(
        partial_out.reshape(exp_count, row_count, feature_slice), "exp", 0, 0, tiled=True
    )
    mamba_out = jnp.sum(arrived.astype(jnp.float32), axis=0)
    hidden_state = (resid_here.astype(jnp.float32) + mamba_out).astype(jnp.bfloat16)

    outgoing = jnp.dot(dispatch, hidden_state, preferred_element_type=jnp.float32)
    outgoing = outgoing.astype(jnp.bfloat16).reshape(exp_count, pitch, feature_slice)
    rows_here = lax.all_to_all(outgoing, "exp", 0, 0, tiled=True)
    rows_here = rows_here.reshape(exp_count * pitch, feature_slice)
    act = expert_hidden(z_one, x_one, gathered(rows_here), norm_gain, w_gate, w_up)

    hidden_own = lax.ppermute(hidden_state, ("seq", "exp"), swap)

    by_distance = sorted(range(1, z_count), key=lambda r: abs(r - z_count // 2)) + [0]
    down = {}
    for r in by_distance:
        block = ((z_at + r) % z_count).reshape(1).astype(jnp.int32)
        down[r] = expert_down(x_one, block, x_count, z_count, act, w_down)
    crossed = {}
    for r in by_distance:
        crossed[r] = [from_x(down[r][i], x_count - i) for i in range(1, x_count)]

    def over_x(r):
        return functools.reduce(
            jnp.add, [p.astype(jnp.float32) for p in [down[r][0]] + crossed[r]]
        )

    arrivals = [
        from_z(over_x(r).astype(jnp.bfloat16), z_count - r) for r in by_distance if r
    ]
    total = over_x(0)
    for sent in arrivals:
        total = total + sent.astype(jnp.float32)
    expert_out = total.astype(jnp.bfloat16)
    pieces = expert_out.reshape(exp_count, pitch, feature_slice)
    back = []
    for k in range(exp_count):
        piece = lax.dynamic_index_in_dim(pieces, (exp_at - k) % exp_count, 0, keepdims=False)
        pairs = [
            (
                (e * x_count + x) * exp_count + (z + k) % exp_count,
                (z * x_count + x) * exp_count + e,
            )
            for z in range(z_count)
            for x in range(x_count)
            for e in range(exp_count)
        ]
        back.append(lax.ppermute(piece, ("seq", "exp"), pairs))
    back = jnp.concatenate(back, axis=0)
    picked = jnp.dot(choose, back, preferred_element_type=jnp.float32)
    picked = picked.reshape(top_count, row_count, feature_slice)
    moe = jnp.sum(route_gate.T[:, :, None] * picked, axis=0)
    return (hidden_own.astype(jnp.float32) + moe).astype(jnp.bfloat16)


def solution(mesh):
    return jax.shard_map(
        per_device,
        mesh=mesh,
        in_specs=(
            P("seq", "exp"),
            P("seq", "exp"),
            P(None, "exp"),
            P("exp"),
            P("exp", None),
            P(None, "exp"),
            P("exp"),
            P("exp", None),
            P("exp"),
            P("exp", "seq"),
            P("seq", "exp"),
            P(),
            P("seq", None),
            P("seq", None),
            P("exp", None, "seq"),
            P("exp", None, "seq"),
            P("exp", "seq", None),
        ),
        out_specs=P("seq", "exp"),
        check_vma=False,
    )
```

```python
import functools
import math

import jax
import jax.numpy as jnp
from jax import lax
from jax.experimental import pallas as pl
from jax.experimental.pallas import tpu as pltpu
from jax.sharding import PartitionSpec as P

eps = 1e-05
LOG2E = 1.4426950408889634
MIB = 1 << 20


def tile_of(size, most=512):
    return max(t for t in range(128, most + 1, 128) if size % t == 0)


def whole_vmem():
    return pl.BlockSpec(memory_space=pltpu.VMEM)


def whole_smem():
    return pl.BlockSpec(memory_space=pltpu.SMEM)


def conv_kernel(x_ref, halo_ref, weight_ref, bias_ref, proj_ref, xconv_ref, partial_ref):
    rows = x_ref.shape[0]
    taps = weight_ref.shape[0]
    extended = jnp.concatenate(
        [halo_ref[...].astype(jnp.float32), x_ref[...].astype(jnp.float32)], axis=0
    )
    pad = halo_ref.shape[0]
    conv = jnp.zeros(x_ref.shape, jnp.float32) + bias_ref[...]
    for tap in range(taps):
        start = pad - (taps - 1) + tap
        conv = conv + weight_ref[tap : tap + 1, :] * extended[start : start + rows]
    xconv = (conv / (1.0 + jnp.exp(-conv))).astype(jnp.bfloat16)
    xconv_ref[...] = xconv

    @pl.when(pl.program_id(0) == 0)
    def _():
        partial_ref[0] = jnp.zeros(partial_ref.shape[1:], jnp.float32)

    partial_ref[0] += lax.dot_general(
        xconv, proj_ref[...], (((1,), (1,)), ((), ())), preferred_element_type=jnp.float32
    )

    @pl.when(pl.program_id(0) == pl.num_programs(0) - 1)
    def _():
        for copy in range(1, partial_ref.shape[0]):
            partial_ref[copy] = partial_ref[0]


def conv_and_project(x_in, halo, conv_weight, conv_bias, x_proj_t, copies):
    rows, channels = x_in.shape
    width = tile_of(channels)
    columns = x_proj_t.shape[0]
    return pl.pallas_call(
        conv_kernel,
        grid=(channels // width,),
        in_specs=[
            pl.BlockSpec((rows, width), lambda i: (0, i)),
            pl.BlockSpec((halo.shape[0], width), lambda i: (0, i)),
            pl.BlockSpec((conv_weight.shape[0], width), lambda i: (0, i)),
            pl.BlockSpec((1, width), lambda i: (0, i)),
            pl.BlockSpec((columns, width), lambda i: (0, i)),
        ],
        out_specs=[
            pl.BlockSpec((rows, width), lambda i: (0, i)),
            pl.BlockSpec((copies, rows, columns), lambda i: (0, 0, 0)),
        ],
        out_shape=[
            jax.ShapeDtypeStruct((rows, channels), jnp.bfloat16),
            jax.ShapeDtypeStruct((copies, rows, columns), jnp.float32),
        ],
        compiler_params=pltpu.CompilerParams(vmem_limit_bytes=16 * MIB),
        name="conv_project",
    )(x_in, halo, conv_weight, conv_bias, x_proj_t)


def softplus(v):
    return jnp.maximum(v, 0.0) + jnp.log1p(jnp.exp(-jnp.abs(v)))


def ends_kernel(
    part_ref, proj_ref, bias_ref, rate_ref, x_ref, size_ref, load_ref, b_ref, c_ref, low_ref, drive_ref
):
    rows, width = x_ref.shape
    states = rate_ref.shape[0]
    low_rank = low_ref.shape[1]
    groups = width // 128

    @pl.when(pl.program_id(0) == 0)
    def _():
        total = part_ref[0]
        for e in range(1, part_ref.shape[0]):
            total = total + part_ref[e]
        low_ref[...] = total[:, :low_rank].astype(jnp.bfloat16)
        b_mat = total[:, low_rank : low_rank + states]
        c_mat = total[:, low_rank + states : low_rank + 2 * states]
        b_ref[...] = jnp.broadcast_to(b_mat[:, :, None], b_ref.shape)
        c_ref[...] = jnp.broadcast_to(c_mat[:, :, None], c_ref.shape)

    size = softplus(
        jnp.dot(low_ref[...], proj_ref[...], preferred_element_type=jnp.float32) + bias_ref[...]
    )
    size_ref[...] = size
    drive_ref[...] = size * x_ref[...].astype(jnp.float32)
    rates = rate_ref[...]

    def step(block, state):
        start = pl.multiple_of(block * 8, 8)
        sizes = size_ref[pl.ds(start, 8), :]
        drives = drive_ref[pl.ds(start, 8), :]
        state = list(state)
        for i in range(8):
            b_now = b_ref[start + i]
            for g in range(groups):
                lanes = slice(g * 128, g * 128 + 128)
                decay = jnp.exp2(sizes[i : i + 1, lanes] * rates[:, lanes])
                state[g] = decay * state[g] + drives[i : i + 1, lanes] * b_now
        return tuple(state)

    zero = jnp.zeros((states, 128), jnp.float32)
    state = lax.fori_loop(0, rows // 8, step, (zero,) * groups)
    total = jnp.sum(size, axis=0, keepdims=True)
    high = total.astype(jnp.bfloat16).astype(jnp.float32)
    low = total - high
    rest = jnp.zeros((load_ref.shape[0] - states - 2, width), jnp.float32)
    load_ref[...] = jnp.concatenate(
        [jnp.concatenate(state, axis=1), high, low, rest], axis=0
    ).astype(jnp.bfloat16)


def scan_ends(partials, dt_proj, dt_bias, rates, xconv):
    rows, channels = xconv.shape
    states = rates.shape[0]
    width = tile_of(channels, 1024)
    load_rows = -(-(states + 2) // 8) * 8
    wide = jax.ShapeDtypeStruct((rows, states, 128), jnp.float32)
    return pl.pallas_call(
        ends_kernel,
        grid=(channels // width,),
        in_specs=[
            pl.BlockSpec(partials.shape, lambda i: (0, 0, 0)),
            pl.BlockSpec((dt_proj.shape[0], width), lambda i: (0, i)),
            pl.BlockSpec((1, width), lambda i: (0, i)),
            pl.BlockSpec((states, width), lambda i: (0, i)),
            pl.BlockSpec((rows, width), lambda i: (0, i)),
        ],
        out_specs=[
            pl.BlockSpec((rows, width), lambda i: (0, i)),
            pl.BlockSpec((load_rows, width), lambda i: (0, i)),
            pl.BlockSpec(wide.shape, lambda i: (0, 0, 0)),
            pl.BlockSpec(wide.shape, lambda i: (0, 0, 0)),
        ],
        out_shape=[
            jax.ShapeDtypeStruct((rows, channels), jnp.float32),
            jax.ShapeDtypeStruct((load_rows, channels), jnp.bfloat16),
            wide,
            wide,
        ],
        scratch_shapes=[
            pltpu.VMEM((rows, dt_proj.shape[0]), jnp.bfloat16),
            pltpu.VMEM((rows, width), jnp.float32),
        ],
        compiler_params=pltpu.CompilerParams(vmem_limit_bytes=16 * MIB),
        name="scan_ends",
    )(partials, dt_proj, dt_bias, rates, xconv)


def mix_kernel(z_count, x_count, z_place, x_place, *refs):
    count = z_count * x_count
    loads = refs[:count]
    size_ref, x_ref, z_ref, b_ref, c_ref, rate_ref, skip_ref, out_ref = refs[count : count + 8]
    drive_ref, y_ref, load_ref = refs[count + 8 :]
    for k in range(count):
        z_from = lax.rem(z_place[0] + k // x_count, z_count)
        x_from = lax.rem(x_place[0] + k % x_count, x_count)
        load_ref[z_from * x_count + x_from] = loads[k][...].astype(jnp.float32)
    rows, width = x_ref.shape
    states = rate_ref.shape[0]
    groups = width // 128
    rates = rate_ref[...]
    x_f = x_ref[...].astype(jnp.float32)
    drive_ref[...] = size_ref[...] * x_f

    def earlier(j, state):
        block = load_ref[j]
        total = block[states : states + 1] + block[states + 1 : states + 2]
        return jnp.exp2(total * rates) * state + block[:states]

    place = z_place[0] * x_count + x_place[0]
    incoming = lax.fori_loop(0, place, earlier, jnp.zeros((states, width), jnp.float32))

    def step(block, state):
        start = pl.multiple_of(block * 8, 8)
        sizes = size_ref[pl.ds(start, 8), :]
        drives = drive_ref[pl.ds(start, 8), :]
        state = list(state)
        outs = [[None] * 8 for _ in range(groups)]
        for i in range(8):
            b_now = b_ref[start + i]
            c_now = c_ref[start + i]
            for g in range(groups):
                lanes = slice(g * 128, g * 128 + 128)
                decay = jnp.exp2(sizes[i : i + 1, lanes] * rates[:, lanes])
                state[g] = decay * state[g] + drives[i : i + 1, lanes] * b_now
                outs[g][i] = jnp.sum(state[g] * c_now, axis=0, keepdims=True)
        for g in range(groups):
            y_ref[pl.ds(start, 8), g * 128 : g * 128 + 128] = jnp.concatenate(outs[g], axis=0)
        return tuple(state)

    start_state = tuple(incoming[:, g * 128 : g * 128 + 128] for g in range(groups))
    lax.fori_loop(0, rows // 8, step, start_state)
    z_f = z_ref[...].astype(jnp.float32)
    scanned = y_ref[...] + skip_ref[...] * x_f
    out_ref[...] = (scanned * (z_f / (1.0 + jnp.exp(-z_f)))).astype(jnp.bfloat16)


def scan_mix(z_at, x_at, loads, step_size, xconv, z_in, b_wide, c_wide, rates, d_skip):
    rows, channels = xconv.shape
    states = rates.shape[0]
    width = tile_of(channels, 1024)
    flat = [load for pair in loads for load in pair]

    def by_lane(depth):
        return pl.BlockSpec((depth, width), lambda i: (0, i))

    return pl.pallas_call(
        functools.partial(mix_kernel, len(loads), len(loads[0])),
        grid=(channels // width,),
        in_specs=[
            whole_smem(),
            whole_smem(),
            *[by_lane(load.shape[0]) for load in flat],
            by_lane(rows),
            by_lane(rows),
            by_lane(rows),
            pl.BlockSpec(b_wide.shape, lambda i: (0, 0, 0)),
            pl.BlockSpec(c_wide.shape, lambda i: (0, 0, 0)),
            by_lane(states),
            by_lane(1),
        ],
        out_specs=by_lane(rows),
        out_shape=jax.ShapeDtypeStruct((rows, channels), jnp.bfloat16),
        scratch_shapes=[pltpu.VMEM((rows, width), jnp.float32)] * 2
        + [pltpu.VMEM((len(flat), flat[0].shape[0], width), jnp.float32)],
        compiler_params=pltpu.CompilerParams(vmem_limit_bytes=16 * MIB),
        name="scan_mix",
    )(z_at, x_at, *flat, step_size, xconv, z_in, b_wide, c_wide, rates, d_skip)


def out_kernel(z_count, x_count, z_ref, x_ref, *refs):
    blocks, weights = refs[:z_count], refs[z_count : z_count + x_count]
    out_ref, held_ref = refs[z_count + x_count :]
    rows = blocks[0].shape[0]
    columns = weights[0].shape[1]
    for r in range(z_count):
        at = pl.multiple_of(lax.rem(z_ref[0] + r, z_count) * rows, rows)
        held_ref[pl.ds(at, rows), :] = blocks[r][...]
    for i in range(x_count):
        at = pl.multiple_of(lax.rem(x_ref[0] + i, x_count) * columns, columns)
        out_ref[:, pl.ds(at, columns)] = jnp.dot(
            held_ref[...], weights[i][...], preferred_element_type=jnp.float32
        ).astype(jnp.bfloat16)


def out_product(z_at, x_at, blocks, weights):
    rows, depth = blocks[0].shape
    z_count, x_count = len(blocks), len(weights)
    return pl.pallas_call(
        functools.partial(out_kernel, z_count, x_count),
        in_specs=[whole_smem()] * 2 + [whole_vmem()] * (z_count + x_count),
        out_specs=whole_vmem(),
        out_shape=jax.ShapeDtypeStruct(
            (z_count * rows, x_count * weights[0].shape[1]), jnp.bfloat16
        ),
        scratch_shapes=[pltpu.VMEM((z_count * rows, depth), jnp.bfloat16)],
        compiler_params=pltpu.CompilerParams(vmem_limit_bytes=16 * MIB),
        name="out_product",
    )(z_at, x_at, *blocks, *weights)


def hidden_kernel(z_count, x_count, z_ref, x_ref, *refs):
    count = z_count * x_count
    chunks = refs[:count]
    gain_ref, gate_ref, up_ref, act_ref, scaled_ref = refs[count:]
    rows, depth = chunks[0].shape

    @pl.when(pl.program_id(0) == 0)
    def _():
        for i in range(x_count):
            own = [chunks[r * x_count + i] for r in range(z_count)]
            squares = jnp.zeros((rows, 1), jnp.float32)
            for chunk in own:
                h = chunk[...].astype(jnp.float32)
                squares = squares + jnp.sum(h * h, axis=1, keepdims=True)
            scale = lax.rsqrt(squares / (depth * z_count) + eps)
            down = pl.multiple_of(lax.rem(x_ref[0] + i, x_count) * rows, rows)
            for r, chunk in enumerate(own):
                z_at = lax.rem(z_ref[0] + r, z_count)
                across = pl.multiple_of(z_at * depth, depth)
                h = chunk[...].astype(jnp.float32)
                scaled_ref[pl.ds(down, rows), pl.ds(across, depth)] = (
                    h * scale * gain_ref[z_at]
                ).astype(jnp.bfloat16)

    scaled = scaled_ref[...]
    gate = jnp.dot(scaled, gate_ref[0], preferred_element_type=jnp.float32)
    upper = jnp.dot(scaled, up_ref[0], preferred_element_type=jnp.float32)
    act_ref[...] = (gate / (1.0 + jnp.exp(-gate)) * upper).astype(jnp.bfloat16)


def expert_hidden(z_at, x_at, chunks, gain, w_gate, w_up):
    z_count, x_count = len(chunks), len(chunks[0])
    rows, depth = chunks[0][0].shape
    columns = w_gate.shape[2]
    width = tile_of(columns, 256)
    gain = gain.reshape(z_count, 1, depth)
    weight_spec = pl.BlockSpec((1, depth * z_count, width), lambda n: (0, 0, n))
    return pl.pallas_call(
        functools.partial(hidden_kernel, z_count, x_count),
        grid=(columns // width,),
        in_specs=[whole_smem()] * 2
        + [whole_vmem()] * (z_count * x_count + 1)
        + [weight_spec, weight_spec],
        out_specs=pl.BlockSpec((rows * x_count, width), lambda n: (0, n)),
        out_shape=jax.ShapeDtypeStruct((rows * x_count, columns), jnp.bfloat16),
        scratch_shapes=[pltpu.VMEM((rows * x_count, depth * z_count), jnp.bfloat16)],
        compiler_params=pltpu.CompilerParams(vmem_limit_bytes=32 * MIB),
        name="expert_hidden",
    )(z_at, x_at, *[chunk for pair in chunks for chunk in pair], gain, w_gate, w_up)


def down_kernel(x_count, x_ref, block_ref, act_ref, weight_ref, *refs):
    outs, held_ref = refs[:-1], refs[-1]
    held_ref[...] = jnp.dot(act_ref[...], weight_ref[0], preferred_element_type=jnp.float32)
    rows = outs[0].shape[0]
    for i in range(x_count):
        start = pl.multiple_of(lax.rem(x_ref[0] + i, x_count) * rows, rows)
        outs[i][...] = held_ref[pl.ds(start, rows), :].astype(jnp.bfloat16)


def expert_down(x_at, block, x_count, z_count, act, w_down):
    rows, depth = act.shape
    columns = w_down.shape[2] // z_count
    width = tile_of(columns)
    tiles = columns // width
    return pl.pallas_call(
        functools.partial(down_kernel, x_count),
        grid_spec=pltpu.PrefetchScalarGridSpec(
            num_scalar_prefetch=2,
            grid=(tiles,),
            in_specs=[
                pl.BlockSpec((rows, depth), lambda n, x, block: (0, 0)),
                pl.BlockSpec((1, depth, width), lambda n, x, block: (0, 0, block[0] * tiles + n)),
            ],
            out_specs=[pl.BlockSpec((rows // x_count, width), lambda n, x, block: (0, n))] * x_count,
            scratch_shapes=[pltpu.VMEM((rows, width), jnp.float32)],
        ),
        out_shape=[jax.ShapeDtypeStruct((rows // x_count, columns), jnp.bfloat16)] * x_count,
        compiler_params=pltpu.CompilerParams(vmem_limit_bytes=16 * MIB),
        name="expert_down",
    )(x_at, block, act, w_down)


def per_device(
    x_in,
    z_in,
    conv_weight,
    conv_bias,
    x_proj,
    dt_proj,
    dt_bias,
    a_log,
    d_skip,
    out_proj,
    resid,
    norm_gain,
    routes,
    route_gate,
    w_gate,
    w_up,
    w_down,
):
    row_count, channels = x_in.shape
    seq_count = lax.axis_size("seq")
    exp_count = lax.axis_size("exp")
    x_count = seq_count // exp_count
    z_count = exp_count
    seq_at = lax.axis_index("seq")
    exp_at = lax.axis_index("exp")
    z_at, x_at = seq_at // x_count, seq_at % x_count
    z_one = z_at.reshape(1).astype(jnp.int32)
    x_one = x_at.reshape(1).astype(jnp.int32)
    top_count = routes.shape[1]
    capacity = row_count * top_count * 17 // (16 * exp_count)
    pitch = -(-(z_count * capacity) // 16) * 16 // z_count
    feature_slice = resid.shape[1]

    def from_z(block, r):
        pairs = [
            (((z + r) % z_count) * x_count + x, z * x_count + x)
            for z in range(z_count)
            for x in range(x_count)
        ]
        return lax.ppermute(block, "seq", pairs)

    def from_x(block, i):
        pairs = [
            (z * x_count + (x + i) % x_count, z * x_count + x)
            for z in range(z_count)
            for x in range(x_count)
        ]
        return lax.ppermute(block, "seq", pairs)

    def gathered(block):
        rows = {(0, 0): block}
        for i in range(1, x_count):
            rows[0, i] = from_x(block, i)
        turns = sorted(range(1, z_count), key=lambda r: min(r, z_count - r))
        for k, r in enumerate(turns):
            if k >= 2:
                block, rows[turns[k - 2], 0] = lax.optimization_barrier(
                    (block, rows[turns[k - 2], 0])
                )
            rows[r, 0] = from_z(block, r)
        for r in turns:
            for i in range(1, x_count):
                rows[r, i] = from_x(rows[r, 0], i)
        return [[rows[r, i] for i in range(x_count)] for r in range(z_count)]

    swap = [
        ((e * x_count + x) * exp_count + z, (z * x_count + x) * exp_count + e)
        for z in range(z_count)
        for x in range(x_count)
        for e in range(exp_count)
    ]

    halo = lax.ppermute(
        x_in[row_count - 8 :], "seq", [(i, i + 1) for i in range(seq_count - 1)]
    )

    routes_rows = jnp.pad(
        routes.T.astype(jnp.bfloat16), ((0, 8 - top_count), (0, feature_slice - row_count))
    )
    group = lax.ppermute(jnp.concatenate([resid, routes_rows], axis=0), ("seq", "exp"), swap)

    def slots_of(named):
        flat = named.reshape(-1, row_count * top_count)
        onehot = (flat[:, :, None] == jnp.arange(exp_count, dtype=jnp.int32)).astype(jnp.float32)
        below = jnp.tril(jnp.ones((row_count * top_count,) * 2, jnp.float32), -1)
        counts = jnp.einsum("ij,bje->bie", below, onehot)
        slots = jnp.sum(counts * onehot, axis=2).astype(jnp.int32)
        return slots.reshape(-1, row_count, top_count)

    own_slots = slots_of(routes)[0]
    own_target = (routes - z_at) % exp_count * pitch + own_slots
    slot_ids = jnp.arange(exp_count * pitch, dtype=jnp.int32)
    choose = (own_target.T[:, :, None] == slot_ids[None, None, :]).astype(jnp.bfloat16)
    choose = choose.reshape(top_count * row_count, exp_count * pitch)

    rates = -jnp.exp(a_log.T) * LOG2E
    xconv, copies = conv_and_project(
        x_in, halo, conv_weight, conv_bias[None], x_proj.T, exp_count
    )
    cut = channels * 5 // 8
    copies, group, upper = lax.optimization_barrier((copies, group, out_proj[:cut]))
    uppers = [from_x(upper, i) for i in range(1, x_count)]
    partials = lax.all_to_all(copies, "exp", 0, 0, tiled=True)
    resid_here = group[:row_count]
    group_routes = group[row_count : row_count + top_count, :row_count].T.astype(jnp.int32)
    target = group_routes * pitch + slots_of(group_routes)[0]
    dispatch = jnp.sum(
        (target[None, :, :] == slot_ids[:, None, None]).astype(jnp.float32), axis=2
    ).astype(jnp.bfloat16)
    step_size, load, b_wide, c_wide = scan_ends(partials, dt_proj, dt_bias[None], rates, xconv)
    load, *uppers = lax.optimization_barrier((load, *uppers))
    loads = gathered(load)
    held = lax.optimization_barrier((out_proj[cut:], *[part for pair in loads for part in pair]))
    lowers = [from_x(held[0], i) for i in range(1, x_count)]
    loads = [held[1 + r * x_count : 1 + (r + 1) * x_count] for r in range(z_count)]
    columns = [out_proj] + [jnp.concatenate(pair, axis=0) for pair in zip(uppers, lowers)]
    mixed = scan_mix(
        z_one, x_one, loads, step_size, xconv, z_in, b_wide, c_wide, rates, d_skip[None]
    )
    along_z = [mixed] + [from_z(mixed, r) for r in range(1, z_count)]
    partial_out = out_product(z_one, x_one, along_z, columns)
    arrived = lax.all_to_all(
        partial_out.reshape(exp_count, row_count, feature_slice), "exp", 0, 0, tiled=True
    )
    mamba_out = jnp.sum(arrived.astype(jnp.float32), axis=0)
    hidden_state = (resid_here.astype(jnp.float32) + mamba_out).astype(jnp.bfloat16)

    outgoing = jnp.dot(dispatch, hidden_state, preferred_element_type=jnp.float32)
    outgoing = outgoing.astype(jnp.bfloat16).reshape(exp_count, pitch, feature_slice)
    rows_here = lax.all_to_all(outgoing, "exp", 0, 0, tiled=True)
    rows_here = rows_here.reshape(exp_count * pitch, feature_slice)
    chunks = gathered(rows_here)
    held = lax.optimization_barrier((hidden_state, *[part for pair in chunks for part in pair]))
    hidden_own = lax.ppermute(held[0], ("seq", "exp"), swap)
    chunks = [held[1 + r * x_count : 1 + (r + 1) * x_count] for r in range(z_count)]
    act = expert_hidden(z_one, x_one, chunks, norm_gain, w_gate, w_up)
    act, hidden_own = lax.optimization_barrier((act, hidden_own))

    by_distance = sorted(range(1, z_count), key=lambda r: abs(r - z_count // 2)) + [0]
    down = {}
    for r in by_distance:
        block = ((z_at + r) % z_count).reshape(1).astype(jnp.int32)
        down[r] = expert_down(x_one, block, x_count, z_count, act, w_down)
    crossed = {}
    for r in by_distance:
        crossed[r] = [from_x(down[r][i], x_count - i) for i in range(1, x_count)]

    def over_x(r):
        return functools.reduce(
            jnp.add, [p.astype(jnp.float32) for p in [down[r][0]] + crossed[r]]
        )

    arrivals = [
        from_z(over_x(r).astype(jnp.bfloat16), z_count - r) for r in by_distance if r
    ]
    total = over_x(0)
    for sent in arrivals:
        total = total + sent.astype(jnp.float32)
    expert_out = total.astype(jnp.bfloat16)
    pieces = expert_out.reshape(exp_count, pitch, feature_slice)
    back = []
    for k in range(exp_count):
        piece = lax.dynamic_index_in_dim(pieces, (exp_at - k) % exp_count, 0, keepdims=False)
        pairs = [
            (
                (e * x_count + x) * exp_count + (z + k) % exp_count,
                (z * x_count + x) * exp_count + e,
            )
            for z in range(z_count)
            for x in range(x_count)
            for e in range(exp_count)
        ]
        back.append(lax.ppermute(piece, ("seq", "exp"), pairs))
    back = jnp.concatenate(back, axis=0)
    picked = jnp.dot(choose, back, preferred_element_type=jnp.float32)
    picked = picked.reshape(top_count, row_count, feature_slice)
    moe = jnp.sum(route_gate.T[:, :, None] * picked, axis=0)
    return (hidden_own.astype(jnp.float32) + moe).astype(jnp.bfloat16)


def solution(mesh):
    return jax.shard_map(
        per_device,
        mesh=mesh,
        in_specs=(
            P("seq", "exp"),
            P("seq", "exp"),
            P(None, "exp"),
            P("exp"),
            P("exp", None),
            P(None, "exp"),
            P("exp"),
            P("exp", None),
            P("exp"),
            P("exp", "seq"),
            P("seq", "exp"),
            P(),
            P("seq", None),
            P("seq", None),
            P("exp", None, "seq"),
            P("exp", None, "seq"),
            P("exp", "seq", None),
        ),
        out_specs=P("seq", "exp"),
        check_vma=False,
    )
```

```python
import functools
import math

import jax
import jax.numpy as jnp
from jax import lax
from jax.experimental import pallas as pl
from jax.experimental.pallas import tpu as pltpu
from jax.sharding import PartitionSpec as P

eps = 1e-05
LOG2E = 1.4426950408889634
MIB = 1 << 20


def tile_of(size, most=512):
    return max(t for t in range(128, most + 1, 128) if size % t == 0)


def whole_vmem():
    return pl.BlockSpec(memory_space=pltpu.VMEM)


def whole_smem():
    return pl.BlockSpec(memory_space=pltpu.SMEM)


def conv_kernel(x_ref, halo_ref, weight_ref, bias_ref, proj_ref, xconv_ref, partial_ref):
    rows = x_ref.shape[0]
    taps = weight_ref.shape[0]
    extended = jnp.concatenate(
        [halo_ref[...].astype(jnp.float32), x_ref[...].astype(jnp.float32)], axis=0
    )
    pad = halo_ref.shape[0]
    conv = jnp.zeros(x_ref.shape, jnp.float32) + bias_ref[...]
    for tap in range(taps):
        start = pad - (taps - 1) + tap
        conv = conv + weight_ref[tap : tap + 1, :] * extended[start : start + rows]
    xconv = (conv / (1.0 + jnp.exp(-conv))).astype(jnp.bfloat16)
    xconv_ref[...] = xconv

    @pl.when(pl.program_id(0) == 0)
    def _():
        partial_ref[0] = jnp.zeros(partial_ref.shape[1:], jnp.float32)

    partial_ref[0] += lax.dot_general(
        xconv, proj_ref[...], (((1,), (1,)), ((), ())), preferred_element_type=jnp.float32
    )

    @pl.when(pl.program_id(0) == pl.num_programs(0) - 1)
    def _():
        for copy in range(1, partial_ref.shape[0]):
            partial_ref[copy] = partial_ref[0]


def conv_and_project(x_in, halo, conv_weight, conv_bias, x_proj_t, copies):
    rows, channels = x_in.shape
    width = tile_of(channels)
    columns = x_proj_t.shape[0]
    return pl.pallas_call(
        conv_kernel,
        grid=(channels // width,),
        in_specs=[
            pl.BlockSpec((rows, width), lambda i: (0, i)),
            pl.BlockSpec((halo.shape[0], width), lambda i: (0, i)),
            pl.BlockSpec((conv_weight.shape[0], width), lambda i: (0, i)),
            pl.BlockSpec((1, width), lambda i: (0, i)),
            pl.BlockSpec((columns, width), lambda i: (0, i)),
        ],
        out_specs=[
            pl.BlockSpec((rows, width), lambda i: (0, i)),
            pl.BlockSpec((copies, rows, columns), lambda i: (0, 0, 0)),
        ],
        out_shape=[
            jax.ShapeDtypeStruct((rows, channels), jnp.bfloat16),
            jax.ShapeDtypeStruct((copies, rows, columns), jnp.float32),
        ],
        name="conv_project",
    )(x_in, halo, conv_weight, conv_bias, x_proj_t)


def softplus(v):
    return jnp.maximum(v, 0.0) + jnp.log1p(jnp.exp(-jnp.abs(v)))


def ends_kernel(
    part_ref, proj_ref, bias_ref, rate_ref, x_ref, size_ref, load_ref, b_ref, c_ref, low_ref, drive_ref
):
    rows, width = x_ref.shape
    states = rate_ref.shape[0]
    low_rank = low_ref.shape[1]
    groups = width // 128

    @pl.when(pl.program_id(0) == 0)
    def _():
        total = part_ref[0]
        for e in range(1, part_ref.shape[0]):
            total = total + part_ref[e]
        low_ref[...] = total[:, :low_rank].astype(jnp.bfloat16)
        b_mat = total[:, low_rank : low_rank + states]
        c_mat = total[:, low_rank + states : low_rank + 2 * states]
        b_ref[...] = jnp.broadcast_to(b_mat[:, :, None], b_ref.shape)
        c_ref[...] = jnp.broadcast_to(c_mat[:, :, None], c_ref.shape)

    size = softplus(
        jnp.dot(low_ref[...], proj_ref[...], preferred_element_type=jnp.float32) + bias_ref[...]
    )
    size_ref[...] = size
    drive_ref[...] = size * x_ref[...].astype(jnp.float32)
    rates = rate_ref[...]

    def step(block, state):
        start = pl.multiple_of(block * 8, 8)
        sizes = size_ref[pl.ds(start, 8), :]
        drives = drive_ref[pl.ds(start, 8), :]
        state = list(state)
        for i in range(8):
            b_now = b_ref[start + i]
            for g in range(groups):
                lanes = slice(g * 128, g * 128 + 128)
                decay = jnp.exp2(sizes[i : i + 1, lanes] * rates[:, lanes])
                state[g] = decay * state[g] + drives[i : i + 1, lanes] * b_now
        return tuple(state)

    zero = jnp.zeros((states, 128), jnp.float32)
    state = lax.fori_loop(0, rows // 8, step, (zero,) * groups)
    total = jnp.sum(size, axis=0, keepdims=True)
    high = total.astype(jnp.bfloat16).astype(jnp.float32)
    low = total - high
    rest = jnp.zeros((load_ref.shape[0] - states - 2, width), jnp.float32)
    load_ref[...] = jnp.concatenate(
        [jnp.concatenate(state, axis=1), high, low, rest], axis=0
    ).astype(jnp.bfloat16)


def scan_ends(partials, dt_proj, dt_bias, rates, xconv):
    rows, channels = xconv.shape
    states = rates.shape[0]
    width = tile_of(channels, 1024)
    load_rows = -(-(states + 2) // 8) * 8
    wide = jax.ShapeDtypeStruct((rows, states, 128), jnp.float32)
    return pl.pallas_call(
        ends_kernel,
        grid=(channels // width,),
        in_specs=[
            pl.BlockSpec(partials.shape, lambda i: (0, 0, 0)),
            pl.BlockSpec((dt_proj.shape[0], width), lambda i: (0, i)),
            pl.BlockSpec((1, width), lambda i: (0, i)),
            pl.BlockSpec((states, width), lambda i: (0, i)),
            pl.BlockSpec((rows, width), lambda i: (0, i)),
        ],
        out_specs=[
            pl.BlockSpec((rows, width), lambda i: (0, i)),
            pl.BlockSpec((load_rows, width), lambda i: (0, i)),
            pl.BlockSpec(wide.shape, lambda i: (0, 0, 0)),
            pl.BlockSpec(wide.shape, lambda i: (0, 0, 0)),
        ],
        out_shape=[
            jax.ShapeDtypeStruct((rows, channels), jnp.float32),
            jax.ShapeDtypeStruct((load_rows, channels), jnp.bfloat16),
            wide,
            wide,
        ],
        scratch_shapes=[
            pltpu.VMEM((rows, dt_proj.shape[0]), jnp.bfloat16),
            pltpu.VMEM((rows, width), jnp.float32),
        ],
        name="scan_ends",
    )(partials, dt_proj, dt_bias, rates, xconv)


def mix_kernel(z_count, x_count, z_place, x_place, *refs):
    count = z_count * x_count
    loads = refs[:count]
    size_ref, x_ref, z_ref, b_ref, c_ref, rate_ref, skip_ref, out_ref = refs[count : count + 8]
    drive_ref, y_ref, load_ref = refs[count + 8 :]
    for k in range(count):
        z_from = lax.rem(z_place[0] + k // x_count, z_count)
        x_from = lax.rem(x_place[0] + k % x_count, x_count)
        load_ref[z_from * x_count + x_from] = loads[k][...].astype(jnp.float32)
    rows, width = x_ref.shape
    states = rate_ref.shape[0]
    groups = width // 128
    rates = rate_ref[...]
    x_f = x_ref[...].astype(jnp.float32)
    drive_ref[...] = size_ref[...] * x_f

    def earlier(j, state):
        block = load_ref[j]
        total = block[states : states + 1] + block[states + 1 : states + 2]
        return jnp.exp2(total * rates) * state + block[:states]

    place = z_place[0] * x_count + x_place[0]
    incoming = lax.fori_loop(0, place, earlier, jnp.zeros((states, width), jnp.float32))

    def step(block, state):
        start = pl.multiple_of(block * 8, 8)
        sizes = size_ref[pl.ds(start, 8), :]
        drives = drive_ref[pl.ds(start, 8), :]
        state = list(state)
        outs = [[None] * 8 for _ in range(groups)]
        for i in range(8):
            b_now = b_ref[start + i]
            c_now = c_ref[start + i]
            for g in range(groups):
                lanes = slice(g * 128, g * 128 + 128)
                decay = jnp.exp2(sizes[i : i + 1, lanes] * rates[:, lanes])
                state[g] = decay * state[g] + drives[i : i + 1, lanes] * b_now
                outs[g][i] = jnp.sum(state[g] * c_now, axis=0, keepdims=True)
        for g in range(groups):
            y_ref[pl.ds(start, 8), g * 128 : g * 128 + 128] = jnp.concatenate(outs[g], axis=0)
        return tuple(state)

    start_state = tuple(incoming[:, g * 128 : g * 128 + 128] for g in range(groups))
    lax.fori_loop(0, rows // 8, step, start_state)
    z_f = z_ref[...].astype(jnp.float32)
    scanned = y_ref[...] + skip_ref[...] * x_f
    out_ref[...] = (scanned * (z_f / (1.0 + jnp.exp(-z_f)))).astype(jnp.bfloat16)


def scan_mix(z_at, x_at, loads, step_size, xconv, z_in, b_wide, c_wide, rates, d_skip):
    rows, channels = xconv.shape
    states = rates.shape[0]
    width = tile_of(channels, 1024)
    flat = [load for pair in loads for load in pair]

    def by_lane(depth):
        return pl.BlockSpec((depth, width), lambda i: (0, i))

    return pl.pallas_call(
        functools.partial(mix_kernel, len(loads), len(loads[0])),
        grid=(channels // width,),
        in_specs=[
            whole_smem(),
            whole_smem(),
            *[by_lane(load.shape[0]) for load in flat],
            by_lane(rows),
            by_lane(rows),
            by_lane(rows),
            pl.BlockSpec(b_wide.shape, lambda i: (0, 0, 0)),
            pl.BlockSpec(c_wide.shape, lambda i: (0, 0, 0)),
            by_lane(states),
            by_lane(1),
        ],
        out_specs=by_lane(rows),
        out_shape=jax.ShapeDtypeStruct((rows, channels), jnp.bfloat16),
        scratch_shapes=[pltpu.VMEM((rows, width), jnp.float32)] * 2
        + [pltpu.VMEM((len(flat), flat[0].shape[0], width), jnp.float32)],
        name="scan_mix",
    )(z_at, x_at, *flat, step_size, xconv, z_in, b_wide, c_wide, rates, d_skip)


def out_kernel(z_count, x_count, z_ref, x_ref, *refs):
    blocks, weights = refs[:z_count], refs[z_count : z_count + x_count]
    out_ref, held_ref = refs[z_count + x_count :]
    rows = blocks[0].shape[0]
    columns = weights[0].shape[1]
    for r in range(z_count):
        at = pl.multiple_of(lax.rem(z_ref[0] + r, z_count) * rows, rows)
        held_ref[pl.ds(at, rows), :] = blocks[r][...]
    for i in range(x_count):
        at = pl.multiple_of(lax.rem(x_ref[0] + i, x_count) * columns, columns)
        out_ref[:, pl.ds(at, columns)] = jnp.dot(
            held_ref[...], weights[i][...], preferred_element_type=jnp.float32
        ).astype(jnp.bfloat16)


def out_product(z_at, x_at, blocks, weights):
    rows, depth = blocks[0].shape
    z_count, x_count = len(blocks), len(weights)
    return pl.pallas_call(
        functools.partial(out_kernel, z_count, x_count),
        in_specs=[whole_smem()] * 2 + [whole_vmem()] * (z_count + x_count),
        out_specs=whole_vmem(),
        out_shape=jax.ShapeDtypeStruct(
            (z_count * rows, x_count * weights[0].shape[1]), jnp.bfloat16
        ),
        scratch_shapes=[pltpu.VMEM((z_count * rows, depth), jnp.bfloat16)],
        compiler_params=pltpu.CompilerParams(vmem_limit_bytes=16 * MIB),
        name="out_product",
    )(z_at, x_at, *blocks, *weights)


def hidden_kernel(turns, z_count, x_count, first, last, z_ref, x_ref, *refs):
    refs = list(refs)
    take = lambda count: [refs.pop(0) for _ in range(count)]
    chunks = take(len(turns) * x_count)
    (gain_ref,) = take(1)
    gates, uppers = take(len(turns)), take(len(turns))
    before = None if first else take(3)
    outs = take(1) if last else take(3)
    scaled_ref, squares_ref = refs
    rows, depth = chunks[0].shape
    padded = scaled_ref.shape[0] // x_count

    @pl.when(pl.program_id(0) == 0)
    def _():
        rest = jnp.zeros((padded - rows, depth), jnp.float32)
        for i in range(x_count):
            down = pl.ds(pl.multiple_of(lax.rem(x_ref[0] + i, x_count) * padded, padded), padded)
            squares = jnp.zeros((padded, 1), jnp.float32)
            for j, r in enumerate(turns):
                h = chunks[j * x_count + i][...].astype(jnp.float32)
                if padded > rows:
                    h = jnp.concatenate([h, rest], axis=0)
                squares = squares + jnp.sum(h * h, axis=1, keepdims=True)
                gain = gain_ref[lax.rem(z_ref[0] + r, z_count)]
                scaled_ref[down, j * depth : (j + 1) * depth] = (h * gain).astype(jnp.bfloat16)
            squares_ref[down, :] = jnp.broadcast_to(squares, (padded, 128))
        if not first:
            squares_ref[...] += before[2][...]
        if not last:
            outs[2][...] = squares_ref[...]

    def product(weights):
        parts = [
            jnp.dot(
                scaled_ref[:, j * depth : (j + 1) * depth],
                weight[0],
                preferred_element_type=jnp.float32,
            )
            for j, weight in enumerate(weights)
        ]
        return functools.reduce(jnp.add, parts)

    gate, upper = product(gates), product(uppers)
    if not first:
        gate, upper = gate + before[0][...], upper + before[1][...]
    if last:
        scale = lax.rsqrt(squares_ref[:, :1] / (depth * z_count) + eps)
        gate, upper = gate * scale, upper * scale
        outs[0][...] = (gate / (1.0 + jnp.exp(-gate)) * upper).astype(jnp.bfloat16)
    else:
        outs[0][...] = gate
        outs[1][...] = upper


def expert_hidden(z_at, x_at, z_count, turns, chunks, gain, w_gate, w_up, before, last):
    x_count = len(chunks[0])
    rows, depth = chunks[0][0].shape
    columns = w_gate.shape[2]
    width = tile_of(columns, 256)
    padded = -(-rows // 16) * 16 * x_count
    gain = gain.reshape(z_count, 1, depth)

    def weight_spec(r):
        return pl.BlockSpec((1, depth, width), lambda n, z, x: (0, lax.rem(z[0] + r, z_count), n))

    sums = pl.BlockSpec((padded, width), lambda n, z, x: (0, n))
    squares = pl.BlockSpec((padded, 128), lambda n, z, x: (0, 0))
    weights = [weight_spec(r) for r in turns]
    out_specs = [sums] if last else [sums, sums, squares]
    out_shape = [jax.ShapeDtypeStruct((padded, columns), jnp.bfloat16)]
    if not last:
        out_shape = [jax.ShapeDtypeStruct((padded, columns), jnp.float32)] * 2
        out_shape.append(jax.ShapeDtypeStruct((padded, 128), jnp.float32))
    flat = [chunk for pair in chunks for chunk in pair]
    flops = 4 * padded * depth * len(turns) * columns
    return pl.pallas_call(
        functools.partial(hidden_kernel, turns, z_count, x_count, before is None, last),
        grid_spec=pltpu.PrefetchScalarGridSpec(
            num_scalar_prefetch=2,
            grid=(columns // width,),
            in_specs=[whole_vmem()] * (len(flat) + 1)
            + weights * 2
            + ([] if before is None else [sums, sums, squares]),
            out_specs=out_specs,
            scratch_shapes=[
                pltpu.VMEM((padded, depth * len(turns)), jnp.bfloat16),
                pltpu.VMEM((padded, 128), jnp.float32),
            ],
        ),
        out_shape=out_shape,
        compiler_params=pltpu.CompilerParams(vmem_limit_bytes=50 * MIB),
        cost_estimate=pl.CostEstimate(
            flops=flops, bytes_accessed=4 * depth * len(turns) * columns, transcendentals=0
        ),
        name="expert_hidden",
    )(
        z_at,
        x_at,
        *flat,
        gain,
        *[w_gate] * len(turns),
        *[w_up] * len(turns),
        *(before or []),
    )


def down_kernel(x_count, x_ref, block_ref, act_ref, weight_ref, *refs):
    outs, held_ref = refs[:-1], refs[-1]
    held_ref[...] = jnp.dot(act_ref[...], weight_ref[0], preferred_element_type=jnp.float32)
    rows = outs[0].shape[0]
    padded = held_ref.shape[0] // x_count
    for i in range(x_count):
        start = pl.multiple_of(lax.rem(x_ref[0] + i, x_count) * padded, padded)
        outs[i][...] = held_ref[pl.ds(start, rows), :].astype(jnp.bfloat16)


def expert_down(x_at, block, x_count, z_count, rows, act, w_down):
    padded, depth = act.shape
    columns = w_down.shape[2] // z_count
    width = tile_of(columns)
    tiles = columns // width
    return pl.pallas_call(
        functools.partial(down_kernel, x_count),
        grid_spec=pltpu.PrefetchScalarGridSpec(
            num_scalar_prefetch=2,
            grid=(tiles,),
            in_specs=[
                pl.BlockSpec((padded, depth), lambda n, x, block: (0, 0)),
                pl.BlockSpec((1, depth, width), lambda n, x, block: (0, 0, block[0] * tiles + n)),
            ],
            out_specs=[pl.BlockSpec((rows, width), lambda n, x, block: (0, n))] * x_count,
            scratch_shapes=[pltpu.VMEM((padded, width), jnp.float32)],
        ),
        out_shape=[jax.ShapeDtypeStruct((rows, columns), jnp.bfloat16)] * x_count,
        compiler_params=pltpu.CompilerParams(vmem_limit_bytes=50 * MIB),
        cost_estimate=pl.CostEstimate(
            flops=2 * padded * depth * columns,
            bytes_accessed=2 * depth * columns,
            transcendentals=0,
        ),
        name="expert_down",
    )(x_at, block, act, w_down)


def per_device(
    x_in,
    z_in,
    conv_weight,
    conv_bias,
    x_proj,
    dt_proj,
    dt_bias,
    a_log,
    d_skip,
    out_proj,
    resid,
    norm_gain,
    routes,
    route_gate,
    w_gate,
    w_up,
    w_down,
):
    row_count, channels = x_in.shape
    seq_count = lax.axis_size("seq")
    exp_count = lax.axis_size("exp")
    x_count = seq_count // exp_count
    z_count = exp_count
    seq_at = lax.axis_index("seq")
    exp_at = lax.axis_index("exp")
    z_at, x_at = seq_at // x_count, seq_at % x_count
    z_one = z_at.reshape(1).astype(jnp.int32)
    x_one = x_at.reshape(1).astype(jnp.int32)
    top_count = routes.shape[1]
    capacity = row_count * top_count * 17 // (16 * exp_count)
    pitch = capacity
    feature_slice = resid.shape[1]

    def from_z(block, r):
        pairs = [
            (((z + r) % z_count) * x_count + x, z * x_count + x)
            for z in range(z_count)
            for x in range(x_count)
        ]
        return lax.ppermute(block, "seq", pairs)

    def from_x(block, i):
        pairs = [
            (z * x_count + (x + i) % x_count, z * x_count + x)
            for z in range(z_count)
            for x in range(x_count)
        ]
        return lax.ppermute(block, "seq", pairs)

    turns = sorted(range(1, z_count), key=lambda r: min(r, z_count - r))

    def gathered(block, between=None):
        rows = {(0, 0): block}
        for i in range(1, x_count):
            rows[0, i] = from_x(block, i)
        for k, r in enumerate(turns):
            if k >= 2:
                block, rows[turns[k - 2], 0] = lax.optimization_barrier(
                    (block, rows[turns[k - 2], 0])
                )
            rows[r, 0] = from_z(block, r)
        for r in turns:
            if r == turns[-1] and between is not None:
                rows[r, 0] = between(rows)
            for i in range(1, x_count):
                rows[r, i] = from_x(rows[r, 0], i)
        return [[rows[r, i] for i in range(x_count)] for r in range(z_count)]

    swap = [
        ((e * x_count + x) * exp_count + z, (z * x_count + x) * exp_count + e)
        for z in range(z_count)
        for x in range(x_count)
        for e in range(exp_count)
    ]

    halo = lax.ppermute(
        x_in[row_count - 8 :], "seq", [(i, i + 1) for i in range(seq_count - 1)]
    )

    routes_rows = jnp.pad(
        routes.T.astype(jnp.bfloat16), ((0, 8 - top_count), (0, feature_slice - row_count))
    )
    group = lax.ppermute(jnp.concatenate([resid, routes_rows], axis=0), ("seq", "exp"), swap)

    def slots_of(named):
        flat = named.reshape(-1, row_count * top_count)
        onehot = (flat[:, :, None] == jnp.arange(exp_count, dtype=jnp.int32)).astype(jnp.float32)
        below = jnp.tril(jnp.ones((row_count * top_count,) * 2, jnp.float32), -1)
        counts = jnp.einsum("ij,bje->bie", below, onehot)
        slots = jnp.sum(counts * onehot, axis=2).astype(jnp.int32)
        return slots.reshape(-1, row_count, top_count)

    own_slots = slots_of(routes)[0]
    own_target = (routes - z_at) % exp_count * pitch + own_slots
    slot_ids = jnp.arange(exp_count * pitch, dtype=jnp.int32)
    choose = (own_target.T[:, :, None] == slot_ids[None, None, :]).astype(jnp.bfloat16)
    choose = choose.reshape(top_count * row_count, exp_count * pitch)

    rates = -jnp.exp(a_log.T) * LOG2E
    xconv, copies = conv_and_project(
        x_in, halo, conv_weight, conv_bias[None], x_proj.T, exp_count
    )
    cut = channels * 3 // 8
    copies, group, held_proj = lax.optimization_barrier((copies, group, out_proj))
    uppers = [from_x(held_proj[:cut], i) for i in range(1, x_count)]
    partials = lax.all_to_all(copies, "exp", 0, 0, tiled=True)
    resid_here = group[:row_count]
    group_routes = group[row_count : row_count + top_count, :row_count].T.astype(jnp.int32)
    target = group_routes * pitch + slots_of(group_routes)[0]
    dispatch = jnp.sum(
        (target[None, :, :] == slot_ids[:, None, None]).astype(jnp.float32), axis=2
    ).astype(jnp.bfloat16)
    step_size, load, b_wide, c_wide = scan_ends(partials, dt_proj, dt_bias[None], rates, xconv)
    load, *uppers = lax.optimization_barrier((load, *uppers))
    loads = gathered(load)
    held = lax.optimization_barrier((held_proj, *[part for pair in loads for part in pair]))
    lowers = [from_x(held[0][cut:], i) for i in range(1, x_count)]
    loads = [held[1 + r * x_count : 1 + (r + 1) * x_count] for r in range(z_count)]
    columns = [out_proj] + [jnp.concatenate(pair, axis=0) for pair in zip(uppers, lowers)]
    mixed = scan_mix(
        z_one, x_one, loads, step_size, xconv, z_in, b_wide, c_wide, rates, d_skip[None]
    )
    along_z = [mixed] + [from_z(mixed, r) for r in range(1, z_count)]
    partial_out = out_product(z_one, x_one, along_z, columns)
    arrived = lax.all_to_all(
        partial_out.reshape(exp_count, row_count, feature_slice), "exp", 0, 0, tiled=True
    )
    mamba_out = jnp.sum(arrived.astype(jnp.float32), axis=0)
    hidden_state = (resid_here.astype(jnp.float32) + mamba_out).astype(jnp.bfloat16)

    outgoing = jnp.dot(dispatch, hidden_state, preferred_element_type=jnp.float32)
    outgoing = outgoing.astype(jnp.bfloat16).reshape(exp_count, pitch, feature_slice)
    rows_here = lax.all_to_all(outgoing, "exp", 0, 0, tiled=True)
    rows_here = rows_here.reshape(exp_count * pitch, feature_slice)
    early_turns = [0] + turns[: z_count // 2 - 1]
    late_turns = turns[z_count // 2 - 1 :]
    before = []

    def early_hidden(rows):
        parts = [[rows[r, i] for i in range(x_count)] for r in early_turns]
        sums = expert_hidden(
            z_one, x_one, z_count, early_turns, parts, norm_gain, w_gate, w_up, None, False
        )
        *sums, last = lax.optimization_barrier((*sums, rows[turns[-1], 0]))
        before.extend(sums)
        return last

    chunks = gathered(rows_here, early_hidden)
    chunks = [chunks[r] for r in late_turns]
    held = lax.optimization_barrier((hidden_state, *[part for pair in chunks for part in pair]))
    hidden_own = lax.ppermute(held[0], ("seq", "exp"), swap)
    chunks = [held[1 + k * x_count : 1 + (k + 1) * x_count] for k in range(len(late_turns))]
    (act,) = expert_hidden(
        z_one, x_one, z_count, late_turns, chunks, norm_gain, w_gate, w_up, before, True
    )
    act, hidden_own = lax.optimization_barrier((act, hidden_own))

    by_distance = sorted(range(1, z_count), key=lambda r: abs(r - z_count // 2)) + [0]
    down, crossed = {}, {}
    for k, r in enumerate(by_distance):
        if k >= 2:
            ahead = by_distance[k - 2]
            act, *crossed[ahead] = lax.optimization_barrier((act, *crossed[ahead]))
        block = ((z_at + r) % z_count).reshape(1).astype(jnp.int32)
        down[r] = expert_down(x_one, block, x_count, z_count, exp_count * pitch, act, w_down)
        crossed[r] = [from_x(down[r][i], x_count - i) for i in range(1, x_count)]

    def over_x(r):
        return functools.reduce(
            jnp.add, [p.astype(jnp.float32) for p in [down[r][0]] + crossed[r]]
        )

    arrivals = [
        from_z(over_x(r).astype(jnp.bfloat16), z_count - r) for r in by_distance if r
    ]
    total = over_x(0)
    for sent in arrivals:
        total = total + sent.astype(jnp.float32)
    expert_out = total.astype(jnp.bfloat16)
    pieces = expert_out.reshape(exp_count, pitch, feature_slice)
    back = []
    for k in range(exp_count):
        piece = lax.dynamic_index_in_dim(pieces, (exp_at - k) % exp_count, 0, keepdims=False)
        pairs = [
            (
                (e * x_count + x) * exp_count + (z + k) % exp_count,
                (z * x_count + x) * exp_count + e,
            )
            for z in range(z_count)
            for x in range(x_count)
            for e in range(exp_count)
        ]
        back.append(lax.ppermute(piece, ("seq", "exp"), pairs))
    back = jnp.concatenate(back, axis=0)
    picked = jnp.dot(choose, back, preferred_element_type=jnp.float32)
    picked = picked.reshape(top_count, row_count, feature_slice)
    moe = jnp.sum(route_gate.T[:, :, None] * picked, axis=0)
    return (hidden_own.astype(jnp.float32) + moe).astype(jnp.bfloat16)


def solution(mesh):
    return jax.shard_map(
        per_device,
        mesh=mesh,
        in_specs=(
            P("seq", "exp"),
            P("seq", "exp"),
            P(None, "exp"),
            P("exp"),
            P("exp", None),
            P(None, "exp"),
            P("exp"),
            P("exp", None),
            P("exp"),
            P("exp", "seq"),
            P("seq", "exp"),
            P(),
            P("seq", None),
            P("seq", None),
            P("exp", None, "seq"),
            P("exp", None, "seq"),
            P("exp", "seq", None),
        ),
        out_specs=P("seq", "exp"),
        check_vma=False,
    )
```

```python
import functools
import math

import jax
import jax.numpy as jnp
from jax import lax
from jax.experimental import pallas as pl
from jax.experimental.pallas import tpu as pltpu
from jax.sharding import PartitionSpec as P

eps = 1e-05
LOG2E = 1.4426950408889634
MIB = 1 << 20


def tile_of(size, most=512):
    return max(t for t in range(128, most + 1, 128) if size % t == 0)


def after(value, *others):
    return lax.optimization_barrier((value, *others))[0]


def whole_vmem():
    return pl.BlockSpec(memory_space=pltpu.VMEM)


def whole_smem():
    return pl.BlockSpec(memory_space=pltpu.SMEM)


def conv_kernel(x_ref, halo_ref, weight_ref, bias_ref, proj_ref, xconv_ref, partial_ref):
    rows = x_ref.shape[0]
    taps = weight_ref.shape[0]
    extended = jnp.concatenate(
        [halo_ref[...].astype(jnp.float32), x_ref[...].astype(jnp.float32)], axis=0
    )
    pad = halo_ref.shape[0]
    conv = jnp.zeros(x_ref.shape, jnp.float32) + bias_ref[...]
    for tap in range(taps):
        start = pad - (taps - 1) + tap
        conv = conv + weight_ref[tap : tap + 1, :] * extended[start : start + rows]
    xconv = (conv / (1.0 + jnp.exp(-conv))).astype(jnp.bfloat16)
    xconv_ref[...] = xconv

    @pl.when(pl.program_id(0) == 0)
    def _():
        partial_ref[0] = jnp.zeros(partial_ref.shape[1:], jnp.float32)

    partial_ref[0] += lax.dot_general(
        xconv, proj_ref[...], (((1,), (1,)), ((), ())), preferred_element_type=jnp.float32
    )

    @pl.when(pl.program_id(0) == pl.num_programs(0) - 1)
    def _():
        for copy in range(1, partial_ref.shape[0]):
            partial_ref[copy] = partial_ref[0]


def conv_and_project(x_in, halo, conv_weight, conv_bias, x_proj_t, copies):
    rows, channels = x_in.shape
    width = tile_of(channels)
    columns = x_proj_t.shape[0]
    return pl.pallas_call(
        conv_kernel,
        grid=(channels // width,),
        in_specs=[
            pl.BlockSpec((rows, width), lambda i: (0, i)),
            pl.BlockSpec((halo.shape[0], width), lambda i: (0, i)),
            pl.BlockSpec((conv_weight.shape[0], width), lambda i: (0, i)),
            pl.BlockSpec((1, width), lambda i: (0, i)),
            pl.BlockSpec((columns, width), lambda i: (0, i)),
        ],
        out_specs=[
            pl.BlockSpec((rows, width), lambda i: (0, i)),
            pl.BlockSpec((copies, rows, columns), lambda i: (0, 0, 0)),
        ],
        out_shape=[
            jax.ShapeDtypeStruct((rows, channels), jnp.bfloat16),
            jax.ShapeDtypeStruct((copies, rows, columns), jnp.float32),
        ],
        compiler_params=pltpu.CompilerParams(vmem_limit_bytes=16 * MIB),
        name="conv_project",
    )(x_in, halo, conv_weight, conv_bias, x_proj_t)


def softplus(v):
    return jnp.maximum(v, 0.0) + jnp.log1p(jnp.exp(-jnp.abs(v)))


def ends_kernel(
    part_ref, proj_ref, bias_ref, rate_ref, x_ref, size_ref, load_ref, b_ref, c_ref, low_ref, drive_ref
):
    rows, width = x_ref.shape
    states = rate_ref.shape[0]
    low_rank = low_ref.shape[1]
    groups = width // 128

    @pl.when(pl.program_id(0) == 0)
    def _():
        total = part_ref[0]
        for e in range(1, part_ref.shape[0]):
            total = total + part_ref[e]
        low_ref[...] = total[:, :low_rank].astype(jnp.bfloat16)
        b_mat = total[:, low_rank : low_rank + states]
        c_mat = total[:, low_rank + states : low_rank + 2 * states]
        b_ref[...] = jnp.broadcast_to(b_mat[:, :, None], b_ref.shape)
        c_ref[...] = jnp.broadcast_to(c_mat[:, :, None], c_ref.shape)

    size = softplus(
        jnp.dot(low_ref[...], proj_ref[...], preferred_element_type=jnp.float32) + bias_ref[...]
    )
    size_ref[...] = size
    drive_ref[...] = size * x_ref[...].astype(jnp.float32)
    rates = rate_ref[...]

    def step(block, state):
        start = pl.multiple_of(block * 8, 8)
        sizes = size_ref[pl.ds(start, 8), :]
        drives = drive_ref[pl.ds(start, 8), :]
        state = list(state)
        for i in range(8):
            b_now = b_ref[start + i]
            for g in range(groups):
                lanes = slice(g * 128, g * 128 + 128)
                decay = jnp.exp2(sizes[i : i + 1, lanes] * rates[:, lanes])
                state[g] = decay * state[g] + drives[i : i + 1, lanes] * b_now
        return tuple(state)

    zero = jnp.zeros((states, 128), jnp.float32)
    state = lax.fori_loop(0, rows // 8, step, (zero,) * groups)
    total = jnp.sum(size, axis=0, keepdims=True)
    high = total.astype(jnp.bfloat16).astype(jnp.float32)
    low = total - high
    rest = jnp.zeros((load_ref.shape[0] - states - 2, width), jnp.float32)
    load_ref[...] = jnp.concatenate(
        [jnp.concatenate(state, axis=1), high, low, rest], axis=0
    ).astype(jnp.bfloat16)


def scan_ends(partials, dt_proj, dt_bias, rates, xconv):
    rows, channels = xconv.shape
    states = rates.shape[0]
    width = tile_of(channels, 1024)
    load_rows = -(-(states + 2) // 8) * 8
    wide = jax.ShapeDtypeStruct((rows, states, 128), jnp.float32)
    return pl.pallas_call(
        ends_kernel,
        grid=(channels // width,),
        in_specs=[
            pl.BlockSpec(partials.shape, lambda i: (0, 0, 0)),
            pl.BlockSpec((dt_proj.shape[0], width), lambda i: (0, i)),
            pl.BlockSpec((1, width), lambda i: (0, i)),
            pl.BlockSpec((states, width), lambda i: (0, i)),
            pl.BlockSpec((rows, width), lambda i: (0, i)),
        ],
        out_specs=[
            pl.BlockSpec((rows, width), lambda i: (0, i)),
            pl.BlockSpec((load_rows, width), lambda i: (0, i)),
            pl.BlockSpec(wide.shape, lambda i: (0, 0, 0)),
            pl.BlockSpec(wide.shape, lambda i: (0, 0, 0)),
        ],
        out_shape=[
            jax.ShapeDtypeStruct((rows, channels), jnp.float32),
            jax.ShapeDtypeStruct((load_rows, channels), jnp.bfloat16),
            wide,
            wide,
        ],
        scratch_shapes=[
            pltpu.VMEM((rows, dt_proj.shape[0]), jnp.bfloat16),
            pltpu.VMEM((rows, width), jnp.float32),
        ],
        name="scan_ends",
    )(partials, dt_proj, dt_bias, rates, xconv)


def mix_kernel(z_count, x_count, z_place, x_place, *refs):
    count = z_count * x_count
    loads = refs[:count]
    size_ref, x_ref, z_ref, b_ref, c_ref, rate_ref, skip_ref, out_ref = refs[count : count + 8]
    drive_ref, y_ref, load_ref = refs[count + 8 :]
    for k in range(count):
        z_from = lax.rem(z_place[0] + k // x_count, z_count)
        x_from = lax.rem(x_place[0] + k % x_count, x_count)
        load_ref[z_from * x_count + x_from] = loads[k][...].astype(jnp.float32)
    rows, width = x_ref.shape
    states = rate_ref.shape[0]
    groups = width // 128
    rates = rate_ref[...]
    x_f = x_ref[...].astype(jnp.float32)
    drive_ref[...] = size_ref[...] * x_f

    def earlier(j, state):
        block = load_ref[j]
        total = block[states : states + 1] + block[states + 1 : states + 2]
        return jnp.exp2(total * rates) * state + block[:states]

    place = z_place[0] * x_count + x_place[0]
    incoming = lax.fori_loop(0, place, earlier, jnp.zeros((states, width), jnp.float32))

    def step(block, state):
        start = pl.multiple_of(block * 8, 8)
        sizes = size_ref[pl.ds(start, 8), :]
        drives = drive_ref[pl.ds(start, 8), :]
        state = list(state)
        outs = [[None] * 8 for _ in range(groups)]
        for i in range(8):
            b_now = b_ref[start + i]
            c_now = c_ref[start + i]
            for g in range(groups):
                lanes = slice(g * 128, g * 128 + 128)
                decay = jnp.exp2(sizes[i : i + 1, lanes] * rates[:, lanes])
                state[g] = decay * state[g] + drives[i : i + 1, lanes] * b_now
                outs[g][i] = jnp.sum(state[g] * c_now, axis=0, keepdims=True)
        for g in range(groups):
            y_ref[pl.ds(start, 8), g * 128 : g * 128 + 128] = jnp.concatenate(outs[g], axis=0)
        return tuple(state)

    start_state = tuple(incoming[:, g * 128 : g * 128 + 128] for g in range(groups))
    lax.fori_loop(0, rows // 8, step, start_state)
    z_f = z_ref[...].astype(jnp.float32)
    scanned = y_ref[...] + skip_ref[...] * x_f
    out_ref[...] = (scanned * (z_f / (1.0 + jnp.exp(-z_f)))).astype(jnp.bfloat16)


def scan_mix(z_at, x_at, loads, step_size, xconv, z_in, b_wide, c_wide, rates, d_skip):
    rows, channels = xconv.shape
    states = rates.shape[0]
    width = tile_of(channels, 1024)
    flat = [load for pair in loads for load in pair]

    def by_lane(depth):
        return pl.BlockSpec((depth, width), lambda i: (0, i))

    return pl.pallas_call(
        functools.partial(mix_kernel, len(loads), len(loads[0])),
        grid=(channels // width,),
        in_specs=[
            whole_smem(),
            whole_smem(),
            *[by_lane(load.shape[0]) for load in flat],
            by_lane(rows),
            by_lane(rows),
            by_lane(rows),
            pl.BlockSpec(b_wide.shape, lambda i: (0, 0, 0)),
            pl.BlockSpec(c_wide.shape, lambda i: (0, 0, 0)),
            by_lane(states),
            by_lane(1),
        ],
        out_specs=by_lane(rows),
        out_shape=jax.ShapeDtypeStruct((rows, channels), jnp.bfloat16),
        scratch_shapes=[pltpu.VMEM((rows, width), jnp.float32)] * 2
        + [pltpu.VMEM((len(flat), flat[0].shape[0], width), jnp.float32)],
        name="scan_mix",
    )(z_at, x_at, *flat, step_size, xconv, z_in, b_wide, c_wide, rates, d_skip)


def out_kernel(z_count, x_count, z_ref, x_ref, *refs):
    blocks, weights = refs[:z_count], refs[z_count : z_count + x_count]
    out_ref, held_ref = refs[z_count + x_count :]
    rows = blocks[0].shape[0]
    columns = weights[0].shape[1]
    for r in range(z_count):
        at = pl.multiple_of(lax.rem(z_ref[0] + r, z_count) * rows, rows)
        held_ref[pl.ds(at, rows), :] = blocks[r][...]
    for i in range(x_count):
        at = pl.multiple_of(lax.rem(x_ref[0] + i, x_count) * columns, columns)
        out_ref[:, pl.ds(at, columns)] = jnp.dot(
            held_ref[...], weights[i][...], preferred_element_type=jnp.float32
        ).astype(jnp.bfloat16)


def out_product(z_at, x_at, blocks, weights):
    rows, depth = blocks[0].shape
    z_count, x_count = len(blocks), len(weights)
    return pl.pallas_call(
        functools.partial(out_kernel, z_count, x_count),
        in_specs=[whole_smem()] * 2 + [whole_vmem()] * (z_count + x_count),
        out_specs=whole_vmem(),
        out_shape=jax.ShapeDtypeStruct(
            (z_count * rows, x_count * weights[0].shape[1]), jnp.bfloat16
        ),
        scratch_shapes=[pltpu.VMEM((z_count * rows, depth), jnp.bfloat16)],
        compiler_params=pltpu.CompilerParams(vmem_limit_bytes=16 * MIB),
        name="out_product",
    )(z_at, x_at, *blocks, *weights)


def hidden_kernel(z_count, x_count, z_ref, x_ref, *refs):
    count = z_count * x_count
    chunks = refs[:count]
    gain_ref, gate_ref, up_ref, act_ref, scaled_ref = refs[count:]
    rows, depth = chunks[0].shape
    padded = scaled_ref.shape[0] // x_count

    def filled(chunk):
        h = chunk[...].astype(jnp.float32)
        if padded == rows:
            return h
        return jnp.concatenate([h, jnp.zeros((padded - rows, depth), jnp.float32)], axis=0)

    @pl.when(pl.program_id(0) == 0)
    def _():
        for i in range(x_count):
            own = [chunks[r * x_count + i] for r in range(z_count)]
            squares = jnp.zeros((padded, 1), jnp.float32)
            for chunk in own:
                h = filled(chunk)
                squares = squares + jnp.sum(h * h, axis=1, keepdims=True)
            scale = lax.rsqrt(squares / (depth * z_count) + eps)
            down = pl.multiple_of(lax.rem(x_ref[0] + i, x_count) * padded, padded)
            for r, chunk in enumerate(own):
                z_at = lax.rem(z_ref[0] + r, z_count)
                across = pl.multiple_of(z_at * depth, depth)
                h = filled(chunk)
                scaled_ref[pl.ds(down, padded), pl.ds(across, depth)] = (
                    h * scale * gain_ref[z_at]
                ).astype(jnp.bfloat16)

    scaled = scaled_ref[...]
    gate = jnp.dot(scaled, gate_ref[0], preferred_element_type=jnp.float32)
    upper = jnp.dot(scaled, up_ref[0], preferred_element_type=jnp.float32)
    act_ref[...] = (gate / (1.0 + jnp.exp(-gate)) * upper).astype(jnp.bfloat16)


def expert_hidden(z_at, x_at, chunks, gain, w_gate, w_up):
    z_count, x_count = len(chunks), len(chunks[0])
    rows, depth = chunks[0][0].shape
    columns = w_gate.shape[2]
    width = tile_of(columns, 256)
    padded = -(-rows // 16) * 16 * x_count
    gain = gain.reshape(z_count, 1, depth)
    weight_spec = pl.BlockSpec((1, depth * z_count, width), lambda n: (0, 0, n))
    return pl.pallas_call(
        functools.partial(hidden_kernel, z_count, x_count),
        grid=(columns // width,),
        in_specs=[whole_smem()] * 2
        + [whole_vmem()] * (z_count * x_count + 1)
        + [weight_spec, weight_spec],
        out_specs=pl.BlockSpec((padded, width), lambda n: (0, n)),
        out_shape=jax.ShapeDtypeStruct((padded, columns), jnp.bfloat16),
        scratch_shapes=[pltpu.VMEM((padded, depth * z_count), jnp.bfloat16)],
        compiler_params=pltpu.CompilerParams(vmem_limit_bytes=50 * MIB),
        name="expert_hidden",
    )(z_at, x_at, *[chunk for pair in chunks for chunk in pair], gain, w_gate, w_up)


def down_kernel(x_count, x_ref, blocks_ref, act_ref, weight_ref, *refs):
    outs, held_ref = refs[:-1], refs[-1]
    held_ref[...] = jnp.dot(act_ref[...], weight_ref[0], preferred_element_type=jnp.float32)
    rows = outs[0].shape[0]
    padded = held_ref.shape[0] // x_count
    for k in range(len(outs) // x_count):

        @pl.when(pl.program_id(0) == k)
        def _(k=k):
            for i in range(x_count):
                start = pl.multiple_of(lax.rem(x_ref[0] + i, x_count) * padded, padded)
                outs[k * x_count + i][...] = held_ref[pl.ds(start, rows), :].astype(jnp.bfloat16)


def expert_down(x_at, blocks, x_count, z_count, rows, act, w_down):
    padded, depth = act.shape
    columns = w_down.shape[2] // z_count
    width = tile_of(columns)
    tiles = columns // width
    count = blocks.shape[0]

    def out_spec(k):
        def place(m, n, x, blocks):
            return (0, jnp.where(m == k, n, jnp.where(m < k, 0, tiles - 1)))

        return pl.BlockSpec((rows, width), place)

    outs = pl.pallas_call(
        functools.partial(down_kernel, x_count),
        grid_spec=pltpu.PrefetchScalarGridSpec(
            num_scalar_prefetch=2,
            grid=(count, tiles),
            in_specs=[
                pl.BlockSpec((padded, depth), lambda m, n, x, blocks: (0, 0)),
                pl.BlockSpec(
                    (1, depth, width), lambda m, n, x, blocks: (0, 0, blocks[m] * tiles + n)
                ),
            ],
            out_specs=[out_spec(k) for k in range(count) for _ in range(x_count)],
            scratch_shapes=[pltpu.VMEM((padded, width), jnp.float32)],
        ),
        out_shape=[jax.ShapeDtypeStruct((rows, columns), jnp.bfloat16)] * (count * x_count),
        compiler_params=pltpu.CompilerParams(vmem_limit_bytes=50 * MIB),
        name="expert_down",
    )(x_at, blocks, act, w_down)
    return [outs[k * x_count : (k + 1) * x_count] for k in range(count)]


def per_device(
    x_in,
    z_in,
    conv_weight,
    conv_bias,
    x_proj,
    dt_proj,
    dt_bias,
    a_log,
    d_skip,
    out_proj,
    resid,
    norm_gain,
    routes,
    route_gate,
    w_gate,
    w_up,
    w_down,
):
    row_count, channels = x_in.shape
    seq_count = lax.axis_size("seq")
    exp_count = lax.axis_size("exp")
    x_count = seq_count // exp_count
    z_count = exp_count
    seq_at = lax.axis_index("seq")
    exp_at = lax.axis_index("exp")
    z_at, x_at = seq_at // x_count, seq_at % x_count
    z_one = z_at.reshape(1).astype(jnp.int32)
    x_one = x_at.reshape(1).astype(jnp.int32)
    top_count = routes.shape[1]
    capacity = row_count * top_count * 17 // (16 * exp_count)
    pitch = capacity
    feature_slice = resid.shape[1]

    def from_z(block, r):
        pairs = [
            (((z + r) % z_count) * x_count + x, z * x_count + x)
            for z in range(z_count)
            for x in range(x_count)
        ]
        return lax.ppermute(block, "seq", pairs)

    def from_x(block, i):
        pairs = [
            (z * x_count + (x + i) % x_count, z * x_count + x)
            for z in range(z_count)
            for x in range(x_count)
        ]
        return lax.ppermute(block, "seq", pairs)

    turns = sorted(range(1, z_count), key=lambda r: min(r, z_count - r))

    def gathered(block):
        rows = {(0, 0): block}
        others = range(1, x_count)
        for i in others:
            rows[0, i] = from_x(block, i)
        sent = block
        for k, r in enumerate(turns):
            if k >= 2:
                sent = after(sent, rows[turns[k - 2], 0], *[rows[0, i] for i in others])
            rows[r, 0] = from_z(sent, r)
        for k, r in enumerate(turns):
            earlier = turns[max(k - 2, 0) : max(k - 1, 0)] if r != turns[-1] else turns[:k]
            forward = after(rows[r, 0], *[rows[q, i] for q in earlier for i in others])
            for i in others:
                rows[r, i] = from_x(forward, i)
        return [[rows[r, i] for i in range(x_count)] for r in range(z_count)]

    swap = [
        ((e * x_count + x) * exp_count + z, (z * x_count + x) * exp_count + e)
        for z in range(z_count)
        for x in range(x_count)
        for e in range(exp_count)
    ]

    halo = lax.ppermute(
        x_in[row_count - 8 :], "seq", [(i, i + 1) for i in range(seq_count - 1)]
    )

    routes_rows = jnp.pad(
        routes.T.astype(jnp.bfloat16), ((0, 8 - top_count), (0, feature_slice - row_count))
    )
    group = lax.ppermute(jnp.concatenate([resid, routes_rows], axis=0), ("seq", "exp"), swap)

    def slots_of(named):
        flat = named.reshape(-1, row_count * top_count)
        onehot = (flat[:, :, None] == jnp.arange(exp_count, dtype=jnp.int32)).astype(jnp.float32)
        below = jnp.tril(jnp.ones((row_count * top_count,) * 2, jnp.float32), -1)
        counts = jnp.einsum("ij,bje->bie", below, onehot)
        slots = jnp.sum(counts * onehot, axis=2).astype(jnp.int32)
        return slots.reshape(-1, row_count, top_count)

    own_slots = slots_of(routes)[0]
    own_target = (routes - z_at) % exp_count * pitch + own_slots
    slot_ids = jnp.arange(exp_count * pitch, dtype=jnp.int32)
    choose = (own_target.T[:, :, None] == slot_ids[None, None, :]).astype(jnp.bfloat16)
    choose = choose.reshape(top_count * row_count, exp_count * pitch)

    rates = -jnp.exp(a_log.T) * LOG2E
    xconv, copies = conv_and_project(
        x_in, halo, conv_weight, conv_bias[None], x_proj.T, exp_count
    )
    cut = channels * 3 // 8
    uppers = [from_x(after(out_proj, xconv)[:cut], i) for i in range(1, x_count)]
    partials = lax.all_to_all(copies, "exp", 0, 0, tiled=True)
    resid_here = group[:row_count]
    group_routes = group[row_count : row_count + top_count, :row_count].T.astype(jnp.int32)
    target = group_routes * pitch + slots_of(group_routes)[0]
    dispatch = jnp.sum(
        (target[None, :, :] == slot_ids[:, None, None]).astype(jnp.float32), axis=2
    ).astype(jnp.bfloat16)
    step_size, load, b_wide, c_wide = scan_ends(partials, dt_proj, dt_bias[None], rates, xconv)
    loads = gathered(after(load, group, *uppers))
    held_proj = after(out_proj, *[part for pair in loads for part in pair])
    lowers = [from_x(held_proj[cut:], i) for i in range(1, x_count)]
    columns = [out_proj] + [jnp.concatenate(pair, axis=0) for pair in zip(uppers, lowers)]
    mixed = scan_mix(
        z_one, x_one, loads, step_size, xconv, z_in, b_wide, c_wide, rates, d_skip[None]
    )
    along_z = [mixed] + [from_z(mixed, r) for r in range(1, z_count)]
    partial_out = out_product(z_one, x_one, along_z, columns)
    arrived = lax.all_to_all(
        partial_out.reshape(exp_count, row_count, feature_slice), "exp", 0, 0, tiled=True
    )
    mamba_out = jnp.sum(arrived.astype(jnp.float32), axis=0)
    hidden_state = (resid_here.astype(jnp.float32) + mamba_out).astype(jnp.bfloat16)

    outgoing = jnp.dot(dispatch, hidden_state, preferred_element_type=jnp.float32)
    outgoing = outgoing.astype(jnp.bfloat16).reshape(exp_count, pitch, feature_slice)
    rows_here = lax.all_to_all(outgoing, "exp", 0, 0, tiled=True)
    rows_here = rows_here.reshape(exp_count * pitch, feature_slice)
    chunks = gathered(rows_here)
    hidden_own = lax.ppermute(
        after(hidden_state, *chunks[turns[-1]][1:]), ("seq", "exp"), swap
    )
    act = expert_hidden(z_one, x_one, chunks, norm_gain, w_gate, w_up)
    act = after(act, hidden_own)

    by_distance = sorted(range(1, z_count), key=lambda r: abs(r - z_count // 2)) + [0]
    down, crossed = {}, {}
    for some in (by_distance[:1], by_distance[1:]):
        blocks = jnp.stack([(z_at + r) % z_count for r in some]).astype(jnp.int32)
        outs = expert_down(x_one, blocks, x_count, z_count, exp_count * pitch, act, w_down)
        down.update(zip(some, outs))
    def over_x(r):
        return functools.reduce(
            jnp.add, [p.astype(jnp.float32) for p in [down[r][0]] + crossed[r]]
        )

    arrivals = []
    for k, r in enumerate(by_distance):
        pieces = down[r][1:]
        if r == 0:
            pieces = [after(piece, arrivals[0]) for piece in pieces]
        elif k >= 2:
            pieces = [after(piece, *crossed[by_distance[k - 2]]) for piece in pieces]
        crossed[r] = [from_x(piece, x_count - i) for i, piece in enumerate(pieces, 1)]
        if r:
            arrivals.append(from_z(over_x(r).astype(jnp.bfloat16), z_count - r))
    total = over_x(0)
    for sent in arrivals:
        total = total + sent.astype(jnp.float32)
    expert_out = total.astype(jnp.bfloat16)
    pieces = expert_out.reshape(exp_count, pitch, feature_slice)
    back = []
    for k in range(exp_count):
        piece = lax.dynamic_index_in_dim(pieces, (exp_at - k) % exp_count, 0, keepdims=False)
        pairs = [
            (
                (e * x_count + x) * exp_count + (z + k) % exp_count,
                (z * x_count + x) * exp_count + e,
            )
            for z in range(z_count)
            for x in range(x_count)
            for e in range(exp_count)
        ]
        back.append(lax.ppermute(piece, ("seq", "exp"), pairs))
    back = jnp.concatenate(back, axis=0)
    picked = jnp.dot(choose, back, preferred_element_type=jnp.float32)
    picked = picked.reshape(top_count, row_count, feature_slice)
    moe = jnp.sum(route_gate.T[:, :, None] * picked, axis=0)
    return (hidden_own.astype(jnp.float32) + moe).astype(jnp.bfloat16)


def solution(mesh):
    return jax.shard_map(
        per_device,
        mesh=mesh,
        in_specs=(
            P("seq", "exp"),
            P("seq", "exp"),
            P(None, "exp"),
            P("exp"),
            P("exp", None),
            P(None, "exp"),
            P("exp"),
            P("exp", None),
            P("exp"),
            P("exp", "seq"),
            P("seq", "exp"),
            P(),
            P("seq", None),
            P("seq", None),
            P("exp", None, "seq"),
            P("exp", None, "seq"),
            P("exp", "seq", None),
        ),
        out_specs=P("seq", "exp"),
        check_vma=False,
    )
```

```python
import functools
import math

import jax
import jax.numpy as jnp
from jax import lax
from jax.experimental import pallas as pl
from jax.experimental.pallas import tpu as pltpu
from jax.sharding import PartitionSpec as P

eps = 1e-05
LOG2E = 1.4426950408889634
MIB = 1 << 20


def tile_of(size, most=512):
    return max(t for t in range(128, most + 1, 128) if size % t == 0)


def after(value, *others):
    return lax.optimization_barrier((value, *others))[0]


def pieces_of(depth):
    return max(count for count in range(1, 5) if depth % (128 * count) == 0)


def product(rows, weights):
    depth = weights[0].shape[1]
    return functools.reduce(
        jnp.add,
        [
            jnp.dot(
                rows[:, p * depth : (p + 1) * depth],
                weight[0],
                preferred_element_type=jnp.float32,
            )
            for p, weight in enumerate(weights)
        ],
    )


def whole_vmem():
    return pl.BlockSpec(memory_space=pltpu.VMEM)


def lanes_of(width):
    return pl.ds(pl.multiple_of(pl.program_id(0) * width, width), width)


def whole_smem():
    return pl.BlockSpec(memory_space=pltpu.SMEM)


def conv_kernel(x_ref, halo_ref, weight_ref, bias_ref, proj_ref, xconv_ref, partial_ref):
    rows = x_ref.shape[0]
    taps = weight_ref.shape[0]
    across = lanes_of(x_ref.shape[1])
    extended = jnp.concatenate(
        [halo_ref[:, across].astype(jnp.float32), x_ref[...].astype(jnp.float32)], axis=0
    )
    pad = halo_ref.shape[0]
    conv = jnp.zeros(x_ref.shape, jnp.float32) + bias_ref[...]
    for tap in range(taps):
        start = pad - (taps - 1) + tap
        conv = conv + weight_ref[tap : tap + 1, :] * extended[start : start + rows]
    xconv = (conv / (1.0 + jnp.exp(-conv))).astype(jnp.bfloat16)
    xconv_ref[...] = xconv

    @pl.when(pl.program_id(0) == 0)
    def _():
        partial_ref[0] = jnp.zeros(partial_ref.shape[1:], jnp.float32)

    partial_ref[0] += lax.dot_general(
        xconv, proj_ref[...], (((1,), (1,)), ((), ())), preferred_element_type=jnp.float32
    )

    @pl.when(pl.program_id(0) == pl.num_programs(0) - 1)
    def _():
        for copy in range(1, partial_ref.shape[0]):
            partial_ref[copy] = partial_ref[0]


def conv_and_project(x_in, halo, conv_weight, conv_bias, x_proj_t, copies):
    rows, channels = x_in.shape
    width = tile_of(channels, 1024)
    columns = x_proj_t.shape[0]
    return pl.pallas_call(
        conv_kernel,
        grid=(channels // width,),
        in_specs=[
            pl.BlockSpec((rows, width), lambda i: (0, i)),
            whole_vmem(),
            pl.BlockSpec((conv_weight.shape[0], width), lambda i: (0, i)),
            pl.BlockSpec((1, width), lambda i: (0, i)),
            pl.BlockSpec((columns, width), lambda i: (0, i)),
        ],
        out_specs=[
            pl.BlockSpec((rows, width), lambda i: (0, i)),
            pl.BlockSpec((copies, rows, columns), lambda i: (0, 0, 0)),
        ],
        out_shape=[
            jax.ShapeDtypeStruct((rows, channels), jnp.bfloat16),
            jax.ShapeDtypeStruct((copies, rows, columns), jnp.float32),
        ],
        name="conv_project",
    )(x_in, halo, conv_weight, conv_bias, x_proj_t)


def softplus(v):
    return jnp.maximum(v, 0.0) + jnp.log1p(jnp.exp(-jnp.abs(v)))


def ends_kernel(
    part_ref, proj_ref, bias_ref, rate_ref, x_ref, size_ref, load_ref, b_ref, c_ref, low_ref, drive_ref
):
    rows, width = x_ref.shape
    states = rate_ref.shape[0]
    low_rank = low_ref.shape[1]
    groups = width // 128

    @pl.when(pl.program_id(0) == 0)
    def _():
        total = part_ref[0]
        for e in range(1, part_ref.shape[0]):
            total = total + part_ref[e]
        low_ref[...] = total[:, :low_rank].astype(jnp.bfloat16)
        b_mat = total[:, low_rank : low_rank + states]
        c_mat = total[:, low_rank + states : low_rank + 2 * states]
        b_ref[...] = jnp.broadcast_to(b_mat[:, :, None], b_ref.shape)
        c_ref[...] = jnp.broadcast_to(c_mat[:, :, None], c_ref.shape)

    size = softplus(
        jnp.dot(low_ref[...], proj_ref[...], preferred_element_type=jnp.float32) + bias_ref[...]
    )
    size_ref[...] = size
    drive_ref[...] = size * x_ref[...].astype(jnp.float32)
    rates = rate_ref[...]

    def step(block, state):
        start = pl.multiple_of(block * 8, 8)
        sizes = size_ref[pl.ds(start, 8), :]
        drives = drive_ref[pl.ds(start, 8), :]
        state = list(state)
        for i in range(8):
            b_now = b_ref[start + i]
            for g in range(groups):
                lanes = slice(g * 128, g * 128 + 128)
                decay = jnp.exp2(sizes[i : i + 1, lanes] * rates[:, lanes])
                state[g] = decay * state[g] + drives[i : i + 1, lanes] * b_now
        return tuple(state)

    zero = jnp.zeros((states, 128), jnp.float32)
    state = lax.fori_loop(0, rows // 8, step, (zero,) * groups)
    total = jnp.sum(size, axis=0, keepdims=True)
    high = total.astype(jnp.bfloat16).astype(jnp.float32)
    low = total - high
    rest = jnp.zeros((load_ref.shape[0] - states - 2, width), jnp.float32)
    load_ref[...] = jnp.concatenate(
        [jnp.concatenate(state, axis=1), high, low, rest], axis=0
    ).astype(jnp.bfloat16)


def scan_ends(partials, dt_proj, dt_bias, rates, xconv):
    rows, channels = xconv.shape
    states = rates.shape[0]
    width = tile_of(channels, 1024)
    load_rows = -(-(states + 2) // 8) * 8
    wide = jax.ShapeDtypeStruct((rows, states, 128), jnp.float32)
    return pl.pallas_call(
        ends_kernel,
        grid=(channels // width,),
        in_specs=[
            whole_vmem(),
            pl.BlockSpec((dt_proj.shape[0], width), lambda i: (0, i)),
            pl.BlockSpec((1, width), lambda i: (0, i)),
            pl.BlockSpec((states, width), lambda i: (0, i)),
            pl.BlockSpec((rows, width), lambda i: (0, i)),
        ],
        out_specs=[
            pl.BlockSpec((rows, width), lambda i: (0, i)),
            pl.BlockSpec((load_rows, width), lambda i: (0, i)),
            pl.BlockSpec(wide.shape, lambda i: (0, 0, 0)),
            pl.BlockSpec(wide.shape, lambda i: (0, 0, 0)),
        ],
        out_shape=[
            jax.ShapeDtypeStruct((rows, channels), jnp.float32),
            jax.ShapeDtypeStruct((load_rows, channels), jnp.bfloat16),
            wide,
            wide,
        ],
        scratch_shapes=[
            pltpu.VMEM((rows, dt_proj.shape[0]), jnp.bfloat16),
            pltpu.VMEM((rows, width), jnp.float32),
        ],
        name="scan_ends",
    )(partials, dt_proj, dt_bias, rates, xconv)


def mix_kernel(z_count, x_count, z_place, x_place, *refs):
    count = z_count * x_count
    loads = refs[:count]
    size_ref, x_ref, z_ref, b_ref, c_ref, rate_ref, skip_ref, out_ref = refs[count : count + 8]
    drive_ref, y_ref, load_ref = refs[count + 8 :]
    across = lanes_of(x_ref.shape[1])
    for k in range(count):
        z_from = lax.rem(z_place[0] + k // x_count, z_count)
        x_from = lax.rem(x_place[0] + k % x_count, x_count)
        load_ref[z_from * x_count + x_from] = loads[k][:, across].astype(jnp.float32)
    rows, width = x_ref.shape
    states = rate_ref.shape[0]
    groups = width // 128
    rates = rate_ref[...]
    x_f = x_ref[...].astype(jnp.float32)
    drive_ref[...] = size_ref[...] * x_f

    def earlier(j, state):
        block = load_ref[j]
        total = block[states : states + 1] + block[states + 1 : states + 2]
        return jnp.exp2(total * rates) * state + block[:states]

    place = z_place[0] * x_count + x_place[0]
    incoming = lax.fori_loop(0, place, earlier, jnp.zeros((states, width), jnp.float32))

    def step(block, state):
        start = pl.multiple_of(block * 8, 8)
        sizes = size_ref[pl.ds(start, 8), :]
        drives = drive_ref[pl.ds(start, 8), :]
        state = list(state)
        outs = [[None] * 8 for _ in range(groups)]
        for i in range(8):
            b_now = b_ref[start + i]
            c_now = c_ref[start + i]
            for g in range(groups):
                lanes = slice(g * 128, g * 128 + 128)
                decay = jnp.exp2(sizes[i : i + 1, lanes] * rates[:, lanes])
                state[g] = decay * state[g] + drives[i : i + 1, lanes] * b_now
                outs[g][i] = jnp.sum(state[g] * c_now, axis=0, keepdims=True)
        for g in range(groups):
            y_ref[pl.ds(start, 8), g * 128 : g * 128 + 128] = jnp.concatenate(outs[g], axis=0)
        return tuple(state)

    start_state = tuple(incoming[:, g * 128 : g * 128 + 128] for g in range(groups))
    lax.fori_loop(0, rows // 8, step, start_state)
    z_f = z_ref[...].astype(jnp.float32)
    scanned = y_ref[...] + skip_ref[...] * x_f
    out_ref[...] = (scanned * (z_f / (1.0 + jnp.exp(-z_f)))).astype(jnp.bfloat16)


def scan_mix(z_at, x_at, loads, step_size, xconv, z_in, b_wide, c_wide, rates, d_skip):
    rows, channels = xconv.shape
    states = rates.shape[0]
    width = tile_of(channels, 1024)
    flat = [load for pair in loads for load in pair]

    def by_lane(depth):
        return pl.BlockSpec((depth, width), lambda i: (0, i))

    return pl.pallas_call(
        functools.partial(mix_kernel, len(loads), len(loads[0])),
        grid=(channels // width,),
        in_specs=[
            whole_smem(),
            whole_smem(),
            *[whole_vmem() for _ in flat],
            by_lane(rows),
            by_lane(rows),
            by_lane(rows),
            pl.BlockSpec(b_wide.shape, lambda i: (0, 0, 0)),
            pl.BlockSpec(c_wide.shape, lambda i: (0, 0, 0)),
            by_lane(states),
            by_lane(1),
        ],
        out_specs=by_lane(rows),
        out_shape=jax.ShapeDtypeStruct((rows, channels), jnp.bfloat16),
        scratch_shapes=[pltpu.VMEM((rows, width), jnp.float32)] * 2
        + [pltpu.VMEM((len(flat), flat[0].shape[0], width), jnp.float32)],
        name="scan_mix",
    )(z_at, x_at, *flat, step_size, xconv, z_in, b_wide, c_wide, rates, d_skip)


def out_kernel(z_count, x_count, z_ref, x_ref, *refs):
    blocks, weights = refs[:z_count], refs[z_count : z_count + x_count]
    out_ref, held_ref = refs[z_count + x_count :]
    rows = blocks[0].shape[0]
    columns = weights[0].shape[1]
    for r in range(z_count):
        at = pl.multiple_of(lax.rem(z_ref[0] + r, z_count) * rows, rows)
        held_ref[pl.ds(at, rows), :] = blocks[r][...]
    for i in range(x_count):
        at = pl.multiple_of(lax.rem(x_ref[0] + i, x_count) * columns, columns)
        out_ref[:, pl.ds(at, columns)] = jnp.dot(
            held_ref[...], weights[i][...], preferred_element_type=jnp.float32
        ).astype(jnp.bfloat16)


def out_product(z_at, x_at, blocks, weights):
    rows, depth = blocks[0].shape
    z_count, x_count = len(blocks), len(weights)
    return pl.pallas_call(
        functools.partial(out_kernel, z_count, x_count),
        in_specs=[whole_smem()] * 2 + [whole_vmem()] * (z_count + x_count),
        out_specs=whole_vmem(),
        out_shape=jax.ShapeDtypeStruct(
            (z_count * rows, x_count * weights[0].shape[1]), jnp.bfloat16
        ),
        scratch_shapes=[pltpu.VMEM((z_count * rows, depth), jnp.bfloat16)],
        compiler_params=pltpu.CompilerParams(vmem_limit_bytes=16 * MIB),
        name="out_product",
    )(z_at, x_at, *blocks, *weights)


def hidden_kernel(z_count, x_count, z_ref, x_ref, *refs):
    count = z_count * x_count
    chunks, gain_ref = refs[:count], refs[count]
    weights, act_ref, scaled_ref = refs[count + 1 : -2], refs[-2], refs[-1]
    rows, depth = chunks[0].shape
    padded = scaled_ref.shape[0] // x_count

    def filled(chunk):
        h = chunk[...].astype(jnp.float32)
        if padded == rows:
            return h
        return jnp.concatenate([h, jnp.zeros((padded - rows, depth), jnp.float32)], axis=0)

    @pl.when(pl.program_id(0) == 0)
    def _():
        for i in range(x_count):
            own = [chunks[r * x_count + i] for r in range(z_count)]
            squares = jnp.zeros((padded, 1), jnp.float32)
            for chunk in own:
                h = filled(chunk)
                squares = squares + jnp.sum(h * h, axis=1, keepdims=True)
            scale = lax.rsqrt(squares / (depth * z_count) + eps)
            down = pl.multiple_of(lax.rem(x_ref[0] + i, x_count) * padded, padded)
            for r, chunk in enumerate(own):
                z_at = lax.rem(z_ref[0] + r, z_count)
                across = pl.multiple_of(z_at * depth, depth)
                h = filled(chunk)
                scaled_ref[pl.ds(down, padded), pl.ds(across, depth)] = (
                    h * scale * gain_ref[z_at]
                ).astype(jnp.bfloat16)

    half = len(weights) // 2
    gate, upper = product(scaled_ref, weights[:half]), product(scaled_ref, weights[half:])
    act_ref[...] = (gate / (1.0 + jnp.exp(-gate)) * upper).astype(jnp.bfloat16)


def expert_hidden(z_at, x_at, chunks, gain, w_gate, w_up):
    z_count, x_count = len(chunks), len(chunks[0])
    rows, depth = chunks[0][0].shape
    columns = w_gate.shape[2]
    width = tile_of(columns, 256)
    padded = -(-rows // 16) * 16 * x_count
    gain = gain.reshape(z_count, 1, depth)
    pieces = pieces_of(depth * z_count)
    weight_specs = [
        pl.BlockSpec((1, depth * z_count // pieces, width), lambda n, p=p: (0, p, n))
        for p in range(pieces)
    ]
    return pl.pallas_call(
        functools.partial(hidden_kernel, z_count, x_count),
        grid=(columns // width,),
        in_specs=[whole_smem()] * 2
        + [whole_vmem()] * (z_count * x_count + 1)
        + weight_specs * 2,
        out_specs=pl.BlockSpec((padded, width), lambda n: (0, n)),
        out_shape=jax.ShapeDtypeStruct((padded, columns), jnp.bfloat16),
        scratch_shapes=[pltpu.VMEM((padded, depth * z_count), jnp.bfloat16)],
        compiler_params=pltpu.CompilerParams(vmem_limit_bytes=50 * MIB),
        name="expert_hidden",
    )(z_at, x_at, *[chunk for pair in chunks for chunk in pair], gain, *[w_gate] * pieces, *[w_up] * pieces)


def down_kernel(x_count, pieces, x_ref, blocks_ref, act_ref, *refs):
    weights, outs, held_ref = refs[:pieces], refs[pieces:-1], refs[-1]
    held_ref[...] = product(act_ref, weights)
    rows = outs[0].shape[0]
    padded = held_ref.shape[0] // x_count
    for k in range(len(outs) // x_count):

        @pl.when(pl.program_id(0) == k)
        def _(k=k):
            for i in range(x_count):
                start = pl.multiple_of(lax.rem(x_ref[0] + i, x_count) * padded, padded)
                outs[k * x_count + i][...] = held_ref[pl.ds(start, rows), :].astype(jnp.bfloat16)


def expert_down(x_at, blocks, x_count, z_count, rows, act, w_down):
    padded, depth = act.shape
    columns = w_down.shape[2] // z_count
    width = tile_of(columns)
    tiles = columns // width
    count = blocks.shape[0]
    pieces = pieces_of(depth)

    def weight_spec(p):
        return pl.BlockSpec(
            (1, depth // pieces, width), lambda m, n, x, blocks: (0, p, blocks[m] * tiles + n)
        )

    def out_spec(k):
        def place(m, n, x, blocks):
            return (0, jnp.where(m == k, n, jnp.where(m < k, 0, tiles - 1)))

        return pl.BlockSpec((rows, width), place)

    outs = pl.pallas_call(
        functools.partial(down_kernel, x_count, pieces),
        grid_spec=pltpu.PrefetchScalarGridSpec(
            num_scalar_prefetch=2,
            grid=(count, tiles),
            in_specs=[
                pl.BlockSpec((padded, depth), lambda m, n, x, blocks: (0, 0)),
                *[weight_spec(p) for p in range(pieces)],
            ],
            out_specs=[out_spec(k) for k in range(count) for _ in range(x_count)],
            scratch_shapes=[pltpu.VMEM((padded, width), jnp.float32)],
        ),
        out_shape=[jax.ShapeDtypeStruct((rows, columns), jnp.bfloat16)] * (count * x_count),
        compiler_params=pltpu.CompilerParams(vmem_limit_bytes=50 * MIB),
        name="expert_down",
    )(x_at, blocks, act, *[w_down] * pieces)
    return [outs[k * x_count : (k + 1) * x_count] for k in range(count)]


def per_device(
    x_in,
    z_in,
    conv_weight,
    conv_bias,
    x_proj,
    dt_proj,
    dt_bias,
    a_log,
    d_skip,
    out_proj,
    resid,
    norm_gain,
    routes,
    route_gate,
    w_gate,
    w_up,
    w_down,
):
    row_count, channels = x_in.shape
    seq_count = lax.axis_size("seq")
    exp_count = lax.axis_size("exp")
    x_count = seq_count // exp_count
    z_count = exp_count
    seq_at = lax.axis_index("seq")
    exp_at = lax.axis_index("exp")
    z_at, x_at = seq_at // x_count, seq_at % x_count
    z_one = z_at.reshape(1).astype(jnp.int32)
    x_one = x_at.reshape(1).astype(jnp.int32)
    top_count = routes.shape[1]
    capacity = row_count * top_count * 17 // (16 * exp_count)
    pitch = capacity
    feature_slice = resid.shape[1]

    def from_z(block, r):
        pairs = [
            (((z + r) % z_count) * x_count + x, z * x_count + x)
            for z in range(z_count)
            for x in range(x_count)
        ]
        return lax.ppermute(block, "seq", pairs)

    def from_x(block, i):
        pairs = [
            (z * x_count + (x + i) % x_count, z * x_count + x)
            for z in range(z_count)
            for x in range(x_count)
        ]
        return lax.ppermute(block, "seq", pairs)

    turns = sorted(range(1, z_count), key=lambda r: min(r, z_count - r))

    def gathered(block):
        rows = {(0, 0): block}
        others = range(1, x_count)
        for i in others:
            rows[0, i] = from_x(block, i)
        sent = block
        for k, r in enumerate(turns):
            if k >= 2:
                sent = after(sent, rows[turns[k - 2], 0], *[rows[0, i] for i in others])
            rows[r, 0] = from_z(sent, r)
        for k, r in enumerate(turns):
            earlier = turns[max(k - 2, 0) : max(k - 1, 0)] if r != turns[-1] else turns[:k]
            forward = after(rows[r, 0], *[rows[q, i] for q in earlier for i in others])
            for i in others:
                rows[r, i] = from_x(forward, i)
        return [[rows[r, i] for i in range(x_count)] for r in range(z_count)]

    swap = [
        ((e * x_count + x) * exp_count + z, (z * x_count + x) * exp_count + e)
        for z in range(z_count)
        for x in range(x_count)
        for e in range(exp_count)
    ]

    halo = lax.ppermute(
        x_in[row_count - 8 :], "seq", [(i, i + 1) for i in range(seq_count - 1)]
    )

    routes_rows = jnp.pad(
        routes.T.astype(jnp.bfloat16), ((0, 8 - top_count), (0, feature_slice - row_count))
    )
    group = lax.ppermute(jnp.concatenate([resid, routes_rows], axis=0), ("seq", "exp"), swap)

    def slots_of(named):
        flat = named.reshape(-1, row_count * top_count)
        onehot = (flat[:, :, None] == jnp.arange(exp_count, dtype=jnp.int32)).astype(jnp.float32)
        below = jnp.tril(jnp.ones((row_count * top_count,) * 2, jnp.float32), -1)
        counts = jnp.einsum("ij,bje->bie", below, onehot)
        slots = jnp.sum(counts * onehot, axis=2).astype(jnp.int32)
        return slots.reshape(-1, row_count, top_count)

    own_slots = slots_of(routes)[0]
    own_target = (routes - z_at) % exp_count * pitch + own_slots
    slot_ids = jnp.arange(exp_count * pitch, dtype=jnp.int32)
    choose = (own_target.T[:, :, None] == slot_ids[None, None, :]).astype(jnp.bfloat16)
    choose = choose.reshape(top_count * row_count, exp_count * pitch)

    rates = -jnp.exp(a_log.T) * LOG2E
    xconv, copies = conv_and_project(
        x_in, halo, conv_weight, conv_bias[None], x_proj.T, exp_count
    )
    cut = channels * 3 // 8
    uppers = [from_x(after(out_proj, xconv)[:cut], i) for i in range(1, x_count)]
    partials = lax.all_to_all(copies, "exp", 0, 0, tiled=True)
    resid_here = group[:row_count]
    group_routes = group[row_count : row_count + top_count, :row_count].T.astype(jnp.int32)
    target = group_routes * pitch + slots_of(group_routes)[0]
    dispatch = jnp.sum(
        (target[None, :, :] == slot_ids[:, None, None]).astype(jnp.float32), axis=2
    ).astype(jnp.bfloat16)
    step_size, load, b_wide, c_wide = scan_ends(partials, dt_proj, dt_bias[None], rates, xconv)
    loads = gathered(after(load, group, *uppers))
    held_proj = after(out_proj, *[part for pair in loads for part in pair])
    lowers = [from_x(held_proj[cut:], i) for i in range(1, x_count)]
    columns = [out_proj] + [jnp.concatenate(pair, axis=0) for pair in zip(uppers, lowers)]
    mixed = scan_mix(
        z_one, x_one, loads, step_size, xconv, z_in, b_wide, c_wide, rates, d_skip[None]
    )
    along_z = [mixed] + [from_z(mixed, r) for r in range(1, z_count)]
    partial_out = out_product(z_one, x_one, along_z, columns)
    arrived = lax.all_to_all(
        partial_out.reshape(exp_count, row_count, feature_slice), "exp", 0, 0, tiled=True
    )
    mamba_out = jnp.sum(arrived.astype(jnp.float32), axis=0)
    hidden_state = (resid_here.astype(jnp.float32) + mamba_out).astype(jnp.bfloat16)

    outgoing = jnp.dot(dispatch, hidden_state, preferred_element_type=jnp.float32)
    outgoing = outgoing.astype(jnp.bfloat16).reshape(exp_count, pitch, feature_slice)
    rows_here = lax.all_to_all(outgoing, "exp", 0, 0, tiled=True)
    rows_here = rows_here.reshape(exp_count * pitch, feature_slice)
    chunks = gathered(rows_here)
    hidden_own = lax.ppermute(
        after(hidden_state, *chunks[turns[-1]][1:]), ("seq", "exp"), swap
    )
    act = expert_hidden(z_one, x_one, chunks, norm_gain, w_gate, w_up)
    act = after(act, hidden_own)

    by_distance = sorted(range(1, z_count), key=lambda r: abs(r - z_count // 2)) + [0]
    down, crossed = {}, {}
    for some in (by_distance[:1], by_distance[1:]):
        blocks = jnp.stack([(z_at + r) % z_count for r in some]).astype(jnp.int32)
        outs = expert_down(x_one, blocks, x_count, z_count, exp_count * pitch, act, w_down)
        down.update(zip(some, outs))
    def over_x(r):
        return functools.reduce(
            jnp.add, [p.astype(jnp.float32) for p in [down[r][0]] + crossed[r]]
        )

    arrivals = []
    for k, r in enumerate(by_distance):
        pieces = down[r][1:]
        if r == 0:
            pieces = [after(piece, arrivals[0]) for piece in pieces]
        elif k >= 2:
            pieces = [after(piece, *crossed[by_distance[k - 2]]) for piece in pieces]
        crossed[r] = [from_x(piece, x_count - i) for i, piece in enumerate(pieces, 1)]
        if r:
            arrivals.append(from_z(over_x(r).astype(jnp.bfloat16), z_count - r))
    total = over_x(0)
    for sent in arrivals:
        total = total + sent.astype(jnp.float32)
    expert_out = total.astype(jnp.bfloat16)
    pieces = expert_out.reshape(exp_count, pitch, feature_slice)
    back = []
    for k in range(exp_count):
        piece = lax.dynamic_index_in_dim(pieces, (exp_at - k) % exp_count, 0, keepdims=False)
        pairs = [
            (
                (e * x_count + x) * exp_count + (z + k) % exp_count,
                (z * x_count + x) * exp_count + e,
            )
            for z in range(z_count)
            for x in range(x_count)
            for e in range(exp_count)
        ]
        back.append(lax.ppermute(piece, ("seq", "exp"), pairs))
    back = jnp.concatenate(back, axis=0)
    picked = jnp.dot(choose, back, preferred_element_type=jnp.float32)
    picked = picked.reshape(top_count, row_count, feature_slice)
    moe = jnp.sum(route_gate.T[:, :, None] * picked, axis=0)
    return (hidden_own.astype(jnp.float32) + moe).astype(jnp.bfloat16)


def solution(mesh):
    return jax.shard_map(
        per_device,
        mesh=mesh,
        in_specs=(
            P("seq", "exp"),
            P("seq", "exp"),
            P(None, "exp"),
            P("exp"),
            P("exp", None),
            P(None, "exp"),
            P("exp"),
            P("exp", None),
            P("exp"),
            P("exp", "seq"),
            P("seq", "exp"),
            P(),
            P("seq", None),
            P("seq", None),
            P("exp", None, "seq"),
            P("exp", None, "seq"),
            P("exp", "seq", None),
        ),
        out_specs=P("seq", "exp"),
        check_vma=False,
    )
```

```python
import functools
import math

import jax
import jax.numpy as jnp
from jax import lax
from jax.experimental import pallas as pl
from jax.experimental.pallas import tpu as pltpu
from jax.sharding import PartitionSpec as P

eps = 1e-05
LOG2E = 1.4426950408889634
MIB = 1 << 20


def tile_of(size, most=512):
    return max(t for t in range(128, most + 1, 128) if size % t == 0)


def after(value, *others):
    return lax.optimization_barrier((value, *others))[0]


def whole_vmem():
    return pl.BlockSpec(memory_space=pltpu.VMEM)


def lanes_of(width):
    return pl.ds(pl.multiple_of(pl.program_id(0) * width, width), width)


def whole_smem():
    return pl.BlockSpec(memory_space=pltpu.SMEM)


def conv_kernel(x_ref, halo_ref, weight_ref, bias_ref, proj_ref, xconv_ref, partial_ref):
    rows = x_ref.shape[0]
    taps = weight_ref.shape[0]
    across = lanes_of(x_ref.shape[1])
    extended = jnp.concatenate(
        [halo_ref[:, across].astype(jnp.float32), x_ref[...].astype(jnp.float32)], axis=0
    )
    pad = halo_ref.shape[0]
    conv = jnp.zeros(x_ref.shape, jnp.float32) + bias_ref[...]
    for tap in range(taps):
        start = pad - (taps - 1) + tap
        conv = conv + weight_ref[tap : tap + 1, :] * extended[start : start + rows]
    xconv = (conv / (1.0 + jnp.exp(-conv))).astype(jnp.bfloat16)
    xconv_ref[...] = xconv

    @pl.when(pl.program_id(0) == 0)
    def _():
        partial_ref[0] = jnp.zeros(partial_ref.shape[1:], jnp.float32)

    partial_ref[0] += lax.dot_general(
        xconv, proj_ref[...], (((1,), (1,)), ((), ())), preferred_element_type=jnp.float32
    )

    @pl.when(pl.program_id(0) == pl.num_programs(0) - 1)
    def _():
        for copy in range(1, partial_ref.shape[0]):
            partial_ref[copy] = partial_ref[0]


def conv_and_project(x_in, halo, conv_weight, conv_bias, x_proj_t, copies):
    rows, channels = x_in.shape
    width = tile_of(channels, 1024)
    columns = x_proj_t.shape[0]
    return pl.pallas_call(
        conv_kernel,
        grid=(channels // width,),
        in_specs=[
            pl.BlockSpec((rows, width), lambda i: (0, i)),
            whole_vmem(),
            pl.BlockSpec((conv_weight.shape[0], width), lambda i: (0, i)),
            pl.BlockSpec((1, width), lambda i: (0, i)),
            pl.BlockSpec((columns, width), lambda i: (0, i)),
        ],
        out_specs=[
            pl.BlockSpec((rows, width), lambda i: (0, i)),
            pl.BlockSpec((copies, rows, columns), lambda i: (0, 0, 0)),
        ],
        out_shape=[
            jax.ShapeDtypeStruct((rows, channels), jnp.bfloat16),
            jax.ShapeDtypeStruct((copies, rows, columns), jnp.float32),
        ],
        name="conv_project",
    )(x_in, halo, conv_weight, conv_bias, x_proj_t)


def softplus(v):
    return jnp.maximum(v, 0.0) + jnp.log1p(jnp.exp(-jnp.abs(v)))


def ends_kernel(
    part_ref, proj_ref, bias_ref, rate_ref, x_ref, info_ref, size_ref, load_ref, b_ref, c_ref, low_ref, drive_ref
):
    rows, width = x_ref.shape
    states = rate_ref.shape[0]
    low_rank = low_ref.shape[1]
    groups = width // 128

    @pl.when(pl.program_id(0) == 0)
    def _():
        total = part_ref[0]
        for e in range(1, part_ref.shape[0]):
            total = total + part_ref[e]
        low_ref[...] = total[:, :low_rank].astype(jnp.bfloat16)
        b_mat = total[:, low_rank : low_rank + states]
        c_mat = total[:, low_rank + states : low_rank + 2 * states]
        b_ref[...] = jnp.broadcast_to(b_mat[:, :, None], b_ref.shape)
        c_ref[...] = jnp.broadcast_to(c_mat[:, :, None], c_ref.shape)

    size = softplus(
        jnp.dot(low_ref[...], proj_ref[...], preferred_element_type=jnp.float32) + bias_ref[...]
    )
    size_ref[...] = size
    drive_ref[...] = size * x_ref[...].astype(jnp.float32)
    rates = rate_ref[...]

    def step(block, state):
        start = pl.multiple_of(block * 8, 8)
        sizes = size_ref[pl.ds(start, 8), :]
        drives = drive_ref[pl.ds(start, 8), :]
        state = list(state)
        for i in range(8):
            b_now = b_ref[start + i]
            for g in range(groups):
                lanes = slice(g * 128, g * 128 + 128)
                decay = jnp.exp2(sizes[i : i + 1, lanes] * rates[:, lanes])
                state[g] = decay * state[g] + drives[i : i + 1, lanes] * b_now
        return tuple(state)

    zero = jnp.zeros((states, 128), jnp.float32)
    state = lax.fori_loop(0, rows // 8, step, (zero,) * groups)
    total = jnp.sum(size, axis=0, keepdims=True)
    high = total.astype(jnp.bfloat16).astype(jnp.float32)
    low = total - high
    rest = info_ref[: load_ref.shape[0] - states - 2, :]
    load_ref[...] = jnp.concatenate(
        [jnp.concatenate(state, axis=1), high, low, rest], axis=0
    ).astype(jnp.bfloat16)


def scan_ends(partials, dt_proj, dt_bias, rates, xconv, info):
    rows, channels = xconv.shape
    states = rates.shape[0]
    width = tile_of(channels, 1024)
    load_rows = -(-(states + 2) // 8) * 8
    wide = jax.ShapeDtypeStruct((rows, states, 128), jnp.float32)
    return pl.pallas_call(
        ends_kernel,
        grid=(channels // width,),
        in_specs=[
            whole_vmem(),
            pl.BlockSpec((dt_proj.shape[0], width), lambda i: (0, i)),
            pl.BlockSpec((1, width), lambda i: (0, i)),
            pl.BlockSpec((states, width), lambda i: (0, i)),
            pl.BlockSpec((rows, width), lambda i: (0, i)),
            pl.BlockSpec((info.shape[0], width), lambda i: (0, i)),
        ],
        out_specs=[
            pl.BlockSpec((rows, width), lambda i: (0, i)),
            pl.BlockSpec((load_rows, width), lambda i: (0, i)),
            pl.BlockSpec(wide.shape, lambda i: (0, 0, 0)),
            pl.BlockSpec(wide.shape, lambda i: (0, 0, 0)),
        ],
        out_shape=[
            jax.ShapeDtypeStruct((rows, channels), jnp.float32),
            jax.ShapeDtypeStruct((load_rows, channels), jnp.bfloat16),
            wide,
            wide,
        ],
        scratch_shapes=[
            pltpu.VMEM((rows, dt_proj.shape[0]), jnp.bfloat16),
            pltpu.VMEM((rows, width), jnp.float32),
        ],
        name="scan_ends",
    )(partials, dt_proj, dt_bias, rates, xconv, info)


def mix_kernel(z_count, x_count, z_place, x_place, *refs):
    count = z_count * x_count
    loads = refs[:count]
    size_ref, x_ref, z_ref, b_ref, c_ref, rate_ref, skip_ref, out_ref = refs[count : count + 8]
    drive_ref, y_ref, load_ref = refs[count + 8 :]
    across = lanes_of(x_ref.shape[1])
    for k in range(count):
        z_from = lax.rem(z_place[0] + k // x_count, z_count)
        x_from = lax.rem(x_place[0] + k % x_count, x_count)
        load_ref[z_from * x_count + x_from] = loads[k][:, across].astype(jnp.float32)
    rows, width = x_ref.shape
    states = rate_ref.shape[0]
    groups = width // 128
    rates = rate_ref[...]
    x_f = x_ref[...].astype(jnp.float32)
    drive_ref[...] = size_ref[...] * x_f

    def earlier(j, state):
        block = load_ref[j]
        total = block[states : states + 1] + block[states + 1 : states + 2]
        return jnp.exp2(total * rates) * state + block[:states]

    place = z_place[0] * x_count + x_place[0]
    incoming = lax.fori_loop(0, place, earlier, jnp.zeros((states, width), jnp.float32))

    def step(block, state):
        start = pl.multiple_of(block * 8, 8)
        sizes = size_ref[pl.ds(start, 8), :]
        drives = drive_ref[pl.ds(start, 8), :]
        state = list(state)
        outs = [[None] * 8 for _ in range(groups)]
        for i in range(8):
            b_now = b_ref[start + i]
            c_now = c_ref[start + i]
            for g in range(groups):
                lanes = slice(g * 128, g * 128 + 128)
                decay = jnp.exp2(sizes[i : i + 1, lanes] * rates[:, lanes])
                state[g] = decay * state[g] + drives[i : i + 1, lanes] * b_now
                outs[g][i] = jnp.sum(state[g] * c_now, axis=0, keepdims=True)
        for g in range(groups):
            y_ref[pl.ds(start, 8), g * 128 : g * 128 + 128] = jnp.concatenate(outs[g], axis=0)
        return tuple(state)

    start_state = tuple(incoming[:, g * 128 : g * 128 + 128] for g in range(groups))
    lax.fori_loop(0, rows // 8, step, start_state)
    z_f = z_ref[...].astype(jnp.float32)
    scanned = y_ref[...] + skip_ref[...] * x_f
    out_ref[...] = (scanned * (z_f / (1.0 + jnp.exp(-z_f)))).astype(jnp.bfloat16)


def scan_mix(z_at, x_at, loads, step_size, xconv, z_in, b_wide, c_wide, rates, d_skip):
    rows, channels = xconv.shape
    states = rates.shape[0]
    width = tile_of(channels, 1024)
    flat = [load for pair in loads for load in pair]

    def by_lane(depth):
        return pl.BlockSpec((depth, width), lambda i: (0, i))

    return pl.pallas_call(
        functools.partial(mix_kernel, len(loads), len(loads[0])),
        grid=(channels // width,),
        in_specs=[
            whole_smem(),
            whole_smem(),
            *[whole_vmem() for _ in flat],
            by_lane(rows),
            by_lane(rows),
            by_lane(rows),
            pl.BlockSpec(b_wide.shape, lambda i: (0, 0, 0)),
            pl.BlockSpec(c_wide.shape, lambda i: (0, 0, 0)),
            by_lane(states),
            by_lane(1),
        ],
        out_specs=by_lane(rows),
        out_shape=jax.ShapeDtypeStruct((rows, channels), jnp.bfloat16),
        scratch_shapes=[pltpu.VMEM((rows, width), jnp.float32)] * 2
        + [pltpu.VMEM((len(flat), flat[0].shape[0], width), jnp.float32)],
        name="scan_mix",
    )(z_at, x_at, *flat, step_size, xconv, z_in, b_wide, c_wide, rates, d_skip)


def out_kernel(z_count, x_count, z_ref, x_ref, e_ref, pick_ref, resid_ref, *refs):
    blocks, weights = refs[:z_count], refs[z_count : z_count + x_count]
    out_ref, held_ref, sum_ref = refs[z_count + x_count :]
    rows = blocks[0].shape[0]
    columns = weights[0].shape[1]
    for r in range(z_count):
        at = pl.multiple_of(lax.rem(z_ref[0] + r, z_count) * rows, rows)
        held_ref[pl.ds(at, rows), :] = blocks[r][...]
    own = pl.ds(pl.multiple_of(e_ref[0] * rows, rows), rows)
    for i in range(x_count):
        at = pl.ds(pl.multiple_of(lax.rem(x_ref[0] + i, x_count) * columns, columns), columns)
        sum_ref[...] = jnp.dot(held_ref[...], weights[i][...], preferred_element_type=jnp.float32)
        sum_ref[own, :] += resid_ref[:, at].astype(jnp.float32)
        out_ref[:, at] = jnp.dot(
            pick_ref[...], sum_ref[...].astype(jnp.bfloat16), preferred_element_type=jnp.float32
        ).astype(jnp.bfloat16)


def out_product(z_at, x_at, e_at, pick, resid, blocks, weights):
    rows, depth = blocks[0].shape
    z_count, x_count = len(blocks), len(weights)
    columns = weights[0].shape[1]
    return pl.pallas_call(
        functools.partial(out_kernel, z_count, x_count),
        in_specs=[whole_smem()] * 3 + [whole_vmem()] * (2 + z_count + x_count),
        out_specs=whole_vmem(),
        out_shape=jax.ShapeDtypeStruct((pick.shape[0], x_count * columns), jnp.bfloat16),
        scratch_shapes=[
            pltpu.VMEM((z_count * rows, depth), jnp.bfloat16),
            pltpu.VMEM((z_count * rows, columns), jnp.float32),
        ],
        compiler_params=pltpu.CompilerParams(vmem_limit_bytes=16 * MIB),
        name="out_product",
    )(z_at, x_at, e_at, pick, resid, *blocks, *weights)


def hidden_kernel(z_count, x_count, z_ref, x_ref, *refs):
    count = z_count * x_count
    chunks = refs[:count]
    gain_ref, gate_ref, up_ref, act_ref, scaled_ref = refs[count:]
    rows, depth = chunks[0].shape
    padded = scaled_ref.shape[0] // x_count

    def filled(chunk):
        h = chunk[...].astype(jnp.float32)
        if padded == rows:
            return h
        return jnp.concatenate([h, jnp.zeros((padded - rows, depth), jnp.float32)], axis=0)

    @pl.when(pl.program_id(0) == 0)
    def _():
        for i in range(x_count):
            own = [chunks[r * x_count + i] for r in range(z_count)]
            squares = jnp.zeros((padded, 1), jnp.float32)
            for chunk in own:
                h = filled(chunk)
                squares = squares + jnp.sum(h * h, axis=1, keepdims=True)
            scale = lax.rsqrt(squares / (depth * z_count) + eps)
            down = pl.multiple_of(lax.rem(x_ref[0] + i, x_count) * padded, padded)
            for r, chunk in enumerate(own):
                z_at = lax.rem(z_ref[0] + r, z_count)
                across = pl.multiple_of(z_at * depth, depth)
                h = filled(chunk)
                scaled_ref[pl.ds(down, padded), pl.ds(across, depth)] = (
                    h * scale * gain_ref[z_at]
                ).astype(jnp.bfloat16)

    scaled = scaled_ref[...]
    gate = jnp.dot(scaled, gate_ref[0], preferred_element_type=jnp.float32)
    upper = jnp.dot(scaled, up_ref[0], preferred_element_type=jnp.float32)
    act_ref[...] = (gate / (1.0 + jnp.exp(-gate)) * upper).astype(jnp.bfloat16)


def expert_hidden(z_at, x_at, chunks, gain, w_gate, w_up):
    z_count, x_count = len(chunks), len(chunks[0])
    rows, depth = chunks[0][0].shape
    columns = w_gate.shape[2]
    width = tile_of(columns, 256)
    padded = -(-rows // 16) * 16 * x_count
    gain = gain.reshape(z_count, 1, depth)
    weight_spec = pl.BlockSpec((1, depth * z_count, width), lambda n: (0, 0, n))
    return pl.pallas_call(
        functools.partial(hidden_kernel, z_count, x_count),
        grid=(columns // width,),
        in_specs=[whole_smem()] * 2
        + [whole_vmem()] * (z_count * x_count + 1)
        + [weight_spec, weight_spec],
        out_specs=pl.BlockSpec((padded, width), lambda n: (0, n)),
        out_shape=jax.ShapeDtypeStruct((padded, columns), jnp.bfloat16),
        scratch_shapes=[pltpu.VMEM((padded, depth * z_count), jnp.bfloat16)],
        compiler_params=pltpu.CompilerParams(vmem_limit_bytes=40 * MIB),
        name="expert_hidden",
    )(z_at, x_at, *[chunk for pair in chunks for chunk in pair], gain, w_gate, w_up)


def down_kernel(x_count, x_ref, blocks_ref, act_ref, weight_ref, *refs):
    outs, held_ref = refs[:-1], refs[-1]
    held_ref[...] = jnp.dot(act_ref[...], weight_ref[0], preferred_element_type=jnp.float32)
    rows = outs[0].shape[0]
    padded = held_ref.shape[0] // x_count
    for k in range(len(outs) // x_count):

        @pl.when(pl.program_id(0) == k)
        def _(k=k):
            for i in range(x_count):
                start = pl.multiple_of(lax.rem(x_ref[0] + i, x_count) * padded, padded)
                outs[k * x_count + i][...] = held_ref[pl.ds(start, rows), :].astype(jnp.bfloat16)


def expert_down(x_at, blocks, x_count, z_count, rows, act, w_down):
    padded, depth = act.shape
    columns = w_down.shape[2] // z_count
    width = tile_of(columns)
    tiles = columns // width
    count = blocks.shape[0]

    def out_spec(k):
        def place(m, n, x, blocks):
            return (0, jnp.where(m == k, n, jnp.where(m < k, 0, tiles - 1)))

        return pl.BlockSpec((rows, width), place)

    outs = pl.pallas_call(
        functools.partial(down_kernel, x_count),
        grid_spec=pltpu.PrefetchScalarGridSpec(
            num_scalar_prefetch=2,
            grid=(count, tiles),
            in_specs=[
                pl.BlockSpec((padded, depth), lambda m, n, x, blocks: (0, 0)),
                pl.BlockSpec(
                    (1, depth, width), lambda m, n, x, blocks: (0, 0, blocks[m] * tiles + n)
                ),
            ],
            out_specs=[out_spec(k) for k in range(count) for _ in range(x_count)],
            scratch_shapes=[pltpu.VMEM((padded, width), jnp.float32)],
        ),
        out_shape=[jax.ShapeDtypeStruct((rows, columns), jnp.bfloat16)] * (count * x_count),
        compiler_params=pltpu.CompilerParams(vmem_limit_bytes=32 * MIB),
        name="expert_down",
    )(x_at, blocks, act, w_down)
    return [outs[k * x_count : (k + 1) * x_count] for k in range(count)]


def per_device(
    x_in,
    z_in,
    conv_weight,
    conv_bias,
    x_proj,
    dt_proj,
    dt_bias,
    a_log,
    d_skip,
    out_proj,
    resid,
    norm_gain,
    routes,
    route_gate,
    w_gate,
    w_up,
    w_down,
):
    row_count, channels = x_in.shape
    seq_count = lax.axis_size("seq")
    exp_count = lax.axis_size("exp")
    x_count = seq_count // exp_count
    z_count = exp_count
    seq_at = lax.axis_index("seq")
    exp_at = lax.axis_index("exp")
    z_at, x_at = seq_at // x_count, seq_at % x_count
    z_one = z_at.reshape(1).astype(jnp.int32)
    x_one = x_at.reshape(1).astype(jnp.int32)
    e_one = exp_at.reshape(1).astype(jnp.int32)
    top_count = routes.shape[1]
    capacity = row_count * top_count * 17 // (16 * exp_count)
    pitch = capacity
    feature_slice = resid.shape[1]

    def from_z(block, r):
        pairs = [
            (((z + r) % z_count) * x_count + x, z * x_count + x)
            for z in range(z_count)
            for x in range(x_count)
        ]
        return lax.ppermute(block, "seq", pairs)

    def from_x(block, i):
        pairs = [
            (z * x_count + (x + i) % x_count, z * x_count + x)
            for z in range(z_count)
            for x in range(x_count)
        ]
        return lax.ppermute(block, "seq", pairs)

    turns = sorted(range(1, z_count), key=lambda r: min(r, z_count - r))

    def gathered(block):
        rows = {(0, 0): block}
        others = range(1, x_count)
        for i in others:
            rows[0, i] = from_x(block, i)
        sent = block
        for k, r in enumerate(turns):
            if k >= 2:
                sent = after(sent, rows[turns[k - 2], 0], *[rows[0, i] for i in others])
            rows[r, 0] = from_z(sent, r)
        for k, r in enumerate(turns):
            earlier = turns[max(k - 2, 0) : max(k - 1, 0)] if r != turns[-1] else turns[:k]
            forward = after(rows[r, 0], *[rows[q, i] for q in earlier for i in others])
            for i in others:
                rows[r, i] = from_x(forward, i)
        return [[rows[r, i] for i in range(x_count)] for r in range(z_count)]

    swap = [
        ((e * x_count + x) * exp_count + z, (z * x_count + x) * exp_count + e)
        for z in range(z_count)
        for x in range(x_count)
        for e in range(exp_count)
    ]

    halo = lax.ppermute(
        x_in[row_count - 8 :], "seq", [(i, i + 1) for i in range(seq_count - 1)]
    )

    resid_here = lax.ppermute(resid, ("seq", "exp"), swap)

    def part_of(v):
        return v.astype(jnp.bfloat16).astype(jnp.float32)

    gate_high = part_of(route_gate)
    gate_mid = part_of(route_gate - gate_high)
    gate_low = route_gate - gate_high - gate_mid
    info = jnp.stack([routes.astype(jnp.float32), gate_high, gate_mid, gate_low])
    info = info.transpose(0, 2, 1).reshape(4, top_count * row_count)
    info = jnp.pad(info, ((0, 4), (0, channels - top_count * row_count)))

    def slots_of(named):
        flat = named.reshape(-1, row_count * top_count)
        onehot = (flat[:, :, None] == jnp.arange(exp_count, dtype=jnp.int32)).astype(jnp.float32)
        below = jnp.tril(jnp.ones((row_count * top_count,) * 2, jnp.float32), -1)
        counts = jnp.einsum("ij,bje->bie", below, onehot)
        slots = jnp.sum(counts * onehot, axis=2).astype(jnp.int32)
        return slots.reshape(-1, row_count, top_count)

    own_target = (routes - z_at) % exp_count * pitch + slots_of(routes)[0]
    slot_ids = jnp.arange(exp_count * pitch, dtype=jnp.int32)
    choose = jnp.sum(
        (own_target[:, :, None] == slot_ids[None, None, :]).astype(jnp.float32), axis=1
    ).astype(jnp.bfloat16)

    rates = -jnp.exp(a_log.T) * LOG2E
    xconv, copies = conv_and_project(
        x_in, halo, conv_weight, conv_bias[None], x_proj.T, exp_count
    )
    cut = channels * 3 // 8
    uppers = [from_x(after(out_proj, xconv)[:cut], i) for i in range(1, x_count)]
    partials = lax.all_to_all(copies, "exp", 0, 0, tiled=True)
    step_size, load, b_wide, c_wide = scan_ends(partials, dt_proj, dt_bias[None], rates, xconv, info)
    loads = gathered(after(load, resid_here, *uppers))
    held_proj = after(out_proj, *[part for pair in loads for part in pair])
    lowers = [from_x(held_proj[cut:], i) for i in range(1, x_count)]
    columns = [out_proj] + [jnp.concatenate(pair, axis=0) for pair in zip(uppers, lowers)]
    mixed = scan_mix(
        z_one, x_one, loads, step_size, xconv, z_in, b_wide, c_wide, rates, d_skip[None]
    )
    along_z = [mixed] + [from_z(mixed, r) for r in range(1, z_count)]

    first_row = a_log.shape[1] + 2
    spare = after(jnp.stack([loads[r][0][first_row:] for r in range(z_count)]), mixed)
    spare = spare[:, :4, : top_count * row_count].astype(jnp.float32)
    spare = lax.dynamic_slice_in_dim(
        jnp.concatenate([spare, spare]), (z_count - z_at) % z_count, z_count, 0
    ).reshape(z_count, 4, top_count, row_count)
    all_routes = spare[:, 0].transpose(0, 2, 1).astype(jnp.int32)
    all_gates = (spare[:, 1] + spare[:, 2] + spare[:, 3]).transpose(0, 2, 1)
    z_ids = jnp.arange(z_count, dtype=jnp.int32)[:, None, None]
    target = (all_routes * z_count + z_ids) * pitch + slots_of(all_routes)
    target = target.reshape(z_count * row_count, top_count)
    all_ids = jnp.arange(exp_count * z_count * pitch, dtype=jnp.int32)
    pick = jnp.sum(
        (target[None, :, :] == all_ids[:, None, None]).astype(jnp.float32), axis=2
    ).astype(jnp.bfloat16)
    here_ids = exp_at * z_count * pitch + jnp.arange(z_count * pitch, dtype=jnp.int32)
    here = target[None, :, :] == here_ids[:, None, None]
    gate_here = jnp.sum(
        jnp.where(here, all_gates.reshape(1, z_count * row_count, top_count), 0.0), axis=(1, 2)
    )[:, None]
    first_here = jnp.sum(here[:, :, 0].astype(jnp.float32), axis=1)[:, None]

    partial_rows = out_product(z_one, x_one, e_one, pick, resid_here, along_z, columns)
    arrived = lax.all_to_all(
        partial_rows.reshape(exp_count, z_count * pitch, feature_slice), "exp", 0, 0, tiled=True
    )
    rows_here = jnp.sum(arrived.astype(jnp.float32), axis=0).astype(jnp.bfloat16)

    chunks = gathered(rows_here)
    act = expert_hidden(z_one, x_one, chunks, norm_gain, w_gate, w_up)

    by_distance = sorted(range(1, z_count), key=lambda r: abs(r - z_count // 2)) + [0]
    down, crossed = {}, {}
    for some in (by_distance[:1], by_distance[1:]):
        blocks = jnp.stack([(z_at + r) % z_count for r in some]).astype(jnp.int32)
        outs = expert_down(x_one, blocks, x_count, z_count, exp_count * pitch, act, w_down)
        down.update(zip(some, outs))
    def over_x(r):
        return functools.reduce(
            jnp.add, [p.astype(jnp.float32) for p in [down[r][0]] + crossed[r]]
        )

    arrivals = []
    for k, r in enumerate(by_distance):
        pieces = down[r][1:]
        if r == 0:
            pieces = [after(piece, arrivals[0]) for piece in pieces]
        elif k >= 2:
            pieces = [after(piece, *crossed[by_distance[k - 2]]) for piece in pieces]
        crossed[r] = [from_x(piece, x_count - i) for i, piece in enumerate(pieces, 1)]
        if r:
            arrivals.append(from_z(over_x(r).astype(jnp.bfloat16), z_count - r))
    total = over_x(0)
    for sent in arrivals:
        total = total + sent.astype(jnp.float32)
    expert_out = total.astype(jnp.bfloat16).astype(jnp.float32)
    expert_out = gate_here * expert_out + first_here * rows_here.astype(jnp.float32)
    expert_out = expert_out.astype(jnp.bfloat16)
    pieces = expert_out.reshape(exp_count, pitch, feature_slice)
    back = []
    for k in range(exp_count):
        piece = lax.dynamic_index_in_dim(pieces, (exp_at - k) % exp_count, 0, keepdims=False)
        pairs = [
            (
                (e * x_count + x) * exp_count + (z + k) % exp_count,
                (z * x_count + x) * exp_count + e,
            )
            for z in range(z_count)
            for x in range(x_count)
            for e in range(exp_count)
        ]
        back.append(lax.ppermute(piece, ("seq", "exp"), pairs))
    back = jnp.concatenate(back, axis=0)
    return jnp.dot(choose, back, preferred_element_type=jnp.float32).astype(jnp.bfloat16)


def solution(mesh):
    return jax.shard_map(
        per_device,
        mesh=mesh,
        in_specs=(
            P("seq", "exp"),
            P("seq", "exp"),
            P(None, "exp"),
            P("exp"),
            P("exp", None),
            P(None, "exp"),
            P("exp"),
            P("exp", None),
            P("exp"),
            P("exp", "seq"),
            P("seq", "exp"),
            P(),
            P("seq", None),
            P("seq", None),
            P("exp", None, "seq"),
            P("exp", None, "seq"),
            P("exp", "seq", None),
        ),
        out_specs=P("seq", "exp"),
        check_vma=False,
    )
```

```python
import functools
import math

import jax
import jax.numpy as jnp
from jax import lax
from jax.experimental import pallas as pl
from jax.experimental.pallas import tpu as pltpu
from jax.sharding import PartitionSpec as P

eps = 1e-05
LOG2E = 1.4426950408889634
MIB = 1 << 20


def tile_of(size, most=512):
    return max(t for t in range(128, most + 1, 128) if size % t == 0)


def after(value, *others):
    return lax.optimization_barrier((value, *others))[0]


def whole_vmem():
    return pl.BlockSpec(memory_space=pltpu.VMEM)


def lanes_of(width):
    return pl.ds(pl.multiple_of(pl.program_id(0) * width, width), width)


def whole_smem():
    return pl.BlockSpec(memory_space=pltpu.SMEM)


def conv_kernel(x_ref, halo_ref, weight_ref, bias_ref, proj_ref, xconv_ref, partial_ref):
    rows = x_ref.shape[0]
    taps = weight_ref.shape[0]
    across = lanes_of(x_ref.shape[1])
    extended = jnp.concatenate(
        [halo_ref[:, across].astype(jnp.float32), x_ref[...].astype(jnp.float32)], axis=0
    )
    pad = halo_ref.shape[0]
    conv = jnp.zeros(x_ref.shape, jnp.float32) + bias_ref[...]
    for tap in range(taps):
        start = pad - (taps - 1) + tap
        conv = conv + weight_ref[tap : tap + 1, :] * extended[start : start + rows]
    xconv = (conv / (1.0 + jnp.exp(-conv))).astype(jnp.bfloat16)
    xconv_ref[...] = xconv

    @pl.when(pl.program_id(0) == 0)
    def _():
        partial_ref[...] = jnp.zeros_like(partial_ref)

    partial_ref[...] += lax.dot_general(
        xconv, proj_ref[...], (((1,), (1,)), ((), ())), preferred_element_type=jnp.float32
    )


def conv_and_project(x_in, halo, conv_weight, conv_bias, x_proj_t):
    rows, channels = x_in.shape
    width = tile_of(channels, 1024)
    columns = x_proj_t.shape[0]
    return pl.pallas_call(
        conv_kernel,
        grid=(channels // width,),
        in_specs=[
            pl.BlockSpec((rows, width), lambda i: (0, i)),
            whole_vmem(),
            pl.BlockSpec((conv_weight.shape[0], width), lambda i: (0, i)),
            pl.BlockSpec((1, width), lambda i: (0, i)),
            pl.BlockSpec((columns, width), lambda i: (0, i)),
        ],
        out_specs=[
            pl.BlockSpec((rows, width), lambda i: (0, i)),
            pl.BlockSpec((rows, columns), lambda i: (0, 0)),
        ],
        out_shape=[
            jax.ShapeDtypeStruct((rows, channels), jnp.bfloat16),
            jax.ShapeDtypeStruct((rows, columns), jnp.float32),
        ],
        name="conv_project",
    )(x_in, halo, conv_weight, conv_bias, x_proj_t)


def softplus(v):
    return jnp.maximum(v, 0.0) + jnp.log1p(jnp.exp(-jnp.abs(v)))


def ends_kernel(count, *refs):
    parts = refs[:count]
    proj_ref, bias_ref, rate_ref, x_ref, info_ref = refs[count : count + 5]
    size_ref, load_ref, b_ref, c_ref, low_ref, drive_ref = refs[count + 5 :]
    rows, width = x_ref.shape
    states = rate_ref.shape[0]
    low_rank = low_ref.shape[1]
    groups = width // 128

    @pl.when(pl.program_id(0) == 0)
    def _():
        total = parts[0][...]
        for part in parts[1:]:
            total = total + part[...]
        low_ref[...] = total[:, :low_rank].astype(jnp.bfloat16)
        b_mat = total[:, low_rank : low_rank + states]
        c_mat = total[:, low_rank + states : low_rank + 2 * states]
        b_ref[...] = jnp.broadcast_to(b_mat[:, :, None], b_ref.shape)
        c_ref[...] = jnp.broadcast_to(c_mat[:, :, None], c_ref.shape)

    size = softplus(
        jnp.dot(low_ref[...], proj_ref[...], preferred_element_type=jnp.float32) + bias_ref[...]
    )
    size_ref[...] = size
    drive_ref[...] = size * x_ref[...].astype(jnp.float32)
    rates = rate_ref[...]

    def step(block, state):
        start = pl.multiple_of(block * 8, 8)
        sizes = size_ref[pl.ds(start, 8), :]
        drives = drive_ref[pl.ds(start, 8), :]
        state = list(state)
        for i in range(8):
            b_now = b_ref[start + i]
            for g in range(groups):
                lanes = slice(g * 128, g * 128 + 128)
                decay = jnp.exp2(sizes[i : i + 1, lanes] * rates[:, lanes])
                state[g] = decay * state[g] + drives[i : i + 1, lanes] * b_now
        return tuple(state)

    zero = jnp.zeros((states, 128), jnp.float32)
    state = lax.fori_loop(0, rows // 8, step, (zero,) * groups)
    total = jnp.sum(size, axis=0, keepdims=True)
    high = total.astype(jnp.bfloat16).astype(jnp.float32)
    low = total - high
    rest = info_ref[: load_ref.shape[0] - states - 2, :]
    load_ref[...] = jnp.concatenate(
        [jnp.concatenate(state, axis=1), high, low, rest], axis=0
    ).astype(jnp.bfloat16)


def scan_ends(partials, dt_proj, dt_bias, rates, xconv, info):
    rows, channels = xconv.shape
    states = rates.shape[0]
    width = tile_of(channels, 1024)
    load_rows = -(-(states + 2) // 8) * 8
    wide = jax.ShapeDtypeStruct((rows, states, 128), jnp.float32)
    return pl.pallas_call(
        functools.partial(ends_kernel, len(partials)),
        grid=(channels // width,),
        in_specs=[
            *[whole_vmem() for _ in partials],
            pl.BlockSpec((dt_proj.shape[0], width), lambda i: (0, i)),
            pl.BlockSpec((1, width), lambda i: (0, i)),
            pl.BlockSpec((states, width), lambda i: (0, i)),
            pl.BlockSpec((rows, width), lambda i: (0, i)),
            pl.BlockSpec((info.shape[0], width), lambda i: (0, i)),
        ],
        out_specs=[
            pl.BlockSpec((rows, width), lambda i: (0, i)),
            pl.BlockSpec((load_rows, width), lambda i: (0, i)),
            pl.BlockSpec(wide.shape, lambda i: (0, 0, 0)),
            pl.BlockSpec(wide.shape, lambda i: (0, 0, 0)),
        ],
        out_shape=[
            jax.ShapeDtypeStruct((rows, channels), jnp.float32),
            jax.ShapeDtypeStruct((load_rows, channels), jnp.bfloat16),
            wide,
            wide,
        ],
        scratch_shapes=[
            pltpu.VMEM((rows, dt_proj.shape[0]), jnp.bfloat16),
            pltpu.VMEM((rows, width), jnp.float32),
        ],
        name="scan_ends",
    )(*partials, dt_proj, dt_bias, rates, xconv, info)


def mix_kernel(z_count, x_count, z_place, x_place, *refs):
    count = z_count * x_count
    loads = refs[:count]
    size_ref, x_ref, z_ref, b_ref, c_ref, rate_ref, skip_ref, out_ref = refs[count : count + 8]
    drive_ref, y_ref, load_ref = refs[count + 8 :]
    across = lanes_of(x_ref.shape[1])
    for k in range(count):
        z_from = lax.rem(z_place[0] + k // x_count, z_count)
        x_from = lax.rem(x_place[0] + k % x_count, x_count)
        load_ref[z_from * x_count + x_from] = loads[k][:, across].astype(jnp.float32)
    rows, width = x_ref.shape
    states = rate_ref.shape[0]
    groups = width // 128
    rates = rate_ref[...]
    x_f = x_ref[...].astype(jnp.float32)
    drive_ref[...] = size_ref[...] * x_f

    def earlier(j, state):
        block = load_ref[j]
        total = block[states : states + 1] + block[states + 1 : states + 2]
        return jnp.exp2(total * rates) * state + block[:states]

    place = z_place[0] * x_count + x_place[0]
    incoming = lax.fori_loop(0, place, earlier, jnp.zeros((states, width), jnp.float32))

    def step(block, state):
        start = pl.multiple_of(block * 8, 8)
        sizes = size_ref[pl.ds(start, 8), :]
        drives = drive_ref[pl.ds(start, 8), :]
        state = list(state)
        outs = [[None] * 8 for _ in range(groups)]
        for i in range(8):
            b_now = b_ref[start + i]
            c_now = c_ref[start + i]
            for g in range(groups):
                lanes = slice(g * 128, g * 128 + 128)
                decay = jnp.exp2(sizes[i : i + 1, lanes] * rates[:, lanes])
                state[g] = decay * state[g] + drives[i : i + 1, lanes] * b_now
                outs[g][i] = jnp.sum(state[g] * c_now, axis=0, keepdims=True)
        for g in range(groups):
            y_ref[pl.ds(start, 8), g * 128 : g * 128 + 128] = jnp.concatenate(outs[g], axis=0)
        return tuple(state)

    start_state = tuple(incoming[:, g * 128 : g * 128 + 128] for g in range(groups))
    lax.fori_loop(0, rows // 8, step, start_state)
    z_f = z_ref[...].astype(jnp.float32)
    scanned = y_ref[...] + skip_ref[...] * x_f
    out_ref[...] = (scanned * (z_f / (1.0 + jnp.exp(-z_f)))).astype(jnp.bfloat16)


def scan_mix(z_at, x_at, loads, step_size, xconv, z_in, b_wide, c_wide, rates, d_skip):
    rows, channels = xconv.shape
    states = rates.shape[0]
    width = tile_of(channels, 1024)
    flat = [load for pair in loads for load in pair]

    def by_lane(depth):
        return pl.BlockSpec((depth, width), lambda i: (0, i))

    return pl.pallas_call(
        functools.partial(mix_kernel, len(loads), len(loads[0])),
        grid=(channels // width,),
        in_specs=[
            whole_smem(),
            whole_smem(),
            *[whole_vmem() for _ in flat],
            by_lane(rows),
            by_lane(rows),
            by_lane(rows),
            pl.BlockSpec(b_wide.shape, lambda i: (0, 0, 0)),
            pl.BlockSpec(c_wide.shape, lambda i: (0, 0, 0)),
            by_lane(states),
            by_lane(1),
        ],
        out_specs=by_lane(rows),
        out_shape=jax.ShapeDtypeStruct((rows, channels), jnp.bfloat16),
        scratch_shapes=[pltpu.VMEM((rows, width), jnp.float32)] * 2
        + [pltpu.VMEM((len(flat), flat[0].shape[0], width), jnp.float32)],
        name="scan_mix",
    )(z_at, x_at, *flat, step_size, xconv, z_in, b_wide, c_wide, rates, d_skip)


def out_kernel(z_count, counts, z_ref, x_ref, e_ref, keep_pick_ref, send_pick_ref, resid_ref, *refs):
    x_count = len(counts)
    blocks = refs[:z_count]
    keep_ref, send_ref, held_ref, sum_ref = refs[z_count + sum(counts) :]
    weights = list(refs[z_count : z_count + sum(counts)])
    rows = blocks[0].shape[0]
    columns = weights[0].shape[1]
    for r in range(z_count):
        at = pl.multiple_of(lax.rem(z_ref[0] + r, z_count) * rows, rows)
        held_ref[pl.ds(at, rows), :] = blocks[r][...]
    own = pl.ds(pl.multiple_of(e_ref[0] * rows, rows), rows)
    for i, count in enumerate(counts):
        at = pl.ds(pl.multiple_of(lax.rem(x_ref[0] + i, x_count) * columns, columns), columns)
        start, parts = 0, []
        for _ in range(count):
            weight = weights.pop(0)
            depth = weight.shape[0]
            parts.append(
                jnp.dot(
                    held_ref[:, start : start + depth],
                    weight[...],
                    preferred_element_type=jnp.float32,
                )
            )
            start += depth
        sum_ref[...] = functools.reduce(jnp.add, parts)
        sum_ref[own, :] += resid_ref[:, at].astype(jnp.float32)
        summed = sum_ref[...].astype(jnp.bfloat16)
        for pick_ref, out_ref in ((keep_pick_ref, keep_ref), (send_pick_ref, send_ref)):
            out_ref[:, at] = jnp.dot(
                pick_ref[...], summed, preferred_element_type=jnp.float32
            ).astype(jnp.bfloat16)


def out_product(z_at, x_at, e_at, keep_pick, send_pick, resid, blocks, weights):
    rows, depth = blocks[0].shape
    z_count, x_count = len(blocks), len(weights)
    counts = [len(parts) for parts in weights]
    columns = weights[0][0].shape[1]
    return pl.pallas_call(
        functools.partial(out_kernel, z_count, counts),
        in_specs=[whole_smem()] * 3 + [whole_vmem()] * (3 + z_count + sum(counts)),
        out_specs=[whole_vmem()] * 2,
        out_shape=[jax.ShapeDtypeStruct((keep_pick.shape[0], x_count * columns), jnp.bfloat16)] * 2,
        scratch_shapes=[
            pltpu.VMEM((z_count * rows, depth), jnp.bfloat16),
            pltpu.VMEM((z_count * rows, columns), jnp.float32),
        ],
        compiler_params=pltpu.CompilerParams(vmem_limit_bytes=16 * MIB),
        name="out_product",
    )(
        z_at,
        x_at,
        e_at,
        keep_pick,
        send_pick,
        resid,
        *blocks,
        *[part for parts in weights for part in parts],
    )


def hidden_kernel(z_count, x_count, z_ref, x_ref, *refs):
    count = z_count * x_count
    chunks = refs[:count]
    gain_ref, gate_ref, up_ref, act_ref, scaled_ref = refs[count:]
    rows, depth = chunks[0].shape
    padded = scaled_ref.shape[0] // x_count

    def filled(chunk):
        h = chunk[...].astype(jnp.float32)
        if padded == rows:
            return h
        return jnp.concatenate([h, jnp.zeros((padded - rows, depth), jnp.float32)], axis=0)

    @pl.when(pl.program_id(0) == 0)
    def _():
        for i in range(x_count):
            own = [chunks[r * x_count + i] for r in range(z_count)]
            squares = jnp.zeros((padded, 1), jnp.float32)
            for chunk in own:
                h = filled(chunk)
                squares = squares + jnp.sum(h * h, axis=1, keepdims=True)
            scale = lax.rsqrt(squares / (depth * z_count) + eps)
            down = pl.multiple_of(lax.rem(x_ref[0] + i, x_count) * padded, padded)
            for r, chunk in enumerate(own):
                z_at = lax.rem(z_ref[0] + r, z_count)
                across = pl.multiple_of(z_at * depth, depth)
                h = filled(chunk)
                scaled_ref[pl.ds(down, padded), pl.ds(across, depth)] = (
                    h * scale * gain_ref[z_at]
                ).astype(jnp.bfloat16)

    scaled = scaled_ref[...]
    gate = jnp.dot(scaled, gate_ref[0], preferred_element_type=jnp.float32)
    upper = jnp.dot(scaled, up_ref[0], preferred_element_type=jnp.float32)
    act_ref[...] = (gate / (1.0 + jnp.exp(-gate)) * upper).astype(jnp.bfloat16)


def expert_hidden(z_at, x_at, chunks, gain, w_gate, w_up):
    z_count, x_count = len(chunks), len(chunks[0])
    rows, depth = chunks[0][0].shape
    columns = w_gate.shape[2]
    width = tile_of(columns, 256)
    padded = -(-rows // 16) * 16 * x_count
    gain = gain.reshape(z_count, 1, depth)
    weight_spec = pl.BlockSpec((1, depth * z_count, width), lambda n: (0, 0, n))
    return pl.pallas_call(
        functools.partial(hidden_kernel, z_count, x_count),
        grid=(columns // width,),
        in_specs=[whole_smem()] * 2
        + [whole_vmem()] * (z_count * x_count + 1)
        + [weight_spec, weight_spec],
        out_specs=pl.BlockSpec((padded, width), lambda n: (0, n)),
        out_shape=jax.ShapeDtypeStruct((padded, columns), jnp.bfloat16),
        scratch_shapes=[pltpu.VMEM((padded, depth * z_count), jnp.bfloat16)],
        compiler_params=pltpu.CompilerParams(vmem_limit_bytes=50 * MIB),
        name="expert_hidden",
    )(z_at, x_at, *[chunk for pair in chunks for chunk in pair], gain, w_gate, w_up)


def down_kernel(x_count, x_ref, blocks_ref, act_ref, weight_ref, *refs):
    outs, held_ref = refs[:-1], refs[-1]
    held_ref[...] = jnp.dot(act_ref[...], weight_ref[0], preferred_element_type=jnp.float32)
    rows = outs[0].shape[0]
    padded = held_ref.shape[0] // x_count
    for k in range(len(outs) // x_count):

        @pl.when(pl.program_id(0) == k)
        def _(k=k):
            for i in range(x_count):
                start = pl.multiple_of(lax.rem(x_ref[0] + i, x_count) * padded, padded)
                outs[k * x_count + i][...] = held_ref[pl.ds(start, rows), :].astype(jnp.bfloat16)


def expert_down(x_at, blocks, x_count, z_count, rows, act, w_down):
    padded, depth = act.shape
    columns = w_down.shape[2] // z_count
    width = tile_of(columns)
    tiles = columns // width
    count = blocks.shape[0]

    def out_spec(k):
        def place(m, n, x, blocks):
            return (0, jnp.where(m == k, n, jnp.where(m < k, 0, tiles - 1)))

        return pl.BlockSpec((rows, width), place)

    outs = pl.pallas_call(
        functools.partial(down_kernel, x_count),
        grid_spec=pltpu.PrefetchScalarGridSpec(
            num_scalar_prefetch=2,
            grid=(count, tiles),
            in_specs=[
                pl.BlockSpec((padded, depth), lambda m, n, x, blocks: (0, 0)),
                pl.BlockSpec(
                    (1, depth, width), lambda m, n, x, blocks: (0, 0, blocks[m] * tiles + n)
                ),
            ],
            out_specs=[out_spec(k) for k in range(count) for _ in range(x_count)],
            scratch_shapes=[pltpu.VMEM((padded, width), jnp.float32)],
        ),
        out_shape=[jax.ShapeDtypeStruct((rows, columns), jnp.bfloat16)] * (count * x_count),
        compiler_params=pltpu.CompilerParams(vmem_limit_bytes=50 * MIB),
        name="expert_down",
    )(x_at, blocks, act, w_down)
    return [outs[k * x_count : (k + 1) * x_count] for k in range(count)]


def per_device(
    x_in,
    z_in,
    conv_weight,
    conv_bias,
    x_proj,
    dt_proj,
    dt_bias,
    a_log,
    d_skip,
    out_proj,
    resid,
    norm_gain,
    routes,
    route_gate,
    w_gate,
    w_up,
    w_down,
):
    row_count, channels = x_in.shape
    seq_count = lax.axis_size("seq")
    exp_count = lax.axis_size("exp")
    x_count = seq_count // exp_count
    z_count = exp_count
    seq_at = lax.axis_index("seq")
    exp_at = lax.axis_index("exp")
    z_at, x_at = seq_at // x_count, seq_at % x_count
    z_one = z_at.reshape(1).astype(jnp.int32)
    x_one = x_at.reshape(1).astype(jnp.int32)
    e_one = exp_at.reshape(1).astype(jnp.int32)
    top_count = routes.shape[1]
    capacity = row_count * top_count * 17 // (16 * exp_count)
    pitch = capacity
    feature_slice = resid.shape[1]

    def from_z(block, r):
        pairs = [
            (((z + r) % z_count) * x_count + x, z * x_count + x)
            for z in range(z_count)
            for x in range(x_count)
        ]
        return lax.ppermute(block, "seq", pairs)

    def from_x(block, i):
        pairs = [
            (z * x_count + (x + i) % x_count, z * x_count + x)
            for z in range(z_count)
            for x in range(x_count)
        ]
        return lax.ppermute(block, "seq", pairs)

    turns = sorted(range(1, z_count), key=lambda r: min(r, z_count - r))

    def gathered(block):
        rows = {(0, 0): block}
        others = range(1, x_count)
        for i in others:
            rows[0, i] = from_x(block, i)
        sent = block
        for k, r in enumerate(turns):
            if k >= 2:
                sent = after(sent, rows[turns[k - 2], 0], *[rows[0, i] for i in others])
            rows[r, 0] = from_z(sent, r)
        for k, r in enumerate(turns):
            earlier = turns[max(k - 2, 0) : max(k - 1, 0)] if r != turns[-1] else turns[:k]
            forward = after(rows[r, 0], *[rows[q, i] for q in earlier for i in others])
            for i in others:
                rows[r, i] = from_x(forward, i)
        return [[rows[r, i] for i in range(x_count)] for r in range(z_count)]

    y_count = exp_count // 2

    def other_core(block):
        return lax.ppermute(block, "exp", [(e ^ 1, e) for e in range(exp_count)])

    def from_y(block, r):
        pairs = [
            ((y + r) % y_count * 2 + core, y * 2 + core)
            for y in range(y_count)
            for core in range(2)
        ]
        return lax.ppermute(block, "exp", pairs)

    swap = [
        ((e * x_count + x) * exp_count + z, (z * x_count + x) * exp_count + e)
        for z in range(z_count)
        for x in range(x_count)
        for e in range(exp_count)
    ]

    halo = lax.ppermute(
        x_in[row_count - 8 :], "seq", [(i, i + 1) for i in range(seq_count - 1)]
    )

    xconv, partial = conv_and_project(x_in, halo, conv_weight, conv_bias[None], x_proj.T)
    a_log, resid, routes, route_gate = lax.optimization_barrier(
        (a_log, resid, routes, route_gate, xconv)
    )[:4]
    rates = -jnp.exp(a_log.T) * LOG2E

    resid_here = lax.ppermute(resid, ("seq", "exp"), swap)

    def part_of(v):
        return v.astype(jnp.bfloat16).astype(jnp.float32)

    gate_high = part_of(route_gate)
    gate_mid = part_of(route_gate - gate_high)
    gate_low = route_gate - gate_high - gate_mid
    info = jnp.stack([routes.astype(jnp.float32), gate_high, gate_mid, gate_low])
    info = info.transpose(0, 2, 1).reshape(4, top_count * row_count)
    info = jnp.pad(info, ((0, 4), (0, channels - top_count * row_count)))

    def slots_of(named):
        flat = named.reshape(-1, row_count * top_count)
        onehot = (flat[:, :, None] == jnp.arange(exp_count, dtype=jnp.int32)).astype(jnp.float32)
        below = jnp.tril(jnp.ones((row_count * top_count,) * 2, jnp.float32), -1)
        counts = jnp.einsum("ij,bje->bie", below, onehot)
        slots = jnp.sum(counts * onehot, axis=2).astype(jnp.int32)
        return slots.reshape(-1, row_count, top_count)

    own_target = (routes - z_at) % exp_count * pitch + slots_of(routes)[0]
    slot_ids = jnp.arange(exp_count * pitch, dtype=jnp.int32)
    choose = jnp.sum(
        (own_target[:, :, None] == slot_ids[None, None, :]).astype(jnp.float32), axis=1
    ).astype(jnp.bfloat16)

    cut = channels // 2
    uppers = [from_x(after(out_proj, xconv)[:cut], i) for i in range(1, x_count)]
    chip_sum = partial + other_core(partial)
    partials = [chip_sum] + [from_y(chip_sum, r) for r in range(1, y_count)]
    step_size, load, b_wide, c_wide = scan_ends(partials, dt_proj, dt_bias[None], rates, xconv, info)
    loads = gathered(after(load, resid_here, *uppers))
    held_proj = after(out_proj, *[part for pair in loads for part in pair])
    lowers = [from_x(held_proj[cut:], i) for i in range(1, x_count)]
    columns = [[out_proj]] + [list(pair) for pair in zip(uppers, lowers)]
    mixed = scan_mix(
        z_one, x_one, loads, step_size, xconv, z_in, b_wide, c_wide, rates, d_skip[None]
    )
    along_z = [mixed] + [from_z(mixed, r) for r in range(1, z_count)]

    first_row = a_log.shape[1] + 2
    spare = after(jnp.stack([loads[r][0][first_row:] for r in range(z_count)]), mixed)
    spare = spare[:, :4, : top_count * row_count].astype(jnp.float32)
    spare = lax.dynamic_slice_in_dim(
        jnp.concatenate([spare, spare]), (z_count - z_at) % z_count, z_count, 0
    ).reshape(z_count, 4, top_count, row_count)
    all_routes = spare[:, 0].transpose(0, 2, 1).astype(jnp.int32)
    all_gates = (spare[:, 1] + spare[:, 2] + spare[:, 3]).transpose(0, 2, 1)
    z_ids = jnp.arange(z_count, dtype=jnp.int32)[:, None, None]
    target = (all_routes * z_count + z_ids) * pitch + slots_of(all_routes)
    target = target.reshape(z_count * row_count, top_count)
    count = z_count * pitch
    y_at, core_at = exp_at // 2, exp_at % 2

    def picked(core):
        experts = (y_at + jnp.arange(y_count, dtype=jnp.int32)) % y_count * 2 + core
        ids = experts[:, None] * count + jnp.arange(count, dtype=jnp.int32)[None, :]
        same = target[None, :, :] == ids.reshape(-1)[:, None, None]
        return jnp.sum(same.astype(jnp.float32), axis=2).astype(jnp.bfloat16)

    here_ids = exp_at * z_count * pitch + jnp.arange(z_count * pitch, dtype=jnp.int32)
    here = target[None, :, :] == here_ids[:, None, None]
    gate_here = jnp.sum(
        jnp.where(here, all_gates.reshape(1, z_count * row_count, top_count), 0.0), axis=(1, 2)
    )[:, None]
    first_here = jnp.sum(here[:, :, 0].astype(jnp.float32), axis=1)[:, None]

    keep, send = out_product(
        z_one, x_one, e_one, picked(core_at), picked(1 - core_at), resid_here, along_z, columns
    )
    over_chip = keep.astype(jnp.float32) + other_core(send).astype(jnp.float32)
    over_chip = over_chip.reshape(y_count, count, feature_slice)
    rows_here = over_chip[0]
    for r in range(1, y_count):
        arrived = from_y(over_chip[r].astype(jnp.bfloat16), y_count - r)
        rows_here = rows_here + arrived.astype(jnp.float32)
    rows_here = rows_here.astype(jnp.bfloat16)

    chunks = gathered(rows_here)
    act = expert_hidden(z_one, x_one, chunks, norm_gain, w_gate, w_up)

    by_distance = sorted(range(1, z_count), key=lambda r: abs(r - z_count // 2)) + [0]
    down, crossed = {}, {}
    for some in (by_distance[:1], by_distance[1:2], by_distance[2:]):
        if some == by_distance[2:]:
            act = after(act, *first_over)
        blocks = jnp.stack([(z_at + r) % z_count for r in some]).astype(jnp.int32)
        outs = expert_down(x_one, blocks, x_count, z_count, exp_count * pitch, act, w_down)
        down.update(zip(some, outs))
        if some == by_distance[:1]:
            first_over = [from_x(piece, x_count - i) for i, piece in enumerate(outs[0][1:], 1)]
    def over_x(r):
        return functools.reduce(
            jnp.add, [p.astype(jnp.float32) for p in [down[r][0]] + crossed[r]]
        )

    arrivals = []
    for k, r in enumerate(by_distance):
        pieces = down[r][1:]
        if r == 0:
            pieces = [after(piece, arrivals[0]) for piece in pieces]
        elif k >= 2:
            pieces = [after(piece, *crossed[by_distance[k - 2]]) for piece in pieces]
        crossed[r] = [from_x(piece, x_count - i) for i, piece in enumerate(pieces, 1)]
        if k == 0:
            crossed[r] = first_over
        if r:
            arrivals.append(from_z(over_x(r).astype(jnp.bfloat16), z_count - r))
    total = over_x(0)
    for sent in arrivals:
        total = total + sent.astype(jnp.float32)
    expert_out = total.astype(jnp.bfloat16).astype(jnp.float32)
    expert_out = gate_here * expert_out + first_here * rows_here.astype(jnp.float32)
    expert_out = expert_out.astype(jnp.bfloat16)
    pieces = expert_out.reshape(exp_count, pitch, feature_slice)
    back = []
    for k in range(exp_count):
        piece = lax.dynamic_index_in_dim(pieces, (exp_at - k) % exp_count, 0, keepdims=False)
        pairs = [
            (
                (e * x_count + x) * exp_count + (z + k) % exp_count,
                (z * x_count + x) * exp_count + e,
            )
            for z in range(z_count)
            for x in range(x_count)
            for e in range(exp_count)
        ]
        back.append(lax.ppermute(piece, ("seq", "exp"), pairs))
    back = jnp.concatenate(back, axis=0)
    return jnp.dot(choose, back, preferred_element_type=jnp.float32).astype(jnp.bfloat16)


def solution(mesh):
    return jax.shard_map(
        per_device,
        mesh=mesh,
        in_specs=(
            P("seq", "exp"),
            P("seq", "exp"),
            P(None, "exp"),
            P("exp"),
            P("exp", None),
            P(None, "exp"),
            P("exp"),
            P("exp", None),
            P("exp"),
            P("exp", "seq"),
            P("seq", "exp"),
            P(),
            P("seq", None),
            P("seq", None),
            P("exp", None, "seq"),
            P("exp", None, "seq"),
            P("exp", "seq", None),
        ),
        out_specs=P("seq", "exp"),
        check_vma=False,
    )
```

```python
import functools
import math

import jax
import jax.numpy as jnp
from jax import lax
from jax.experimental import pallas as pl
from jax.experimental.pallas import tpu as pltpu
from jax.sharding import PartitionSpec as P

eps = 1e-05
LOG2E = 1.4426950408889634
MIB = 1 << 20


def tile_of(size, most=512):
    return max(t for t in range(128, most + 1, 128) if size % t == 0)


def after(value, *others):
    return lax.optimization_barrier((value, *others))[0]


def whole_vmem():
    return pl.BlockSpec(memory_space=pltpu.VMEM)


def lanes_of(width):
    return pl.ds(pl.multiple_of(pl.program_id(0) * width, width), width)


def whole_smem():
    return pl.BlockSpec(memory_space=pltpu.SMEM)


def conv_kernel(x_ref, halo_ref, weight_ref, bias_ref, proj_ref, xconv_ref, partial_ref):
    rows = x_ref.shape[0]
    taps = weight_ref.shape[0]
    across = lanes_of(x_ref.shape[1])
    extended = jnp.concatenate(
        [halo_ref[:, across].astype(jnp.float32), x_ref[...].astype(jnp.float32)], axis=0
    )
    pad = halo_ref.shape[0]
    conv = jnp.zeros(x_ref.shape, jnp.float32) + bias_ref[...]
    for tap in range(taps):
        start = pad - (taps - 1) + tap
        conv = conv + weight_ref[tap : tap + 1, :] * extended[start : start + rows]
    xconv = (conv / (1.0 + jnp.exp(-conv))).astype(jnp.bfloat16)
    xconv_ref[...] = xconv

    @pl.when(pl.program_id(0) == 0)
    def _():
        partial_ref[...] = jnp.zeros_like(partial_ref)

    partial_ref[...] += lax.dot_general(
        xconv, proj_ref[...], (((1,), (1,)), ((), ())), preferred_element_type=jnp.float32
    )


def conv_and_project(x_in, halo, conv_weight, conv_bias, x_proj_t):
    rows, channels = x_in.shape
    width = tile_of(channels, 1024)
    columns = x_proj_t.shape[0]
    return pl.pallas_call(
        conv_kernel,
        grid=(channels // width,),
        in_specs=[
            pl.BlockSpec((rows, width), lambda i: (0, i)),
            whole_vmem(),
            pl.BlockSpec((conv_weight.shape[0], width), lambda i: (0, i)),
            pl.BlockSpec((1, width), lambda i: (0, i)),
            pl.BlockSpec((columns, width), lambda i: (0, i)),
        ],
        out_specs=[
            pl.BlockSpec((rows, width), lambda i: (0, i)),
            pl.BlockSpec((rows, columns), lambda i: (0, 0)),
        ],
        out_shape=[
            jax.ShapeDtypeStruct((rows, channels), jnp.bfloat16),
            jax.ShapeDtypeStruct((rows, columns), jnp.float32),
        ],
        name="conv_project",
    )(x_in, halo, conv_weight, conv_bias, x_proj_t)


def softplus(v):
    return jnp.maximum(v, 0.0) + jnp.log1p(jnp.exp(-jnp.abs(v)))


def ends_kernel(count, *refs):
    parts = refs[:count]
    proj_ref, bias_ref, rate_ref, x_ref, info_ref = refs[count : count + 5]
    size_ref, load_ref, b_ref, c_ref, low_ref, drive_ref = refs[count + 5 :]
    rows, width = x_ref.shape
    states = rate_ref.shape[0]
    low_rank = low_ref.shape[1]
    groups = width // 128

    @pl.when(pl.program_id(0) == 0)
    def _():
        total = parts[0][...]
        for part in parts[1:]:
            total = total + part[...]
        low_ref[...] = total[:, :low_rank].astype(jnp.bfloat16)
        b_mat = total[:, low_rank : low_rank + states]
        c_mat = total[:, low_rank + states : low_rank + 2 * states]
        b_ref[...] = jnp.broadcast_to(b_mat[:, :, None], b_ref.shape)
        c_ref[...] = jnp.broadcast_to(c_mat[:, :, None], c_ref.shape)

    size = softplus(
        jnp.dot(low_ref[...], proj_ref[...], preferred_element_type=jnp.float32) + bias_ref[...]
    )
    size_ref[...] = size
    drive_ref[...] = size * x_ref[...].astype(jnp.float32)
    rates = rate_ref[...]

    def step(block, state):
        start = pl.multiple_of(block * 8, 8)
        sizes = size_ref[pl.ds(start, 8), :]
        drives = drive_ref[pl.ds(start, 8), :]
        state = list(state)
        for i in range(8):
            b_now = b_ref[start + i]
            for g in range(groups):
                lanes = slice(g * 128, g * 128 + 128)
                decay = jnp.exp2(sizes[i : i + 1, lanes] * rates[:, lanes])
                state[g] = decay * state[g] + drives[i : i + 1, lanes] * b_now
        return tuple(state)

    zero = jnp.zeros((states, 128), jnp.float32)
    state = lax.fori_loop(0, rows // 8, step, (zero,) * groups)
    total = jnp.sum(size, axis=0, keepdims=True)
    high = total.astype(jnp.bfloat16).astype(jnp.float32)
    low = total - high
    rest = info_ref[: load_ref.shape[0] - states - 2, :]
    load_ref[...] = jnp.concatenate(
        [jnp.concatenate(state, axis=1), high, low, rest], axis=0
    ).astype(jnp.bfloat16)


def scan_ends(partials, dt_proj, dt_bias, rates, xconv, info):
    rows, channels = xconv.shape
    states = rates.shape[0]
    width = tile_of(channels, 1024)
    load_rows = -(-(states + 2) // 8) * 8
    wide = jax.ShapeDtypeStruct((rows, states, 128), jnp.float32)
    return pl.pallas_call(
        functools.partial(ends_kernel, len(partials)),
        grid=(channels // width,),
        in_specs=[
            *[whole_vmem() for _ in partials],
            pl.BlockSpec((dt_proj.shape[0], width), lambda i: (0, i)),
            pl.BlockSpec((1, width), lambda i: (0, i)),
            pl.BlockSpec((states, width), lambda i: (0, i)),
            pl.BlockSpec((rows, width), lambda i: (0, i)),
            pl.BlockSpec((info.shape[0], width), lambda i: (0, i)),
        ],
        out_specs=[
            pl.BlockSpec((rows, width), lambda i: (0, i)),
            pl.BlockSpec((load_rows, width), lambda i: (0, i)),
            pl.BlockSpec(wide.shape, lambda i: (0, 0, 0)),
            pl.BlockSpec(wide.shape, lambda i: (0, 0, 0)),
        ],
        out_shape=[
            jax.ShapeDtypeStruct((rows, channels), jnp.float32),
            jax.ShapeDtypeStruct((load_rows, channels), jnp.bfloat16),
            wide,
            wide,
        ],
        scratch_shapes=[
            pltpu.VMEM((rows, dt_proj.shape[0]), jnp.bfloat16),
            pltpu.VMEM((rows, width), jnp.float32),
        ],
        name="scan_ends",
    )(*partials, dt_proj, dt_bias, rates, xconv, info)


def mix_kernel(z_count, x_count, z_place, x_place, *refs):
    count = z_count * x_count
    loads = refs[:count]
    size_ref, x_ref, z_ref, b_ref, c_ref, rate_ref, skip_ref, out_ref = refs[count : count + 8]
    drive_ref, y_ref, load_ref = refs[count + 8 :]
    across = lanes_of(x_ref.shape[1])
    for k in range(count):
        z_from = lax.rem(z_place[0] + k // x_count, z_count)
        x_from = lax.rem(x_place[0] + k % x_count, x_count)
        load_ref[z_from * x_count + x_from] = loads[k][:, across].astype(jnp.float32)
    rows, width = x_ref.shape
    states = rate_ref.shape[0]
    groups = width // 128
    rates = rate_ref[...]
    x_f = x_ref[...].astype(jnp.float32)
    drive_ref[...] = size_ref[...] * x_f

    def earlier(j, state):
        block = load_ref[j]
        total = block[states : states + 1] + block[states + 1 : states + 2]
        return jnp.exp2(total * rates) * state + block[:states]

    place = z_place[0] * x_count + x_place[0]
    incoming = lax.fori_loop(0, place, earlier, jnp.zeros((states, width), jnp.float32))

    def step(block, state):
        start = pl.multiple_of(block * 8, 8)
        sizes = size_ref[pl.ds(start, 8), :]
        drives = drive_ref[pl.ds(start, 8), :]
        state = list(state)
        outs = [[None] * 8 for _ in range(groups)]
        for i in range(8):
            b_now = b_ref[start + i]
            c_now = c_ref[start + i]
            for g in range(groups):
                lanes = slice(g * 128, g * 128 + 128)
                decay = jnp.exp2(sizes[i : i + 1, lanes] * rates[:, lanes])
                state[g] = decay * state[g] + drives[i : i + 1, lanes] * b_now
                outs[g][i] = jnp.sum(state[g] * c_now, axis=0, keepdims=True)
        for g in range(groups):
            y_ref[pl.ds(start, 8), g * 128 : g * 128 + 128] = jnp.concatenate(outs[g], axis=0)
        return tuple(state)

    start_state = tuple(incoming[:, g * 128 : g * 128 + 128] for g in range(groups))
    lax.fori_loop(0, rows // 8, step, start_state)
    z_f = z_ref[...].astype(jnp.float32)
    scanned = y_ref[...] + skip_ref[...] * x_f
    out_ref[...] = (scanned * (z_f / (1.0 + jnp.exp(-z_f)))).astype(jnp.bfloat16)


def scan_mix(z_at, x_at, loads, step_size, xconv, z_in, b_wide, c_wide, rates, d_skip):
    rows, channels = xconv.shape
    states = rates.shape[0]
    width = tile_of(channels, 1024)
    flat = [load for pair in loads for load in pair]

    def by_lane(depth):
        return pl.BlockSpec((depth, width), lambda i: (0, i))

    return pl.pallas_call(
        functools.partial(mix_kernel, len(loads), len(loads[0])),
        grid=(channels // width,),
        in_specs=[
            whole_smem(),
            whole_smem(),
            *[whole_vmem() for _ in flat],
            by_lane(rows),
            by_lane(rows),
            by_lane(rows),
            pl.BlockSpec(b_wide.shape, lambda i: (0, 0, 0)),
            pl.BlockSpec(c_wide.shape, lambda i: (0, 0, 0)),
            by_lane(states),
            by_lane(1),
        ],
        out_specs=by_lane(rows),
        out_shape=jax.ShapeDtypeStruct((rows, channels), jnp.bfloat16),
        scratch_shapes=[pltpu.VMEM((rows, width), jnp.float32)] * 2
        + [pltpu.VMEM((len(flat), flat[0].shape[0], width), jnp.float32)],
        name="scan_mix",
    )(z_at, x_at, *flat, step_size, xconv, z_in, b_wide, c_wide, rates, d_skip)


def out_kernel(z_count, counts, z_ref, x_ref, e_ref, keep_pick_ref, send_pick_ref, resid_ref, *refs):
    x_count = len(counts)
    blocks = refs[:z_count]
    keep_ref, send_ref, held_ref, sum_ref = refs[z_count + sum(counts) :]
    weights = list(refs[z_count : z_count + sum(counts)])
    rows = blocks[0].shape[0]
    columns = weights[0].shape[1]
    for r in range(z_count):
        at = pl.multiple_of(lax.rem(z_ref[0] + r, z_count) * rows, rows)
        held_ref[pl.ds(at, rows), :] = blocks[r][...]
    own = pl.ds(pl.multiple_of(e_ref[0] * rows, rows), rows)
    for i, count in enumerate(counts):
        at = pl.ds(pl.multiple_of(lax.rem(x_ref[0] + i, x_count) * columns, columns), columns)
        start, parts = 0, []
        for _ in range(count):
            weight = weights.pop(0)
            depth = weight.shape[0]
            parts.append(
                jnp.dot(
                    held_ref[:, start : start + depth],
                    weight[...],
                    preferred_element_type=jnp.float32,
                )
            )
            start += depth
        sum_ref[...] = functools.reduce(jnp.add, parts)
        sum_ref[own, :] += resid_ref[:, at].astype(jnp.float32)
        summed = sum_ref[...].astype(jnp.bfloat16)
        for pick_ref, out_ref in ((keep_pick_ref, keep_ref), (send_pick_ref, send_ref)):
            out_ref[:, at] = jnp.dot(
                pick_ref[...], summed, preferred_element_type=jnp.float32
            ).astype(jnp.bfloat16)


def out_product(z_at, x_at, e_at, keep_pick, send_pick, resid, blocks, weights):
    rows, depth = blocks[0].shape
    z_count, x_count = len(blocks), len(weights)
    counts = [len(parts) for parts in weights]
    columns = weights[0][0].shape[1]
    return pl.pallas_call(
        functools.partial(out_kernel, z_count, counts),
        in_specs=[whole_smem()] * 3 + [whole_vmem()] * (3 + z_count + sum(counts)),
        out_specs=[whole_vmem()] * 2,
        out_shape=[jax.ShapeDtypeStruct((keep_pick.shape[0], x_count * columns), jnp.bfloat16)] * 2,
        scratch_shapes=[
            pltpu.VMEM((z_count * rows, depth), jnp.bfloat16),
            pltpu.VMEM((z_count * rows, columns), jnp.float32),
        ],
        compiler_params=pltpu.CompilerParams(vmem_limit_bytes=16 * MIB),
        name="out_product",
    )(
        z_at,
        x_at,
        e_at,
        keep_pick,
        send_pick,
        resid,
        *blocks,
        *[part for parts in weights for part in parts],
    )


def hidden_kernel(z_count, x_count, z_ref, x_ref, *refs):
    count = z_count * x_count
    chunks = refs[:count]
    gain_ref, gate_ref, up_ref, act_ref, scaled_ref = refs[count:]
    rows, depth = chunks[0].shape
    padded = scaled_ref.shape[0] // x_count

    def filled(chunk):
        h = chunk[...].astype(jnp.float32)
        if padded == rows:
            return h
        return jnp.concatenate([h, jnp.zeros((padded - rows, depth), jnp.float32)], axis=0)

    @pl.when(pl.program_id(0) == 0)
    def _():
        for i in range(x_count):
            own = [chunks[r * x_count + i] for r in range(z_count)]
            squares = jnp.zeros((padded, 1), jnp.float32)
            for chunk in own:
                h = filled(chunk)
                squares = squares + jnp.sum(h * h, axis=1, keepdims=True)
            scale = lax.rsqrt(squares / (depth * z_count) + eps)
            down = pl.multiple_of(lax.rem(x_ref[0] + i, x_count) * padded, padded)
            for r, chunk in enumerate(own):
                z_at = lax.rem(z_ref[0] + r, z_count)
                across = pl.multiple_of(z_at * depth, depth)
                h = filled(chunk)
                scaled_ref[pl.ds(down, padded), pl.ds(across, depth)] = (
                    h * scale * gain_ref[z_at]
                ).astype(jnp.bfloat16)

    scaled = scaled_ref[...]
    gate = jnp.dot(scaled, gate_ref[0], preferred_element_type=jnp.float32)
    upper = jnp.dot(scaled, up_ref[0], preferred_element_type=jnp.float32)
    act_ref[...] = (gate / (1.0 + jnp.exp(-gate)) * upper).astype(jnp.bfloat16)


def expert_hidden(z_at, x_at, chunks, gain, w_gate, w_up):
    z_count, x_count = len(chunks), len(chunks[0])
    rows, depth = chunks[0][0].shape
    columns = w_gate.shape[2]
    width = tile_of(columns, 256)
    padded = -(-rows // 16) * 16 * x_count
    gain = gain.reshape(z_count, 1, depth)
    weight_spec = pl.BlockSpec((1, depth * z_count, width), lambda n: (0, 0, n))
    return pl.pallas_call(
        functools.partial(hidden_kernel, z_count, x_count),
        grid=(columns // width,),
        in_specs=[whole_smem()] * 2
        + [whole_vmem()] * (z_count * x_count + 1)
        + [weight_spec, weight_spec],
        out_specs=pl.BlockSpec((padded, width), lambda n: (0, n)),
        out_shape=jax.ShapeDtypeStruct((padded, columns), jnp.bfloat16),
        scratch_shapes=[pltpu.VMEM((padded, depth * z_count), jnp.bfloat16)],
        compiler_params=pltpu.CompilerParams(vmem_limit_bytes=50 * MIB),
        name="expert_hidden",
    )(z_at, x_at, *[chunk for pair in chunks for chunk in pair], gain, w_gate, w_up)


def down_kernel(x_count, x_ref, blocks_ref, act_ref, weight_ref, *refs):
    outs, held_ref = refs[:-1], refs[-1]
    held_ref[...] = jnp.dot(act_ref[...], weight_ref[0], preferred_element_type=jnp.float32)
    rows = outs[0].shape[0]
    padded = held_ref.shape[0] // x_count
    for k in range(len(outs) // x_count):

        @pl.when(pl.program_id(0) == k)
        def _(k=k):
            for i in range(x_count):
                start = pl.multiple_of(lax.rem(x_ref[0] + i, x_count) * padded, padded)
                outs[k * x_count + i][...] = held_ref[pl.ds(start, rows), :].astype(jnp.bfloat16)


def expert_down(x_at, blocks, x_count, z_count, rows, act, w_down):
    padded, depth = act.shape
    columns = w_down.shape[2] // z_count
    width = tile_of(columns)
    tiles = columns // width
    count = blocks.shape[0]

    def out_spec(k):
        def place(m, n, x, blocks):
            return (0, jnp.where(m == k, n, jnp.where(m < k, 0, tiles - 1)))

        return pl.BlockSpec((rows, width), place)

    outs = pl.pallas_call(
        functools.partial(down_kernel, x_count),
        grid_spec=pltpu.PrefetchScalarGridSpec(
            num_scalar_prefetch=2,
            grid=(count, tiles),
            in_specs=[
                pl.BlockSpec((padded, depth), lambda m, n, x, blocks: (0, 0)),
                pl.BlockSpec(
                    (1, depth, width), lambda m, n, x, blocks: (0, 0, blocks[m] * tiles + n)
                ),
            ],
            out_specs=[out_spec(k) for k in range(count) for _ in range(x_count)],
            scratch_shapes=[pltpu.VMEM((padded, width), jnp.float32)],
        ),
        out_shape=[jax.ShapeDtypeStruct((rows, columns), jnp.bfloat16)] * (count * x_count),
        compiler_params=pltpu.CompilerParams(vmem_limit_bytes=50 * MIB),
        name="expert_down",
    )(x_at, blocks, act, w_down)
    return [outs[k * x_count : (k + 1) * x_count] for k in range(count)]


def per_device(
    x_in,
    z_in,
    conv_weight,
    conv_bias,
    x_proj,
    dt_proj,
    dt_bias,
    a_log,
    d_skip,
    out_proj,
    resid,
    norm_gain,
    routes,
    route_gate,
    w_gate,
    w_up,
    w_down,
):
    row_count, channels = x_in.shape
    seq_count = lax.axis_size("seq")
    exp_count = lax.axis_size("exp")
    x_count = seq_count // exp_count
    z_count = exp_count
    seq_at = lax.axis_index("seq")
    exp_at = lax.axis_index("exp")
    z_at, x_at = seq_at // x_count, seq_at % x_count
    z_one = z_at.reshape(1).astype(jnp.int32)
    x_one = x_at.reshape(1).astype(jnp.int32)
    e_one = exp_at.reshape(1).astype(jnp.int32)
    top_count = routes.shape[1]
    capacity = row_count * top_count * 17 // (16 * exp_count)
    pitch = capacity
    feature_slice = resid.shape[1]

    def from_z(block, r):
        pairs = [
            (((z + r) % z_count) * x_count + x, z * x_count + x)
            for z in range(z_count)
            for x in range(x_count)
        ]
        return lax.ppermute(block, "seq", pairs)

    def from_x(block, i):
        pairs = [
            (z * x_count + (x + i) % x_count, z * x_count + x)
            for z in range(z_count)
            for x in range(x_count)
        ]
        return lax.ppermute(block, "seq", pairs)

    turns = sorted(range(1, z_count), key=lambda r: min(r, z_count - r))

    def gathered(block):
        rows = {(0, 0): block}
        others = range(1, x_count)
        for i in others:
            rows[0, i] = from_x(block, i)
        sent = block
        for k, r in enumerate(turns):
            if k >= 2:
                sent = after(sent, rows[turns[k - 2], 0], *[rows[0, i] for i in others])
            rows[r, 0] = from_z(sent, r)
        for k, r in enumerate(turns):
            earlier = turns[max(k - 2, 0) : max(k - 1, 0)] if r != turns[-1] else turns[:k]
            forward = after(rows[r, 0], *[rows[q, i] for q in earlier for i in others])
            for i in others:
                rows[r, i] = from_x(forward, i)
        return [[rows[r, i] for i in range(x_count)] for r in range(z_count)]

    y_count = exp_count // 2

    def other_core(block):
        return lax.ppermute(block, "exp", [(e ^ 1, e) for e in range(exp_count)])

    def from_y(block, r):
        pairs = [
            ((y + r) % y_count * 2 + core, y * 2 + core)
            for y in range(y_count)
            for core in range(2)
        ]
        return lax.ppermute(block, "exp", pairs)

    swap = [
        ((e * x_count + x) * exp_count + z, (z * x_count + x) * exp_count + e)
        for z in range(z_count)
        for x in range(x_count)
        for e in range(exp_count)
    ]

    halo = lax.ppermute(
        x_in[row_count - 8 :], "seq", [(i, i + 1) for i in range(seq_count - 1)]
    )

    xconv, partial = conv_and_project(x_in, halo, conv_weight, conv_bias[None], x_proj.T)
    chip_sum = partial + other_core(partial)
    a_log, resid, routes, route_gate = lax.optimization_barrier(
        (a_log, resid, routes, route_gate, chip_sum)
    )[:4]
    rates = -jnp.exp(a_log.T) * LOG2E

    resid_here = lax.ppermute(resid, ("seq", "exp"), swap)

    def part_of(v):
        return v.astype(jnp.bfloat16).astype(jnp.float32)

    gate_high = part_of(route_gate)
    gate_mid = part_of(route_gate - gate_high)
    gate_low = route_gate - gate_high - gate_mid
    info = jnp.stack([routes.astype(jnp.float32), gate_high, gate_mid, gate_low])
    info = info.transpose(0, 2, 1).reshape(4, top_count * row_count)
    info = jnp.pad(info, ((0, 4), (0, channels - top_count * row_count)))

    def slots_of(named):
        flat = named.reshape(-1, row_count * top_count)
        onehot = (flat[:, :, None] == jnp.arange(exp_count, dtype=jnp.int32)).astype(jnp.float32)
        below = jnp.tril(jnp.ones((row_count * top_count,) * 2, jnp.float32), -1)
        counts = jnp.einsum("ij,bje->bie", below, onehot)
        slots = jnp.sum(counts * onehot, axis=2).astype(jnp.int32)
        return slots.reshape(-1, row_count, top_count)

    own_target = (routes - z_at) % exp_count * pitch + slots_of(routes)[0]
    slot_ids = jnp.arange(exp_count * pitch, dtype=jnp.int32)
    choose = jnp.sum(
        (own_target[:, :, None] == slot_ids[None, None, :]).astype(jnp.float32), axis=1
    ).astype(jnp.bfloat16)

    cut = channels * 5 // 16
    uppers = [from_x(after(out_proj, chip_sum)[:cut], i) for i in range(1, x_count)]
    partials = [chip_sum] + [from_y(chip_sum, r) for r in range(1, y_count)]
    step_size, load, b_wide, c_wide = scan_ends(partials, dt_proj, dt_bias[None], rates, xconv, info)
    loads = gathered(after(load, resid_here, *uppers))
    held_proj = after(out_proj, *[part for pair in loads for part in pair])
    lowers = [from_x(held_proj[cut:], i) for i in range(1, x_count)]
    columns = [[out_proj]] + [list(pair) for pair in zip(uppers, lowers)]
    mixed = scan_mix(
        z_one, x_one, loads, step_size, xconv, z_in, b_wide, c_wide, rates, d_skip[None]
    )
    along_z = [mixed] + [from_z(mixed, r) for r in range(1, z_count)]

    first_row = a_log.shape[1] + 2
    spare = after(jnp.stack([loads[r][0][first_row:] for r in range(z_count)]), mixed)
    spare = spare[:, :4, : top_count * row_count].astype(jnp.float32)
    spare = lax.dynamic_slice_in_dim(
        jnp.concatenate([spare, spare]), (z_count - z_at) % z_count, z_count, 0
    ).reshape(z_count, 4, top_count, row_count)
    all_routes = spare[:, 0].transpose(0, 2, 1).astype(jnp.int32)
    all_gates = (spare[:, 1] + spare[:, 2] + spare[:, 3]).transpose(0, 2, 1)
    z_ids = jnp.arange(z_count, dtype=jnp.int32)[:, None, None]
    target = (all_routes * z_count + z_ids) * pitch + slots_of(all_routes)
    target = target.reshape(z_count * row_count, top_count)
    count = z_count * pitch
    exp_late = after(exp_at, mixed)
    y_at, core_at = exp_late // 2, exp_late % 2

    def picked(core):
        experts = (y_at + jnp.arange(y_count, dtype=jnp.int32)) % y_count * 2 + core
        ids = experts[:, None] * count + jnp.arange(count, dtype=jnp.int32)[None, :]
        same = target[None, :, :] == ids.reshape(-1)[:, None, None]
        return jnp.sum(same.astype(jnp.float32), axis=2).astype(jnp.bfloat16)

    here_ids = exp_at * z_count * pitch + jnp.arange(z_count * pitch, dtype=jnp.int32)
    here = target[None, :, :] == here_ids[:, None, None]
    gate_here = jnp.sum(
        jnp.where(here, all_gates.reshape(1, z_count * row_count, top_count), 0.0), axis=(1, 2)
    )[:, None]
    first_here = jnp.sum(here[:, :, 0].astype(jnp.float32), axis=1)[:, None]

    keep, send = out_product(
        z_one, x_one, e_one, picked(core_at), picked(1 - core_at), resid_here, along_z, columns
    )
    over_chip = keep.astype(jnp.float32) + other_core(send).astype(jnp.float32)
    over_chip = over_chip.reshape(y_count, count, feature_slice)
    rows_here = over_chip[0]
    for r in range(1, y_count):
        arrived = from_y(over_chip[r].astype(jnp.bfloat16), y_count - r)
        rows_here = rows_here + arrived.astype(jnp.float32)
    rows_here = rows_here.astype(jnp.bfloat16)

    chunks = gathered(rows_here)
    act = expert_hidden(z_one, x_one, chunks, norm_gain, w_gate, w_up)

    by_distance = sorted(range(1, z_count), key=lambda r: abs(r - z_count // 2)) + [0]
    down, crossed, arrivals = {}, {}, []

    def products(turns_now, rows):
        blocks = jnp.stack([(z_at + r) % z_count for r in turns_now]).astype(jnp.int32)
        outs = expert_down(x_one, blocks, x_count, z_count, exp_count * pitch, rows, w_down)
        down.update(zip(turns_now, outs))

    def over_x(r):
        return functools.reduce(
            jnp.add, [p.astype(jnp.float32) for p in [down[r][0]] + crossed[r]]
        )

    products(by_distance[:1], act)
    products(by_distance[1:-1], act)
    for k, r in enumerate(by_distance):
        if r == 0:
            products([0], after(act, arrivals[0]))
        pieces = down[r][1:]
        if r and k >= 2:
            pieces = [after(piece, *crossed[by_distance[k - 2]]) for piece in pieces]
        crossed[r] = [from_x(piece, x_count - i) for i, piece in enumerate(pieces, 1)]
        if r:
            arrivals.append(from_z(over_x(r).astype(jnp.bfloat16), z_count - r))
    total = over_x(0)
    for sent in arrivals:
        total = total + sent.astype(jnp.float32)
    expert_out = total.astype(jnp.bfloat16).astype(jnp.float32)
    expert_out = gate_here * expert_out + first_here * rows_here.astype(jnp.float32)
    expert_out = expert_out.astype(jnp.bfloat16)
    pieces = expert_out.reshape(exp_count, pitch, feature_slice)
    back = []
    for k in range(exp_count):
        piece = lax.dynamic_index_in_dim(pieces, (exp_at - k) % exp_count, 0, keepdims=False)
        pairs = [
            (
                (e * x_count + x) * exp_count + (z + k) % exp_count,
                (z * x_count + x) * exp_count + e,
            )
            for z in range(z_count)
            for x in range(x_count)
            for e in range(exp_count)
        ]
        back.append(lax.ppermute(piece, ("seq", "exp"), pairs))
    back = jnp.concatenate(back, axis=0)
    return jnp.dot(choose, back, preferred_element_type=jnp.float32).astype(jnp.bfloat16)


def solution(mesh):
    return jax.shard_map(
        per_device,
        mesh=mesh,
        in_specs=(
            P("seq", "exp"),
            P("seq", "exp"),
            P(None, "exp"),
            P("exp"),
            P("exp", None),
            P(None, "exp"),
            P("exp"),
            P("exp", None),
            P("exp"),
            P("exp", "seq"),
            P("seq", "exp"),
            P(),
            P("seq", None),
            P("seq", None),
            P("exp", None, "seq"),
            P("exp", None, "seq"),
            P("exp", "seq", None),
        ),
        out_specs=P("seq", "exp"),
        check_vma=False,
    )
```

```python
import functools
import math

import jax
import jax.numpy as jnp
from jax import lax
from jax.experimental import pallas as pl
from jax.experimental.pallas import tpu as pltpu
from jax.sharding import PartitionSpec as P

eps = 1e-05
LOG2E = 1.4426950408889634
MIB = 1 << 20


def tile_of(size, most=512):
    return max(t for t in range(128, most + 1, 128) if size % t == 0)


def after(value, *others):
    return lax.optimization_barrier((value, *others))[0]


def whole_vmem():
    return pl.BlockSpec(memory_space=pltpu.VMEM)


def lanes_of(width):
    return pl.ds(pl.multiple_of(pl.program_id(0) * width, width), width)


def whole_smem():
    return pl.BlockSpec(memory_space=pltpu.SMEM)


def conv_kernel(x_ref, halo_ref, weight_ref, bias_ref, proj_ref, xconv_ref, partial_ref):
    rows = x_ref.shape[0]
    taps = weight_ref.shape[0]
    across = lanes_of(x_ref.shape[1])
    extended = jnp.concatenate(
        [halo_ref[:, across].astype(jnp.float32), x_ref[...].astype(jnp.float32)], axis=0
    )
    pad = halo_ref.shape[0]
    conv = jnp.zeros(x_ref.shape, jnp.float32) + bias_ref[...]
    for tap in range(taps):
        start = pad - (taps - 1) + tap
        conv = conv + weight_ref[tap : tap + 1, :] * extended[start : start + rows]
    xconv = (conv / (1.0 + jnp.exp(-conv))).astype(jnp.bfloat16)
    xconv_ref[...] = xconv

    @pl.when(pl.program_id(0) == 0)
    def _():
        partial_ref[...] = jnp.zeros_like(partial_ref)

    partial_ref[...] += lax.dot_general(
        xconv, proj_ref[...], (((1,), (1,)), ((), ())), preferred_element_type=jnp.float32
    )


def conv_and_project(x_in, halo, conv_weight, conv_bias, x_proj_t):
    rows, channels = x_in.shape
    width = tile_of(channels, 1024)
    columns = x_proj_t.shape[0]
    return pl.pallas_call(
        conv_kernel,
        grid=(channels // width,),
        in_specs=[
            pl.BlockSpec((rows, width), lambda i: (0, i)),
            whole_vmem(),
            pl.BlockSpec((conv_weight.shape[0], width), lambda i: (0, i)),
            pl.BlockSpec((1, width), lambda i: (0, i)),
            pl.BlockSpec((columns, width), lambda i: (0, i)),
        ],
        out_specs=[
            pl.BlockSpec((rows, width), lambda i: (0, i)),
            pl.BlockSpec((rows, columns), lambda i: (0, 0)),
        ],
        out_shape=[
            jax.ShapeDtypeStruct((rows, channels), jnp.bfloat16),
            jax.ShapeDtypeStruct((rows, columns), jnp.float32),
        ],
        name="conv_project",
    )(x_in, halo, conv_weight, conv_bias, x_proj_t)


def softplus(v):
    return jnp.maximum(v, 0.0) + jnp.log1p(jnp.exp(-jnp.abs(v)))


def ends_kernel(count, *refs):
    parts = refs[:count]
    proj_ref, bias_ref, rate_ref, x_ref, info_ref = refs[count : count + 5]
    size_ref, load_ref, b_ref, c_ref, low_ref, drive_ref = refs[count + 5 :]
    rows, width = x_ref.shape
    states = rate_ref.shape[0]
    low_rank = low_ref.shape[1]
    groups = width // 128

    @pl.when(pl.program_id(0) == 0)
    def _():
        total = parts[0][...]
        for part in parts[1:]:
            total = total + part[...]
        low_ref[...] = total[:, :low_rank].astype(jnp.bfloat16)
        b_mat = total[:, low_rank : low_rank + states]
        c_mat = total[:, low_rank + states : low_rank + 2 * states]
        b_ref[...] = jnp.broadcast_to(b_mat[:, :, None], b_ref.shape)
        c_ref[...] = jnp.broadcast_to(c_mat[:, :, None], c_ref.shape)

    size = softplus(
        jnp.dot(low_ref[...], proj_ref[...], preferred_element_type=jnp.float32) + bias_ref[...]
    )
    size_ref[...] = size
    drive_ref[...] = size * x_ref[...].astype(jnp.float32)
    rates = rate_ref[...]

    def step(block, state):
        start = pl.multiple_of(block * 8, 8)
        sizes = size_ref[pl.ds(start, 8), :]
        drives = drive_ref[pl.ds(start, 8), :]
        state = list(state)
        for i in range(8):
            b_now = b_ref[start + i]
            for g in range(groups):
                lanes = slice(g * 128, g * 128 + 128)
                decay = jnp.exp2(sizes[i : i + 1, lanes] * rates[:, lanes])
                state[g] = decay * state[g] + drives[i : i + 1, lanes] * b_now
        return tuple(state)

    zero = jnp.zeros((states, 128), jnp.float32)
    state = lax.fori_loop(0, rows // 8, step, (zero,) * groups)
    total = jnp.sum(size, axis=0, keepdims=True)
    high = total.astype(jnp.bfloat16).astype(jnp.float32)
    low = total - high
    rest = info_ref[: load_ref.shape[0] - states - 2, :]
    load_ref[...] = jnp.concatenate(
        [jnp.concatenate(state, axis=1), high, low, rest], axis=0
    ).astype(jnp.bfloat16)


def scan_ends(partials, dt_proj, dt_bias, rates, xconv, info):
    rows, channels = xconv.shape
    states = rates.shape[0]
    width = tile_of(channels, 1024)
    load_rows = -(-(states + 2) // 8) * 8
    wide = jax.ShapeDtypeStruct((rows, states, 128), jnp.float32)
    return pl.pallas_call(
        functools.partial(ends_kernel, len(partials)),
        grid=(channels // width,),
        in_specs=[
            *[whole_vmem() for _ in partials],
            pl.BlockSpec((dt_proj.shape[0], width), lambda i: (0, i)),
            pl.BlockSpec((1, width), lambda i: (0, i)),
            pl.BlockSpec((states, width), lambda i: (0, i)),
            pl.BlockSpec((rows, width), lambda i: (0, i)),
            pl.BlockSpec((info.shape[0], width), lambda i: (0, i)),
        ],
        out_specs=[
            pl.BlockSpec((rows, width), lambda i: (0, i)),
            pl.BlockSpec((load_rows, width), lambda i: (0, i)),
            pl.BlockSpec(wide.shape, lambda i: (0, 0, 0)),
            pl.BlockSpec(wide.shape, lambda i: (0, 0, 0)),
        ],
        out_shape=[
            jax.ShapeDtypeStruct((rows, channels), jnp.float32),
            jax.ShapeDtypeStruct((load_rows, channels), jnp.bfloat16),
            wide,
            wide,
        ],
        scratch_shapes=[
            pltpu.VMEM((rows, dt_proj.shape[0]), jnp.bfloat16),
            pltpu.VMEM((rows, width), jnp.float32),
        ],
        name="scan_ends",
    )(*partials, dt_proj, dt_bias, rates, xconv, info)


def mix_kernel(z_count, x_count, z_place, x_place, *refs):
    count = z_count * x_count
    loads = refs[:count]
    size_ref, x_ref, z_ref, b_ref, c_ref, rate_ref, skip_ref, out_ref = refs[count : count + 8]
    drive_ref, y_ref, load_ref = refs[count + 8 :]
    across = lanes_of(x_ref.shape[1])
    for k in range(count):
        z_from = lax.rem(z_place[0] + k // x_count, z_count)
        x_from = lax.rem(x_place[0] + k % x_count, x_count)
        load_ref[z_from * x_count + x_from] = loads[k][:, across].astype(jnp.float32)
    rows, width = x_ref.shape
    states = rate_ref.shape[0]
    groups = width // 128
    rates = rate_ref[...]
    x_f = x_ref[...].astype(jnp.float32)
    drive_ref[...] = size_ref[...] * x_f

    def earlier(j, state):
        block = load_ref[j]
        total = block[states : states + 1] + block[states + 1 : states + 2]
        return jnp.exp2(total * rates) * state + block[:states]

    place = z_place[0] * x_count + x_place[0]
    incoming = lax.fori_loop(0, place, earlier, jnp.zeros((states, width), jnp.float32))

    def step(block, state):
        start = pl.multiple_of(block * 8, 8)
        sizes = size_ref[pl.ds(start, 8), :]
        drives = drive_ref[pl.ds(start, 8), :]
        state = list(state)
        outs = [[None] * 8 for _ in range(groups)]
        for i in range(8):
            b_now = b_ref[start + i]
            c_now = c_ref[start + i]
            for g in range(groups):
                lanes = slice(g * 128, g * 128 + 128)
                decay = jnp.exp2(sizes[i : i + 1, lanes] * rates[:, lanes])
                state[g] = decay * state[g] + drives[i : i + 1, lanes] * b_now
                outs[g][i] = jnp.sum(state[g] * c_now, axis=0, keepdims=True)
        for g in range(groups):
            y_ref[pl.ds(start, 8), g * 128 : g * 128 + 128] = jnp.concatenate(outs[g], axis=0)
        return tuple(state)

    start_state = tuple(incoming[:, g * 128 : g * 128 + 128] for g in range(groups))
    lax.fori_loop(0, rows // 8, step, start_state)
    z_f = z_ref[...].astype(jnp.float32)
    scanned = y_ref[...] + skip_ref[...] * x_f
    out_ref[...] = (scanned * (z_f / (1.0 + jnp.exp(-z_f)))).astype(jnp.bfloat16)


def scan_mix(z_at, x_at, loads, step_size, xconv, z_in, b_wide, c_wide, rates, d_skip):
    rows, channels = xconv.shape
    states = rates.shape[0]
    width = tile_of(channels, 1024)
    flat = [load for pair in loads for load in pair]

    def by_lane(depth):
        return pl.BlockSpec((depth, width), lambda i: (0, i))

    return pl.pallas_call(
        functools.partial(mix_kernel, len(loads), len(loads[0])),
        grid=(channels // width,),
        in_specs=[
            whole_smem(),
            whole_smem(),
            *[whole_vmem() for _ in flat],
            by_lane(rows),
            by_lane(rows),
            by_lane(rows),
            pl.BlockSpec(b_wide.shape, lambda i: (0, 0, 0)),
            pl.BlockSpec(c_wide.shape, lambda i: (0, 0, 0)),
            by_lane(states),
            by_lane(1),
        ],
        out_specs=by_lane(rows),
        out_shape=jax.ShapeDtypeStruct((rows, channels), jnp.bfloat16),
        scratch_shapes=[pltpu.VMEM((rows, width), jnp.float32)] * 2
        + [pltpu.VMEM((len(flat), flat[0].shape[0], width), jnp.float32)],
        name="scan_mix",
    )(z_at, x_at, *flat, step_size, xconv, z_in, b_wide, c_wide, rates, d_skip)


def out_kernel(z_count, counts, z_ref, x_ref, e_ref, keep_pick_ref, send_pick_ref, resid_ref, *refs):
    x_count = len(counts)
    blocks = refs[:z_count]
    keep_ref, send_ref, held_ref, sum_ref = refs[z_count + sum(counts) :]
    weights = list(refs[z_count : z_count + sum(counts)])
    rows = blocks[0].shape[0]
    columns = weights[0].shape[1]
    for r in range(z_count):
        at = pl.multiple_of(lax.rem(z_ref[0] + r, z_count) * rows, rows)
        held_ref[pl.ds(at, rows), :] = blocks[r][...]
    own = pl.ds(pl.multiple_of(e_ref[0] * rows, rows), rows)
    for i, count in enumerate(counts):
        at = pl.ds(pl.multiple_of(lax.rem(x_ref[0] + i, x_count) * columns, columns), columns)
        start, parts = 0, []
        for _ in range(count):
            weight = weights.pop(0)
            depth = weight.shape[0]
            parts.append(
                jnp.dot(
                    held_ref[:, start : start + depth],
                    weight[...],
                    preferred_element_type=jnp.float32,
                )
            )
            start += depth
        sum_ref[...] = functools.reduce(jnp.add, parts)
        sum_ref[own, :] += resid_ref[:, at].astype(jnp.float32)
        summed = sum_ref[...].astype(jnp.bfloat16)
        for pick_ref, out_ref in ((keep_pick_ref, keep_ref), (send_pick_ref, send_ref)):
            out_ref[:, at] = jnp.dot(
                pick_ref[...], summed, preferred_element_type=jnp.float32
            ).astype(jnp.bfloat16)


def out_product(z_at, x_at, e_at, keep_pick, send_pick, resid, blocks, weights):
    rows, depth = blocks[0].shape
    z_count, x_count = len(blocks), len(weights)
    counts = [len(parts) for parts in weights]
    columns = weights[0][0].shape[1]
    return pl.pallas_call(
        functools.partial(out_kernel, z_count, counts),
        in_specs=[whole_smem()] * 3 + [whole_vmem()] * (3 + z_count + sum(counts)),
        out_specs=[whole_vmem()] * 2,
        out_shape=[jax.ShapeDtypeStruct((keep_pick.shape[0], x_count * columns), jnp.bfloat16)] * 2,
        scratch_shapes=[
            pltpu.VMEM((z_count * rows, depth), jnp.bfloat16),
            pltpu.VMEM((z_count * rows, columns), jnp.float32),
        ],
        compiler_params=pltpu.CompilerParams(vmem_limit_bytes=16 * MIB),
        name="out_product",
    )(
        z_at,
        x_at,
        e_at,
        keep_pick,
        send_pick,
        resid,
        *blocks,
        *[part for parts in weights for part in parts],
    )


def hidden_kernel(steps, z_count, x_count, z_ref, x_ref, *refs):
    count = z_count * x_count
    chunks = refs[:count]
    gain_ref, gate_ref, up_ref, down_ref, act_ref = refs[count : count + 5]
    outs, scaled_ref, held_ref, sum_ref = refs[count + 5 : -3], *refs[-3:]
    step = pl.program_id(0)
    width = act_ref.shape[1]
    rows, depth = chunks[0].shape
    padded = scaled_ref.shape[0] // x_count

    def filled(chunk):
        h = chunk[...].astype(jnp.float32)
        if padded == rows:
            return h
        return jnp.concatenate([h, jnp.zeros((padded - rows, depth), jnp.float32)], axis=0)

    @pl.when(step == 0)
    def _():
        for i in range(x_count):
            own = [chunks[r * x_count + i] for r in range(z_count)]
            squares = jnp.zeros((padded, 1), jnp.float32)
            for chunk in own:
                h = filled(chunk)
                squares = squares + jnp.sum(h * h, axis=1, keepdims=True)
            scale = lax.rsqrt(squares / (depth * z_count) + eps)
            down = pl.multiple_of(lax.rem(x_ref[0] + i, x_count) * padded, padded)
            for r, chunk in enumerate(own):
                z_at = lax.rem(z_ref[0] + r, z_count)
                across = pl.multiple_of(z_at * depth, depth)
                h = filled(chunk)
                scaled_ref[pl.ds(down, padded), pl.ds(across, depth)] = (
                    h * scale * gain_ref[z_at]
                ).astype(jnp.bfloat16)

    @pl.when(step < steps)
    def _():
        scaled = scaled_ref[...]
        gate = jnp.dot(scaled, gate_ref[0], preferred_element_type=jnp.float32)
        upper = jnp.dot(scaled, up_ref[0], preferred_element_type=jnp.float32)
        act = (gate / (1.0 + jnp.exp(-gate)) * upper).astype(jnp.bfloat16)
        act_ref[...] = act
        held_ref[:, pl.ds(pl.multiple_of(step * width, width), width)] = act

    @pl.when(step >= steps)
    def _():
        sum_ref[...] = jnp.dot(held_ref[...], down_ref[0], preferred_element_type=jnp.float32)
        for i, out_ref in enumerate(outs):
            start = pl.multiple_of(lax.rem(x_ref[0] + i, x_count) * padded, padded)
            out_ref[...] = sum_ref[pl.ds(start, rows), :].astype(jnp.bfloat16)


def expert_hidden(z_at, x_at, far, chunks, gain, w_gate, w_up, w_down):
    z_count, x_count = len(chunks), len(chunks[0])
    rows, depth = chunks[0][0].shape
    columns = w_gate.shape[2]
    width = tile_of(columns, 256)
    steps = columns // width
    padded = -(-rows // 16) * 16 * x_count
    gain = gain.reshape(z_count, 1, depth)
    down_width = tile_of(depth)
    tiles = depth // down_width

    def before(n):
        return jnp.minimum(n, steps - 1)

    def beyond(n):
        return jnp.maximum(n - steps, 0)

    weight_spec = pl.BlockSpec((1, depth * z_count, width), lambda n, z, x: (0, 0, before(n)))
    down_spec = pl.BlockSpec(
        (1, columns, down_width),
        lambda n, z, x: (0, 0, lax.rem(z[0] + far, z_count) * tiles + beyond(n)),
    )
    act, *outs = pl.pallas_call(
        functools.partial(hidden_kernel, steps, z_count, x_count),
        grid_spec=pltpu.PrefetchScalarGridSpec(
            num_scalar_prefetch=2,
            grid=(steps + tiles,),
            in_specs=[whole_vmem()] * (z_count * x_count + 1)
            + [weight_spec, weight_spec, down_spec],
            out_specs=[pl.BlockSpec((padded, width), lambda n, z, x: (0, before(n)))]
            + [pl.BlockSpec((rows, down_width), lambda n, z, x: (0, beyond(n)))] * x_count,
            scratch_shapes=[
                pltpu.VMEM((padded, depth * z_count), jnp.bfloat16),
                pltpu.VMEM((padded, columns), jnp.bfloat16),
                pltpu.VMEM((padded, down_width), jnp.float32),
            ],
        ),
        out_shape=[jax.ShapeDtypeStruct((padded, columns), jnp.bfloat16)]
        + [jax.ShapeDtypeStruct((rows, depth), jnp.bfloat16)] * x_count,
        compiler_params=pltpu.CompilerParams(vmem_limit_bytes=50 * MIB),
        name="expert_hidden",
    )(z_at, x_at, *[chunk for pair in chunks for chunk in pair], gain, w_gate, w_up, w_down)
    return act, outs


def down_kernel(x_count, x_ref, blocks_ref, act_ref, weight_ref, *refs):
    outs, held_ref = refs[:-1], refs[-1]
    held_ref[...] = jnp.dot(act_ref[...], weight_ref[0], preferred_element_type=jnp.float32)
    rows = outs[0].shape[0]
    padded = held_ref.shape[0] // x_count
    for k in range(len(outs) // x_count):

        @pl.when(pl.program_id(0) == k)
        def _(k=k):
            for i in range(x_count):
                start = pl.multiple_of(lax.rem(x_ref[0] + i, x_count) * padded, padded)
                outs[k * x_count + i][...] = held_ref[pl.ds(start, rows), :].astype(jnp.bfloat16)


def expert_down(x_at, blocks, x_count, z_count, rows, act, w_down):
    padded, depth = act.shape
    columns = w_down.shape[2] // z_count
    width = tile_of(columns)
    tiles = columns // width
    count = blocks.shape[0]

    def out_spec(k):
        def place(m, n, x, blocks):
            return (0, jnp.where(m == k, n, jnp.where(m < k, 0, tiles - 1)))

        return pl.BlockSpec((rows, width), place)

    outs = pl.pallas_call(
        functools.partial(down_kernel, x_count),
        grid_spec=pltpu.PrefetchScalarGridSpec(
            num_scalar_prefetch=2,
            grid=(count, tiles),
            in_specs=[
                pl.BlockSpec((padded, depth), lambda m, n, x, blocks: (0, 0)),
                pl.BlockSpec(
                    (1, depth, width), lambda m, n, x, blocks: (0, 0, blocks[m] * tiles + n)
                ),
            ],
            out_specs=[out_spec(k) for k in range(count) for _ in range(x_count)],
            scratch_shapes=[pltpu.VMEM((padded, width), jnp.float32)],
        ),
        out_shape=[jax.ShapeDtypeStruct((rows, columns), jnp.bfloat16)] * (count * x_count),
        compiler_params=pltpu.CompilerParams(vmem_limit_bytes=50 * MIB),
        name="expert_down",
    )(x_at, blocks, act, w_down)
    return [outs[k * x_count : (k + 1) * x_count] for k in range(count)]


def per_device(
    x_in,
    z_in,
    conv_weight,
    conv_bias,
    x_proj,
    dt_proj,
    dt_bias,
    a_log,
    d_skip,
    out_proj,
    resid,
    norm_gain,
    routes,
    route_gate,
    w_gate,
    w_up,
    w_down,
):
    row_count, channels = x_in.shape
    seq_count = lax.axis_size("seq")
    exp_count = lax.axis_size("exp")
    x_count = seq_count // exp_count
    z_count = exp_count
    seq_at = lax.axis_index("seq")
    exp_at = lax.axis_index("exp")
    z_at, x_at = seq_at // x_count, seq_at % x_count
    z_one = z_at.reshape(1).astype(jnp.int32)
    x_one = x_at.reshape(1).astype(jnp.int32)
    e_one = exp_at.reshape(1).astype(jnp.int32)
    top_count = routes.shape[1]
    capacity = row_count * top_count * 17 // (16 * exp_count)
    pitch = capacity
    feature_slice = resid.shape[1]

    def from_z(block, r):
        pairs = [
            (((z + r) % z_count) * x_count + x, z * x_count + x)
            for z in range(z_count)
            for x in range(x_count)
        ]
        return lax.ppermute(block, "seq", pairs)

    def from_x(block, i):
        pairs = [
            (z * x_count + (x + i) % x_count, z * x_count + x)
            for z in range(z_count)
            for x in range(x_count)
        ]
        return lax.ppermute(block, "seq", pairs)

    turns = sorted(range(1, z_count), key=lambda r: min(r, z_count - r))

    def gathered(block):
        rows = {(0, 0): block}
        others = range(1, x_count)
        for i in others:
            rows[0, i] = from_x(block, i)
        sent = block
        for k, r in enumerate(turns):
            if k >= 2:
                sent = after(sent, rows[turns[k - 2], 0], *[rows[0, i] for i in others])
            rows[r, 0] = from_z(sent, r)
        for k, r in enumerate(turns):
            earlier = turns[max(k - 2, 0) : max(k - 1, 0)] if r != turns[-1] else turns[:k]
            forward = after(rows[r, 0], *[rows[q, i] for q in earlier for i in others])
            for i in others:
                rows[r, i] = from_x(forward, i)
        return [[rows[r, i] for i in range(x_count)] for r in range(z_count)]

    y_count = exp_count // 2

    def other_core(block):
        return lax.ppermute(block, "exp", [(e ^ 1, e) for e in range(exp_count)])

    def from_y(block, r):
        pairs = [
            ((y + r) % y_count * 2 + core, y * 2 + core)
            for y in range(y_count)
            for core in range(2)
        ]
        return lax.ppermute(block, "exp", pairs)

    swap = [
        ((e * x_count + x) * exp_count + z, (z * x_count + x) * exp_count + e)
        for z in range(z_count)
        for x in range(x_count)
        for e in range(exp_count)
    ]

    halo = lax.ppermute(
        x_in[row_count - 8 :], "seq", [(i, i + 1) for i in range(seq_count - 1)]
    )

    xconv, partial = conv_and_project(x_in, halo, conv_weight, conv_bias[None], x_proj.T)
    resid_here = lax.ppermute(resid, ("seq", "exp"), swap)

    chip_sum = partial + other_core(after(partial, resid_here))
    a_log, routes, route_gate = lax.optimization_barrier(
        (a_log, routes, route_gate, chip_sum)
    )[:3]
    rates = -jnp.exp(a_log.T) * LOG2E

    def part_of(v):
        return v.astype(jnp.bfloat16).astype(jnp.float32)

    gate_high = part_of(route_gate)
    gate_mid = part_of(route_gate - gate_high)
    gate_low = route_gate - gate_high - gate_mid
    info = jnp.stack([routes.astype(jnp.float32), gate_high, gate_mid, gate_low])
    info = info.transpose(0, 2, 1).reshape(4, top_count * row_count)
    info = jnp.pad(info, ((0, 4), (0, channels - top_count * row_count)))

    def slots_of(named):
        flat = named.reshape(-1, row_count * top_count)
        onehot = (flat[:, :, None] == jnp.arange(exp_count, dtype=jnp.int32)).astype(jnp.float32)
        below = jnp.tril(jnp.ones((row_count * top_count,) * 2, jnp.float32), -1)
        counts = jnp.einsum("ij,bje->bie", below, onehot)
        slots = jnp.sum(counts * onehot, axis=2).astype(jnp.int32)
        return slots.reshape(-1, row_count, top_count)

    own_target = (routes - z_at) % exp_count * pitch + slots_of(routes)[0]
    slot_ids = jnp.arange(exp_count * pitch, dtype=jnp.int32)
    choose = jnp.sum(
        (own_target[:, :, None] == slot_ids[None, None, :]).astype(jnp.float32), axis=1
    ).astype(jnp.bfloat16)

    cut = channels * 5 // 16
    uppers = [from_x(after(out_proj, chip_sum)[:cut], i) for i in range(1, x_count)]
    partials = [chip_sum] + [from_y(chip_sum, r) for r in range(1, y_count)]
    step_size, load, b_wide, c_wide = scan_ends(partials, dt_proj, dt_bias[None], rates, xconv, info)
    loads = gathered(after(load, resid_here, *uppers))
    held_proj = after(out_proj, *[part for pair in loads for part in pair])
    lowers = [from_x(held_proj[cut:], i) for i in range(1, x_count)]
    columns = [[out_proj]] + [list(pair) for pair in zip(uppers, lowers)]
    mixed = scan_mix(
        z_one, x_one, loads, step_size, xconv, z_in, b_wide, c_wide, rates, d_skip[None]
    )
    along_z = [mixed] + [from_z(mixed, r) for r in range(1, z_count)]

    first_row = a_log.shape[1] + 2
    spare = after(jnp.stack([loads[r][0][first_row:] for r in range(z_count)]), mixed)
    spare = spare[:, :4, : top_count * row_count].astype(jnp.float32)
    spare = lax.dynamic_slice_in_dim(
        jnp.concatenate([spare, spare]), (z_count - z_at) % z_count, z_count, 0
    ).reshape(z_count, 4, top_count, row_count)
    all_routes = spare[:, 0].transpose(0, 2, 1).astype(jnp.int32)
    all_gates = (spare[:, 1] + spare[:, 2] + spare[:, 3]).transpose(0, 2, 1)
    z_ids = jnp.arange(z_count, dtype=jnp.int32)[:, None, None]
    target = (all_routes * z_count + z_ids) * pitch + slots_of(all_routes)
    target = target.reshape(z_count * row_count, top_count)
    count = z_count * pitch
    exp_late = after(exp_at, mixed)
    y_at, core_at = exp_late // 2, exp_late % 2

    def picked(core):
        experts = (y_at + jnp.arange(y_count, dtype=jnp.int32)) % y_count * 2 + core
        ids = experts[:, None] * count + jnp.arange(count, dtype=jnp.int32)[None, :]
        same = target[None, :, :] == ids.reshape(-1)[:, None, None]
        return jnp.sum(same.astype(jnp.float32), axis=2).astype(jnp.bfloat16)

    here_ids = exp_at * z_count * pitch + jnp.arange(z_count * pitch, dtype=jnp.int32)
    here = target[None, :, :] == here_ids[:, None, None]
    gate_here = jnp.sum(
        jnp.where(here, all_gates.reshape(1, z_count * row_count, top_count), 0.0), axis=(1, 2)
    )[:, None]
    first_here = jnp.sum(here[:, :, 0].astype(jnp.float32), axis=1)[:, None]

    keep, send = out_product(
        z_one, x_one, e_one, picked(core_at), picked(1 - core_at), resid_here, along_z, columns
    )
    over_chip = keep.astype(jnp.float32) + other_core(send).astype(jnp.float32)
    over_chip = over_chip.reshape(y_count, count, feature_slice)
    rows_here = over_chip[0]
    for r in range(1, y_count):
        arrived = from_y(over_chip[r].astype(jnp.bfloat16), y_count - r)
        rows_here = rows_here + arrived.astype(jnp.float32)
    rows_here = rows_here.astype(jnp.bfloat16)

    chunks = gathered(rows_here)
    by_distance = sorted(range(1, z_count), key=lambda r: abs(r - z_count // 2)) + [0]
    act, far_outs = expert_hidden(
        z_one, x_one, by_distance[0], chunks, norm_gain, w_gate, w_up, w_down
    )
    down, crossed, arrivals = {by_distance[0]: far_outs}, {}, []

    def products(turns_now, rows):
        blocks = jnp.stack([(z_at + r) % z_count for r in turns_now]).astype(jnp.int32)
        outs = expert_down(x_one, blocks, x_count, z_count, exp_count * pitch, rows, w_down)
        down.update(zip(turns_now, outs))

    def over_x(r):
        return functools.reduce(
            jnp.add, [p.astype(jnp.float32) for p in [down[r][0]] + crossed[r]]
        )

    products(by_distance[1:-1], act)
    for k, r in enumerate(by_distance):
        if r == 0:
            products([0], after(act, arrivals[0][0]))
        pieces = down[r][1:]
        if r and k >= 2:
            pieces = [after(piece, *crossed[by_distance[k - 2]]) for piece in pieces]
        crossed[r] = [from_x(piece, x_count - i) for i, piece in enumerate(pieces, 1)]
        if r:
            sums = over_x(r).astype(jnp.bfloat16)
            most = feature_slice * 3 // 4
            cuts = [sums] if k else [sums[:, :most], sums[:, most:]]
            arrivals.append([from_z(part, z_count - r) for part in cuts])
    total = over_x(0)
    for sent in arrivals:
        total = total + jnp.concatenate(sent, axis=1).astype(jnp.float32)
    expert_out = total.astype(jnp.bfloat16).astype(jnp.float32)
    expert_out = gate_here * expert_out + first_here * rows_here.astype(jnp.float32)
    expert_out = expert_out.astype(jnp.bfloat16)
    pieces = expert_out.reshape(exp_count, pitch, feature_slice)
    back = []
    for k in range(exp_count):
        piece = lax.dynamic_index_in_dim(pieces, (exp_at - k) % exp_count, 0, keepdims=False)
        pairs = [
            (
                (e * x_count + x) * exp_count + (z + k) % exp_count,
                (z * x_count + x) * exp_count + e,
            )
            for z in range(z_count)
            for x in range(x_count)
            for e in range(exp_count)
        ]
        back.append(lax.ppermute(piece, ("seq", "exp"), pairs))
    back = jnp.concatenate(back, axis=0)
    return jnp.dot(choose, back, preferred_element_type=jnp.float32).astype(jnp.bfloat16)


def solution(mesh):
    return jax.shard_map(
        per_device,
        mesh=mesh,
        in_specs=(
            P("seq", "exp"),
            P("seq", "exp"),
            P(None, "exp"),
            P("exp"),
            P("exp", None),
            P(None, "exp"),
            P("exp"),
            P("exp", None),
            P("exp"),
            P("exp", "seq"),
            P("seq", "exp"),
            P(),
            P("seq", None),
            P("seq", None),
            P("exp", None, "seq"),
            P("exp", None, "seq"),
            P("exp", "seq", None),
        ),
        out_specs=P("seq", "exp"),
        check_vma=False,
    )
```

```python
import functools
import math

import jax
import jax.numpy as jnp
from jax import lax
from jax.experimental import pallas as pl
from jax.experimental.pallas import tpu as pltpu
from jax.sharding import PartitionSpec as P

eps = 1e-05
LOG2E = 1.4426950408889634
MIB = 1 << 20


def tile_of(size, most=512):
    return max(t for t in range(128, most + 1, 128) if size % t == 0)


def after(value, *others):
    return lax.optimization_barrier((value, *others))[0]


def whole_vmem():
    return pl.BlockSpec(memory_space=pltpu.VMEM)


def lanes_of(width):
    return pl.ds(pl.multiple_of(pl.program_id(0) * width, width), width)


def whole_smem():
    return pl.BlockSpec(memory_space=pltpu.SMEM)


def conv_kernel(x_ref, halo_ref, weight_ref, bias_ref, proj_ref, xconv_ref, partial_ref):
    rows = x_ref.shape[0]
    taps = weight_ref.shape[0]
    across = lanes_of(x_ref.shape[1])
    extended = jnp.concatenate(
        [halo_ref[:, across].astype(jnp.float32), x_ref[...].astype(jnp.float32)], axis=0
    )
    pad = halo_ref.shape[0]
    conv = jnp.zeros(x_ref.shape, jnp.float32) + bias_ref[...]
    for tap in range(taps):
        start = pad - (taps - 1) + tap
        conv = conv + weight_ref[tap : tap + 1, :] * extended[start : start + rows]
    xconv = (conv / (1.0 + jnp.exp(-conv))).astype(jnp.bfloat16)
    xconv_ref[...] = xconv

    @pl.when(pl.program_id(0) == 0)
    def _():
        partial_ref[...] = jnp.zeros_like(partial_ref)

    partial_ref[...] += lax.dot_general(
        xconv, proj_ref[...], (((1,), (1,)), ((), ())), preferred_element_type=jnp.float32
    )


def conv_and_project(x_in, halo, conv_weight, conv_bias, x_proj_t):
    rows, channels = x_in.shape
    width = tile_of(channels, 1024)
    columns = x_proj_t.shape[0]
    return pl.pallas_call(
        conv_kernel,
        grid=(channels // width,),
        in_specs=[
            pl.BlockSpec((rows, width), lambda i: (0, i)),
            whole_vmem(),
            pl.BlockSpec((conv_weight.shape[0], width), lambda i: (0, i)),
            pl.BlockSpec((1, width), lambda i: (0, i)),
            pl.BlockSpec((columns, width), lambda i: (0, i)),
        ],
        out_specs=[
            pl.BlockSpec((rows, width), lambda i: (0, i)),
            pl.BlockSpec((rows, columns), lambda i: (0, 0)),
        ],
        out_shape=[
            jax.ShapeDtypeStruct((rows, channels), jnp.bfloat16),
            jax.ShapeDtypeStruct((rows, columns), jnp.float32),
        ],
        name="conv_project",
    )(x_in, halo, conv_weight, conv_bias, x_proj_t)


def softplus(v):
    return jnp.maximum(v, 0.0) + jnp.log1p(jnp.exp(-jnp.abs(v)))


def ends_kernel(count, *refs):
    parts = refs[:count]
    proj_ref, bias_ref, rate_ref, x_ref, info_ref = refs[count : count + 5]
    size_ref, load_ref, b_ref, c_ref, low_ref, drive_ref = refs[count + 5 :]
    rows, width = x_ref.shape
    states = rate_ref.shape[0]
    low_rank = low_ref.shape[1]
    groups = width // 128

    @pl.when(pl.program_id(0) == 0)
    def _():
        total = parts[0][...]
        for part in parts[1:]:
            total = total + part[...]
        low_ref[...] = total[:, :low_rank].astype(jnp.bfloat16)
        b_mat = total[:, low_rank : low_rank + states]
        c_mat = total[:, low_rank + states : low_rank + 2 * states]
        b_ref[...] = jnp.broadcast_to(b_mat[:, :, None], b_ref.shape)
        c_ref[...] = jnp.broadcast_to(c_mat[:, :, None], c_ref.shape)

    size = softplus(
        jnp.dot(low_ref[...], proj_ref[...], preferred_element_type=jnp.float32) + bias_ref[...]
    )
    size_ref[...] = size
    drive_ref[...] = size * x_ref[...].astype(jnp.float32)
    rates = rate_ref[...]

    def step(block, state):
        start = pl.multiple_of(block * 8, 8)
        sizes = size_ref[pl.ds(start, 8), :]
        drives = drive_ref[pl.ds(start, 8), :]
        state = list(state)
        for i in range(8):
            b_now = b_ref[start + i]
            for g in range(groups):
                lanes = slice(g * 128, g * 128 + 128)
                decay = jnp.exp2(sizes[i : i + 1, lanes] * rates[:, lanes])
                state[g] = decay * state[g] + drives[i : i + 1, lanes] * b_now
        return tuple(state)

    zero = jnp.zeros((states, 128), jnp.float32)
    state = lax.fori_loop(0, rows // 8, step, (zero,) * groups)
    total = jnp.sum(size, axis=0, keepdims=True)
    high = total.astype(jnp.bfloat16).astype(jnp.float32)
    low = total - high
    rest = info_ref[: load_ref.shape[0] - states - 2, :]
    load_ref[...] = jnp.concatenate(
        [jnp.concatenate(state, axis=1), high, low, rest], axis=0
    ).astype(jnp.bfloat16)


def scan_ends(partials, dt_proj, dt_bias, rates, xconv, info):
    rows, channels = xconv.shape
    states = rates.shape[0]
    width = tile_of(channels, 1024)
    load_rows = -(-(states + 2) // 8) * 8
    wide = jax.ShapeDtypeStruct((rows, states, 128), jnp.float32)
    return pl.pallas_call(
        functools.partial(ends_kernel, len(partials)),
        grid=(channels // width,),
        in_specs=[
            *[whole_vmem() for _ in partials],
            pl.BlockSpec((dt_proj.shape[0], width), lambda i: (0, i)),
            pl.BlockSpec((1, width), lambda i: (0, i)),
            pl.BlockSpec((states, width), lambda i: (0, i)),
            pl.BlockSpec((rows, width), lambda i: (0, i)),
            pl.BlockSpec((info.shape[0], width), lambda i: (0, i)),
        ],
        out_specs=[
            pl.BlockSpec((rows, width), lambda i: (0, i)),
            pl.BlockSpec((load_rows, width), lambda i: (0, i)),
            pl.BlockSpec(wide.shape, lambda i: (0, 0, 0)),
            pl.BlockSpec(wide.shape, lambda i: (0, 0, 0)),
        ],
        out_shape=[
            jax.ShapeDtypeStruct((rows, channels), jnp.float32),
            jax.ShapeDtypeStruct((load_rows, channels), jnp.bfloat16),
            wide,
            wide,
        ],
        scratch_shapes=[
            pltpu.VMEM((rows, dt_proj.shape[0]), jnp.bfloat16),
            pltpu.VMEM((rows, width), jnp.float32),
        ],
        name="scan_ends",
    )(*partials, dt_proj, dt_bias, rates, xconv, info)


def mix_kernel(z_count, x_count, z_place, x_place, *refs):
    count = z_count * x_count
    loads = refs[:count]
    size_ref, x_ref, z_ref, b_ref, c_ref, rate_ref, skip_ref, out_ref = refs[count : count + 8]
    drive_ref, y_ref, load_ref = refs[count + 8 :]
    across = lanes_of(x_ref.shape[1])
    for k in range(count):
        z_from = lax.rem(z_place[0] + k // x_count, z_count)
        x_from = lax.rem(x_place[0] + k % x_count, x_count)
        load_ref[z_from * x_count + x_from] = loads[k][:, across].astype(jnp.float32)
    rows, width = x_ref.shape
    states = rate_ref.shape[0]
    groups = width // 128
    rates = rate_ref[...]
    x_f = x_ref[...].astype(jnp.float32)
    drive_ref[...] = size_ref[...] * x_f

    def earlier(j, state):
        block = load_ref[j]
        total = block[states : states + 1] + block[states + 1 : states + 2]
        return jnp.exp2(total * rates) * state + block[:states]

    place = z_place[0] * x_count + x_place[0]
    incoming = lax.fori_loop(0, place, earlier, jnp.zeros((states, width), jnp.float32))

    def step(block, state):
        start = pl.multiple_of(block * 8, 8)
        sizes = size_ref[pl.ds(start, 8), :]
        drives = drive_ref[pl.ds(start, 8), :]
        state = list(state)
        outs = [[None] * 8 for _ in range(groups)]
        for i in range(8):
            b_now = b_ref[start + i]
            c_now = c_ref[start + i]
            for g in range(groups):
                lanes = slice(g * 128, g * 128 + 128)
                decay = jnp.exp2(sizes[i : i + 1, lanes] * rates[:, lanes])
                state[g] = decay * state[g] + drives[i : i + 1, lanes] * b_now
                outs[g][i] = jnp.sum(state[g] * c_now, axis=0, keepdims=True)
        for g in range(groups):
            y_ref[pl.ds(start, 8), g * 128 : g * 128 + 128] = jnp.concatenate(outs[g], axis=0)
        return tuple(state)

    start_state = tuple(incoming[:, g * 128 : g * 128 + 128] for g in range(groups))
    lax.fori_loop(0, rows // 8, step, start_state)
    z_f = z_ref[...].astype(jnp.float32)
    scanned = y_ref[...] + skip_ref[...] * x_f
    out_ref[...] = (scanned * (z_f / (1.0 + jnp.exp(-z_f)))).astype(jnp.bfloat16)


def scan_mix(z_at, x_at, loads, step_size, xconv, z_in, b_wide, c_wide, rates, d_skip):
    rows, channels = xconv.shape
    states = rates.shape[0]
    width = tile_of(channels, 1024)
    flat = [load for pair in loads for load in pair]

    def by_lane(depth):
        return pl.BlockSpec((depth, width), lambda i: (0, i))

    return pl.pallas_call(
        functools.partial(mix_kernel, len(loads), len(loads[0])),
        grid=(channels // width,),
        in_specs=[
            whole_smem(),
            whole_smem(),
            *[whole_vmem() for _ in flat],
            by_lane(rows),
            by_lane(rows),
            by_lane(rows),
            pl.BlockSpec(b_wide.shape, lambda i: (0, 0, 0)),
            pl.BlockSpec(c_wide.shape, lambda i: (0, 0, 0)),
            by_lane(states),
            by_lane(1),
        ],
        out_specs=by_lane(rows),
        out_shape=jax.ShapeDtypeStruct((rows, channels), jnp.bfloat16),
        scratch_shapes=[pltpu.VMEM((rows, width), jnp.float32)] * 2
        + [pltpu.VMEM((len(flat), flat[0].shape[0], width), jnp.float32)],
        name="scan_mix",
    )(z_at, x_at, *flat, step_size, xconv, z_in, b_wide, c_wide, rates, d_skip)


def out_kernel(z_count, counts, z_ref, x_ref, e_ref, keep_pick_ref, send_pick_ref, resid_ref, *refs):
    x_count = len(counts)
    blocks = refs[:z_count]
    keep_ref, send_ref, held_ref, sum_ref = refs[z_count + sum(counts) :]
    weights = list(refs[z_count : z_count + sum(counts)])
    rows = blocks[0].shape[0]
    columns = weights[0].shape[1]
    for r in range(z_count):
        at = pl.multiple_of(lax.rem(z_ref[0] + r, z_count) * rows, rows)
        held_ref[pl.ds(at, rows), :] = blocks[r][...]
    own = pl.ds(pl.multiple_of(e_ref[0] * rows, rows), rows)
    for i, count in enumerate(counts):
        at = pl.ds(pl.multiple_of(lax.rem(x_ref[0] + i, x_count) * columns, columns), columns)
        start, parts = 0, []
        for _ in range(count):
            weight = weights.pop(0)
            depth = weight.shape[0]
            parts.append(
                jnp.dot(
                    held_ref[:, start : start + depth],
                    weight[...],
                    preferred_element_type=jnp.float32,
                )
            )
            start += depth
        sum_ref[...] = functools.reduce(jnp.add, parts)
        sum_ref[own, :] += resid_ref[:, at].astype(jnp.float32)
        summed = sum_ref[...].astype(jnp.bfloat16)
        for pick_ref, out_ref in ((keep_pick_ref, keep_ref), (send_pick_ref, send_ref)):
            out_ref[:, at] = jnp.dot(
                pick_ref[...], summed, preferred_element_type=jnp.float32
            ).astype(jnp.bfloat16)


def out_product(z_at, x_at, e_at, keep_pick, send_pick, resid, blocks, weights):
    rows, depth = blocks[0].shape
    z_count, x_count = len(blocks), len(weights)
    counts = [len(parts) for parts in weights]
    columns = weights[0][0].shape[1]
    return pl.pallas_call(
        functools.partial(out_kernel, z_count, counts),
        in_specs=[whole_smem()] * 3 + [whole_vmem()] * (3 + z_count + sum(counts)),
        out_specs=[whole_vmem()] * 2,
        out_shape=[jax.ShapeDtypeStruct((keep_pick.shape[0], x_count * columns), jnp.bfloat16)] * 2,
        scratch_shapes=[
            pltpu.VMEM((z_count * rows, depth), jnp.bfloat16),
            pltpu.VMEM((z_count * rows, columns), jnp.float32),
        ],
        compiler_params=pltpu.CompilerParams(vmem_limit_bytes=16 * MIB),
        name="out_product",
    )(
        z_at,
        x_at,
        e_at,
        keep_pick,
        send_pick,
        resid,
        *blocks,
        *[part for parts in weights for part in parts],
    )


def hidden_kernel(z_count, x_count, z_ref, x_ref, *refs):
    count = z_count * x_count
    chunks = refs[:count]
    gain_ref, gate_ref, up_ref, act_ref, scaled_ref = refs[count:]
    rows, depth = chunks[0].shape
    padded = scaled_ref.shape[0] // x_count

    def filled(chunk):
        h = chunk[...].astype(jnp.float32)
        if padded == rows:
            return h
        return jnp.concatenate([h, jnp.zeros((padded - rows, depth), jnp.float32)], axis=0)

    @pl.when(pl.program_id(0) == 0)
    def _():
        for i in range(x_count):
            own = [chunks[r * x_count + i] for r in range(z_count)]
            squares = jnp.zeros((padded, 1), jnp.float32)
            for chunk in own:
                h = filled(chunk)
                squares = squares + jnp.sum(h * h, axis=1, keepdims=True)
            scale = lax.rsqrt(squares / (depth * z_count) + eps)
            down = pl.multiple_of(lax.rem(x_ref[0] + i, x_count) * padded, padded)
            for r, chunk in enumerate(own):
                z_at = lax.rem(z_ref[0] + r, z_count)
                across = pl.multiple_of(z_at * depth, depth)
                h = filled(chunk)
                scaled_ref[pl.ds(down, padded), pl.ds(across, depth)] = (
                    h * scale * gain_ref[z_at]
                ).astype(jnp.bfloat16)

    scaled = scaled_ref[...]
    gate = jnp.dot(scaled, gate_ref[0], preferred_element_type=jnp.float32)
    upper = jnp.dot(scaled, up_ref[0], preferred_element_type=jnp.float32)
    act_ref[...] = (gate / (1.0 + jnp.exp(-gate)) * upper).astype(jnp.bfloat16)


def expert_hidden(z_at, x_at, chunks, gain, w_gate, w_up):
    z_count, x_count = len(chunks), len(chunks[0])
    rows, depth = chunks[0][0].shape
    columns = w_gate.shape[2]
    width = tile_of(columns, 256)
    padded = -(-rows // 16) * 16 * x_count
    gain = gain.reshape(z_count, 1, depth)
    weight_spec = pl.BlockSpec((1, depth * z_count, width), lambda n: (0, 0, n))
    return pl.pallas_call(
        functools.partial(hidden_kernel, z_count, x_count),
        grid=(columns // width,),
        in_specs=[whole_smem()] * 2
        + [whole_vmem()] * (z_count * x_count + 1)
        + [weight_spec, weight_spec],
        out_specs=pl.BlockSpec((padded, width), lambda n: (0, n)),
        out_shape=jax.ShapeDtypeStruct((padded, columns), jnp.bfloat16),
        scratch_shapes=[pltpu.VMEM((padded, depth * z_count), jnp.bfloat16)],
        compiler_params=pltpu.CompilerParams(vmem_limit_bytes=50 * MIB),
        name="expert_hidden",
    )(z_at, x_at, *[chunk for pair in chunks for chunk in pair], gain, w_gate, w_up)


def down_kernel(x_count, x_ref, blocks_ref, act_ref, weight_ref, *refs):
    outs, held_ref = refs[:-1], refs[-1]
    held_ref[...] = jnp.dot(act_ref[...], weight_ref[0], preferred_element_type=jnp.float32)
    rows = outs[0].shape[0]
    padded = held_ref.shape[0] // x_count
    for k in range(len(outs) // x_count):

        @pl.when(pl.program_id(0) == k)
        def _(k=k):
            for i in range(x_count):
                start = pl.multiple_of(lax.rem(x_ref[0] + i, x_count) * padded, padded)
                outs[k * x_count + i][...] = held_ref[pl.ds(start, rows), :].astype(jnp.bfloat16)


def expert_down(x_at, blocks, x_count, z_count, rows, act, w_down):
    padded, depth = act.shape
    columns = w_down.shape[2] // z_count
    width = tile_of(columns)
    tiles = columns // width
    count = blocks.shape[0]

    def out_spec(k):
        def place(m, n, x, blocks):
            return (0, jnp.where(m == k, n, jnp.where(m < k, 0, tiles - 1)))

        return pl.BlockSpec((rows, width), place)

    outs = pl.pallas_call(
        functools.partial(down_kernel, x_count),
        grid_spec=pltpu.PrefetchScalarGridSpec(
            num_scalar_prefetch=2,
            grid=(count, tiles),
            in_specs=[
                pl.BlockSpec((padded, depth), lambda m, n, x, blocks: (0, 0)),
                pl.BlockSpec(
                    (1, depth, width), lambda m, n, x, blocks: (0, 0, blocks[m] * tiles + n)
                ),
            ],
            out_specs=[out_spec(k) for k in range(count) for _ in range(x_count)],
            scratch_shapes=[pltpu.VMEM((padded, width), jnp.float32)],
        ),
        out_shape=[jax.ShapeDtypeStruct((rows, columns), jnp.bfloat16)] * (count * x_count),
        compiler_params=pltpu.CompilerParams(vmem_limit_bytes=50 * MIB),
        name="expert_down",
    )(x_at, blocks, act, w_down)
    return [outs[k * x_count : (k + 1) * x_count] for k in range(count)]


def per_device(
    x_in,
    z_in,
    conv_weight,
    conv_bias,
    x_proj,
    dt_proj,
    dt_bias,
    a_log,
    d_skip,
    out_proj,
    resid,
    norm_gain,
    routes,
    route_gate,
    w_gate,
    w_up,
    w_down,
):
    row_count, channels = x_in.shape
    seq_count = lax.axis_size("seq")
    exp_count = lax.axis_size("exp")
    x_count = seq_count // exp_count
    z_count = exp_count
    seq_at = lax.axis_index("seq")
    exp_at = lax.axis_index("exp")
    z_at, x_at = seq_at // x_count, seq_at % x_count
    z_one = z_at.reshape(1).astype(jnp.int32)
    x_one = x_at.reshape(1).astype(jnp.int32)
    e_one = exp_at.reshape(1).astype(jnp.int32)
    top_count = routes.shape[1]
    capacity = row_count * top_count * 17 // (16 * exp_count)
    pitch = capacity
    feature_slice = resid.shape[1]

    def from_z(block, r):
        pairs = [
            (((z + r) % z_count) * x_count + x, z * x_count + x)
            for z in range(z_count)
            for x in range(x_count)
        ]
        return lax.ppermute(block, "seq", pairs)

    def from_x(block, i):
        pairs = [
            (z * x_count + (x + i) % x_count, z * x_count + x)
            for z in range(z_count)
            for x in range(x_count)
        ]
        return lax.ppermute(block, "seq", pairs)

    turns = sorted(range(1, z_count), key=lambda r: min(r, z_count - r))

    def gathered(block):
        rows = {(0, 0): block}
        others = range(1, x_count)
        for i in others:
            rows[0, i] = from_x(block, i)
        sent = block
        for k, r in enumerate(turns):
            if k >= 2:
                sent = after(sent, rows[turns[k - 2], 0], *[rows[0, i] for i in others])
            rows[r, 0] = from_z(sent, r)
        for k, r in enumerate(turns):
            earlier = turns[max(k - 2, 0) : max(k - 1, 0)] if r != turns[-1] else turns[:k]
            forward = after(rows[r, 0], *[rows[q, i] for q in earlier for i in others])
            for i in others:
                rows[r, i] = from_x(forward, i)
        return [[rows[r, i] for i in range(x_count)] for r in range(z_count)]

    y_count = exp_count // 2

    def other_core(block):
        return lax.ppermute(block, "exp", [(e ^ 1, e) for e in range(exp_count)])

    def from_y(block, r):
        pairs = [
            ((y + r) % y_count * 2 + core, y * 2 + core)
            for y in range(y_count)
            for core in range(2)
        ]
        return lax.ppermute(block, "exp", pairs)

    swap = [
        ((e * x_count + x) * exp_count + z, (z * x_count + x) * exp_count + e)
        for z in range(z_count)
        for x in range(x_count)
        for e in range(exp_count)
    ]

    halo = lax.ppermute(
        x_in[row_count - 8 :], "seq", [(i, i + 1) for i in range(seq_count - 1)]
    )

    xconv, partial = conv_and_project(x_in, halo, conv_weight, conv_bias[None], x_proj.T)
    resid_here = lax.ppermute(resid, ("seq", "exp"), swap)

    chip_sum = partial + other_core(after(partial, resid_here))
    a_log, routes, route_gate = lax.optimization_barrier(
        (a_log, routes, route_gate, chip_sum)
    )[:3]
    rates = -jnp.exp(a_log.T) * LOG2E

    def part_of(v):
        return v.astype(jnp.bfloat16).astype(jnp.float32)

    gate_high = part_of(route_gate)
    gate_mid = part_of(route_gate - gate_high)
    gate_low = route_gate - gate_high - gate_mid
    info = jnp.stack([routes.astype(jnp.float32), gate_high, gate_mid, gate_low])
    info = info.transpose(0, 2, 1).reshape(4, top_count * row_count)
    info = jnp.pad(info, ((0, 4), (0, channels - top_count * row_count)))

    def slots_of(named):
        flat = named.reshape(-1, row_count * top_count)
        onehot = (flat[:, :, None] == jnp.arange(exp_count, dtype=jnp.int32)).astype(jnp.float32)
        below = jnp.tril(jnp.ones((row_count * top_count,) * 2, jnp.float32), -1)
        counts = jnp.einsum("ij,bje->bie", below, onehot)
        slots = jnp.sum(counts * onehot, axis=2).astype(jnp.int32)
        return slots.reshape(-1, row_count, top_count)

    own_target = (routes - z_at) % exp_count * pitch + slots_of(routes)[0]
    slot_ids = jnp.arange(exp_count * pitch, dtype=jnp.int32)
    choose = jnp.sum(
        (own_target[:, :, None] == slot_ids[None, None, :]).astype(jnp.float32), axis=1
    ).astype(jnp.bfloat16)

    cut = channels * 5 // 16
    uppers = [from_x(after(out_proj, halo)[:cut], i) for i in range(1, x_count)]
    partials = [chip_sum] + [from_y(chip_sum, r) for r in range(1, y_count)]
    step_size, load, b_wide, c_wide = scan_ends(partials, dt_proj, dt_bias[None], rates, xconv, info)
    loads = gathered(after(load, resid_here, *uppers))
    held_proj = after(out_proj, *[part for pair in loads for part in pair])
    lowers = [from_x(held_proj[cut:], i) for i in range(1, x_count)]
    columns = [[out_proj]] + [list(pair) for pair in zip(uppers, lowers)]
    mixed = scan_mix(
        z_one, x_one, loads, step_size, xconv, z_in, b_wide, c_wide, rates, d_skip[None]
    )
    along_z = [mixed] + [from_z(mixed, r) for r in range(1, z_count)]

    first_row = a_log.shape[1] + 2
    spare = after(jnp.stack([loads[r][0][first_row:] for r in range(z_count)]), mixed)
    spare = spare[:, :4, : top_count * row_count].astype(jnp.float32)
    spare = lax.dynamic_slice_in_dim(
        jnp.concatenate([spare, spare]), (z_count - z_at) % z_count, z_count, 0
    ).reshape(z_count, 4, top_count, row_count)
    all_routes = spare[:, 0].transpose(0, 2, 1).astype(jnp.int32)
    all_gates = (spare[:, 1] + spare[:, 2] + spare[:, 3]).transpose(0, 2, 1)
    z_ids = jnp.arange(z_count, dtype=jnp.int32)[:, None, None]
    target = (all_routes * z_count + z_ids) * pitch + slots_of(all_routes)
    target = target.reshape(z_count * row_count, top_count)
    count = z_count * pitch
    exp_late = after(exp_at, mixed)
    y_at, core_at = exp_late // 2, exp_late % 2

    def picked(core):
        experts = (y_at + jnp.arange(y_count, dtype=jnp.int32)) % y_count * 2 + core
        ids = experts[:, None] * count + jnp.arange(count, dtype=jnp.int32)[None, :]
        same = target[None, :, :] == ids.reshape(-1)[:, None, None]
        return jnp.sum(same.astype(jnp.float32), axis=2).astype(jnp.bfloat16)

    here_ids = exp_at * z_count * pitch + jnp.arange(z_count * pitch, dtype=jnp.int32)
    here = target[None, :, :] == here_ids[:, None, None]
    gate_here = jnp.sum(
        jnp.where(here, all_gates.reshape(1, z_count * row_count, top_count), 0.0), axis=(1, 2)
    )[:, None]
    first_here = jnp.sum(here[:, :, 0].astype(jnp.float32), axis=1)[:, None]

    keep, send = out_product(
        z_one, x_one, e_one, picked(core_at), picked(1 - core_at), resid_here, along_z, columns
    )
    over_chip = keep.astype(jnp.float32) + other_core(send).astype(jnp.float32)
    over_chip = over_chip.reshape(y_count, count, feature_slice)
    rows_here = over_chip[0]
    for r in range(1, y_count):
        arrived = from_y(over_chip[r].astype(jnp.bfloat16), y_count - r)
        rows_here = rows_here + arrived.astype(jnp.float32)
    rows_here = rows_here.astype(jnp.bfloat16)

    chunks = gathered(rows_here)
    act = expert_hidden(z_one, x_one, chunks, norm_gain, w_gate, w_up)

    by_distance = sorted(range(1, z_count), key=lambda r: abs(r - z_count // 2)) + [0]
    down, crossed, arrivals = {}, {}, []

    def products(turns_now, rows):
        blocks = jnp.stack([(z_at + r) % z_count for r in turns_now]).astype(jnp.int32)
        outs = expert_down(x_one, blocks, x_count, z_count, exp_count * pitch, rows, w_down)
        down.update(zip(turns_now, outs))

    def over_x(r):
        return functools.reduce(
            jnp.add, [p.astype(jnp.float32) for p in [down[r][0]] + crossed[r]]
        )

    products(by_distance[:1], act)
    products(by_distance[1:], act)
    for k, r in enumerate(by_distance):
        pieces = down[r][1:]
        if r == 0:
            pieces = [after(piece, arrivals[0]) for piece in pieces]
        elif k >= 2:
            pieces = [after(piece, *crossed[by_distance[k - 2]]) for piece in pieces]
        crossed[r] = [from_x(piece, x_count - i) for i, piece in enumerate(pieces, 1)]
        if r:
            arrivals.append(from_z(over_x(r).astype(jnp.bfloat16), z_count - r))
    total = over_x(0)
    for sent in arrivals:
        total = total + sent.astype(jnp.float32)
    expert_out = total.astype(jnp.bfloat16).astype(jnp.float32)
    expert_out = gate_here * expert_out + first_here * rows_here.astype(jnp.float32)
    expert_out = expert_out.astype(jnp.bfloat16)
    pieces = expert_out.reshape(exp_count, pitch, feature_slice)
    back = []
    for k in range(exp_count):
        piece = lax.dynamic_index_in_dim(pieces, (exp_at - k) % exp_count, 0, keepdims=False)
        pairs = [
            (
                (e * x_count + x) * exp_count + (z + k) % exp_count,
                (z * x_count + x) * exp_count + e,
            )
            for z in range(z_count)
            for x in range(x_count)
            for e in range(exp_count)
        ]
        back.append(lax.ppermute(piece, ("seq", "exp"), pairs))
    back = jnp.concatenate(back, axis=0)
    return jnp.dot(choose, back, preferred_element_type=jnp.float32).astype(jnp.bfloat16)


def solution(mesh):
    return jax.shard_map(
        per_device,
        mesh=mesh,
        in_specs=(
            P("seq", "exp"),
            P("seq", "exp"),
            P(None, "exp"),
            P("exp"),
            P("exp", None),
            P(None, "exp"),
            P("exp"),
            P("exp", None),
            P("exp"),
            P("exp", "seq"),
            P("seq", "exp"),
            P(),
            P("seq", None),
            P("seq", None),
            P("exp", None, "seq"),
            P("exp", None, "seq"),
            P("exp", "seq", None),
        ),
        out_specs=P("seq", "exp"),
        check_vma=False,
    )
```

```python
import functools
import math

import jax
import jax.numpy as jnp
from jax import lax
from jax.experimental import pallas as pl
from jax.experimental.pallas import tpu as pltpu
from jax.sharding import PartitionSpec as P

eps = 1e-05
LOG2E = 1.4426950408889634
MIB = 1 << 20


def tile_of(size, most=512):
    return max(t for t in range(128, most + 1, 128) if size % t == 0)


def after(value, *others):
    return lax.optimization_barrier((value, *others))[0]


def whole_vmem():
    return pl.BlockSpec(memory_space=pltpu.VMEM)


def lanes_of(width):
    return pl.ds(pl.multiple_of(pl.program_id(0) * width, width), width)


def whole_smem():
    return pl.BlockSpec(memory_space=pltpu.SMEM)


def conv_kernel(x_ref, halo_ref, weight_ref, bias_ref, proj_ref, xconv_ref, partial_ref):
    rows = x_ref.shape[0]
    taps = weight_ref.shape[0]
    across = lanes_of(x_ref.shape[1])
    extended = jnp.concatenate(
        [halo_ref[:, across].astype(jnp.float32), x_ref[...].astype(jnp.float32)], axis=0
    )
    pad = halo_ref.shape[0]
    conv = jnp.zeros(x_ref.shape, jnp.float32) + bias_ref[...]
    for tap in range(taps):
        start = pad - (taps - 1) + tap
        conv = conv + weight_ref[tap : tap + 1, :] * extended[start : start + rows]
    xconv = (conv / (1.0 + jnp.exp(-conv))).astype(jnp.bfloat16)
    xconv_ref[...] = xconv

    @pl.when(pl.program_id(0) == 0)
    def _():
        partial_ref[...] = jnp.zeros_like(partial_ref)

    partial_ref[...] += lax.dot_general(
        xconv, proj_ref[...], (((1,), (1,)), ((), ())), preferred_element_type=jnp.float32
    )


def conv_and_project(x_in, halo, conv_weight, conv_bias, x_proj_t):
    rows, channels = x_in.shape
    width = tile_of(channels, 1024)
    columns = x_proj_t.shape[0]
    return pl.pallas_call(
        conv_kernel,
        grid=(channels // width,),
        in_specs=[
            pl.BlockSpec((rows, width), lambda i: (0, i)),
            whole_vmem(),
            pl.BlockSpec((conv_weight.shape[0], width), lambda i: (0, i)),
            pl.BlockSpec((1, width), lambda i: (0, i)),
            pl.BlockSpec((columns, width), lambda i: (0, i)),
        ],
        out_specs=[
            pl.BlockSpec((rows, width), lambda i: (0, i)),
            pl.BlockSpec((rows, columns), lambda i: (0, 0)),
        ],
        out_shape=[
            jax.ShapeDtypeStruct((rows, channels), jnp.bfloat16),
            jax.ShapeDtypeStruct((rows, columns), jnp.float32),
        ],
        name="conv_project",
    )(x_in, halo, conv_weight, conv_bias, x_proj_t)


def softplus(v):
    return jnp.maximum(v, 0.0) + jnp.log1p(jnp.exp(-jnp.abs(v)))


def ends_kernel(count, *refs):
    parts = refs[:count]
    proj_ref, bias_ref, rate_ref, x_ref, info_ref = refs[count : count + 5]
    size_ref, load_ref, b_ref, c_ref, low_ref, drive_ref = refs[count + 5 :]
    rows, width = x_ref.shape
    states = rate_ref.shape[0]
    low_rank = low_ref.shape[1]
    groups = width // 128

    @pl.when(pl.program_id(0) == 0)
    def _():
        total = parts[0][...]
        for part in parts[1:]:
            total = total + part[...]
        low_ref[...] = total[:, :low_rank].astype(jnp.bfloat16)
        b_mat = total[:, low_rank : low_rank + states]
        c_mat = total[:, low_rank + states : low_rank + 2 * states]
        b_ref[...] = jnp.broadcast_to(b_mat[:, :, None], b_ref.shape)
        c_ref[...] = jnp.broadcast_to(c_mat[:, :, None], c_ref.shape)

    size = softplus(
        jnp.dot(low_ref[...], proj_ref[...], preferred_element_type=jnp.float32) + bias_ref[...]
    )
    size_ref[...] = size
    drive_ref[...] = size * x_ref[...].astype(jnp.float32)
    rates = rate_ref[...]

    def step(block, state):
        start = pl.multiple_of(block * 8, 8)
        sizes = size_ref[pl.ds(start, 8), :]
        drives = drive_ref[pl.ds(start, 8), :]
        state = list(state)
        for i in range(8):
            b_now = b_ref[start + i]
            for g in range(groups):
                lanes = slice(g * 128, g * 128 + 128)
                decay = jnp.exp2(sizes[i : i + 1, lanes] * rates[:, lanes])
                state[g] = decay * state[g] + drives[i : i + 1, lanes] * b_now
        return tuple(state)

    zero = jnp.zeros((states, 128), jnp.float32)
    state = lax.fori_loop(0, rows // 8, step, (zero,) * groups)
    total = jnp.sum(size, axis=0, keepdims=True)
    high = total.astype(jnp.bfloat16).astype(jnp.float32)
    low = total - high
    rest = info_ref[: load_ref.shape[0] - states - 2, :]
    load_ref[...] = jnp.concatenate(
        [jnp.concatenate(state, axis=1), high, low, rest], axis=0
    ).astype(jnp.bfloat16)


def scan_ends(partials, dt_proj, dt_bias, rates, xconv, info):
    rows, channels = xconv.shape
    states = rates.shape[0]
    width = tile_of(channels, 1024)
    load_rows = -(-(states + 2) // 8) * 8
    wide = jax.ShapeDtypeStruct((rows, states, 128), jnp.float32)
    return pl.pallas_call(
        functools.partial(ends_kernel, len(partials)),
        grid=(channels // width,),
        in_specs=[
            *[whole_vmem() for _ in partials],
            pl.BlockSpec((dt_proj.shape[0], width), lambda i: (0, i)),
            pl.BlockSpec((1, width), lambda i: (0, i)),
            pl.BlockSpec((states, width), lambda i: (0, i)),
            pl.BlockSpec((rows, width), lambda i: (0, i)),
            pl.BlockSpec((info.shape[0], width), lambda i: (0, i)),
        ],
        out_specs=[
            pl.BlockSpec((rows, width), lambda i: (0, i)),
            pl.BlockSpec((load_rows, width), lambda i: (0, i)),
            pl.BlockSpec(wide.shape, lambda i: (0, 0, 0)),
            pl.BlockSpec(wide.shape, lambda i: (0, 0, 0)),
        ],
        out_shape=[
            jax.ShapeDtypeStruct((rows, channels), jnp.float32),
            jax.ShapeDtypeStruct((load_rows, channels), jnp.bfloat16),
            wide,
            wide,
        ],
        scratch_shapes=[
            pltpu.VMEM((rows, dt_proj.shape[0]), jnp.bfloat16),
            pltpu.VMEM((rows, width), jnp.float32),
        ],
        name="scan_ends",
    )(*partials, dt_proj, dt_bias, rates, xconv, info)


def mix_kernel(z_count, x_count, z_place, x_place, *refs):
    count = z_count * x_count
    loads = refs[:count]
    size_ref, x_ref, z_ref, b_ref, c_ref, rate_ref, skip_ref, out_ref = refs[count : count + 8]
    drive_ref, y_ref, load_ref = refs[count + 8 :]
    across = lanes_of(x_ref.shape[1])
    for k in range(count):
        z_from = lax.rem(z_place[0] + k // x_count, z_count)
        x_from = lax.rem(x_place[0] + k % x_count, x_count)
        load_ref[z_from * x_count + x_from] = loads[k][:, across].astype(jnp.float32)
    rows, width = x_ref.shape
    states = rate_ref.shape[0]
    groups = width // 128
    rates = rate_ref[...]
    x_f = x_ref[...].astype(jnp.float32)
    drive_ref[...] = size_ref[...] * x_f

    def earlier(j, state):
        block = load_ref[j]
        total = block[states : states + 1] + block[states + 1 : states + 2]
        return jnp.exp2(total * rates) * state + block[:states]

    place = z_place[0] * x_count + x_place[0]
    incoming = lax.fori_loop(0, place, earlier, jnp.zeros((states, width), jnp.float32))

    def step(block, state):
        start = pl.multiple_of(block * 8, 8)
        sizes = size_ref[pl.ds(start, 8), :]
        drives = drive_ref[pl.ds(start, 8), :]
        state = list(state)
        outs = [[None] * 8 for _ in range(groups)]
        for i in range(8):
            b_now = b_ref[start + i]
            c_now = c_ref[start + i]
            for g in range(groups):
                lanes = slice(g * 128, g * 128 + 128)
                decay = jnp.exp2(sizes[i : i + 1, lanes] * rates[:, lanes])
                state[g] = decay * state[g] + drives[i : i + 1, lanes] * b_now
                outs[g][i] = jnp.sum(state[g] * c_now, axis=0, keepdims=True)
        for g in range(groups):
            y_ref[pl.ds(start, 8), g * 128 : g * 128 + 128] = jnp.concatenate(outs[g], axis=0)
        return tuple(state)

    start_state = tuple(incoming[:, g * 128 : g * 128 + 128] for g in range(groups))
    lax.fori_loop(0, rows // 8, step, start_state)
    z_f = z_ref[...].astype(jnp.float32)
    scanned = y_ref[...] + skip_ref[...] * x_f
    out_ref[...] = (scanned * (z_f / (1.0 + jnp.exp(-z_f)))).astype(jnp.bfloat16)


def scan_mix(z_at, x_at, loads, step_size, xconv, z_in, b_wide, c_wide, rates, d_skip):
    rows, channels = xconv.shape
    states = rates.shape[0]
    width = tile_of(channels, 1024)
    flat = [load for pair in loads for load in pair]

    def by_lane(depth):
        return pl.BlockSpec((depth, width), lambda i: (0, i))

    return pl.pallas_call(
        functools.partial(mix_kernel, len(loads), len(loads[0])),
        grid=(channels // width,),
        in_specs=[
            whole_smem(),
            whole_smem(),
            *[whole_vmem() for _ in flat],
            by_lane(rows),
            by_lane(rows),
            by_lane(rows),
            pl.BlockSpec(b_wide.shape, lambda i: (0, 0, 0)),
            pl.BlockSpec(c_wide.shape, lambda i: (0, 0, 0)),
            by_lane(states),
            by_lane(1),
        ],
        out_specs=by_lane(rows),
        out_shape=jax.ShapeDtypeStruct((rows, channels), jnp.bfloat16),
        scratch_shapes=[pltpu.VMEM((rows, width), jnp.float32)] * 2
        + [pltpu.VMEM((len(flat), flat[0].shape[0], width), jnp.float32)],
        name="scan_mix",
    )(z_at, x_at, *flat, step_size, xconv, z_in, b_wide, c_wide, rates, d_skip)


def out_kernel(z_count, counts, z_ref, x_ref, e_ref, keep_pick_ref, send_pick_ref, resid_ref, *refs):
    x_count = len(counts)
    blocks = refs[:z_count]
    keep_ref, send_ref, held_ref, sum_ref = refs[z_count + sum(counts) :]
    weights = list(refs[z_count : z_count + sum(counts)])
    rows = blocks[0].shape[0]
    columns = weights[0].shape[1]
    for r in range(z_count):
        at = pl.multiple_of(lax.rem(z_ref[0] + r, z_count) * rows, rows)
        held_ref[pl.ds(at, rows), :] = blocks[r][...]
    own = pl.ds(pl.multiple_of(e_ref[0] * rows, rows), rows)
    for i, count in enumerate(counts):
        at = pl.ds(pl.multiple_of(lax.rem(x_ref[0] + i, x_count) * columns, columns), columns)
        start, parts = 0, []
        for _ in range(count):
            weight = weights.pop(0)
            depth = weight.shape[0]
            parts.append(
                jnp.dot(
                    held_ref[:, start : start + depth],
                    weight[...],
                    preferred_element_type=jnp.float32,
                )
            )
            start += depth
        sum_ref[...] = functools.reduce(jnp.add, parts)
        sum_ref[own, :] += resid_ref[:, at].astype(jnp.float32)
        summed = sum_ref[...].astype(jnp.bfloat16)
        for pick_ref, out_ref in ((keep_pick_ref, keep_ref), (send_pick_ref, send_ref)):
            out_ref[:, at] = jnp.dot(
                pick_ref[...], summed, preferred_element_type=jnp.float32
            ).astype(jnp.bfloat16)


def out_product(z_at, x_at, e_at, keep_pick, send_pick, resid, blocks, weights):
    rows, depth = blocks[0].shape
    z_count, x_count = len(blocks), len(weights)
    counts = [len(parts) for parts in weights]
    columns = weights[0][0].shape[1]
    return pl.pallas_call(
        functools.partial(out_kernel, z_count, counts),
        in_specs=[whole_smem()] * 3 + [whole_vmem()] * (3 + z_count + sum(counts)),
        out_specs=[whole_vmem()] * 2,
        out_shape=[jax.ShapeDtypeStruct((keep_pick.shape[0], x_count * columns), jnp.bfloat16)] * 2,
        scratch_shapes=[
            pltpu.VMEM((z_count * rows, depth), jnp.bfloat16),
            pltpu.VMEM((z_count * rows, columns), jnp.float32),
        ],
        compiler_params=pltpu.CompilerParams(vmem_limit_bytes=16 * MIB),
        name="out_product",
    )(
        z_at,
        x_at,
        e_at,
        keep_pick,
        send_pick,
        resid,
        *blocks,
        *[part for parts in weights for part in parts],
    )


def hidden_kernel(z_count, x_count, z_ref, x_ref, *refs):
    count = z_count * x_count
    chunks = refs[:count]
    gain_ref, gate_ref, up_ref, act_ref, scaled_ref = refs[count:]
    rows, depth = chunks[0].shape
    padded = scaled_ref.shape[0] // x_count

    def filled(chunk):
        h = chunk[...].astype(jnp.float32)
        if padded == rows:
            return h
        return jnp.concatenate([h, jnp.zeros((padded - rows, depth), jnp.float32)], axis=0)

    @pl.when(pl.program_id(0) == 0)
    def _():
        for i in range(x_count):
            own = [chunks[r * x_count + i] for r in range(z_count)]
            squares = jnp.zeros((padded, 1), jnp.float32)
            for chunk in own:
                h = filled(chunk)
                squares = squares + jnp.sum(h * h, axis=1, keepdims=True)
            scale = lax.rsqrt(squares / (depth * z_count) + eps)
            down = pl.multiple_of(lax.rem(x_ref[0] + i, x_count) * padded, padded)
            for r, chunk in enumerate(own):
                z_at = lax.rem(z_ref[0] + r, z_count)
                across = pl.multiple_of(z_at * depth, depth)
                h = filled(chunk)
                scaled_ref[pl.ds(down, padded), pl.ds(across, depth)] = (
                    h * scale * gain_ref[z_at]
                ).astype(jnp.bfloat16)

    scaled = scaled_ref[...]
    gate = jnp.dot(scaled, gate_ref[0], preferred_element_type=jnp.float32)
    upper = jnp.dot(scaled, up_ref[0], preferred_element_type=jnp.float32)
    act_ref[...] = (gate / (1.0 + jnp.exp(-gate)) * upper).astype(jnp.bfloat16)


def expert_hidden(z_at, x_at, chunks, gain, w_gate, w_up):
    z_count, x_count = len(chunks), len(chunks[0])
    rows, depth = chunks[0][0].shape
    columns = w_gate.shape[2]
    width = tile_of(columns, 256)
    padded = -(-rows // 16) * 16 * x_count
    gain = gain.reshape(z_count, 1, depth)
    weight_spec = pl.BlockSpec((1, depth * z_count, width), lambda n: (0, 0, n))
    return pl.pallas_call(
        functools.partial(hidden_kernel, z_count, x_count),
        grid=(columns // width,),
        in_specs=[whole_smem()] * 2
        + [whole_vmem()] * (z_count * x_count + 1)
        + [weight_spec, weight_spec],
        out_specs=pl.BlockSpec((padded, width), lambda n: (0, n)),
        out_shape=jax.ShapeDtypeStruct((padded, columns), jnp.bfloat16),
        scratch_shapes=[pltpu.VMEM((padded, depth * z_count), jnp.bfloat16)],
        compiler_params=pltpu.CompilerParams(vmem_limit_bytes=50 * MIB),
        name="expert_hidden",
    )(z_at, x_at, *[chunk for pair in chunks for chunk in pair], gain, w_gate, w_up)


def down_kernel(x_count, x_ref, blocks_ref, act_ref, weight_ref, *refs):
    outs, held_ref = refs[:-1], refs[-1]
    held_ref[...] = jnp.dot(act_ref[...], weight_ref[0], preferred_element_type=jnp.float32)
    rows = outs[0].shape[0]
    padded = held_ref.shape[0] // x_count
    for k in range(len(outs) // x_count):

        @pl.when(pl.program_id(0) == k)
        def _(k=k):
            for i in range(x_count):
                start = pl.multiple_of(lax.rem(x_ref[0] + i, x_count) * padded, padded)
                outs[k * x_count + i][...] = held_ref[pl.ds(start, rows), :].astype(jnp.bfloat16)


def expert_down(x_at, blocks, x_count, z_count, rows, act, w_down):
    padded, depth = act.shape
    columns = w_down.shape[2] // z_count
    width = tile_of(columns)
    tiles = columns // width
    count = blocks.shape[0]

    def out_spec(k):
        def place(m, n, x, blocks):
            return (0, jnp.where(m == k, n, jnp.where(m < k, 0, tiles - 1)))

        return pl.BlockSpec((rows, width), place)

    outs = pl.pallas_call(
        functools.partial(down_kernel, x_count),
        grid_spec=pltpu.PrefetchScalarGridSpec(
            num_scalar_prefetch=2,
            grid=(count, tiles),
            in_specs=[
                pl.BlockSpec((padded, depth), lambda m, n, x, blocks: (0, 0)),
                pl.BlockSpec(
                    (1, depth, width), lambda m, n, x, blocks: (0, 0, blocks[m] * tiles + n)
                ),
            ],
            out_specs=[out_spec(k) for k in range(count) for _ in range(x_count)],
            scratch_shapes=[pltpu.VMEM((padded, width), jnp.float32)],
        ),
        out_shape=[jax.ShapeDtypeStruct((rows, columns), jnp.bfloat16)] * (count * x_count),
        compiler_params=pltpu.CompilerParams(vmem_limit_bytes=50 * MIB),
        name="expert_down",
    )(x_at, blocks, act, w_down)
    return [outs[k * x_count : (k + 1) * x_count] for k in range(count)]


def per_device(
    x_in,
    z_in,
    conv_weight,
    conv_bias,
    x_proj,
    dt_proj,
    dt_bias,
    a_log,
    d_skip,
    out_proj,
    resid,
    norm_gain,
    routes,
    route_gate,
    w_gate,
    w_up,
    w_down,
):
    row_count, channels = x_in.shape
    seq_count = lax.axis_size("seq")
    exp_count = lax.axis_size("exp")
    x_count = seq_count // exp_count
    z_count = exp_count
    seq_at = lax.axis_index("seq")
    exp_at = lax.axis_index("exp")
    z_at, x_at = seq_at // x_count, seq_at % x_count
    z_one = z_at.reshape(1).astype(jnp.int32)
    x_one = x_at.reshape(1).astype(jnp.int32)
    e_one = exp_at.reshape(1).astype(jnp.int32)
    top_count = routes.shape[1]
    capacity = row_count * top_count * 17 // (16 * exp_count)
    pitch = capacity
    feature_slice = resid.shape[1]

    def from_z(block, r):
        pairs = [
            (((z + r) % z_count) * x_count + x, z * x_count + x)
            for z in range(z_count)
            for x in range(x_count)
        ]
        return lax.ppermute(block, "seq", pairs)

    def from_x(block, i):
        pairs = [
            (z * x_count + (x + i) % x_count, z * x_count + x)
            for z in range(z_count)
            for x in range(x_count)
        ]
        return lax.ppermute(block, "seq", pairs)

    turns = sorted(range(1, z_count), key=lambda r: min(r, z_count - r))

    def gathered(block):
        rows = {(0, 0): block}
        others = range(1, x_count)
        for i in others:
            rows[0, i] = from_x(block, i)
        sent = block
        for k, r in enumerate(turns):
            if k >= 2:
                sent = after(sent, rows[turns[k - 2], 0], *[rows[0, i] for i in others])
            rows[r, 0] = from_z(sent, r)
        for k, r in enumerate(turns):
            earlier = turns[max(k - 2, 0) : max(k - 1, 0)] if r != turns[-1] else turns[:k]
            forward = after(rows[r, 0], *[rows[q, i] for q in earlier for i in others])
            for i in others:
                rows[r, i] = from_x(forward, i)
        return [[rows[r, i] for i in range(x_count)] for r in range(z_count)]

    y_count = exp_count // 2

    def other_core(block):
        return lax.ppermute(block, "exp", [(e ^ 1, e) for e in range(exp_count)])

    def from_y(block, r):
        pairs = [
            ((y + r) % y_count * 2 + core, y * 2 + core)
            for y in range(y_count)
            for core in range(2)
        ]
        return lax.ppermute(block, "exp", pairs)

    swap = [
        ((e * x_count + x) * exp_count + z, (z * x_count + x) * exp_count + e)
        for z in range(z_count)
        for x in range(x_count)
        for e in range(exp_count)
    ]

    halo = lax.ppermute(
        x_in[row_count - 8 :], "seq", [(i, i + 1) for i in range(seq_count - 1)]
    )

    xconv, partial = conv_and_project(x_in, halo, conv_weight, conv_bias[None], x_proj.T)
    resid_here = lax.ppermute(resid, ("seq", "exp"), swap)

    chip_sum = partial + other_core(after(partial, resid_here))
    a_log, routes, route_gate = lax.optimization_barrier(
        (a_log, routes, route_gate, chip_sum)
    )[:3]
    rates = -jnp.exp(a_log.T) * LOG2E

    def part_of(v):
        return v.astype(jnp.bfloat16).astype(jnp.float32)

    gate_high = part_of(route_gate)
    gate_mid = part_of(route_gate - gate_high)
    gate_low = route_gate - gate_high - gate_mid
    info = jnp.stack([routes.astype(jnp.float32), gate_high, gate_mid, gate_low])
    info = info.transpose(0, 2, 1).reshape(4, top_count * row_count)
    info = jnp.pad(info, ((0, 4), (0, channels - top_count * row_count)))

    def slots_of(named):
        flat = named.reshape(-1, row_count * top_count)
        onehot = (flat[:, :, None] == jnp.arange(exp_count, dtype=jnp.int32)).astype(jnp.float32)
        below = jnp.tril(jnp.ones((row_count * top_count,) * 2, jnp.float32), -1)
        counts = jnp.einsum("ij,bje->bie", below, onehot)
        slots = jnp.sum(counts * onehot, axis=2).astype(jnp.int32)
        return slots.reshape(-1, row_count, top_count)

    own_target = (routes - z_at) % exp_count * pitch + slots_of(routes)[0]
    slot_ids = jnp.arange(exp_count * pitch, dtype=jnp.int32)
    choose = jnp.sum(
        (own_target[:, :, None] == slot_ids[None, None, :]).astype(jnp.float32), axis=1
    ).astype(jnp.bfloat16)

    cut = channels * 5 // 16
    uppers = [from_x(after(out_proj, halo)[:cut], i) for i in range(1, x_count)]
    partials = [chip_sum] + [from_y(chip_sum, r) for r in range(1, y_count)]
    step_size, load, b_wide, c_wide = scan_ends(partials, dt_proj, dt_bias[None], rates, xconv, info)
    loads = gathered(after(load, resid_here, *uppers))
    held_proj = after(out_proj, *[part for pair in loads for part in pair])
    lowers = [from_x(held_proj[cut:], i) for i in range(1, x_count)]
    columns = [[out_proj]] + [list(pair) for pair in zip(uppers, lowers)]
    mixed = scan_mix(
        z_one, x_one, loads, step_size, xconv, z_in, b_wide, c_wide, rates, d_skip[None]
    )
    along_z = [mixed] + [from_z(mixed, r) for r in range(1, z_count)]

    first_row = a_log.shape[1] + 2
    spare = after(jnp.stack([loads[r][0][first_row:] for r in range(z_count)]), mixed)
    spare = spare[:, :4, : top_count * row_count].astype(jnp.float32)
    spare = lax.dynamic_slice_in_dim(
        jnp.concatenate([spare, spare]), (z_count - z_at) % z_count, z_count, 0
    ).reshape(z_count, 4, top_count, row_count)
    all_routes = spare[:, 0].transpose(0, 2, 1).astype(jnp.int32)
    all_gates = (spare[:, 1] + spare[:, 2] + spare[:, 3]).transpose(0, 2, 1)
    z_ids = jnp.arange(z_count, dtype=jnp.int32)[:, None, None]
    target = (all_routes * z_count + z_ids) * pitch + slots_of(all_routes)
    target = target.reshape(z_count * row_count, top_count)
    count = z_count * pitch
    exp_late = after(exp_at, mixed)
    y_at, core_at = exp_late // 2, exp_late % 2

    def picked(core):
        experts = (y_at + jnp.arange(y_count, dtype=jnp.int32)) % y_count * 2 + core
        ids = experts[:, None] * count + jnp.arange(count, dtype=jnp.int32)[None, :]
        same = target[None, :, :] == ids.reshape(-1)[:, None, None]
        return jnp.sum(same.astype(jnp.float32), axis=2).astype(jnp.bfloat16)

    here_ids = exp_at * z_count * pitch + jnp.arange(z_count * pitch, dtype=jnp.int32)
    here = target[None, :, :] == here_ids[:, None, None]
    gate_here = jnp.sum(
        jnp.where(here, all_gates.reshape(1, z_count * row_count, top_count), 0.0), axis=(1, 2)
    )[:, None]
    first_here = jnp.sum(here[:, :, 0].astype(jnp.float32), axis=1)[:, None]

    keep, send = out_product(
        z_one, x_one, e_one, picked(core_at), picked(1 - core_at), resid_here, along_z, columns
    )
    over_chip = keep.astype(jnp.float32) + other_core(send).astype(jnp.float32)
    over_chip = over_chip.reshape(y_count, count, feature_slice)
    rows_here = over_chip[0]
    for r in range(1, y_count):
        arrived = from_y(over_chip[r].astype(jnp.bfloat16), y_count - r)
        rows_here = rows_here + arrived.astype(jnp.float32)
    rows_here = rows_here.astype(jnp.bfloat16)

    chunks = gathered(rows_here)
    act = expert_hidden(z_one, x_one, chunks, norm_gain, w_gate, w_up)

    by_distance = sorted(range(1, z_count), key=lambda r: abs(r - z_count // 2)) + [0]
    down, crossed, arrivals = {}, {}, []

    def products(turns_now, rows):
        blocks = jnp.stack([(z_at + r) % z_count for r in turns_now]).astype(jnp.int32)
        outs = expert_down(x_one, blocks, x_count, z_count, exp_count * pitch, rows, w_down)
        down.update(zip(turns_now, outs))

    def over_x(r):
        return functools.reduce(
            jnp.add, [p.astype(jnp.float32) for p in [down[r][0]] + crossed[r]]
        )

    products(by_distance[:1], act)
    products(by_distance[1:-1], act)
    for k, r in enumerate(by_distance):
        if r == 0:
            products([0], after(act, *crossed[by_distance[1]]))
        pieces = down[r][1:]
        if r == 0:
            pieces = [after(piece, arrivals[0]) for piece in pieces]
        elif k >= 2:
            pieces = [after(piece, *crossed[by_distance[k - 2]]) for piece in pieces]
        crossed[r] = [from_x(piece, x_count - i) for i, piece in enumerate(pieces, 1)]
        if r:
            arrivals.append(from_z(over_x(r).astype(jnp.bfloat16), z_count - r))
    total = over_x(0)
    for sent in arrivals:
        total = total + sent.astype(jnp.float32)
    expert_out = total.astype(jnp.bfloat16).astype(jnp.float32)
    expert_out = gate_here * expert_out + first_here * rows_here.astype(jnp.float32)
    expert_out = expert_out.astype(jnp.bfloat16)
    pieces = expert_out.reshape(exp_count, pitch, feature_slice)
    back = []
    for k in range(exp_count):
        piece = lax.dynamic_index_in_dim(pieces, (exp_at - k) % exp_count, 0, keepdims=False)
        pairs = [
            (
                (e * x_count + x) * exp_count + (z + k) % exp_count,
                (z * x_count + x) * exp_count + e,
            )
            for z in range(z_count)
            for x in range(x_count)
            for e in range(exp_count)
        ]
        back.append(lax.ppermute(piece, ("seq", "exp"), pairs))
    back = jnp.concatenate(back, axis=0)
    return jnp.dot(choose, back, preferred_element_type=jnp.float32).astype(jnp.bfloat16)


def solution(mesh):
    return jax.shard_map(
        per_device,
        mesh=mesh,
        in_specs=(
            P("seq", "exp"),
            P("seq", "exp"),
            P(None, "exp"),
            P("exp"),
            P("exp", None),
            P(None, "exp"),
            P("exp"),
            P("exp", None),
            P("exp"),
            P("exp", "seq"),
            P("seq", "exp"),
            P(),
            P("seq", None),
            P("seq", None),
            P("exp", None, "seq"),
            P("exp", None, "seq"),
            P("exp", "seq", None),
        ),
        out_specs=P("seq", "exp"),
        check_vma=False,
    )
```

```python
import functools
import math

import jax
import jax.numpy as jnp
from jax import lax
from jax.experimental import pallas as pl
from jax.experimental.pallas import tpu as pltpu
from jax.sharding import PartitionSpec as P

eps = 1e-05
LOG2E = 1.4426950408889634
MIB = 1 << 20


def tile_of(size, most=512):
    return max(t for t in range(128, most + 1, 128) if size % t == 0)


def after(value, *others):
    return lax.optimization_barrier((value, *others))[0]


def whole_vmem():
    return pl.BlockSpec(memory_space=pltpu.VMEM)


def lanes_of(width):
    return pl.ds(pl.multiple_of(pl.program_id(0) * width, width), width)


def whole_smem():
    return pl.BlockSpec(memory_space=pltpu.SMEM)


def conv_kernel(x_ref, halo_ref, weight_ref, bias_ref, proj_ref, xconv_ref, partial_ref):
    rows = x_ref.shape[0]
    taps = weight_ref.shape[0]
    across = lanes_of(x_ref.shape[1])
    extended = jnp.concatenate(
        [halo_ref[:, across].astype(jnp.float32), x_ref[...].astype(jnp.float32)], axis=0
    )
    pad = halo_ref.shape[0]
    conv = jnp.zeros(x_ref.shape, jnp.float32) + bias_ref[...]
    for tap in range(taps):
        start = pad - (taps - 1) + tap
        conv = conv + weight_ref[tap : tap + 1, :] * extended[start : start + rows]
    xconv = (conv / (1.0 + jnp.exp(-conv))).astype(jnp.bfloat16)
    xconv_ref[...] = xconv

    @pl.when(pl.program_id(0) == 0)
    def _():
        partial_ref[...] = jnp.zeros_like(partial_ref)

    partial_ref[...] += lax.dot_general(
        xconv, proj_ref[...], (((1,), (1,)), ((), ())), preferred_element_type=jnp.float32
    )


def conv_and_project(x_in, halo, conv_weight, conv_bias, x_proj_t):
    rows, channels = x_in.shape
    width = tile_of(channels, 1024)
    columns = x_proj_t.shape[0]
    return pl.pallas_call(
        conv_kernel,
        grid=(channels // width,),
        in_specs=[
            pl.BlockSpec((rows, width), lambda i: (0, i)),
            whole_vmem(),
            pl.BlockSpec((conv_weight.shape[0], width), lambda i: (0, i)),
            pl.BlockSpec((1, width), lambda i: (0, i)),
            pl.BlockSpec((columns, width), lambda i: (0, i)),
        ],
        out_specs=[
            pl.BlockSpec((rows, width), lambda i: (0, i)),
            pl.BlockSpec((rows, columns), lambda i: (0, 0)),
        ],
        out_shape=[
            jax.ShapeDtypeStruct((rows, channels), jnp.bfloat16),
            jax.ShapeDtypeStruct((rows, columns), jnp.float32),
        ],
        name="conv_project",
    )(x_in, halo, conv_weight, conv_bias, x_proj_t)


def softplus(v):
    return jnp.maximum(v, 0.0) + jnp.log1p(jnp.exp(-jnp.abs(v)))


def ends_kernel(count, *refs):
    parts = refs[:count]
    proj_ref, bias_ref, rate_ref, x_ref, info_ref = refs[count : count + 5]
    size_ref, load_ref, both_ref, b_ref, low_ref, drive_ref = refs[count + 5 :]
    rows, width = x_ref.shape
    states = rate_ref.shape[0]
    low_rank = low_ref.shape[1]
    groups = width // 128

    @pl.when(pl.program_id(0) == 0)
    def _():
        total = parts[0][...]
        for part in parts[1:]:
            total = total + part[...]
        low_ref[...] = total[:, :low_rank].astype(jnp.bfloat16)
        both_ref[...] = total[:, low_rank : low_rank + 2 * states]
        b_mat = total[:, low_rank : low_rank + states]
        b_ref[...] = jnp.broadcast_to(b_mat[:, :, None], b_ref.shape)

    size = softplus(
        jnp.dot(low_ref[...], proj_ref[...], preferred_element_type=jnp.float32) + bias_ref[...]
    )
    size_ref[...] = size
    drive_ref[...] = size * x_ref[...].astype(jnp.float32)
    rates = rate_ref[...]

    def step(block, state):
        start = pl.multiple_of(block * 8, 8)
        sizes = size_ref[pl.ds(start, 8), :]
        drives = drive_ref[pl.ds(start, 8), :]
        state = list(state)
        for i in range(8):
            b_now = b_ref[start + i]
            for g in range(groups):
                lanes = slice(g * 128, g * 128 + 128)
                decay = jnp.exp2(sizes[i : i + 1, lanes] * rates[:, lanes])
                state[g] = decay * state[g] + drives[i : i + 1, lanes] * b_now
        return tuple(state)

    zero = jnp.zeros((states, 128), jnp.float32)
    state = lax.fori_loop(0, rows // 8, step, (zero,) * groups)
    total = jnp.sum(size, axis=0, keepdims=True)
    high = total.astype(jnp.bfloat16).astype(jnp.float32)
    low = total - high
    rest = info_ref[: load_ref.shape[0] - states - 2, :]
    load_ref[...] = jnp.concatenate(
        [jnp.concatenate(state, axis=1), high, low, rest], axis=0
    ).astype(jnp.bfloat16)


def scan_ends(partials, dt_proj, dt_bias, rates, xconv, info):
    rows, channels = xconv.shape
    states = rates.shape[0]
    width = tile_of(channels, 1024)
    load_rows = -(-(states + 2) // 8) * 8
    return pl.pallas_call(
        functools.partial(ends_kernel, len(partials)),
        grid=(channels // width,),
        in_specs=[
            *[whole_vmem() for _ in partials],
            pl.BlockSpec((dt_proj.shape[0], width), lambda i: (0, i)),
            pl.BlockSpec((1, width), lambda i: (0, i)),
            pl.BlockSpec((states, width), lambda i: (0, i)),
            pl.BlockSpec((rows, width), lambda i: (0, i)),
            pl.BlockSpec((info.shape[0], width), lambda i: (0, i)),
        ],
        out_specs=[
            pl.BlockSpec((rows, width), lambda i: (0, i)),
            pl.BlockSpec((load_rows, width), lambda i: (0, i)),
            pl.BlockSpec((rows, 2 * states), lambda i: (0, 0)),
        ],
        out_shape=[
            jax.ShapeDtypeStruct((rows, channels), jnp.float32),
            jax.ShapeDtypeStruct((load_rows, channels), jnp.bfloat16),
            jax.ShapeDtypeStruct((rows, 2 * states), jnp.float32),
        ],
        scratch_shapes=[
            pltpu.VMEM((rows, states, 128), jnp.float32),
            pltpu.VMEM((rows, dt_proj.shape[0]), jnp.bfloat16),
            pltpu.VMEM((rows, width), jnp.float32),
        ],
        name="scan_ends",
    )(*partials, dt_proj, dt_bias, rates, xconv, info)


def mix_kernel(z_count, x_count, z_place, x_place, *refs):
    count = z_count * x_count
    loads = refs[:count]
    size_ref, x_ref, z_ref, both_ref, rate_ref, skip_ref, out_ref = refs[count : count + 7]
    drive_ref, y_ref, load_ref, b_ref, c_ref = refs[count + 7 :]
    across = lanes_of(x_ref.shape[1])
    for k in range(count):
        z_from = lax.rem(z_place[0] + k // x_count, z_count)
        x_from = lax.rem(x_place[0] + k % x_count, x_count)
        load_ref[z_from * x_count + x_from] = loads[k][:, across].astype(jnp.float32)
    rows, width = x_ref.shape
    states = rate_ref.shape[0]
    groups = width // 128

    @pl.when(pl.program_id(0) == 0)
    def _():
        both = both_ref[...]
        b_ref[...] = jnp.broadcast_to(both[:, :states, None], b_ref.shape)
        c_ref[...] = jnp.broadcast_to(both[:, states:, None], c_ref.shape)

    rates = rate_ref[...]
    x_f = x_ref[...].astype(jnp.float32)
    drive_ref[...] = size_ref[...] * x_f

    def earlier(j, state):
        block = load_ref[j]
        total = block[states : states + 1] + block[states + 1 : states + 2]
        return jnp.exp2(total * rates) * state + block[:states]

    place = z_place[0] * x_count + x_place[0]
    incoming = lax.fori_loop(0, place, earlier, jnp.zeros((states, width), jnp.float32))

    def step(block, state):
        start = pl.multiple_of(block * 8, 8)
        sizes = size_ref[pl.ds(start, 8), :]
        drives = drive_ref[pl.ds(start, 8), :]
        state = list(state)
        outs = [[None] * 8 for _ in range(groups)]
        for i in range(8):
            b_now = b_ref[start + i]
            c_now = c_ref[start + i]
            for g in range(groups):
                lanes = slice(g * 128, g * 128 + 128)
                decay = jnp.exp2(sizes[i : i + 1, lanes] * rates[:, lanes])
                state[g] = decay * state[g] + drives[i : i + 1, lanes] * b_now
                outs[g][i] = jnp.sum(state[g] * c_now, axis=0, keepdims=True)
        for g in range(groups):
            y_ref[pl.ds(start, 8), g * 128 : g * 128 + 128] = jnp.concatenate(outs[g], axis=0)
        return tuple(state)

    start_state = tuple(incoming[:, g * 128 : g * 128 + 128] for g in range(groups))
    lax.fori_loop(0, rows // 8, step, start_state)
    z_f = z_ref[...].astype(jnp.float32)
    scanned = y_ref[...] + skip_ref[...] * x_f
    out_ref[...] = (scanned * (z_f / (1.0 + jnp.exp(-z_f)))).astype(jnp.bfloat16)


def scan_mix(z_at, x_at, loads, step_size, xconv, z_in, both, rates, d_skip):
    rows, channels = xconv.shape
    states = rates.shape[0]
    width = tile_of(channels, 1024)
    flat = [load for pair in loads for load in pair]

    def by_lane(depth):
        return pl.BlockSpec((depth, width), lambda i: (0, i))

    return pl.pallas_call(
        functools.partial(mix_kernel, len(loads), len(loads[0])),
        grid=(channels // width,),
        in_specs=[
            whole_smem(),
            whole_smem(),
            *[whole_vmem() for _ in flat],
            by_lane(rows),
            by_lane(rows),
            by_lane(rows),
            pl.BlockSpec(both.shape, lambda i: (0, 0)),
            by_lane(states),
            by_lane(1),
        ],
        out_specs=by_lane(rows),
        out_shape=jax.ShapeDtypeStruct((rows, channels), jnp.bfloat16),
        scratch_shapes=[pltpu.VMEM((rows, width), jnp.float32)] * 2
        + [pltpu.VMEM((len(flat), flat[0].shape[0], width), jnp.float32)]
        + [pltpu.VMEM((rows, states, 128), jnp.float32)] * 2,
        name="scan_mix",
    )(z_at, x_at, *flat, step_size, xconv, z_in, both, rates, d_skip)


def out_kernel(z_count, counts, z_ref, x_ref, e_ref, keep_pick_ref, send_pick_ref, resid_ref, *refs):
    x_count = len(counts)
    blocks = refs[:z_count]
    keep_ref, send_ref, held_ref, sum_ref = refs[z_count + sum(counts) :]
    weights = list(refs[z_count : z_count + sum(counts)])
    rows = blocks[0].shape[0]
    columns = weights[0].shape[1]
    for r in range(z_count):
        at = pl.multiple_of(lax.rem(z_ref[0] + r, z_count) * rows, rows)
        held_ref[pl.ds(at, rows), :] = blocks[r][...]
    own = pl.ds(pl.multiple_of(e_ref[0] * rows, rows), rows)
    for i, count in enumerate(counts):
        at = pl.ds(pl.multiple_of(lax.rem(x_ref[0] + i, x_count) * columns, columns), columns)
        start, parts = 0, []
        for _ in range(count):
            weight = weights.pop(0)
            depth = weight.shape[0]
            parts.append(
                jnp.dot(
                    held_ref[:, start : start + depth],
                    weight[...],
                    preferred_element_type=jnp.float32,
                )
            )
            start += depth
        sum_ref[...] = functools.reduce(jnp.add, parts)
        sum_ref[own, :] += resid_ref[:, at].astype(jnp.float32)
        summed = sum_ref[...].astype(jnp.bfloat16)
        for pick_ref, out_ref in ((keep_pick_ref, keep_ref), (send_pick_ref, send_ref)):
            out_ref[:, at] = jnp.dot(
                pick_ref[...], summed, preferred_element_type=jnp.float32
            ).astype(jnp.bfloat16)


def out_product(z_at, x_at, e_at, keep_pick, send_pick, resid, blocks, weights):
    rows, depth = blocks[0].shape
    z_count, x_count = len(blocks), len(weights)
    counts = [len(parts) for parts in weights]
    columns = weights[0][0].shape[1]
    return pl.pallas_call(
        functools.partial(out_kernel, z_count, counts),
        in_specs=[whole_smem()] * 3 + [whole_vmem()] * (3 + z_count + sum(counts)),
        out_specs=[whole_vmem()] * 2,
        out_shape=[jax.ShapeDtypeStruct((keep_pick.shape[0], x_count * columns), jnp.bfloat16)] * 2,
        scratch_shapes=[
            pltpu.VMEM((z_count * rows, depth), jnp.bfloat16),
            pltpu.VMEM((z_count * rows, columns), jnp.float32),
        ],
        compiler_params=pltpu.CompilerParams(vmem_limit_bytes=16 * MIB),
        name="out_product",
    )(
        z_at,
        x_at,
        e_at,
        keep_pick,
        send_pick,
        resid,
        *blocks,
        *[part for parts in weights for part in parts],
    )


def hidden_kernel(z_count, x_count, z_ref, x_ref, *refs):
    count = z_count * x_count
    chunks = refs[:count]
    gain_ref, gate_ref, up_ref, act_ref, scaled_ref = refs[count:]
    rows, depth = chunks[0].shape
    padded = scaled_ref.shape[0] // x_count

    def filled(chunk):
        h = chunk[...].astype(jnp.float32)
        if padded == rows:
            return h
        return jnp.concatenate([h, jnp.zeros((padded - rows, depth), jnp.float32)], axis=0)

    @pl.when(pl.program_id(0) == 0)
    def _():
        for i in range(x_count):
            own = [chunks[r * x_count + i] for r in range(z_count)]
            squares = jnp.zeros((padded, 1), jnp.float32)
            for chunk in own:
                h = filled(chunk)
                squares = squares + jnp.sum(h * h, axis=1, keepdims=True)
            scale = lax.rsqrt(squares / (depth * z_count) + eps)
            down = pl.multiple_of(lax.rem(x_ref[0] + i, x_count) * padded, padded)
            for r, chunk in enumerate(own):
                z_at = lax.rem(z_ref[0] + r, z_count)
                across = pl.multiple_of(z_at * depth, depth)
                h = filled(chunk)
                scaled_ref[pl.ds(down, padded), pl.ds(across, depth)] = (
                    h * scale * gain_ref[z_at]
                ).astype(jnp.bfloat16)

    scaled = scaled_ref[...]
    gate = jnp.dot(scaled, gate_ref[0], preferred_element_type=jnp.float32)
    upper = jnp.dot(scaled, up_ref[0], preferred_element_type=jnp.float32)
    act_ref[...] = (gate / (1.0 + jnp.exp(-gate)) * upper).astype(jnp.bfloat16)


def expert_hidden(z_at, x_at, chunks, gain, w_gate, w_up):
    z_count, x_count = len(chunks), len(chunks[0])
    rows, depth = chunks[0][0].shape
    columns = w_gate.shape[2]
    width = tile_of(columns, 256)
    padded = -(-rows // 16) * 16 * x_count
    gain = gain.reshape(z_count, 1, depth)
    weight_spec = pl.BlockSpec((1, depth * z_count, width), lambda n: (0, 0, n))
    return pl.pallas_call(
        functools.partial(hidden_kernel, z_count, x_count),
        grid=(columns // width,),
        in_specs=[whole_smem()] * 2
        + [whole_vmem()] * (z_count * x_count + 1)
        + [weight_spec, weight_spec],
        out_specs=pl.BlockSpec((padded, width), lambda n: (0, n)),
        out_shape=jax.ShapeDtypeStruct((padded, columns), jnp.bfloat16),
        scratch_shapes=[pltpu.VMEM((padded, depth * z_count), jnp.bfloat16)],
        compiler_params=pltpu.CompilerParams(vmem_limit_bytes=50 * MIB),
        name="expert_hidden",
    )(z_at, x_at, *[chunk for pair in chunks for chunk in pair], gain, w_gate, w_up)


def down_kernel(x_count, x_ref, blocks_ref, act_ref, weight_ref, *refs):
    outs, held_ref = refs[:-1], refs[-1]
    held_ref[...] = jnp.dot(act_ref[...], weight_ref[0], preferred_element_type=jnp.float32)
    rows = outs[0].shape[0]
    padded = held_ref.shape[0] // x_count
    for k in range(len(outs) // x_count):

        @pl.when(pl.program_id(0) == k)
        def _(k=k):
            for i in range(x_count):
                start = pl.multiple_of(lax.rem(x_ref[0] + i, x_count) * padded, padded)
                outs[k * x_count + i][...] = held_ref[pl.ds(start, rows), :].astype(jnp.bfloat16)


def expert_down(x_at, blocks, x_count, z_count, rows, act, w_down):
    padded, depth = act.shape
    columns = w_down.shape[2] // z_count
    width = tile_of(columns)
    tiles = columns // width
    count = blocks.shape[0]

    def out_spec(k):
        def place(m, n, x, blocks):
            return (0, jnp.where(m == k, n, jnp.where(m < k, 0, tiles - 1)))

        return pl.BlockSpec((rows, width), place)

    outs = pl.pallas_call(
        functools.partial(down_kernel, x_count),
        grid_spec=pltpu.PrefetchScalarGridSpec(
            num_scalar_prefetch=2,
            grid=(count, tiles),
            in_specs=[
                pl.BlockSpec((padded, depth), lambda m, n, x, blocks: (0, 0)),
                pl.BlockSpec(
                    (1, depth, width), lambda m, n, x, blocks: (0, 0, blocks[m] * tiles + n)
                ),
            ],
            out_specs=[out_spec(k) for k in range(count) for _ in range(x_count)],
            scratch_shapes=[pltpu.VMEM((padded, width), jnp.float32)],
        ),
        out_shape=[jax.ShapeDtypeStruct((rows, columns), jnp.bfloat16)] * (count * x_count),
        compiler_params=pltpu.CompilerParams(vmem_limit_bytes=50 * MIB),
        name="expert_down",
    )(x_at, blocks, act, w_down)
    return [outs[k * x_count : (k + 1) * x_count] for k in range(count)]


def per_device(
    x_in,
    z_in,
    conv_weight,
    conv_bias,
    x_proj,
    dt_proj,
    dt_bias,
    a_log,
    d_skip,
    out_proj,
    resid,
    norm_gain,
    routes,
    route_gate,
    w_gate,
    w_up,
    w_down,
):
    row_count, channels = x_in.shape
    seq_count = lax.axis_size("seq")
    exp_count = lax.axis_size("exp")
    x_count = seq_count // exp_count
    z_count = exp_count
    seq_at = lax.axis_index("seq")
    exp_at = lax.axis_index("exp")
    z_at, x_at = seq_at // x_count, seq_at % x_count
    z_one = z_at.reshape(1).astype(jnp.int32)
    x_one = x_at.reshape(1).astype(jnp.int32)
    e_one = exp_at.reshape(1).astype(jnp.int32)
    top_count = routes.shape[1]
    capacity = row_count * top_count * 17 // (16 * exp_count)
    pitch = capacity
    feature_slice = resid.shape[1]

    def from_z(block, r):
        pairs = [
            (((z + r) % z_count) * x_count + x, z * x_count + x)
            for z in range(z_count)
            for x in range(x_count)
        ]
        return lax.ppermute(block, "seq", pairs)

    def from_x(block, i):
        pairs = [
            (z * x_count + (x + i) % x_count, z * x_count + x)
            for z in range(z_count)
            for x in range(x_count)
        ]
        return lax.ppermute(block, "seq", pairs)

    turns = sorted(range(1, z_count), key=lambda r: min(r, z_count - r))

    def gathered(block, chained=True):
        rows = {(0, 0): block}
        others = range(1, x_count)
        for i in others:
            rows[0, i] = from_x(block, i)
        sent = block
        for k, r in enumerate(turns):
            if chained and k >= 2:
                sent = after(sent, rows[turns[k - 2], 0], *[rows[0, i] for i in others])
            rows[r, 0] = from_z(sent, r)
        for k, r in enumerate(turns):
            earlier = turns[max(k - 2, 0) : max(k - 1, 0)] if r != turns[-1] else turns[:k]
            forward = after(rows[r, 0], *[rows[q, i] for q in earlier for i in others])
            for i in others:
                rows[r, i] = from_x(forward, i)
        return [[rows[r, i] for i in range(x_count)] for r in range(z_count)]

    y_count = exp_count // 2

    def other_core(block):
        return lax.ppermute(block, "exp", [(e ^ 1, e) for e in range(exp_count)])

    def from_y(block, r):
        pairs = [
            ((y + r) % y_count * 2 + core, y * 2 + core)
            for y in range(y_count)
            for core in range(2)
        ]
        return lax.ppermute(block, "exp", pairs)

    swap = [
        ((e * x_count + x) * exp_count + z, (z * x_count + x) * exp_count + e)
        for z in range(z_count)
        for x in range(x_count)
        for e in range(exp_count)
    ]

    halo = lax.ppermute(
        x_in[row_count - 8 :], "seq", [(i, i + 1) for i in range(seq_count - 1)]
    )

    xconv, partial = conv_and_project(x_in, halo, conv_weight, conv_bias[None], x_proj.T)
    resid_here = lax.ppermute(resid, ("seq", "exp"), swap)

    chip_sum = partial + other_core(after(partial, resid_here))
    a_log, routes, route_gate = lax.optimization_barrier(
        (a_log, routes, route_gate, chip_sum)
    )[:3]
    rates = -jnp.exp(a_log.T) * LOG2E

    def part_of(v):
        return v.astype(jnp.bfloat16).astype(jnp.float32)

    gate_high = part_of(route_gate)
    gate_mid = part_of(route_gate - gate_high)
    gate_low = route_gate - gate_high - gate_mid
    info = jnp.stack([routes.astype(jnp.float32), gate_high, gate_mid, gate_low])
    info = info.transpose(0, 2, 1).reshape(4, top_count * row_count)
    info = jnp.pad(info, ((0, 4), (0, channels - top_count * row_count)))

    def slots_of(named):
        flat = named.reshape(-1, row_count * top_count)
        onehot = (flat[:, :, None] == jnp.arange(exp_count, dtype=jnp.int32)).astype(jnp.float32)
        below = jnp.tril(jnp.ones((row_count * top_count,) * 2, jnp.float32), -1)
        counts = jnp.einsum("ij,bje->bie", below, onehot)
        slots = jnp.sum(counts * onehot, axis=2).astype(jnp.int32)
        return slots.reshape(-1, row_count, top_count)

    own_target = (routes - z_at) % exp_count * pitch + slots_of(routes)[0]
    slot_ids = jnp.arange(exp_count * pitch, dtype=jnp.int32)
    choose = jnp.sum(
        (own_target[:, :, None] == slot_ids[None, None, :]).astype(jnp.float32), axis=1
    ).astype(jnp.bfloat16)

    cut = channels * 5 // 16
    uppers = [from_x(after(out_proj, halo)[:cut], i) for i in range(1, x_count)]
    partials = [chip_sum] + [from_y(chip_sum, r) for r in range(1, y_count)]
    step_size, load, both = scan_ends(partials, dt_proj, dt_bias[None], rates, xconv, info)
    loads = gathered(after(load, resid_here, *uppers), False)
    held_proj = after(out_proj, *[part for pair in loads for part in pair])
    lowers = [from_x(held_proj[cut:], i) for i in range(1, x_count)]
    columns = [[out_proj]] + [list(pair) for pair in zip(uppers, lowers)]
    mixed = scan_mix(
        z_one, x_one, loads, step_size, xconv, z_in, both, rates, d_skip[None]
    )
    along_z = [mixed] + [from_z(mixed, r) for r in range(1, z_count)]

    first_row = a_log.shape[1] + 2
    spare = after(jnp.stack([loads[r][0][first_row:] for r in range(z_count)]), mixed)
    spare = spare[:, :4, : top_count * row_count].astype(jnp.float32)
    spare = lax.dynamic_slice_in_dim(
        jnp.concatenate([spare, spare]), (z_count - z_at) % z_count, z_count, 0
    ).reshape(z_count, 4, top_count, row_count)
    all_routes = spare[:, 0].transpose(0, 2, 1).astype(jnp.int32)
    all_gates = (spare[:, 1] + spare[:, 2] + spare[:, 3]).transpose(0, 2, 1)
    z_ids = jnp.arange(z_count, dtype=jnp.int32)[:, None, None]
    target = (all_routes * z_count + z_ids) * pitch + slots_of(all_routes)
    target = target.reshape(z_count * row_count, top_count)
    count = z_count * pitch
    exp_late = after(exp_at, mixed)
    y_at, core_at = exp_late // 2, exp_late % 2

    def picked(core):
        experts = (y_at + jnp.arange(y_count, dtype=jnp.int32)) % y_count * 2 + core
        ids = experts[:, None] * count + jnp.arange(count, dtype=jnp.int32)[None, :]
        same = target[None, :, :] == ids.reshape(-1)[:, None, None]
        return jnp.sum(same.astype(jnp.float32), axis=2).astype(jnp.bfloat16)

    here_ids = exp_at * z_count * pitch + jnp.arange(z_count * pitch, dtype=jnp.int32)
    here = target[None, :, :] == here_ids[:, None, None]
    gate_here = jnp.sum(
        jnp.where(here, all_gates.reshape(1, z_count * row_count, top_count), 0.0), axis=(1, 2)
    )[:, None]
    first_here = jnp.sum(here[:, :, 0].astype(jnp.float32), axis=1)[:, None]

    keep, send = out_product(
        z_one, x_one, e_one, picked(core_at), picked(1 - core_at), resid_here, along_z, columns
    )
    over_chip = keep.astype(jnp.float32) + other_core(send).astype(jnp.float32)
    over_chip = over_chip.reshape(y_count, count, feature_slice)
    rows_here = over_chip[0]
    for r in range(1, y_count):
        arrived = from_y(over_chip[r].astype(jnp.bfloat16), y_count - r)
        rows_here = rows_here + arrived.astype(jnp.float32)
    rows_here = rows_here.astype(jnp.bfloat16)

    chunks = gathered(rows_here)
    act = expert_hidden(z_one, x_one, chunks, norm_gain, w_gate, w_up)

    by_distance = sorted(range(1, z_count), key=lambda r: abs(r - z_count // 2)) + [0]
    down, crossed, arrivals = {}, {}, []

    def products(turns_now, rows):
        blocks = jnp.stack([(z_at + r) % z_count for r in turns_now]).astype(jnp.int32)
        outs = expert_down(x_one, blocks, x_count, z_count, exp_count * pitch, rows, w_down)
        down.update(zip(turns_now, outs))

    def over_x(r):
        return functools.reduce(
            jnp.add, [p.astype(jnp.float32) for p in [down[r][0]] + crossed[r]]
        )

    products(by_distance[:1], act)
    products(by_distance[1:-1], act)
    for k, r in enumerate(by_distance):
        if r == 0:
            products([0], after(act, *crossed[by_distance[1]]))
        pieces = down[r][1:]
        if r == 0:
            pieces = [after(piece, arrivals[0]) for piece in pieces]
        elif k >= 2:
            pieces = [after(piece, *crossed[by_distance[k - 2]]) for piece in pieces]
        crossed[r] = [from_x(piece, x_count - i) for i, piece in enumerate(pieces, 1)]
        if r:
            arrivals.append(from_z(over_x(r).astype(jnp.bfloat16), z_count - r))
    total = over_x(0)
    for sent in arrivals:
        total = total + sent.astype(jnp.float32)
    expert_out = total.astype(jnp.bfloat16).astype(jnp.float32)
    expert_out = gate_here * expert_out + first_here * rows_here.astype(jnp.float32)
    expert_out = expert_out.astype(jnp.bfloat16)
    pieces = expert_out.reshape(exp_count, pitch, feature_slice)
    back = []
    for k in range(exp_count):
        piece = lax.dynamic_index_in_dim(pieces, (exp_at - k) % exp_count, 0, keepdims=False)
        pairs = [
            (
                (e * x_count + x) * exp_count + (z + k) % exp_count,
                (z * x_count + x) * exp_count + e,
            )
            for z in range(z_count)
            for x in range(x_count)
            for e in range(exp_count)
        ]
        back.append(lax.ppermute(piece, ("seq", "exp"), pairs))
    back = jnp.concatenate(back, axis=0)
    return jnp.dot(choose, back, preferred_element_type=jnp.float32).astype(jnp.bfloat16)


def solution(mesh):
    return jax.shard_map(
        per_device,
        mesh=mesh,
        in_specs=(
            P("seq", "exp"),
            P("seq", "exp"),
            P(None, "exp"),
            P("exp"),
            P("exp", None),
            P(None, "exp"),
            P("exp"),
            P("exp", None),
            P("exp"),
            P("exp", "seq"),
            P("seq", "exp"),
            P(),
            P("seq", None),
            P("seq", None),
            P("exp", None, "seq"),
            P("exp", None, "seq"),
            P("exp", "seq", None),
        ),
        out_specs=P("seq", "exp"),
        check_vma=False,
    )
```

```python
import functools
import math

import jax
import jax.numpy as jnp
from jax import lax
from jax.experimental import pallas as pl
from jax.experimental.pallas import tpu as pltpu
from jax.sharding import PartitionSpec as P

eps = 1e-05
LOG2E = 1.4426950408889634
MIB = 1 << 20


def tile_of(size, most=512):
    return max(t for t in range(128, most + 1, 128) if size % t == 0)


def after(value, *others):
    return lax.optimization_barrier((value, *others))[0]


def whole_vmem():
    return pl.BlockSpec(memory_space=pltpu.VMEM)


def lanes_of(width):
    return pl.ds(pl.multiple_of(pl.program_id(0) * width, width), width)


def whole_smem():
    return pl.BlockSpec(memory_space=pltpu.SMEM)


def conv_kernel(x_ref, halo_ref, weight_ref, bias_ref, proj_ref, xconv_ref, partial_ref):
    rows = x_ref.shape[0]
    taps = weight_ref.shape[0]
    across = lanes_of(x_ref.shape[1])
    extended = jnp.concatenate(
        [halo_ref[:, across].astype(jnp.float32), x_ref[...].astype(jnp.float32)], axis=0
    )
    pad = halo_ref.shape[0]
    conv = jnp.zeros(x_ref.shape, jnp.float32) + bias_ref[...]
    for tap in range(taps):
        start = pad - (taps - 1) + tap
        conv = conv + weight_ref[tap : tap + 1, :] * extended[start : start + rows]
    xconv = (conv / (1.0 + jnp.exp(-conv))).astype(jnp.bfloat16)
    xconv_ref[...] = xconv

    @pl.when(pl.program_id(0) == 0)
    def _():
        partial_ref[...] = jnp.zeros_like(partial_ref)

    partial_ref[...] += lax.dot_general(
        xconv, proj_ref[...], (((1,), (1,)), ((), ())), preferred_element_type=jnp.float32
    )


def conv_and_project(x_in, halo, conv_weight, conv_bias, x_proj_t):
    rows, channels = x_in.shape
    width = tile_of(channels, 1024)
    columns = x_proj_t.shape[0]
    return pl.pallas_call(
        conv_kernel,
        grid=(channels // width,),
        in_specs=[
            pl.BlockSpec((rows, width), lambda i: (0, i)),
            whole_vmem(),
            pl.BlockSpec((conv_weight.shape[0], width), lambda i: (0, i)),
            pl.BlockSpec((1, width), lambda i: (0, i)),
            pl.BlockSpec((columns, width), lambda i: (0, i)),
        ],
        out_specs=[
            pl.BlockSpec((rows, width), lambda i: (0, i)),
            pl.BlockSpec((rows, columns), lambda i: (0, 0)),
        ],
        out_shape=[
            jax.ShapeDtypeStruct((rows, channels), jnp.bfloat16),
            jax.ShapeDtypeStruct((rows, columns), jnp.float32),
        ],
        name="conv_project",
    )(x_in, halo, conv_weight, conv_bias, x_proj_t)


def softplus(v):
    return jnp.maximum(v, 0.0) + jnp.log1p(jnp.exp(-jnp.abs(v)))


def ends_kernel(count, *refs):
    parts = refs[:count]
    proj_ref, bias_ref, rate_ref, x_ref, info_ref = refs[count : count + 5]
    size_ref, load_ref, both_ref, b_ref, low_ref, drive_ref = refs[count + 5 :]
    rows, width = x_ref.shape
    states = rate_ref.shape[0]
    low_rank = low_ref.shape[1]
    groups = width // 128

    @pl.when(pl.program_id(0) == 0)
    def _():
        total = parts[0][...]
        for part in parts[1:]:
            total = total + part[...]
        low_ref[...] = total[:, :low_rank].astype(jnp.bfloat16)
        both_ref[...] = total[:, low_rank : low_rank + 2 * states]
        b_mat = total[:, low_rank : low_rank + states]
        b_ref[...] = jnp.broadcast_to(b_mat[:, :, None], b_ref.shape)

    size = softplus(
        jnp.dot(low_ref[...], proj_ref[...], preferred_element_type=jnp.float32) + bias_ref[...]
    )
    size_ref[...] = size
    drive_ref[...] = size * x_ref[...].astype(jnp.float32)
    rates = rate_ref[...]

    def step(block, state):
        start = pl.multiple_of(block * 8, 8)
        sizes = size_ref[pl.ds(start, 8), :]
        drives = drive_ref[pl.ds(start, 8), :]
        state = list(state)
        for i in range(8):
            b_now = b_ref[start + i]
            for g in range(groups):
                lanes = slice(g * 128, g * 128 + 128)
                decay = jnp.exp2(sizes[i : i + 1, lanes] * rates[:, lanes])
                state[g] = decay * state[g] + drives[i : i + 1, lanes] * b_now
        return tuple(state)

    zero = jnp.zeros((states, 128), jnp.float32)
    state = lax.fori_loop(0, rows // 8, step, (zero,) * groups)
    total = jnp.sum(size, axis=0, keepdims=True)
    high = total.astype(jnp.bfloat16).astype(jnp.float32)
    low = total - high
    rest = info_ref[: load_ref.shape[0] - states - 2, :]
    load_ref[...] = jnp.concatenate(
        [jnp.concatenate(state, axis=1), high, low, rest], axis=0
    ).astype(jnp.bfloat16)


def scan_ends(partials, dt_proj, dt_bias, rates, xconv, info):
    rows, channels = xconv.shape
    states = rates.shape[0]
    width = tile_of(channels, 1024)
    load_rows = -(-(states + 2) // 8) * 8
    return pl.pallas_call(
        functools.partial(ends_kernel, len(partials)),
        grid=(channels // width,),
        in_specs=[
            *[whole_vmem() for _ in partials],
            pl.BlockSpec((dt_proj.shape[0], width), lambda i: (0, i)),
            pl.BlockSpec((1, width), lambda i: (0, i)),
            pl.BlockSpec((states, width), lambda i: (0, i)),
            pl.BlockSpec((rows, width), lambda i: (0, i)),
            pl.BlockSpec((info.shape[0], width), lambda i: (0, i)),
        ],
        out_specs=[
            pl.BlockSpec((rows, width), lambda i: (0, i)),
            pl.BlockSpec((load_rows, width), lambda i: (0, i)),
            pl.BlockSpec((rows, 2 * states), lambda i: (0, 0)),
        ],
        out_shape=[
            jax.ShapeDtypeStruct((rows, channels), jnp.float32),
            jax.ShapeDtypeStruct((load_rows, channels), jnp.bfloat16),
            jax.ShapeDtypeStruct((rows, 2 * states), jnp.float32),
        ],
        scratch_shapes=[
            pltpu.VMEM((rows, states, 128), jnp.float32),
            pltpu.VMEM((rows, dt_proj.shape[0]), jnp.bfloat16),
            pltpu.VMEM((rows, width), jnp.float32),
        ],
        name="scan_ends",
    )(*partials, dt_proj, dt_bias, rates, xconv, info)


def mix_kernel(z_count, x_count, z_place, x_place, *refs):
    count = z_count * x_count
    loads = refs[:count]
    size_ref, x_ref, z_ref, both_ref, rate_ref, skip_ref, out_ref = refs[count : count + 7]
    drive_ref, y_ref, load_ref, b_ref, c_ref = refs[count + 7 :]
    across = lanes_of(x_ref.shape[1])
    for k in range(count):
        z_from = lax.rem(z_place[0] + k // x_count, z_count)
        x_from = lax.rem(x_place[0] + k % x_count, x_count)
        load_ref[z_from * x_count + x_from] = loads[k][:, across].astype(jnp.float32)
    rows, width = x_ref.shape
    states = rate_ref.shape[0]
    groups = width // 128

    @pl.when(pl.program_id(0) == 0)
    def _():
        both = both_ref[...]
        b_ref[...] = jnp.broadcast_to(both[:, :states, None], b_ref.shape)
        c_ref[...] = jnp.broadcast_to(both[:, states:, None], c_ref.shape)

    rates = rate_ref[...]
    x_f = x_ref[...].astype(jnp.float32)
    drive_ref[...] = size_ref[...] * x_f

    def earlier(j, state):
        block = load_ref[j]
        total = block[states : states + 1] + block[states + 1 : states + 2]
        return jnp.exp2(total * rates) * state + block[:states]

    place = z_place[0] * x_count + x_place[0]
    incoming = lax.fori_loop(0, place, earlier, jnp.zeros((states, width), jnp.float32))

    def step(block, state):
        start = pl.multiple_of(block * 8, 8)
        sizes = size_ref[pl.ds(start, 8), :]
        drives = drive_ref[pl.ds(start, 8), :]
        state = list(state)
        outs = [[None] * 8 for _ in range(groups)]
        for i in range(8):
            b_now = b_ref[start + i]
            c_now = c_ref[start + i]
            for g in range(groups):
                lanes = slice(g * 128, g * 128 + 128)
                decay = jnp.exp2(sizes[i : i + 1, lanes] * rates[:, lanes])
                state[g] = decay * state[g] + drives[i : i + 1, lanes] * b_now
                outs[g][i] = jnp.sum(state[g] * c_now, axis=0, keepdims=True)
        for g in range(groups):
            y_ref[pl.ds(start, 8), g * 128 : g * 128 + 128] = jnp.concatenate(outs[g], axis=0)
        return tuple(state)

    start_state = tuple(incoming[:, g * 128 : g * 128 + 128] for g in range(groups))
    lax.fori_loop(0, rows // 8, step, start_state)
    z_f = z_ref[...].astype(jnp.float32)
    scanned = y_ref[...] + skip_ref[...] * x_f
    out_ref[...] = (scanned * (z_f / (1.0 + jnp.exp(-z_f)))).astype(jnp.bfloat16)


def scan_mix(z_at, x_at, loads, step_size, xconv, z_in, both, rates, d_skip):
    rows, channels = xconv.shape
    states = rates.shape[0]
    width = tile_of(channels, 1024)
    flat = [load for pair in loads for load in pair]

    def by_lane(depth):
        return pl.BlockSpec((depth, width), lambda i: (0, i))

    return pl.pallas_call(
        functools.partial(mix_kernel, len(loads), len(loads[0])),
        grid=(channels // width,),
        in_specs=[
            whole_smem(),
            whole_smem(),
            *[whole_vmem() for _ in flat],
            by_lane(rows),
            by_lane(rows),
            by_lane(rows),
            pl.BlockSpec(both.shape, lambda i: (0, 0)),
            by_lane(states),
            by_lane(1),
        ],
        out_specs=by_lane(rows),
        out_shape=jax.ShapeDtypeStruct((rows, channels), jnp.bfloat16),
        scratch_shapes=[pltpu.VMEM((rows, width), jnp.float32)] * 2
        + [pltpu.VMEM((len(flat), flat[0].shape[0], width), jnp.float32)]
        + [pltpu.VMEM((rows, states, 128), jnp.float32)] * 2,
        name="scan_mix",
    )(z_at, x_at, *flat, step_size, xconv, z_in, both, rates, d_skip)


def out_kernel(z_count, counts, z_ref, x_ref, e_ref, keep_pick_ref, send_pick_ref, resid_ref, *refs):
    x_count = len(counts)
    blocks = refs[:z_count]
    keep_ref, send_ref, held_ref, sum_ref = refs[z_count + sum(counts) :]
    weights = list(refs[z_count : z_count + sum(counts)])
    rows = blocks[0].shape[0]
    columns = weights[0].shape[1]
    for r in range(z_count):
        at = pl.multiple_of(lax.rem(z_ref[0] + r, z_count) * rows, rows)
        held_ref[pl.ds(at, rows), :] = blocks[r][...]
    own = pl.ds(pl.multiple_of(e_ref[0] * rows, rows), rows)
    for i, count in enumerate(counts):
        at = pl.ds(pl.multiple_of(lax.rem(x_ref[0] + i, x_count) * columns, columns), columns)
        start, parts = 0, []
        for _ in range(count):
            weight = weights.pop(0)
            depth = weight.shape[0]
            parts.append(
                jnp.dot(
                    held_ref[:, start : start + depth],
                    weight[...],
                    preferred_element_type=jnp.float32,
                )
            )
            start += depth
        sum_ref[...] = functools.reduce(jnp.add, parts)
        sum_ref[own, :] += resid_ref[:, at].astype(jnp.float32)
        summed = sum_ref[...].astype(jnp.bfloat16)
        for pick_ref, out_ref in ((keep_pick_ref, keep_ref), (send_pick_ref, send_ref)):
            out_ref[:, at] = jnp.dot(
                pick_ref[...], summed, preferred_element_type=jnp.float32
            ).astype(jnp.bfloat16)


def out_product(z_at, x_at, e_at, keep_pick, send_pick, resid, blocks, weights):
    rows, depth = blocks[0].shape
    z_count, x_count = len(blocks), len(weights)
    counts = [len(parts) for parts in weights]
    columns = weights[0][0].shape[1]
    return pl.pallas_call(
        functools.partial(out_kernel, z_count, counts),
        in_specs=[whole_smem()] * 3 + [whole_vmem()] * (3 + z_count + sum(counts)),
        out_specs=[whole_vmem()] * 2,
        out_shape=[jax.ShapeDtypeStruct((keep_pick.shape[0], x_count * columns), jnp.bfloat16)] * 2,
        scratch_shapes=[
            pltpu.VMEM((z_count * rows, depth), jnp.bfloat16),
            pltpu.VMEM((z_count * rows, columns), jnp.float32),
        ],
        compiler_params=pltpu.CompilerParams(vmem_limit_bytes=16 * MIB),
        name="out_product",
    )(
        z_at,
        x_at,
        e_at,
        keep_pick,
        send_pick,
        resid,
        *blocks,
        *[part for parts in weights for part in parts],
    )


def hidden_kernel(z_count, x_count, z_ref, x_ref, *refs):
    count = z_count * x_count
    chunks = refs[:count]
    gain_ref, gate_ref, up_ref, act_ref, scaled_ref = refs[count:]
    rows, depth = chunks[0].shape
    padded = scaled_ref.shape[0] // x_count

    def filled(chunk):
        h = chunk[...].astype(jnp.float32)
        if padded == rows:
            return h
        return jnp.concatenate([h, jnp.zeros((padded - rows, depth), jnp.float32)], axis=0)

    @pl.when(pl.program_id(0) == 0)
    def _():
        for i in range(x_count):
            own = [chunks[r * x_count + i] for r in range(z_count)]
            squares = jnp.zeros((padded, 1), jnp.float32)
            for chunk in own:
                h = filled(chunk)
                squares = squares + jnp.sum(h * h, axis=1, keepdims=True)
            scale = lax.rsqrt(squares / (depth * z_count) + eps)
            down = pl.multiple_of(lax.rem(x_ref[0] + i, x_count) * padded, padded)
            for r, chunk in enumerate(own):
                z_at = lax.rem(z_ref[0] + r, z_count)
                across = pl.multiple_of(z_at * depth, depth)
                h = filled(chunk)
                scaled_ref[pl.ds(down, padded), pl.ds(across, depth)] = (
                    h * scale * gain_ref[z_at]
                ).astype(jnp.bfloat16)

    scaled = scaled_ref[...]
    gate = jnp.dot(scaled, gate_ref[0], preferred_element_type=jnp.float32)
    upper = jnp.dot(scaled, up_ref[0], preferred_element_type=jnp.float32)
    act_ref[...] = (gate / (1.0 + jnp.exp(-gate)) * upper).astype(jnp.bfloat16)


def expert_hidden(z_at, x_at, chunks, gain, w_gate, w_up):
    z_count, x_count = len(chunks), len(chunks[0])
    rows, depth = chunks[0][0].shape
    columns = w_gate.shape[2]
    width = tile_of(columns, 256)
    padded = -(-rows // 16) * 16 * x_count
    gain = gain.reshape(z_count, 1, depth)
    weight_spec = pl.BlockSpec((1, depth * z_count, width), lambda n: (0, 0, n))
    return pl.pallas_call(
        functools.partial(hidden_kernel, z_count, x_count),
        grid=(columns // width,),
        in_specs=[whole_smem()] * 2
        + [whole_vmem()] * (z_count * x_count + 1)
        + [weight_spec, weight_spec],
        out_specs=pl.BlockSpec((padded, width), lambda n: (0, n)),
        out_shape=jax.ShapeDtypeStruct((padded, columns), jnp.bfloat16),
        scratch_shapes=[pltpu.VMEM((padded, depth * z_count), jnp.bfloat16)],
        compiler_params=pltpu.CompilerParams(vmem_limit_bytes=50 * MIB),
        name="expert_hidden",
    )(z_at, x_at, *[chunk for pair in chunks for chunk in pair], gain, w_gate, w_up)


def down_kernel(x_count, x_ref, blocks_ref, act_ref, weight_ref, *refs):
    outs, held_ref = refs[:-1], refs[-1]
    held_ref[...] = jnp.dot(act_ref[...], weight_ref[0], preferred_element_type=jnp.float32)
    rows = outs[0].shape[0]
    padded = held_ref.shape[0] // x_count
    for k in range(len(outs) // x_count):

        @pl.when(pl.program_id(0) == k)
        def _(k=k):
            for i in range(x_count):
                start = pl.multiple_of(lax.rem(x_ref[0] + i, x_count) * padded, padded)
                outs[k * x_count + i][...] = held_ref[pl.ds(start, rows), :].astype(jnp.bfloat16)


def expert_down(x_at, blocks, x_count, z_count, rows, act, w_down):
    padded, depth = act.shape
    columns = w_down.shape[2] // z_count
    width = tile_of(columns)
    tiles = columns // width
    count = blocks.shape[0]

    def out_spec(k):
        def place(m, n, x, blocks):
            return (0, jnp.where(m == k, n, jnp.where(m < k, 0, tiles - 1)))

        return pl.BlockSpec((rows, width), place)

    outs = pl.pallas_call(
        functools.partial(down_kernel, x_count),
        grid_spec=pltpu.PrefetchScalarGridSpec(
            num_scalar_prefetch=2,
            grid=(count, tiles),
            in_specs=[
                pl.BlockSpec((padded, depth), lambda m, n, x, blocks: (0, 0)),
                pl.BlockSpec(
                    (1, depth, width), lambda m, n, x, blocks: (0, 0, blocks[m] * tiles + n)
                ),
            ],
            out_specs=[out_spec(k) for k in range(count) for _ in range(x_count)],
            scratch_shapes=[pltpu.VMEM((padded, width), jnp.float32)],
        ),
        out_shape=[jax.ShapeDtypeStruct((rows, columns), jnp.bfloat16)] * (count * x_count),
        compiler_params=pltpu.CompilerParams(vmem_limit_bytes=50 * MIB),
        name="expert_down",
    )(x_at, blocks, act, w_down)
    return [outs[k * x_count : (k + 1) * x_count] for k in range(count)]


def per_device(
    x_in,
    z_in,
    conv_weight,
    conv_bias,
    x_proj,
    dt_proj,
    dt_bias,
    a_log,
    d_skip,
    out_proj,
    resid,
    norm_gain,
    routes,
    route_gate,
    w_gate,
    w_up,
    w_down,
):
    row_count, channels = x_in.shape
    seq_count = lax.axis_size("seq")
    exp_count = lax.axis_size("exp")
    x_count = seq_count // exp_count
    z_count = exp_count
    seq_at = lax.axis_index("seq")
    exp_at = lax.axis_index("exp")
    z_at, x_at = seq_at // x_count, seq_at % x_count
    z_one = z_at.reshape(1).astype(jnp.int32)
    x_one = x_at.reshape(1).astype(jnp.int32)
    e_one = exp_at.reshape(1).astype(jnp.int32)
    top_count = routes.shape[1]
    capacity = row_count * top_count * 17 // (16 * exp_count)
    pitch = capacity
    feature_slice = resid.shape[1]

    def from_z(block, r):
        pairs = [
            (((z + r) % z_count) * x_count + x, z * x_count + x)
            for z in range(z_count)
            for x in range(x_count)
        ]
        return lax.ppermute(block, "seq", pairs)

    def from_x(block, i):
        pairs = [
            (z * x_count + (x + i) % x_count, z * x_count + x)
            for z in range(z_count)
            for x in range(x_count)
        ]
        return lax.ppermute(block, "seq", pairs)

    turns = sorted(range(1, z_count), key=lambda r: min(r, z_count - r))

    def gathered(block):
        rows = {(0, 0): block}
        others = range(1, x_count)
        for i in others:
            rows[0, i] = from_x(block, i)
        sent = block
        for k, r in enumerate(turns):
            if k >= 2:
                sent = after(sent, rows[turns[k - 2], 0], *[rows[0, i] for i in others])
            rows[r, 0] = from_z(sent, r)
        for k, r in enumerate(turns):
            earlier = turns[max(k - 2, 0) : max(k - 1, 0)] if r != turns[-1] else turns[:k]
            forward = after(rows[r, 0], *[rows[q, i] for q in earlier for i in others])
            for i in others:
                rows[r, i] = from_x(forward, i)
        return [[rows[r, i] for i in range(x_count)] for r in range(z_count)]

    y_count = exp_count // 2

    def other_core(block):
        return lax.ppermute(block, "exp", [(e ^ 1, e) for e in range(exp_count)])

    def from_y(block, r):
        pairs = [
            ((y + r) % y_count * 2 + core, y * 2 + core)
            for y in range(y_count)
            for core in range(2)
        ]
        return lax.ppermute(block, "exp", pairs)

    swap = [
        ((e * x_count + x) * exp_count + z, (z * x_count + x) * exp_count + e)
        for z in range(z_count)
        for x in range(x_count)
        for e in range(exp_count)
    ]

    halo = lax.ppermute(
        x_in[row_count - 8 :], "seq", [(i, i + 1) for i in range(seq_count - 1)]
    )

    xconv, partial = conv_and_project(x_in, halo, conv_weight, conv_bias[None], x_proj.T)
    resid_here = lax.ppermute(resid, ("seq", "exp"), swap)

    chip_sum = partial + other_core(after(partial, resid_here))
    a_log, routes, route_gate = lax.optimization_barrier(
        (a_log, routes, route_gate, chip_sum)
    )[:3]
    rates = -jnp.exp(a_log.T) * LOG2E

    def part_of(v):
        return v.astype(jnp.bfloat16).astype(jnp.float32)

    gate_high = part_of(route_gate)
    gate_mid = part_of(route_gate - gate_high)
    gate_low = route_gate - gate_high - gate_mid
    info = jnp.stack([routes.astype(jnp.float32), gate_high, gate_mid, gate_low])
    info = info.transpose(0, 2, 1).reshape(4, top_count * row_count)
    info = jnp.pad(info, ((0, 4), (0, channels - top_count * row_count)))

    def slots_of(named):
        flat = named.reshape(-1, row_count * top_count)
        onehot = (flat[:, :, None] == jnp.arange(exp_count, dtype=jnp.int32)).astype(jnp.float32)
        below = jnp.tril(jnp.ones((row_count * top_count,) * 2, jnp.float32), -1)
        counts = jnp.einsum("ij,bje->bie", below, onehot)
        slots = jnp.sum(counts * onehot, axis=2).astype(jnp.int32)
        return slots.reshape(-1, row_count, top_count)

    own_target = (routes - z_at) % exp_count * pitch + slots_of(routes)[0]
    slot_ids = jnp.arange(exp_count * pitch, dtype=jnp.int32)
    choose = jnp.sum(
        (own_target[:, :, None] == slot_ids[None, None, :]).astype(jnp.float32), axis=1
    ).astype(jnp.bfloat16)

    cut = channels * 5 // 16
    uppers = [from_x(after(out_proj, halo)[:cut], i) for i in range(1, x_count)]
    partials = [chip_sum] + [from_y(chip_sum, r) for r in range(1, y_count)]
    step_size, load, both = scan_ends(partials, dt_proj, dt_bias[None], rates, xconv, info)
    loads = gathered(after(load, resid_here, *uppers))
    held_proj = after(out_proj, *[part for pair in loads for part in pair])
    lowers = [from_x(held_proj[cut:], i) for i in range(1, x_count)]
    columns = [[out_proj]] + [list(pair) for pair in zip(uppers, lowers)]
    mixed = scan_mix(
        z_one, x_one, loads, step_size, xconv, z_in, both, rates, d_skip[None]
    )
    along_z = [mixed] + [from_z(mixed, r) for r in range(1, z_count)]

    first_row = a_log.shape[1] + 2
    spare = after(jnp.stack([loads[r][0][first_row:] for r in range(z_count)]), mixed)
    spare = spare[:, :4, : top_count * row_count].astype(jnp.float32)
    spare = lax.dynamic_slice_in_dim(
        jnp.concatenate([spare, spare]), (z_count - z_at) % z_count, z_count, 0
    ).reshape(z_count, 4, top_count, row_count)
    all_routes = spare[:, 0].transpose(0, 2, 1).astype(jnp.int32)
    all_gates = (spare[:, 1] + spare[:, 2] + spare[:, 3]).transpose(0, 2, 1)
    z_ids = jnp.arange(z_count, dtype=jnp.int32)[:, None, None]
    target = (all_routes * z_count + z_ids) * pitch + slots_of(all_routes)
    target = target.reshape(z_count * row_count, top_count)
    count = z_count * pitch
    exp_late = after(exp_at, mixed)
    y_at, core_at = exp_late // 2, exp_late % 2

    def picked(core):
        experts = (y_at + jnp.arange(y_count, dtype=jnp.int32)) % y_count * 2 + core
        ids = experts[:, None] * count + jnp.arange(count, dtype=jnp.int32)[None, :]
        same = target[None, :, :] == ids.reshape(-1)[:, None, None]
        return jnp.sum(same.astype(jnp.float32), axis=2).astype(jnp.bfloat16)

    here_ids = exp_at * z_count * pitch + jnp.arange(z_count * pitch, dtype=jnp.int32)
    here = target[None, :, :] == here_ids[:, None, None]
    gate_here = jnp.sum(
        jnp.where(here, all_gates.reshape(1, z_count * row_count, top_count), 0.0), axis=(1, 2)
    )[:, None]
    first_here = jnp.sum(here[:, :, 0].astype(jnp.float32), axis=1)[:, None]

    keep, send = out_product(
        z_one, x_one, e_one, picked(core_at), picked(1 - core_at), resid_here, along_z, columns
    )
    over_chip = keep.astype(jnp.float32) + other_core(send).astype(jnp.float32)
    over_chip = over_chip.reshape(y_count, count, feature_slice)
    rows_here = over_chip[0]
    for r in range(1, y_count):
        arrived = from_y(over_chip[r].astype(jnp.bfloat16), y_count - r)
        rows_here = rows_here + arrived.astype(jnp.float32)
    rows_here = rows_here.astype(jnp.bfloat16)

    chunks = gathered(rows_here)
    act = expert_hidden(z_one, x_one, chunks, norm_gain, w_gate, w_up)

    by_distance = sorted(range(1, z_count), key=lambda r: abs(r - z_count // 2)) + [0]
    down, crossed, arrivals = {}, {}, []

    def products(turns_now, rows):
        blocks = jnp.stack([(z_at + r) % z_count for r in turns_now]).astype(jnp.int32)
        outs = expert_down(x_one, blocks, x_count, z_count, exp_count * pitch, rows, w_down)
        down.update(zip(turns_now, outs))

    def over_x(r):
        return functools.reduce(
            jnp.add, [p.astype(jnp.float32) for p in [down[r][0]] + crossed[r]]
        )

    products(by_distance[:1], act)
    products(by_distance[1:-1], act)
    for k, r in enumerate(by_distance):
        if r == 0:
            products([0], after(act, *crossed[by_distance[1]]))
        pieces = down[r][1:]
        if r == 0:
            pieces = [after(piece, arrivals[0]) for piece in pieces]
        elif k >= 2:
            pieces = [after(piece, *crossed[by_distance[k - 2]]) for piece in pieces]
        crossed[r] = [from_x(piece, x_count - i) for i, piece in enumerate(pieces, 1)]
        if r:
            arrivals.append(from_z(over_x(r).astype(jnp.bfloat16), z_count - r))
    total = over_x(0)
    for sent in arrivals:
        total = total + sent.astype(jnp.float32)
    expert_out = total.astype(jnp.bfloat16).astype(jnp.float32)
    expert_out = gate_here * expert_out + first_here * rows_here.astype(jnp.float32)
    expert_out = expert_out.astype(jnp.bfloat16)
    pieces = expert_out.reshape(exp_count, pitch, feature_slice)
    back = []
    for k in range(exp_count):
        piece = lax.dynamic_index_in_dim(pieces, (exp_at - k) % exp_count, 0, keepdims=False)
        pairs = [
            (
                (e * x_count + x) * exp_count + (z + k) % exp_count,
                (z * x_count + x) * exp_count + e,
            )
            for z in range(z_count)
            for x in range(x_count)
            for e in range(exp_count)
        ]
        back.append(lax.ppermute(piece, ("seq", "exp"), pairs))
    back = jnp.concatenate(back, axis=0)
    return jnp.dot(choose, back, preferred_element_type=jnp.float32).astype(jnp.bfloat16)


def solution(mesh):
    return jax.shard_map(
        per_device,
        mesh=mesh,
        in_specs=(
            P("seq", "exp"),
            P("seq", "exp"),
            P(None, "exp"),
            P("exp"),
            P("exp", None),
            P(None, "exp"),
            P("exp"),
            P("exp", None),
            P("exp"),
            P("exp", "seq"),
            P("seq", "exp"),
            P(),
            P("seq", None),
            P("seq", None),
            P("exp", None, "seq"),
            P("exp", None, "seq"),
            P("exp", "seq", None),
        ),
        out_specs=P("seq", "exp"),
        check_vma=False,
    )
```
